32 devices in a mesh: dp: 4 (over z), expert: 8 (over y, x, core).
Axes of the slice: x: 2, y: 2, z: 4, core: 2. Of those that a mesh axis runs over, the one named last changes fastest.
Arguments:
- tokens_in: bfloat16 [64, 1024, 768], P(('dp', 'expert')), may hold values from -6 to 6
- buckets: int32 [64, 1024], P(('dp', 'expert')), may hold values from 0 to 7, as said below
- ln1_gain: float32 [768], replicated, may hold values from 0.5 to 1.5
- ln1_bias: float32 [768], replicated, may hold values from -1.5 to 1.5
- w_qkv: bfloat16 [768, 2304], P('dp'), may hold values from -0.21875 to 0.21875
- w_out: bfloat16 [768, 768], P('dp'), may hold values from -0.875 to 0.875
- ln2_gain: float32 [768], replicated, may hold values from 0.5 to 1.5
- ln2_bias: float32 [768], replicated, may hold values from -1.5 to 1.5
- w_in: bfloat16 [8, 768, 3072], P('expert'), may hold values from -0.21875 to 0.21875
- w_down: bfloat16 [8, 3072, 768], P('expert'), may hold values from -0.109375 to 0.109375
- cotangent: bfloat16 [64, 1024, 768], P(('dp', 'expert')), may hold values from -6 to 6
Outputs:
- block_out: float32 [64, 1024, 768], P(('dp', 'expert'))
- grad_input: float32 [64, 1024, 768], P(('dp', 'expert'))
- grad_ln1_gain: float32 [768], P('dp')
- grad_ln1_bias: float32 [768], P('dp')
- grad_w_qkv: float32 [768, 2304], P('dp')
- grad_w_out: float32 [768, 768], P('dp')
- grad_ln2_gain: float32 [768], P('dp')
- grad_ln2_bias: float32 [768], P('dp')
- grad_w_in: float32 [8, 768, 3072], P('expert', None, 'dp')
- grad_w_down: float32 [8, 3072, 768], P('expert', 'dp')
The draws below stay inside these ranges and needn't reach their ends.
Inputs may be any that keep to these rules, and one draw needn't show every extreme that they name: `buckets`: within the 1024 tokens of one sequence no bucket is named more than 160 times, and in every draw some bucket (which one may differ from sequence to sequence) is named exactly 160 times in each sequence.
All inputs are finite; a program needn't handle non-finite values.
Results may differ from the reference program's by a relative error of at most 0.019.
Values may be sent and summed in bfloat16 or wider, within the bound.
A program may use at most 384 MiB of HBM per device.

```python
import math
from functools import partial
import jax
import jax.numpy as jnp
from jax import lax

D = 768
H = 12
FF = 3072
LEN = 1024
EXPERT_COUNT = 8
SEQS = 64
EXPERT_CAPACITY = 160


def draw_buckets(key, part):
    key = jax.random.fold_in(key, 11)
    popular_expert_key, extra_score_key, selection_key = jax.random.split(key, 3)
    preferred_expert = jax.random.randint(popular_expert_key, (), 0, EXPERT_COUNT)
    extra_score = jax.random.randint(extra_score_key, (EXPERT_COUNT,), 0, 4)
    extra_score = jnp.where(jnp.arange(EXPERT_COUNT) == preferred_expert, 8, extra_score)
    contender_expert = jnp.repeat(jnp.arange(EXPERT_COUNT, dtype=jnp.int32), EXPERT_CAPACITY)

    def one_sequence(seq_key):
        tie_key, order_key = jax.random.split(seq_key)
        tiebreak_noise = jax.random.permutation(tie_key, EXPERT_COUNT * EXPERT_CAPACITY)
        expert_ranking = extra_score[contender_expert] * (EXPERT_COUNT * EXPERT_CAPACITY) + tiebreak_noise
        chosen = lax.top_k(expert_ranking, LEN)[1]
        picked = contender_expert[chosen]
        return picked[jax.random.permutation(order_key, LEN)]
    return jax.vmap(one_sequence)(jax.random.split(selection_key, SEQS)).astype(jnp.int32)


def block_scale(own_key, shape, cuts, least, top_value):
    gain = 1.0
    for axis_at, parts in cuts:
        draws = jax.random.uniform(jax.random.fold_in(jax.random.fold_in(own_key, 6), axis_at), (parts,), jnp.float32, least / len(cuts), top_value / len(cuts))
        gain = gain * jnp.repeat(jnp.exp(draws), shape[axis_at] // parts).reshape((-1,) + (1,) * (len(shape) - 1 - axis_at))
    return gain


def noise(key, dims, scale, limit, pieces=(), held_as=jnp.bfloat16):
    factor_of = block_scale(key, dims, pieces, -0.22, 0.18) if pieces else 1.0
    entries = jax.random.normal(key, dims, jnp.float32) * scale * factor_of
    return jnp.minimum(jnp.maximum(entries, -limit), limit).astype(held_as)


def setup_inputs(seed: int = 0) -> dict:
    seeds = jax.random.split(jax.random.key(seed), 12)
    tokens_in = noise(seeds[0], (SEQS, LEN, D), 1.0, 6.0, ((0, 32),))
    buckets = draw_buckets(jax.random.fold_in(seeds[11], 71), 0)
    ln1_gain = jnp.clip(1.0 + 0.1 * jax.random.normal(seeds[2], (D,), jnp.float32), 0.5, 1.5)
    ln1_bias = noise(seeds[3], (D,), 0.3, 1.5, (), jnp.float32)
    w_qkv = noise(seeds[4], (D, 3 * D), D ** -0.5, 0.21875, ((0, 4),))
    w_out = noise(seeds[5], (D, D), (D // 16) ** -0.5, 0.875, ((0, 4),))
    ln2_gain = jnp.clip(1.0 + 0.1 * jax.random.normal(seeds[6], (D,), jnp.float32), 0.5, 1.5)
    ln2_bias = noise(seeds[7], (D,), 0.3, 1.5, (), jnp.float32)
    w_in = noise(seeds[8], (EXPERT_COUNT, D, FF), D ** -0.5, 0.21875, ((0, 8),))
    w_down = noise(seeds[9], (EXPERT_COUNT, FF, D), FF ** -0.5, 0.109375, ((0, 8),))
    cotangent = noise(seeds[10], (SEQS, LEN, D), 1.0, 6.0, ((0, 32),))
    return dict(tokens_in=tokens_in, buckets=buckets, ln1_gain=ln1_gain, ln1_bias=ln1_bias, w_qkv=w_qkv, w_out=w_out, ln2_gain=ln2_gain, ln2_bias=ln2_bias, w_in=w_in, w_down=w_down, cotangent=cotangent)


@jax.custom_vjp
def low(v):
    return lax.optimization_barrier(v.astype(jnp.bfloat16)).astype(jnp.float32)

@jax.custom_vjp
def low_back(v):
    return v

def low_keep(v):
    return (low(v), None)

def low_pass(kept, grad):
    return (grad,)

def back_keep(v):
    return (v, None)

def back_low(kept, grad):
    return (low(grad),)
low.defvjp(low_keep, low_pass)
low_back.defvjp(back_keep, back_low)
epsilon = 1e-05
neg_large = -1e+30

def layer_norm(values, gain_row, offset):
    centre = lax.optimization_barrier(jnp.mean(values, axis=-1, keepdims=True))
    shifted = values - centre
    spread = lax.optimization_barrier(jnp.mean(shifted * shifted, axis=-1, keepdims=True))
    return shifted * lax.rsqrt(spread + epsilon) * gain_row + offset

def slot_table(bucket_row, experts, capacity):
    length = bucket_row.shape[0]
    onehot = (bucket_row[:, None] == jnp.arange(experts, dtype=jnp.int32)[None, :]).astype(jnp.int32)
    expert_ranking = lax.optimization_barrier(jnp.sum(jnp.cumsum(onehot, axis=0) * onehot, axis=1)) - 1
    slot_of = (bucket_row * capacity + expert_ranking).astype(jnp.int32)
    owner_of = jnp.full((experts * capacity,), length, jnp.int32).at[slot_of].set(jnp.arange(length, dtype=jnp.int32))
    return (slot_of, owner_of)

def forward_group(params, x_group, bucket_group):
    ln1_gain, ln1_bias, w_qkv, w_out, ln2_gain, ln2_bias, w_in, w_down = params
    highest = lax.Precision.HIGHEST
    seq_count, length, width = x_group.shape
    head_size = width // H
    normed_low = low(layer_norm(x_group, ln1_gain, ln1_bias))
    qkv_rows = low(low_back(jnp.einsum('gld,de->gle', normed_low, w_qkv, precision=highest)))
    split_qkv = qkv_rows.reshape(seq_count, length, 3, H, head_size)
    scores = low_back(jnp.einsum('gqhd,gkhd->ghqk', split_qkv[:, :, 0], split_qkv[:, :, 1], precision=highest) * head_size ** (-0.5))
    future = jnp.arange(length, dtype=jnp.int32)[None, :] > jnp.arange(length, dtype=jnp.int32)[:, None]
    scores = jnp.where(future[None, None], neg_large, scores)
    weights = low(jax.nn.softmax(scores, axis=-1))
    mixed_out = jnp.einsum('ghqk,gkhd->gqhd', weights, split_qkv[:, :, 2], precision=highest).reshape(seq_count, length, width)
    mixed_low = low(low_back(mixed_out))
    after_attn = x_group + low_back(jnp.einsum('gld,de->gle', mixed_low, w_out, precision=highest))
    tokens_low = low(low_back(layer_norm(after_attn, ln2_gain, ln2_bias)))
    slot_of, owner_of = jax.vmap(partial(slot_table, experts=EXPERT_COUNT, capacity=EXPERT_CAPACITY))(bucket_group)
    padded = jnp.concatenate([tokens_low, jnp.zeros((seq_count, 1, width), jnp.float32)], axis=1)
    dispatched = jnp.take_along_axis(padded, owner_of[:, :, None], axis=1).reshape(seq_count, EXPERT_COUNT, EXPERT_CAPACITY, width)
    hidden_pre = low_back(jnp.einsum('gecd,edf->gecf', dispatched, w_in, precision=highest))
    hidden_act = low(jax.nn.gelu(hidden_pre))
    expert_out = low(jnp.einsum('gecf,efd->gecd', hidden_act, w_down, precision=highest)).reshape(seq_count, EXPERT_COUNT * EXPERT_CAPACITY, width)
    returned = jnp.take_along_axis(expert_out, slot_of[:, :, None], axis=1)
    return after_attn + returned

def reference(tokens_in, buckets, ln1_gain, ln1_bias, w_qkv, w_out, ln2_gain, ln2_bias, w_in, w_down, cotangent):
    params = tuple((array_in.astype(jnp.float32) for array_in in (ln1_gain, ln1_bias, w_qkv, w_out, ln2_gain, ln2_bias, w_in, w_down)))
    group_size = math.gcd(SEQS, max(1, 2048 // LEN))
    x_groups = tokens_in.astype(jnp.float32).reshape(SEQS // group_size, group_size, LEN, D)
    bucket_groups = buckets.reshape(SEQS // group_size, group_size, LEN)
    checked = jax.checkpoint(forward_group)

    def whole(param_set, inputs):
        return lax.map(lambda pair_item: checked(param_set, pair_item[0], pair_item[1]), (inputs, bucket_groups))
    result, pullback = jax.vjp(whole, params, x_groups)
    grad_params, grad_inputs = pullback(cotangent.astype(jnp.float32).reshape(result.shape))
    return (result.reshape(SEQS, LEN, D), grad_inputs.reshape(SEQS, LEN, D), grad_params[0], grad_params[1], grad_params[2], grad_params[3], grad_params[4], grad_params[5], grad_params[6], grad_params[7])
```

```python
import functools

import jax
import jax.numpy as jnp
from jax import lax
from jax.experimental import pallas as pl
from jax.experimental.pallas import tpu as pltpu
from jax.sharding import PartitionSpec as P

HEADS = 12
EPS = 1e-5
NEG = -1e30
bf16 = jnp.bfloat16
f32 = jnp.float32
NN = (((1,), (0,)), ((), ()))
NT = (((1,), (1,)), ((), ()))
TN = (((0,), (0,)), ((), ()))
GELU_A = 0.7978845608028654
GELU_B = 0.044715
BLK = 256
FFT = 256


def dot(a, b, dims=NN):
    return lax.dot_general(a, b, dims, preferred_element_type=f32)


def params(mib=56):
    return pltpu.CompilerParams(vmem_limit_bytes=mib << 20)


def cost(flops, nbytes, trans=0):
    return pl.CostEstimate(flops=int(flops), bytes_accessed=int(nbytes), transcendentals=int(trans))


def sds(shape, dtype):
    return jax.ShapeDtypeStruct(shape, dtype)


VM = pl.BlockSpec(memory_space=pltpu.VMEM)


def norm_parts(v):
    centre = jnp.mean(v, axis=-1, keepdims=True)
    shifted = v - centre
    spread = jnp.mean(shifted * shifted, axis=-1, keepdims=True)
    r = lax.rsqrt(spread + EPS)
    return shifted * r, r


def qkv_body(x_ref, g_ref, b_ref, w_ref, o_ref):
    hat, _ = norm_parts(x_ref[0].astype(f32))
    low = (hat * g_ref[...] + b_ref[...]).astype(bf16)
    o_ref[0] = dot(low, w_ref[...]).astype(bf16)


def qkv_call(x, gain, bias, w):
    n, length, width = x.shape
    triple = w.shape[1]
    rows = min(512, length)
    row = pl.BlockSpec((1, width), lambda s, r: (0, 0))
    return pl.pallas_call(
        qkv_body,
        grid=(n, length // rows),
        in_specs=[
            pl.BlockSpec((1, rows, width), lambda s, r: (s, r, 0)),
            row,
            row,
            pl.BlockSpec((width, triple), lambda s, r: (0, 0)),
        ],
        out_specs=pl.BlockSpec((1, rows, triple), lambda s, r: (s, r, 0)),
        out_shape=sds((n, length, triple), bf16),
        compiler_params=params(),
        cost_estimate=cost(2 * n * length * width * triple, n * length * (width + triple) * 2),
    )(x, gain.reshape(1, -1), bias.reshape(1, -1), w)


def attn_fwd_body(q_ref, k_ref, v_ref, o_ref, lse_ref, *, blk, hs, scale, depth):
    length = q_ref.shape[1]
    lane = lax.broadcasted_iota(jnp.int32, (1, 2 * hs), 1) // hs
    v_t = v_ref[0].T
    keys = k_ref[0]
    kh = [jnp.where(lane == h, keys, jnp.zeros_like(keys)) for h in range(2)]
    ones = jnp.ones((16, length), bf16)
    vh = [jnp.concatenate([v_t[h * hs : (h + 1) * hs], ones], axis=0) for h in range(2)]
    future = lax.broadcasted_iota(jnp.int32, (blk, blk), 0) > lax.broadcasted_iota(
        jnp.int32, (blk, blk), 1
    )
    tasks = [(i, h) for i in range(length // blk) for h in range(2)]

    def score(task):
        i, h = task
        top = (i + 1) * blk
        q = q_ref[0, i * blk : top, :] * jnp.asarray(scale, bf16)
        s = dot(kh[h][:top], q, NT)
        diag = jnp.where(future, NEG, s[i * blk :])
        s = jnp.concatenate([s[: i * blk], diag], axis=0) if i else diag
        return s, jnp.max(s, axis=0, keepdims=True)

    queue = [score(t) for t in tasks[:depth]]
    done = {}
    for at, task in enumerate(tasks):
        if at + depth < len(tasks):
            queue.append(score(tasks[at + depth]))
        s, largest = queue.pop(0)
        i, h = task
        top = (i + 1) * blk
        o = dot(vh[h][:, :top], jnp.exp(s - largest).astype(bf16))
        total = o[hs : hs + 1]
        done[task] = o[:hs] * (1.0 / total)
        lse_ref[0, 0, h : h + 1, i * blk : top] = largest + jnp.log(total)
        if h == 1:
            both = jnp.concatenate([done[(i, 0)], done[(i, 1)]], axis=0)
            o_ref[0, i * blk : top, :] = both.T.astype(bf16)


def attn_fwd_call(qkv, heads):
    n, length, triple = qkv.shape
    width = triple // 3
    hs = width // heads
    pairs = heads // 2
    blk = min(BLK, length)

    def spec(o):
        return pl.BlockSpec((1, length, 2 * hs), lambda s, p, o=o: (s, 0, o * pairs + p))

    half = n * heads * length * length // 2
    return pl.pallas_call(
        functools.partial(attn_fwd_body, blk=blk, hs=hs, scale=hs**-0.5, depth=3),
        grid=(n, pairs),
        in_specs=[spec(0), spec(1), spec(2)],
        out_specs=[spec(0), pl.BlockSpec((1, 1, 2, length), lambda s, p: (s, p, 0, 0))],
        out_shape=[sds((n, length, width), bf16), sds((n, pairs, 2, length), f32)],
        compiler_params=params(48),
        cost_estimate=cost(half * 2 * 2 * 256, n * length * width * 8, half),
    )(qkv, qkv, qkv)


def attn_bwd_body(
    q_ref, k_ref, v_ref, o_ref, do_ref, lse_ref, dq_ref, dk_ref, dv_ref, dqa, doa, *, blk, hs, scale, depth
):
    length = q_ref.shape[1]
    n = length // blk
    lanes = lax.broadcasted_iota(jnp.int32, (1, 2 * hs), 1)
    lane = lanes // hs
    spot = lanes % hs
    keys = k_ref[0]
    vals = v_ref[0]
    k_t = (keys * jnp.asarray(scale, bf16)).T
    kh = [jnp.where(lane == h, keys, jnp.zeros_like(keys)) for h in range(2)]
    vh = [
        jnp.where(lane == h, vals, jnp.where(spot < 2, jnp.ones_like(vals), jnp.zeros_like(vals)))
        for h in range(2)
    ]
    future = lax.broadcasted_iota(jnp.int32, (blk, blk), 0) > lax.broadcasted_iota(
        jnp.int32, (blk, blk), 1
    )
    q = q_ref[0] * jnp.asarray(scale, bf16)
    do = do_ref[0]
    prod = do.astype(f32) * o_ref[0].astype(f32)
    for h in range(2):
        inside = lane == h
        inner = -jnp.sum(jnp.where(inside, prod, 0.0), axis=1, keepdims=True)
        high = inner.astype(bf16)
        rest = (inner - high.astype(f32)).astype(bf16)
        doa[h] = jnp.where(
            inside,
            do,
            jnp.where(spot == 0, high, jnp.where(spot == 1, rest, jnp.zeros_like(high))),
        )
    tasks = [(j, h) for j in range(n) for h in range(2)]

    def score(task):
        j, h = task
        a = j * blk
        return (
            dot(kh[h][a : a + blk], q[a:], NT),
            dot(vh[h][a : a + blk], doa[h, a:], NT),
        )

    queue = [score(t) for t in tasks[:depth]]
    kept = None
    for at, task in enumerate(tasks):
        if at + depth < len(tasks):
            queue.append(score(tasks[at + depth]))
        s, dp = queue.pop(0)
        j, h = task
        a = j * blk
        p = jnp.exp(s - lse_ref[0, 0, h : h + 1, a:])
        diag = jnp.where(future, 0.0, p[:, :blk])
        p = jnp.concatenate([diag, p[:, blk:]], axis=1) if j < n - 1 else diag
        ds = (p * dp).astype(bf16)
        dv = dot(p.astype(bf16), do[a:])
        dk = dot(ds, q[a:])
        dq = dot(k_t[h * hs : (h + 1) * hs, a : a + blk], ds)
        if j == 0:
            dqa[h * hs : (h + 1) * hs, :] = dq
        else:
            dqa[h * hs : (h + 1) * hs, a:] += dq
        if h == 0:
            kept = (dk, dv)
        else:
            dk_ref[0, a : a + blk, :] = jnp.where(lane == 0, kept[0], dk).astype(bf16)
            dv_ref[0, a : a + blk, :] = jnp.where(lane == 0, kept[1], dv).astype(bf16)
            dq_ref[0, a : a + blk, :] = dqa[:, a : a + blk].T.astype(bf16)


def attn_bwd_call(qkv, o, do, lse, heads):
    n, length, triple = qkv.shape
    width = triple // 3
    hs = width // heads
    pairs = heads // 2
    blk = min(BLK, length)

    def spec(o):
        return pl.BlockSpec((1, length, 2 * hs), lambda s, p, o=o: (s, 0, o * pairs + p))

    half = n * heads * length * length // 2
    return pl.pallas_call(
        functools.partial(attn_bwd_body, blk=blk, hs=hs, scale=hs**-0.5, depth=2),
        grid=(n, pairs),
        in_specs=[spec(0), spec(1), spec(2), spec(0), spec(0)]
        + [pl.BlockSpec((1, 1, 2, length), lambda s, p: (s, p, 0, 0))],
        out_specs=[spec(0)] * 3,
        out_shape=[sds((n, length, width), bf16)] * 3,
        scratch_shapes=[
            pltpu.VMEM((2 * hs, length), f32),
            pltpu.VMEM((2, length, 2 * hs), bf16),
        ],
        compiler_params=params(48),
        cost_estimate=cost(half * 5 * 2 * 256, n * length * width * 16, half),
    )(qkv, qkv, qkv, o, do, lse)


def slot_chunk(total):
    return 256 if total % 256 == 0 else total


def place_rows(rows, slot_row, out_ref):
    total = out_ref.shape[0]
    step = slot_chunk(total)
    length = rows.shape[0]
    base = lax.broadcasted_iota(jnp.int32, (step, length), 0)
    for at in range(0, total, step):
        hot = jnp.where(base + at == slot_row, 1.0, 0.0).astype(bf16)
        out_ref[at : at + step, :] = dot(hot, rows).astype(bf16)


def take_rows(slots, slot_col):
    total = slots.shape[0]
    at = lax.broadcasted_iota(jnp.int32, (slot_col.shape[0], total), 1)
    return dot(jnp.where(at == slot_col, 1.0, 0.0).astype(bf16), slots)


def send_body(rows_ref, slot_ref, out_ref):
    place_rows(rows_ref[...], slot_ref[...], out_ref)


def send_call(rows, slot_row, total):
    length, width = rows.shape
    return pl.pallas_call(
        send_body,
        in_specs=[VM, VM],
        out_specs=VM,
        out_shape=sds((total, width), bf16),
        compiler_params=params(32),
        cost_estimate=cost(2 * length * total * width, (length + total) * width * 2),
    )(rows, slot_row)


def out_body(x_ref, mixed_ref, w_ref, g_ref, b_ref, slot_ref, after_ref, sent_ref, toks):
    length = x_ref.shape[0]
    blk = min(BLK, length)
    for a in range(0, length, blk):
        rows = slice(a, a + blk)
        after = x_ref[rows].astype(f32) + dot(mixed_ref[rows], w_ref[...])
        after_ref[rows] = after
        hat, _ = norm_parts(after)
        toks[rows] = (hat * g_ref[...] + b_ref[...]).astype(bf16)
    place_rows(toks[...], slot_ref[...], sent_ref)


def out_call(x, mixed, w, gain, bias, slot_row, total):
    length, width = x.shape
    return pl.pallas_call(
        out_body,
        in_specs=[VM] * 6,
        out_specs=[VM] * 2,
        out_shape=[sds((length, width), f32), sds((total, width), bf16)],
        scratch_shapes=[pltpu.VMEM((length, width), bf16)],
        compiler_params=params(40),
        cost_estimate=cost(2 * length * width * (width + total), length * width * 12),
    )(x, mixed, w, gain.reshape(1, -1), bias.reshape(1, -1), slot_row)


def add_back_body(after_ref, back_ref, slot_ref, out_ref):
    length = after_ref.shape[0]
    blk = min(BLK, length)
    for a in range(0, length, blk):
        rows = slice(a, a + blk)
        out_ref[rows] = after_ref[rows] + take_rows(back_ref[...], slot_ref[rows])


def add_back_call(after, back, slot_col):
    length, width = after.shape
    total = back.shape[0]
    return pl.pallas_call(
        add_back_body,
        in_specs=[VM] * 3,
        out_specs=VM,
        out_shape=sds((length, width), f32),
        compiler_params=params(40),
        cost_estimate=cost(2 * length * width * total, length * width * 12),
    )(after, back, slot_col)


def gelu_parts(pre):
    sq = pre * pre
    half = 0.5 + 0.5 * jnp.tanh(pre * (GELU_A + (GELU_A * GELU_B) * sq))
    act = pre * half
    slope = half + (act - act * half) * (2 * GELU_A + (6 * GELU_A * GELU_B) * sq)
    return act, slope


def hidden_rows(rows_ref, cot_ref, w_in, w_down, act_ref, gpre_ref, use=None):
    total = rows_ref.shape[0]
    step = slot_chunk(total)
    starts = list(range(0, total, step))

    def first(a):
        return dot(rows_ref[a : a + step], w_in), dot(cot_ref[a : a + step], w_down, NT)

    ahead = first(starts[0])
    for at, a in enumerate(starts):
        pre, gact = ahead
        if at + 1 < len(starts):
            ahead = first(starts[at + 1])
        act, slope = gelu_parts(pre)
        act_low = act.astype(bf16)
        gpre_low = (gact * slope).astype(bf16)
        act_ref[0, a : a + step] = act_low
        gpre_ref[0, a : a + step] = gpre_low
        if use is not None:
            use(a, a + step, act_low, gpre_low)


def join_cols(refs):
    return jnp.concatenate([r[...] for r in refs], axis=1)


def join_rows(refs):
    return jnp.concatenate([r[...] for r in refs], axis=0)


def expert_a_body(*refs, nz):
    rows_ref, cot_ref = refs[:2]
    w_in = join_cols(refs[2 : 2 + nz])
    w_down = join_rows(refs[2 + nz : 2 + 2 * nz])
    act_ref, gpre_ref, out_ref, gtok_ref, acc_out, acc_tok = refs[2 + 2 * nz :]
    c = pl.program_id(0)
    last = pl.num_programs(0) - 1

    @pl.when(c == 0)
    def _():
        acc_out[...] = jnp.zeros_like(acc_out)
        acc_tok[...] = jnp.zeros_like(acc_tok)

    def use(a, b, act_low, gpre_low):
        acc_out[a:b] += dot(act_low, w_down)
        acc_tok[a:b] += dot(gpre_low, w_in, NT)

    hidden_rows(rows_ref, cot_ref, w_in, w_down, act_ref, gpre_ref, use)

    @pl.when(c == last)
    def _():
        out_ref[...] = acc_out[...].astype(bf16)
        gtok_ref[...] = acc_tok[...].astype(bf16)


def weight_specs(width, hidden, nz, first=0):
    per = hidden // (nz * FFT)
    ins = [
        pl.BlockSpec((width, FFT), lambda c, z=z: (0, z * per + c + first)) for z in range(nz)
    ]
    downs = [
        pl.BlockSpec((FFT, width), lambda c, z=z: (z * per + c + first, 0)) for z in range(nz)
    ]
    return ins + downs


def expert_a_call(rows, cot, w_in, w_down, nz):
    total, width = rows.shape
    hidden = w_in.shape[1]
    chunks = hidden // (nz * FFT)
    tile = nz * FFT
    keep = pl.BlockSpec((total, width), lambda c: (0, 0))
    mid = pl.BlockSpec((1, total, tile), lambda c: (c, 0, 0))
    return pl.pallas_call(
        functools.partial(expert_a_body, nz=nz),
        grid=(chunks,),
        in_specs=[keep, keep] + weight_specs(width, hidden, nz),
        out_specs=[mid, mid, keep, keep],
        out_shape=[sds((chunks, total, tile), bf16)] * 2 + [sds((total, width), bf16)] * 2,
        scratch_shapes=[pltpu.VMEM((total, width), f32)] * 2,
        compiler_params=params(60),
        cost_estimate=cost(8 * total * width * hidden, 30 << 20),
    )(rows, cot, *([w_in] * nz), *([w_down] * nz))


def expert_b_body(*refs, nz):
    rows_a, cot_a, act_a, gpre_a, rows_b, cot_b = refs[:6]
    w_in = join_cols(refs[6 : 6 + nz])
    w_down = join_rows(refs[6 + nz : 6 + 2 * nz])
    act_b, gpre_b, gdown_ref, gin_ref = refs[6 + 2 * nz :]
    hidden_rows(rows_b, cot_b, w_in, w_down, act_b, gpre_b)
    for z in range(nz):
        cols = slice(z * FFT, (z + 1) * FFT)
        gdown = dot(act_a[0, :, cols], cot_a[...], TN) + dot(act_b[0, :, cols], cot_b[...], TN)
        gdown_ref[z, 0] = gdown.astype(bf16)
        gin = dot(rows_a[...], gpre_a[0, :, cols], TN) + dot(rows_b[...], gpre_b[0, :, cols], TN)
        gin_ref[z, 0] = gin.astype(bf16)


def expert_b_call(rows_a, cot_a, act_a, gpre_a, rows_b, cot_b, w_in, w_down, nz, first, count):
    total, width = rows_a.shape
    hidden = w_in.shape[1]
    tile = nz * FFT
    keep = pl.BlockSpec((total, width), lambda c: (0, 0))
    mid = pl.BlockSpec((1, total, tile), lambda c: (c + first, 0, 0))
    mid_out = pl.BlockSpec((1, total, tile), lambda c: (c, 0, 0))
    return pl.pallas_call(
        functools.partial(expert_b_body, nz=nz),
        grid=(count,),
        in_specs=[keep, keep, mid, mid, keep, keep] + weight_specs(width, hidden, nz, first),
        out_specs=[
            mid_out,
            mid_out,
            pl.BlockSpec((nz, 1, FFT, width), lambda c: (0, c, 0, 0)),
            pl.BlockSpec((nz, 1, width, FFT), lambda c: (0, c, 0, 0)),
        ],
        out_shape=[
            sds((count, total, tile), bf16),
            sds((count, total, tile), bf16),
            sds((nz, count, FFT, width), bf16),
            sds((nz, count, width, FFT), bf16),
        ],
        compiler_params=params(60),
        cost_estimate=cost(12 * total * width * tile * count, 30 << 20),
    )(rows_a, cot_a, act_a, gpre_a, rows_b, cot_b, *([w_in] * nz), *([w_down] * nz))


def expert_c_body(*refs, nz, parts, dims):
    mids = refs[:parts]
    w_refs = refs[parts : parts + nz]
    out_ref, acc = refs[parts + nz :]
    w = join_cols(w_refs) if dims is NT else join_rows(w_refs)
    c = pl.program_id(0)
    total = acc.shape[0]
    step = slot_chunk(total)
    counts = [m.shape[0] for m in mids]
    lo = 0
    for m, k in zip(mids, counts):

        @pl.when((c >= lo) & (c < lo + k))
        def _(m=m, lo=lo):
            for a in range(0, total, step):
                term = dot(m[c - lo, a : a + step], w, dims)
                if lo == 0:
                    acc[a : a + step] = jnp.where(c == 0, term, acc[a : a + step] + term)
                else:
                    acc[a : a + step] += term

        lo += k

    @pl.when(c == pl.num_programs(0) - 1)
    def _():
        out_ref[...] = acc[...].astype(bf16)


def expert_c_call(mids, w, nz, dims):
    total, tile = mids[0].shape[1:]
    hidden = tile * sum(m.shape[0] for m in mids)
    width = w.shape[0] if dims is NT else w.shape[1]
    chunks = hidden // tile
    specs = weight_specs(width, hidden, nz)
    specs = specs[:nz] if dims is NT else specs[nz:]
    return pl.pallas_call(
        functools.partial(expert_c_body, nz=nz, parts=len(mids), dims=dims),
        grid=(chunks,),
        in_specs=[pl.BlockSpec(m.shape, lambda c: (0, 0, 0)) for m in mids] + specs,
        out_specs=pl.BlockSpec((total, width), lambda c: (0, 0)),
        out_shape=sds((total, width), bf16),
        scratch_shapes=[pltpu.VMEM((total, width), f32)],
        compiler_params=params(60),
        cost_estimate=cost(2 * total * width * hidden, 14 << 20),
    )(*mids, *([w] * nz))


def norm_two_body(
    back_ref, slot_ref, after_ref, cot_ref, mixed_ref, w_ref, g_ref, seed_ref, ga_ref, gmix_ref, gw_ref, sums_ref, low
):
    length = after_ref.shape[0]
    blk = min(BLK, length)
    gain_sum = 0.0
    bias_sum = 0.0
    for a in range(0, length, blk):
        rows = slice(a, a + blk)
        gt = take_rows(back_ref[...], slot_ref[rows])
        hat, r = norm_parts(after_ref[rows])
        gain_sum = gain_sum + jnp.sum(gt * hat, axis=0, keepdims=True)
        bias_sum = bias_sum + jnp.sum(gt, axis=0, keepdims=True)
        s = gt * g_ref[...]
        ga = cot_ref[rows].astype(f32) + r * (
            s
            - jnp.mean(s, axis=-1, keepdims=True)
            - hat * jnp.mean(s * hat, axis=-1, keepdims=True)
        )
        ga_ref[rows] = ga
        ga_low = ga.astype(bf16)
        low[rows] = ga_low
        gmix_ref[rows] = dot(ga_low, w_ref[...], NT).astype(bf16)
    gw_ref[...] = seed_ref[...] + dot(mixed_ref[...], low[...], TN)
    sums_ref[0:1] = gain_sum
    sums_ref[1:2] = bias_sum


def norm_two_call(back, slot_col, after, cot, mixed, w, gain, seed):
    length, width = after.shape
    total = back.shape[0]
    return pl.pallas_call(
        norm_two_body,
        in_specs=[VM] * 8,
        out_specs=[VM] * 4,
        out_shape=[
            sds((length, width), f32),
            sds((length, width), bf16),
            sds((width, width), f32),
            sds((2, width), f32),
        ],
        scratch_shapes=[pltpu.VMEM((length, width), bf16)],
        compiler_params=params(56),
        cost_estimate=cost(2 * length * width * (total + 2 * width), length * width * 20),
    )(back, slot_col, after, cot, mixed, w, gain.reshape(1, -1), seed)


def norm_one_body(
    dq_ref, dk_ref, dv_ref, x_ref, w_ref, g_ref, b_ref, ga_ref, seed_ref, gx_ref, gw_ref, sums_ref, low
):
    length, width = x_ref.shape
    blk = min(BLK, length)
    gain_sum = 0.0
    bias_sum = 0.0
    parts = (dq_ref, dk_ref, dv_ref)
    for a in range(0, length, blk):
        rows = slice(a, a + blk)
        gn = 0.0
        for t, ref in enumerate(parts):
            gn = gn + dot(ref[rows], w_ref[:, t * width : (t + 1) * width], NT)
        hat, r = norm_parts(x_ref[rows].astype(f32))
        low[rows] = (hat * g_ref[...] + b_ref[...]).astype(bf16)
        gain_sum = gain_sum + jnp.sum(gn * hat, axis=0, keepdims=True)
        bias_sum = bias_sum + jnp.sum(gn, axis=0, keepdims=True)
        s = gn * g_ref[...]
        gx_ref[rows] = ga_ref[rows] + r * (
            s
            - jnp.mean(s, axis=-1, keepdims=True)
            - hat * jnp.mean(s * hat, axis=-1, keepdims=True)
        )
    for t, ref in enumerate(parts):
        cols = slice(t * width, (t + 1) * width)
        term = dot(low[...], ref[...], TN)
        if seed_ref is None:
            gw_ref[:, cols] = term.astype(gw_ref.dtype)
        else:
            gw_ref[:, cols] = (seed_ref[:, cols] + term).astype(gw_ref.dtype)
    sums_ref[0:1] = gain_sum
    sums_ref[1:2] = bias_sum


def norm_one_call(dq, dk, dv, x, w, gain, bias, ga, seed):
    length, width = x.shape
    args = [dq, dk, dv, x, w, gain.reshape(1, -1), bias.reshape(1, -1), ga]
    if seed is None:

        def body(*refs):
            norm_one_body(*refs[:8], None, *refs[8:])

        kind = f32
    else:
        args.append(seed)
        body = norm_one_body
        kind = bf16
    return pl.pallas_call(
        body,
        in_specs=[VM] * len(args),
        out_specs=[VM] * 3,
        out_shape=[sds((length, width), f32), sds((width, 3 * width), kind), sds((2, width), f32)],
        scratch_shapes=[pltpu.VMEM((length, width), bf16)],
        compiler_params=params(60),
        cost_estimate=cost(12 * length * width * width, length * width * 30),
    )(*args)


def gather_line(x, axis):
    size = lax.axis_size(axis)
    me = lax.axis_index(axis)
    up = [(i, i + 1) for i in range(size - 1)]
    down = [(i + 1, i) for i in range(size - 1)]
    full = jnp.zeros((size,) + x.shape, x.dtype)
    full = lax.dynamic_update_index_in_dim(full, x, me, 0)
    from_below = from_above = x
    for step in range(1, size):
        from_below = lax.ppermute(from_below, axis, up)
        from_above = lax.ppermute(from_above, axis, down)
        low = jnp.where(me >= step, me - step, me)
        high = jnp.where(me + step < size, me + step, me)
        own = lax.dynamic_index_in_dim(full, me, 0, keepdims=False)
        full = lax.dynamic_update_index_in_dim(
            full, jnp.where(me >= step, from_below, own), low, 0
        )
        full = lax.dynamic_update_index_in_dim(
            full, jnp.where(me + step < size, from_above, own), high, 0
        )
    return full


def exchange(x, experts, capacity):
    parts = x.reshape(experts, capacity, x.shape[-1])
    got = lax.all_to_all(parts, "expert", split_axis=0, concat_axis=0, tiled=True)
    return got.reshape(x.shape)


def on_device(
    tokens_in,
    buckets,
    ln1_gain,
    ln1_bias,
    w_qkv,
    w_out,
    ln2_gain,
    ln2_bias,
    w_in,
    w_down,
    cotangent,
):
    experts = lax.axis_size("expert")
    nz = lax.axis_size("dp")
    seqs, length, width = tokens_in.shape
    capacity = 5 * length // (4 * experts)
    total = experts * capacity
    w_in_local = w_in[0]
    w_down_local = w_down[0]
    hidden = w_in_local.shape[1]
    chunks = hidden // (nz * FFT)

    hot = (buckets[:, None, :] == jnp.arange(experts, dtype=jnp.int32)[None, :, None]).astype(bf16)
    upto = (
        jnp.arange(length, dtype=jnp.int32)[:, None] <= jnp.arange(length, dtype=jnp.int32)[None, :]
    ).astype(bf16)
    count = jnp.einsum("sel,lm->sem", hot, upto, preferred_element_type=f32)
    rank = jnp.sum(count * hot.astype(f32), axis=1).astype(jnp.int32) - 1
    slot = buckets * capacity + rank
    slot_row = slot[:, None, :]
    slot_col = slot[:, :, None]

    full_qkv = lax.all_gather(w_qkv, "dp", axis=0, tiled=True)
    full_out = lax.all_gather(w_out, "dp", axis=0, tiled=True)

    cots = [
        exchange(send_call(cotangent[s], slot_row[s], total), experts, capacity)
        for s in range(seqs)
    ]
    saved = []
    rows = []
    for s in range(seqs):
        qkv = qkv_call(tokens_in[s : s + 1], ln1_gain, ln1_bias, full_qkv)
        mixed, lse = attn_fwd_call(qkv, HEADS)
        after, sent = out_call(
            tokens_in[s], mixed[0], full_out, ln2_gain, ln2_bias, slot_row[s], total
        )
        rows.append(exchange(sent, experts, capacity))
        saved.append((qkv, mixed, lse, after))

    act_a, gpre_a, out_a, gtok_a = expert_a_call(rows[0], cots[0], w_in_local, w_down_local, nz)
    outs = [exchange(out_a, experts, capacity)]
    gtoks = [exchange(gtok_a, experts, capacity)]

    acts, gpres, gdowns, gins = [], [], [], []
    for first, many in ((0, 1), (1, chunks - 1)):
        act_b, gpre_b, gdown, gin = expert_b_call(
            rows[0], cots[0], act_a, gpre_a, rows[1], cots[1], w_in_local, w_down_local, nz, first, many
        )
        acts.append(act_b)
        gpres.append(gpre_b)
        gdowns.append(lax.psum_scatter(gdown, "dp", scatter_dimension=0, tiled=True))
        gins.append(lax.psum_scatter(gin, "dp", scatter_dimension=0, tiled=True))
    gtoks.append(exchange(expert_c_call(gpres, w_in_local, nz, NT), experts, capacity))
    outs.append(exchange(expert_c_call(acts, w_down_local, nz, NN), experts, capacity))

    results = []
    gxs = []
    gw_out = jnp.zeros((width, width), f32)
    gw_qkv = None
    sums = 0.0
    for s in range(seqs):
        qkv, mixed, lse, after = saved[s]
        ga, gmix, gw_out, sums_two = norm_two_call(
            gtoks[s], slot_col[s], after, cotangent[s], mixed[0], full_out, ln2_gain, gw_out
        )
        dq, dk, dv = attn_bwd_call(qkv, mixed, gmix[None], lse, HEADS)
        gx, gw_qkv, sums_one = norm_one_call(
            dq[0], dk[0], dv[0], tokens_in[s], full_qkv, ln1_gain, ln1_bias, ga, gw_qkv
        )
        gxs.append(gx)
        sums = sums + jnp.concatenate([sums_one, sums_two], axis=0)
        results.append(add_back_call(after, outs[s], slot_col[s]))

    both = ("expert", "dp")
    dense = jnp.concatenate([gw_qkv, gw_out.astype(bf16)], axis=1)
    piece = lax.psum_scatter(
        dense.reshape(nz, experts, width // nz // experts, 4 * width).swapaxes(0, 1),
        "expert",
        scatter_dimension=0,
        tiled=True,
    )
    piece = lax.psum_scatter(piece[0], "dp", scatter_dimension=0, tiled=True)
    dense = lax.all_gather(piece, "expert", axis=0, tiled=True).reshape(width // nz, 4 * width)
    dense = dense.astype(f32)
    sums = lax.psum(sums, both)
    mine = lax.dynamic_slice_in_dim(
        sums, lax.axis_index("dp") * (width // nz), width // nz, axis=1
    )
    gdown = jnp.concatenate([g[0] for g in gdowns], axis=0).reshape(1, hidden // nz, width)
    gin = jnp.concatenate([g[0, i] for g in gins for i in range(g.shape[1])], axis=1)[None]
    return (
        jnp.stack(results),
        jnp.stack(gxs),
        mine[0],
        mine[1],
        dense[:, : 3 * width],
        dense[:, 3 * width :],
        mine[2],
        mine[3],
        gin.astype(f32),
        gdown.astype(f32),
    )


def solution(mesh):
    placed = (
        P(("dp", "expert"), None, None),
        P(("dp", "expert"), None),
        P(),
        P(),
        P("dp", None),
        P("dp", None),
        P(),
        P(),
        P("expert", None, None),
        P("expert", None, None),
        P(("dp", "expert"), None, None),
    )
    return jax.shard_map(
        on_device,
        mesh=mesh,
        in_specs=placed,
        out_specs=(
            P(("dp", "expert"), None, None),
            P(("dp", "expert"), None, None),
            P("dp"),
            P("dp"),
            P("dp", None),
            P("dp", None),
            P("dp"),
            P("dp"),
            P("expert", None, "dp"),
            P("expert", "dp", None),
        ),
        check_vma=False,
    )
```

```python
import functools

import jax
import jax.numpy as jnp
from jax import lax
from jax.experimental import pallas as pl
from jax.experimental.pallas import tpu as pltpu
from jax.sharding import PartitionSpec as P

HEADS = 12
EPS = 1e-5
NEG = -1e30
bf16 = jnp.bfloat16
f32 = jnp.float32
NN = (((1,), (0,)), ((), ()))
NT = (((1,), (1,)), ((), ()))
TN = (((0,), (0,)), ((), ()))
GELU_A = 0.7978845608028654
GELU_B = 0.044715
BLK = 256
FFT = 256


def dot(a, b, dims=NN):
    return lax.dot_general(a, b, dims, preferred_element_type=f32)


def params(mib=56):
    return pltpu.CompilerParams(vmem_limit_bytes=mib << 20)


def cost(flops, nbytes, trans=0):
    return pl.CostEstimate(flops=int(flops), bytes_accessed=int(nbytes), transcendentals=int(trans))


def sds(shape, dtype):
    return jax.ShapeDtypeStruct(shape, dtype)


VM = pl.BlockSpec(memory_space=pltpu.VMEM)
ANY = pl.BlockSpec(memory_space=pl.ANY)


def kernel_call(body, in_specs, args, deps=(), **options):
    count = len(args)
    extra = len(deps)

    def wrapped(*refs):
        body(*refs[:count], *refs[count + extra :])

    return pl.pallas_call(wrapped, in_specs=list(in_specs) + [ANY] * extra, **options)(*args, *deps)


def norm_parts(v):
    centre = jnp.mean(v, axis=-1, keepdims=True)
    shifted = v - centre
    spread = jnp.mean(shifted * shifted, axis=-1, keepdims=True)
    r = lax.rsqrt(spread + EPS)
    return shifted * r, r


MESH = pl.DeviceIdType.MESH


def greet(peers):
    barrier = pltpu.get_barrier_semaphore()
    for peer in peers:
        pl.semaphore_signal(barrier, inc=1, device_id=peer, device_id_type=MESH)
    return barrier


def qkv_body(
    x_ref, g_ref, b_ref, wq_ref, wo_ref, qkv_ref, fq_ref, fo_ref, low, acc, up_s, dn_s, core_s, z_r, core_r, loc
):
    nz = lax.axis_size("dp")
    z = lax.axis_index("dp")
    e = lax.axis_index("expert")
    core = e % 2
    seqs, length, width = x_ref.shape
    per = width // nz
    half = per // 2
    above = (jnp.minimum(z + 1, nz - 1), e)
    below = (jnp.maximum(z - 1, 0), e)
    mate = (z, e + 1 - 2 * core)
    full = (fq_ref, fo_ref)

    barrier = pltpu.get_barrier_semaphore()

    @pl.when(z + 1 < nz)
    def _():
        pl.semaphore_signal(barrier, inc=1, device_id=above, device_id_type=MESH)

    @pl.when(z > 0)
    def _():
        pl.semaphore_signal(barrier, inc=1, device_id=below, device_id_type=MESH)

    pl.semaphore_signal(barrier, inc=1, device_id=mate, device_id_type=MESH)

    @pl.when((z + 1 < nz) & (z > 0))
    def _():
        pl.semaphore_wait(barrier, 3)

    @pl.when((z + 1 >= nz) | (z <= 0))
    def _():
        pl.semaphore_wait(barrier, 2)

    def rows_of(ref, p, c):
        return ref.at[pl.ds(pl.multiple_of(p * per + c * half, 16), half)]

    def hop(t, p, c, src, sem, r_sem, peer):
        return pltpu.make_async_remote_copy(
            src_ref=src,
            dst_ref=rows_of(full[t], p, c),
            send_sem=sem.at[t, p],
            recv_sem=r_sem.at[t, p],
            device_id=peer,
            device_id_type=MESH,
        )

    shard = (wq_ref, wo_ref)
    for t in range(2):
        mine = shard[t].at[pl.ds(pl.multiple_of(core * half, 16), half)]

        @pl.when(z + 1 < nz)
        def _(t=t, mine=mine):
            hop(t, z, core, mine, up_s, z_r, above).start()

        @pl.when(z > 0)
        def _(t=t, mine=mine):
            hop(t, z, core, mine, dn_s, z_r, below).start()

    own = [
        pltpu.make_async_copy(
            shard[t], full[t].at[pl.ds(pl.multiple_of(z * per, 16), per)], loc.at[t]
        )
        for t in range(2)
    ]
    for c in own:
        c.start()

    blk = min(BLK, length)
    for s in range(seqs):
        for a in range(0, length, blk):
            hat, _ = norm_parts(x_ref[s, a : a + blk].astype(f32))
            v = (hat * g_ref[...] + b_ref[...]).astype(bf16)
            for p in range(nz):
                low[p, s * length + a : s * length + a + blk] = v[:, p * per : (p + 1) * per]
    total = seqs * length
    step = min(512, length)

    def product(p, first):
        w = fq_ref[pl.ds(pl.multiple_of(p * per, 16), per)]
        for a in range(0, total, step):
            term = dot(low[p, a : a + step], w)
            if first:
                acc[a : a + step] = term
            else:
                acc[a : a + step] += term

    def arrive(t, p, forward, sem, peer):
        hop(t, p, core, rows_of(full[t], p, core), sem, z_r, peer).wait_recv()
        hop(t, p, core, rows_of(full[t], p, core), core_s, core_r, mate).start()

        @pl.when(forward)
        def _():
            hop(t, p, core, rows_of(full[t], p, core), sem, z_r, peer).start()

    def got(t, p):
        hop(t, p, 1 - core, rows_of(full[t], p, 1 - core), core_s, core_r, mate).wait_recv()

    own[0].wait()
    own[1].wait()
    product(z, True)
    for d in range(1, nz):

        @pl.when(z - d >= 0)
        def _(d=d):
            arrive(0, z - d, z + 1 < nz, up_s, above)

        @pl.when(z + d < nz)
        def _(d=d):
            arrive(0, z + d, z > 0, dn_s, below)

        @pl.when(z - d >= 0)
        def _(d=d):
            got(0, z - d)
            product(z - d, False)

        @pl.when(z + d < nz)
        def _(d=d):
            got(0, z + d)
            product(z + d, False)

    for a in range(0, total, step):
        qkv_ref[a // length, a % length : a % length + step] = acc[a : a + step].astype(bf16)
    for d in range(1, nz):

        @pl.when(z - d >= 0)
        def _(d=d):
            arrive(1, z - d, z + 1 < nz, up_s, above)

        @pl.when(z + d < nz)
        def _(d=d):
            arrive(1, z + d, z > 0, dn_s, below)

    for d in range(1, nz):
        for ok, p in ((z - d >= 0, z - d), (z + d < nz, z + d)):

            @pl.when(ok)
            def _(p=p):
                got(1, p)

    for t in range(2):
        mine = shard[t].at[pl.ds(pl.multiple_of(core * half, 16), half)]

        @pl.when(z + 1 < nz)
        def _(t=t, mine=mine):
            hop(t, z, core, mine, up_s, z_r, above).wait_send()

        @pl.when(z > 0)
        def _(t=t, mine=mine):
            hop(t, z, core, mine, dn_s, z_r, below).wait_send()

        for d in range(1, nz):
            for ok, p, more, sem, peer in (
                (z - d >= 0, z - d, z + 1 < nz, up_s, above),
                (z + d < nz, z + d, z > 0, dn_s, below),
            ):

                @pl.when(ok)
                def _(t=t, p=p):
                    hop(t, p, core, rows_of(full[t], p, core), core_s, core_r, mate).wait_send()

                @pl.when(ok & more)
                def _(t=t, p=p, sem=sem, peer=peer):
                    hop(t, p, core, rows_of(full[t], p, core), sem, z_r, peer).wait_send()


def qkv_call(x, gain, bias, wq, wo, nz):
    seqs, length, width = x.shape
    triple = wq.shape[1]
    dma = pltpu.SemaphoreType.DMA
    return pl.pallas_call(
        qkv_body,
        in_specs=[VM] * 5,
        out_specs=[VM] * 3,
        out_shape=[
            sds((seqs, length, triple), bf16),
            sds((width, triple), bf16),
            sds((width, width), bf16),
        ],
        scratch_shapes=[
            pltpu.VMEM((nz, seqs * length, width // nz), bf16),
            pltpu.VMEM((seqs * length, triple), f32),
        ]
        + [dma((2, nz))] * 5
        + [dma((2,))],
        compiler_params=pltpu.CompilerParams(
            vmem_limit_bytes=58 << 20, collective_id=0, has_side_effects=True
        ),
        cost_estimate=cost(2 * seqs * length * width * triple * 4, 30 << 20),
    )(x, gain.reshape(1, -1), bias.reshape(1, -1), wq, wo)


def attn_fwd_body(q_ref, k_ref, v_ref, o_ref, lse_ref, *, blk, hs, scale, depth):
    length = q_ref.shape[1]
    lane = lax.broadcasted_iota(jnp.int32, (1, 2 * hs), 1) // hs
    v_t = v_ref[0].T
    keys = k_ref[0]
    kh = [jnp.where(lane == h, keys, jnp.zeros_like(keys)) for h in range(2)]
    ones = jnp.ones((16, length), bf16)
    vh = [jnp.concatenate([v_t[h * hs : (h + 1) * hs], ones], axis=0) for h in range(2)]
    future = lax.broadcasted_iota(jnp.int32, (blk, blk), 0) > lax.broadcasted_iota(
        jnp.int32, (blk, blk), 1
    )
    tasks = [(i, h) for i in range(length // blk) for h in range(2)]

    def score(task):
        i, h = task
        top = (i + 1) * blk
        q = q_ref[0, i * blk : top, :] * jnp.asarray(scale, bf16)
        s = dot(kh[h][:top], q, NT)
        diag = jnp.where(future, NEG, s[i * blk :])
        s = jnp.concatenate([s[: i * blk], diag], axis=0) if i else diag
        return s, jnp.max(s, axis=0, keepdims=True)

    queue = [score(t) for t in tasks[:depth]]
    done = {}
    for at, task in enumerate(tasks):
        if at + depth < len(tasks):
            queue.append(score(tasks[at + depth]))
        s, largest = queue.pop(0)
        i, h = task
        top = (i + 1) * blk
        o = dot(vh[h][:, :top], jnp.exp(s - largest).astype(bf16))
        total = o[hs : hs + 1]
        done[task] = o[:hs] * (1.0 / total)
        lse_ref[0, 0, h : h + 1, i * blk : top] = largest + jnp.log(total)
        if h == 1:
            both = jnp.concatenate([done[(i, 0)], done[(i, 1)]], axis=0)
            o_ref[0, i * blk : top, :] = both.T.astype(bf16)


def attn_fwd_call(qkv, heads, at, deps=()):
    n, length, triple = 1, *qkv.shape[1:]
    width = triple // 3
    hs = width // heads
    pairs = heads // 2
    blk = min(BLK, length)

    def spec(o, at=0):
        return pl.BlockSpec((1, length, 2 * hs), lambda s, p: (s + at, 0, o * pairs + p))

    half = n * heads * length * length // 2
    return kernel_call(
        functools.partial(attn_fwd_body, blk=blk, hs=hs, scale=hs**-0.5, depth=3),
        args=[qkv, qkv, qkv],
        deps=deps,
        grid=(n, pairs),
        in_specs=[spec(0, at), spec(1, at), spec(2, at)],
        out_specs=[spec(0), pl.BlockSpec((1, 1, 2, length), lambda s, p: (s, p, 0, 0))],
        out_shape=[sds((n, length, width), bf16), sds((n, pairs, 2, length), f32)],
        compiler_params=params(48),
        cost_estimate=cost(half * 2 * 2 * 256, n * length * width * 8, half),
    )


def attn_bwd_body(
    q_ref, k_ref, v_ref, o_ref, do_ref, lse_ref, dq_ref, dk_ref, dv_ref, dqa, doa, *, blk, hs, scale, depth
):
    length = q_ref.shape[1]
    n = length // blk
    lanes = lax.broadcasted_iota(jnp.int32, (1, 2 * hs), 1)
    lane = lanes // hs
    spot = lanes % hs
    keys = k_ref[0]
    vals = v_ref[0]
    k_t = (keys * jnp.asarray(scale, bf16)).T
    kh = [jnp.where(lane == h, keys, jnp.zeros_like(keys)) for h in range(2)]
    vh = [
        jnp.where(lane == h, vals, jnp.where(spot < 2, jnp.ones_like(vals), jnp.zeros_like(vals)))
        for h in range(2)
    ]
    future = lax.broadcasted_iota(jnp.int32, (blk, blk), 0) > lax.broadcasted_iota(
        jnp.int32, (blk, blk), 1
    )
    q = q_ref[0] * jnp.asarray(scale, bf16)
    do = do_ref[0]
    prod = do.astype(f32) * o_ref[0].astype(f32)
    for h in range(2):
        inside = lane == h
        inner = -jnp.sum(jnp.where(inside, prod, 0.0), axis=1, keepdims=True)
        high = inner.astype(bf16)
        rest = (inner - high.astype(f32)).astype(bf16)
        doa[h] = jnp.where(
            inside,
            do,
            jnp.where(spot == 0, high, jnp.where(spot == 1, rest, jnp.zeros_like(high))),
        )
    tasks = [(j, h) for j in range(n) for h in range(2)]

    def score(task):
        j, h = task
        a = j * blk
        return (
            dot(kh[h][a : a + blk], q[a:], NT),
            dot(vh[h][a : a + blk], doa[h, a:], NT),
        )

    queue = [score(t) for t in tasks[:depth]]
    kept = None
    for at, task in enumerate(tasks):
        if at + depth < len(tasks):
            queue.append(score(tasks[at + depth]))
        s, dp = queue.pop(0)
        j, h = task
        a = j * blk
        p = jnp.exp(s - lse_ref[0, 0, h : h + 1, a:])
        diag = jnp.where(future, 0.0, p[:, :blk])
        p = jnp.concatenate([diag, p[:, blk:]], axis=1) if j < n - 1 else diag
        ds = (p * dp).astype(bf16)
        dv = dot(p.astype(bf16), do[a:])
        dk = dot(ds, q[a:])
        dq = dot(k_t[h * hs : (h + 1) * hs, a : a + blk], ds)
        if j == 0:
            dqa[h * hs : (h + 1) * hs, :] = dq
        else:
            dqa[h * hs : (h + 1) * hs, a:] += dq
        if h == 0:
            kept = (dk, dv)
        else:
            dk_ref[0, a : a + blk, :] = jnp.where(lane == 0, kept[0], dk).astype(bf16)
            dv_ref[0, a : a + blk, :] = jnp.where(lane == 0, kept[1], dv).astype(bf16)
            dq_ref[0, a : a + blk, :] = dqa[:, a : a + blk].T.astype(bf16)


def attn_bwd_call(qkv, o, do, lse, heads, at, deps=()):
    n, length, triple = 1, *qkv.shape[1:]
    width = triple // 3
    hs = width // heads
    pairs = heads // 2
    blk = min(BLK, length)

    def spec(o, at=0):
        return pl.BlockSpec((1, length, 2 * hs), lambda s, p: (s + at, 0, o * pairs + p))

    half = n * heads * length * length // 2
    return kernel_call(
        functools.partial(attn_bwd_body, blk=blk, hs=hs, scale=hs**-0.5, depth=2),
        args=[qkv, qkv, qkv, o, do, lse],
        deps=deps,
        grid=(n, pairs),
        in_specs=[spec(0, at), spec(1, at), spec(2, at), spec(0), spec(0)]
        + [pl.BlockSpec((1, 1, 2, length), lambda s, p: (s, p, 0, 0))],
        out_specs=[spec(0)] * 3,
        out_shape=[sds((n, length, width), bf16)] * 3,
        scratch_shapes=[
            pltpu.VMEM((2 * hs, length), f32),
            pltpu.VMEM((2, length, 2 * hs), bf16),
        ],
        compiler_params=params(48),
        cost_estimate=cost(half * 5 * 2 * 256, n * length * width * 16, half),
    )


def slot_chunk(total):
    return 256 if total % 256 == 0 else total


def place_rows(rows, slot_row, out_ref):
    total = out_ref.shape[0]
    step = slot_chunk(total)
    length = rows.shape[0]
    base = lax.broadcasted_iota(jnp.int32, (step, length), 0)
    for at in range(0, total, step):
        hot = jnp.where(base + at == slot_row, 1.0, 0.0).astype(bf16)
        out_ref[at : at + step, :] = dot(hot, rows).astype(bf16)


def take_rows(slots, slot_col):
    total = slots.shape[0]
    at = lax.broadcasted_iota(jnp.int32, (slot_col.shape[0], total), 1)
    return dot(jnp.where(at == slot_col, 1.0, 0.0).astype(bf16), slots)


def send_body(rows_ref, slot_ref, out_ref):
    place_rows(rows_ref[...], slot_ref[...], out_ref)


def send_call(rows, slot_row, total, deps=()):
    length, width = rows.shape
    return kernel_call(
        send_body,
        args=[rows, slot_row],
        deps=deps,
        in_specs=[VM, VM],
        out_specs=VM,
        out_shape=sds((total, width), bf16),
        compiler_params=params(32),
        cost_estimate=cost(2 * length * total * width, (length + total) * width * 2),
    )


def out_body(x_ref, mixed_ref, w_ref, g_ref, b_ref, slot_ref, after_ref, sent_ref, toks):
    length = x_ref.shape[0]
    blk = min(BLK, length)
    for a in range(0, length, blk):
        rows = slice(a, a + blk)
        after = x_ref[rows].astype(f32) + dot(mixed_ref[rows], w_ref[...])
        after_ref[rows] = after
        hat, _ = norm_parts(after)
        toks[rows] = (hat * g_ref[...] + b_ref[...]).astype(bf16)
    place_rows(toks[...], slot_ref[...], sent_ref)


def out_call(x, mixed, w, gain, bias, slot_row, total, deps=()):
    length, width = x.shape
    return kernel_call(
        out_body,
        args=[x, mixed, w, gain.reshape(1, -1), bias.reshape(1, -1), slot_row],
        deps=deps,
        in_specs=[VM] * 6,
        out_specs=[VM] * 2,
        out_shape=[sds((length, width), f32), sds((total, width), bf16)],
        scratch_shapes=[pltpu.VMEM((length, width), bf16)],
        compiler_params=params(40),
        cost_estimate=cost(2 * length * width * (width + total), length * width * 12),
    )


def add_back_body(after_ref, back_ref, slot_ref, out_ref):
    length = after_ref.shape[0]
    blk = min(BLK, length)
    for a in range(0, length, blk):
        rows = slice(a, a + blk)
        out_ref[rows] = after_ref[rows] + take_rows(back_ref[...], slot_ref[rows])


def add_back_call(after, back, slot_col, deps=()):
    length, width = after.shape
    total = back.shape[0]
    return kernel_call(
        add_back_body,
        args=[after, back, slot_col],
        deps=deps,
        in_specs=[VM] * 3,
        out_specs=VM,
        out_shape=sds((length, width), f32),
        compiler_params=params(40),
        cost_estimate=cost(2 * length * width * total, length * width * 12),
    )


def gelu_parts(pre):
    sq = pre * pre
    half = 0.5 + 0.5 * jnp.tanh(pre * (GELU_A + (GELU_A * GELU_B) * sq))
    act = pre * half
    slope = half + (act - act * half) * (2 * GELU_A + (6 * GELU_A * GELU_B) * sq)
    return act, slope


def hidden_rows(rows_ref, cot_ref, w_in, w_down, act_ref, gpre_ref, use=None):
    total = rows_ref.shape[0]
    step = slot_chunk(total)
    starts = list(range(0, total, step))

    def first(a):
        return dot(rows_ref[a : a + step], w_in), dot(cot_ref[a : a + step], w_down, NT)

    ahead = first(starts[0])
    for at, a in enumerate(starts):
        pre, gact = ahead
        if at + 1 < len(starts):
            ahead = first(starts[at + 1])
        act, slope = gelu_parts(pre)
        act_low = act.astype(bf16)
        gpre_low = (gact * slope).astype(bf16)
        act_ref[0, a : a + step] = act_low
        gpre_ref[0, a : a + step] = gpre_low
        if use is not None:
            use(a, a + step, act_low, gpre_low)


def join_cols(refs):
    return jnp.concatenate([r[...] for r in refs], axis=1)


def join_rows(refs):
    return jnp.concatenate([r[...] for r in refs], axis=0)


def expert_a_body(*refs, nz):
    rows_ref, cot_ref = refs[:2]
    w_in = join_cols(refs[2 : 2 + nz])
    w_down = join_rows(refs[2 + nz : 2 + 2 * nz])
    act_ref, gpre_ref, out_ref, gtok_ref, acc_out, acc_tok = refs[2 + 2 * nz :]
    c = pl.program_id(0)
    last = pl.num_programs(0) - 1

    @pl.when(c == 0)
    def _():
        acc_out[...] = jnp.zeros_like(acc_out)
        acc_tok[...] = jnp.zeros_like(acc_tok)

    def use(a, b, act_low, gpre_low):
        acc_out[a:b] += dot(act_low, w_down)
        acc_tok[a:b] += dot(gpre_low, w_in, NT)

    hidden_rows(rows_ref, cot_ref, w_in, w_down, act_ref, gpre_ref, use)

    @pl.when(c == last)
    def _():
        out_ref[...] = acc_out[...].astype(bf16)
        gtok_ref[...] = acc_tok[...].astype(bf16)


def weight_specs(width, hidden, nz, first=0):
    per = hidden // (nz * FFT)
    ins = [
        pl.BlockSpec((width, FFT), lambda c, z=z: (0, z * per + c + first)) for z in range(nz)
    ]
    downs = [
        pl.BlockSpec((FFT, width), lambda c, z=z: (z * per + c + first, 0)) for z in range(nz)
    ]
    return ins + downs


def expert_a_call(rows, cot, w_in, w_down, nz, deps=()):
    total, width = rows.shape
    hidden = w_in.shape[1]
    chunks = hidden // (nz * FFT)
    tile = nz * FFT
    keep = pl.BlockSpec((total, width), lambda c: (0, 0))
    mid = pl.BlockSpec((1, total, tile), lambda c: (c, 0, 0))
    return kernel_call(
        functools.partial(expert_a_body, nz=nz),
        args=[rows, cot, *([w_in] * nz), *([w_down] * nz)],
        deps=deps,
        grid=(chunks,),
        in_specs=[keep, keep] + weight_specs(width, hidden, nz),
        out_specs=[mid, mid, keep, keep],
        out_shape=[sds((chunks, total, tile), bf16)] * 2 + [sds((total, width), bf16)] * 2,
        scratch_shapes=[pltpu.VMEM((total, width), f32)] * 2,
        compiler_params=params(60),
        cost_estimate=cost(8 * total * width * hidden, 30 << 20),
    )


def expert_b_body(*refs, nz):
    rows_a, cot_a, act_a, gpre_a, rows_b, cot_b = refs[:6]
    w_in = join_cols(refs[6 : 6 + nz])
    w_down = join_rows(refs[6 + nz : 6 + 2 * nz])
    act_b, gpre_b, gdown_ref, gin_ref = refs[6 + 2 * nz :]
    hidden_rows(rows_b, cot_b, w_in, w_down, act_b, gpre_b)
    for z in range(nz):
        cols = slice(z * FFT, (z + 1) * FFT)
        gdown = dot(act_a[0, :, cols], cot_a[...], TN) + dot(act_b[0, :, cols], cot_b[...], TN)
        gdown_ref[z, 0] = gdown.astype(bf16)
        gin = dot(rows_a[...], gpre_a[0, :, cols], TN) + dot(rows_b[...], gpre_b[0, :, cols], TN)
        gin_ref[z, 0] = gin.astype(bf16)


def expert_b_call(rows_a, cot_a, act_a, gpre_a, rows_b, cot_b, w_in, w_down, nz, first, count, deps=()):
    total, width = rows_a.shape
    hidden = w_in.shape[1]
    tile = nz * FFT
    keep = pl.BlockSpec((total, width), lambda c: (0, 0))
    mid = pl.BlockSpec((1, total, tile), lambda c: (c + first, 0, 0))
    mid_out = pl.BlockSpec((1, total, tile), lambda c: (c, 0, 0))
    return kernel_call(
        functools.partial(expert_b_body, nz=nz),
        args=[rows_a, cot_a, act_a, gpre_a, rows_b, cot_b, *([w_in] * nz), *([w_down] * nz)],
        deps=deps,
        grid=(count,),
        in_specs=[keep, keep, mid, mid, keep, keep] + weight_specs(width, hidden, nz, first),
        out_specs=[
            mid_out,
            mid_out,
            pl.BlockSpec((nz, 1, FFT, width), lambda c: (0, c, 0, 0)),
            pl.BlockSpec((nz, 1, width, FFT), lambda c: (0, c, 0, 0)),
        ],
        out_shape=[
            sds((count, total, tile), bf16),
            sds((count, total, tile), bf16),
            sds((nz, count, FFT, width), bf16),
            sds((nz, count, width, FFT), bf16),
        ],
        compiler_params=params(60),
        cost_estimate=cost(12 * total * width * tile * count, 30 << 20),
    )


def expert_c_body(*refs, nz, parts, dims):
    mids = refs[:parts]
    w_refs = refs[parts : parts + nz]
    out_ref, acc = refs[parts + nz :]
    w = join_cols(w_refs) if dims is NT else join_rows(w_refs)
    c = pl.program_id(0)
    total = acc.shape[0]
    step = slot_chunk(total)
    counts = [m.shape[0] for m in mids]
    lo = 0
    for m, k in zip(mids, counts):

        @pl.when((c >= lo) & (c < lo + k))
        def _(m=m, lo=lo):
            for a in range(0, total, step):
                term = dot(m[c - lo, a : a + step], w, dims)
                if lo == 0:
                    acc[a : a + step] = jnp.where(c == 0, term, acc[a : a + step] + term)
                else:
                    acc[a : a + step] += term

        lo += k

    @pl.when(c == pl.num_programs(0) - 1)
    def _():
        out_ref[...] = acc[...].astype(bf16)


def expert_c_call(mids, w, nz, dims, deps=()):
    total, tile = mids[0].shape[1:]
    hidden = tile * sum(m.shape[0] for m in mids)
    width = w.shape[0] if dims is NT else w.shape[1]
    chunks = hidden // tile
    specs = weight_specs(width, hidden, nz)
    specs = specs[:nz] if dims is NT else specs[nz:]
    return kernel_call(
        functools.partial(expert_c_body, nz=nz, parts=len(mids), dims=dims),
        args=[*mids, *([w] * nz)],
        deps=deps,
        grid=(chunks,),
        in_specs=[pl.BlockSpec(m.shape, lambda c: (0, 0, 0)) for m in mids] + specs,
        out_specs=pl.BlockSpec((total, width), lambda c: (0, 0)),
        out_shape=sds((total, width), bf16),
        scratch_shapes=[pltpu.VMEM((total, width), f32)],
        compiler_params=params(60),
        cost_estimate=cost(2 * total * width * hidden, 14 << 20),
    )


def norm_two_body(
    back_ref, slot_ref, after_ref, cot_ref, mixed_ref, w_ref, g_ref, seed_ref, ga_ref, gmix_ref, gw_ref, sums_ref, low
):
    length = after_ref.shape[0]
    blk = min(BLK, length)
    gain_sum = 0.0
    bias_sum = 0.0
    for a in range(0, length, blk):
        rows = slice(a, a + blk)
        gt = take_rows(back_ref[...], slot_ref[rows])
        hat, r = norm_parts(after_ref[rows])
        gain_sum = gain_sum + jnp.sum(gt * hat, axis=0, keepdims=True)
        bias_sum = bias_sum + jnp.sum(gt, axis=0, keepdims=True)
        s = gt * g_ref[...]
        ga = cot_ref[rows].astype(f32) + r * (
            s
            - jnp.mean(s, axis=-1, keepdims=True)
            - hat * jnp.mean(s * hat, axis=-1, keepdims=True)
        )
        ga_ref[rows] = ga
        ga_low = ga.astype(bf16)
        low[rows] = ga_low
        gmix_ref[rows] = dot(ga_low, w_ref[...], NT).astype(bf16)
    gw_ref[...] = seed_ref[...] + dot(mixed_ref[...], low[...], TN)
    sums_ref[0:1] = gain_sum
    sums_ref[1:2] = bias_sum


def norm_two_call(back, slot_col, after, cot, mixed, w, gain, seed, deps=()):
    length, width = after.shape
    total = back.shape[0]
    return kernel_call(
        norm_two_body,
        args=[back, slot_col, after, cot, mixed, w, gain.reshape(1, -1), seed],
        deps=deps,
        in_specs=[VM] * 8,
        out_specs=[VM] * 4,
        out_shape=[
            sds((length, width), f32),
            sds((length, width), bf16),
            sds((width, width), f32),
            sds((2, width), f32),
        ],
        scratch_shapes=[pltpu.VMEM((length, width), bf16)],
        compiler_params=params(56),
        cost_estimate=cost(2 * length * width * (total + 2 * width), length * width * 20),
    )


def pack(out_ref, value, block):
    nz, _, lanes = out_ref.shape
    width = value.shape[1]
    per = value.shape[0] // nz
    low = value.astype(bf16)
    for c in range(width // lanes):
        at = (block * (width // lanes) + c) * per
        for z in range(nz):
            out_ref[z, at : at + per] = low[z * per : (z + 1) * per, c * lanes : (c + 1) * lanes]


def norm_one_body(
    dq_ref, dk_ref, dv_ref, x_ref, w_ref, g_ref, b_ref, ga_ref, seed_ref, gwo_ref, gx_ref, gw_ref, sums_ref, low
):
    length, width = x_ref.shape
    blk = min(BLK, length)
    gain_sum = 0.0
    bias_sum = 0.0
    parts = (dq_ref, dk_ref, dv_ref)
    for a in range(0, length, blk):
        rows = slice(a, a + blk)
        gn = 0.0
        for t, ref in enumerate(parts):
            gn = gn + dot(ref[rows], w_ref[:, t * width : (t + 1) * width], NT)
        hat, r = norm_parts(x_ref[rows].astype(f32))
        low[rows] = (hat * g_ref[...] + b_ref[...]).astype(bf16)
        gain_sum = gain_sum + jnp.sum(gn * hat, axis=0, keepdims=True)
        bias_sum = bias_sum + jnp.sum(gn, axis=0, keepdims=True)
        s = gn * g_ref[...]
        gx_ref[rows] = ga_ref[rows] + r * (
            s
            - jnp.mean(s, axis=-1, keepdims=True)
            - hat * jnp.mean(s * hat, axis=-1, keepdims=True)
        )
    for t, ref in enumerate(parts):
        cols = slice(t * width, (t + 1) * width)
        term = dot(low[...], ref[...], TN)
        if seed_ref is None:
            gw_ref[:, cols] = term
        else:
            pack(gw_ref, seed_ref[:, cols] + term, t)
    if seed_ref is not None:
        pack(gw_ref, gwo_ref[...], len(parts))
    sums_ref[0:1] = gain_sum
    sums_ref[1:2] = bias_sum


def norm_one_call(dq, dk, dv, x, w, gain, bias, ga, seed, gwo, nz, deps=()):
    length, width = x.shape
    args = [dq, dk, dv, x, w, gain.reshape(1, -1), bias.reshape(1, -1), ga]
    if seed is None:

        def body(*refs):
            norm_one_body(*refs[:8], None, None, *refs[8:])

        gw = sds((width, 3 * width), f32)
    else:
        args += [seed, gwo]
        body = norm_one_body
        gw = sds((nz, 4 * width * width // nz // 128, 128), bf16)
    return kernel_call(
        body,
        args=args,
        deps=deps,
        in_specs=[VM] * len(args),
        out_specs=[VM] * 3,
        out_shape=[sds((length, width), f32), gw, sds((2, width), f32)],
        scratch_shapes=[pltpu.VMEM((length, width), bf16)],
        compiler_params=params(60),
        cost_estimate=cost(12 * length * width * width, length * width * 30),
    )


def reduce_body(
    g_ref, sums_ref, gq_ref, go_ref, tot_ref, r1, s1, r2, s2, r3, fin, v1, v2, v3, w1, w2, *sems
):
    nz = lax.axis_size("dp")
    experts = lax.axis_size("expert")
    z = lax.axis_index("dp")
    e = lax.axis_index("expert")
    chips = experts // 2
    core = e % 2
    chip = e // 2
    mate = (z, chip * 2 + 1 - core)
    others = [(z, lax.rem(chip + j, chips) * 2 + core) for j in range(1, chips)]
    layers = [(lax.rem(z + j, nz), e) for j in range(1, nz)]
    peers = [mate] + others + layers
    pl.semaphore_wait(greet(peers), len(peers))
    big, small = sems[:2], sems[2:]
    whole = g_ref.shape[1]
    half = whole // 2
    piece = half // chips

    def copy(src, dst, sem, at, peer):
        return pltpu.make_async_remote_copy(
            src_ref=src,
            dst_ref=dst,
            send_sem=sem[0].at[at],
            recv_sem=sem[1].at[at],
            device_id=peer,
            device_id_type=MESH,
        )

    def rows(start, size):
        return pl.ds(pl.multiple_of(start, 16), size)

    first = [
        copy(g_ref.at[:, rows((1 - core) * half, half)], r1, big, 0, mate),
        copy(sums_ref, v1, small, 0, mate),
    ]
    for c in first:
        c.start()
    for c in first:
        c.wait()
    s1[...] = (g_ref[:, rows(core * half, half)].astype(f32) + r1[...].astype(f32)).astype(bf16)
    w1[...] = sums_ref[...] + v1[...]
    second = []
    for j in range(1, chips):
        k = lax.rem(chip + j, chips)
        second.append(copy(s1.at[:, rows(k * piece, piece)], r2.at[j - 1], big, j, others[j - 1]))
        second.append(copy(w1, v2.at[j - 1], small, j, others[j - 1]))
    for c in second:
        c.start()
    for c in second:
        c.wait()
    part = s1[:, rows(chip * piece, piece)].astype(f32)
    line = w1[...]
    for j in range(1, chips):
        part = part + r2[j - 1].astype(f32)
        line = line + v2[j - 1]
    s2[...] = part.astype(bf16)
    w2[...] = line
    third = []
    for j in range(1, nz):
        k = lax.rem(z + j, nz)
        third.append(copy(s2.at[k], r3.at[j - 1], big, chips + j, layers[j - 1]))
        third.append(copy(w2, v3.at[j - 1], small, chips + j, layers[j - 1]))
    for c in third:
        c.start()
    for c in third:
        c.wait()
    part = s2[z].astype(f32)
    line = w2[...]
    for j in range(1, nz):
        part = part + r3[j - 1].astype(f32)
        line = line + v3[j - 1]
    tot_ref[...] = line
    here = fin.at[rows(core * half + chip * piece, piece)]
    fin[rows(core * half + chip * piece, piece)] = part.astype(bf16)
    fourth = [copy(here, here, big, chips + nz + j, others[j - 1]) for j in range(1, chips)]
    for c in fourth:
        c.start()
    for c in fourth:
        c.wait()
    side = fin.at[rows(core * half, half)]
    last = copy(side, side, big, 2 * chips + nz, mate)
    last.start()
    last.wait()
    per, wide = gq_ref.shape
    lanes = g_ref.shape[2]
    for c in range(whole // per):
        value = fin[c * per : (c + 1) * per].astype(f32)
        at = c * lanes
        if at < wide:
            gq_ref[:, at : at + lanes] = value
        else:
            go_ref[:, at - wide : at - wide + lanes] = value


def reduce_call(g, sums, width, experts, nz):
    whole = g.shape[1]
    chips = experts // 2
    half = whole // 2
    piece = half // chips
    per = width // nz
    count = 2 * chips + nz + 1
    dma = pltpu.SemaphoreType.DMA
    vec = sums.shape
    return pl.pallas_call(
        reduce_body,
        in_specs=[VM] * 2,
        out_specs=[VM] * 3,
        out_shape=[sds((per, 3 * width), f32), sds((per, width), f32), sds(vec, f32)],
        scratch_shapes=[
            pltpu.VMEM((nz, half, 128), bf16),
            pltpu.VMEM((nz, half, 128), bf16),
            pltpu.VMEM((chips - 1, nz, piece, 128), bf16),
            pltpu.VMEM((nz, piece, 128), bf16),
            pltpu.VMEM((nz - 1, piece, 128), bf16),
            pltpu.VMEM((whole, 128), bf16),
            pltpu.VMEM(vec, f32),
            pltpu.VMEM((chips - 1,) + vec, f32),
            pltpu.VMEM((nz - 1,) + vec, f32),
            pltpu.VMEM(vec, f32),
            pltpu.VMEM(vec, f32),
        ]
        + [dma((count,))] * 4,
        compiler_params=pltpu.CompilerParams(
            vmem_limit_bytes=48 << 20, collective_id=1, has_side_effects=True
        ),
        cost_estimate=cost(1 << 24, 150 << 20),
    )(g, sums)


def exchange(x, experts, capacity):
    parts = x.reshape(experts, capacity, x.shape[-1])
    got = lax.all_to_all(parts, "expert", split_axis=0, concat_axis=0, tiled=True)
    return got.reshape(x.shape)


def on_device(
    tokens_in,
    buckets,
    ln1_gain,
    ln1_bias,
    w_qkv,
    w_out,
    ln2_gain,
    ln2_bias,
    w_in,
    w_down,
    cotangent,
):
    experts = lax.axis_size("expert")
    nz = lax.axis_size("dp")
    seqs, length, width = tokens_in.shape
    capacity = 5 * length // (4 * experts)
    total = experts * capacity
    w_in_local = w_in[0]
    w_down_local = w_down[0]
    hidden = w_in_local.shape[1]
    chunks = hidden // (nz * FFT)

    hot = (buckets[:, None, :] == jnp.arange(experts, dtype=jnp.int32)[None, :, None]).astype(bf16)
    upto = (
        jnp.arange(length, dtype=jnp.int32)[:, None] <= jnp.arange(length, dtype=jnp.int32)[None, :]
    ).astype(bf16)
    count = jnp.einsum("sel,lm->sem", hot, upto, preferred_element_type=f32)
    rank = jnp.sum(count * hot.astype(f32), axis=1).astype(jnp.int32) - 1
    slot = buckets * capacity + rank
    slot_row = slot[:, None, :]
    slot_col = slot[:, :, None]

    sends = []
    last = ()
    for s in range(seqs):
        sends.append(send_call(cotangent[s], slot_row[s], total, deps=last))
        last = (sends[-1],)
    cots = [exchange(v, experts, capacity) for v in sends]
    qkv, full_qkv, full_out = qkv_call(tokens_in, ln1_gain, ln1_bias, w_qkv, w_out, nz)
    saved = []
    rows = []
    last = (sends[-1],)
    for s in range(seqs):
        mixed, lse = attn_fwd_call(qkv, HEADS, s, deps=last)
        after, sent = out_call(
            tokens_in[s], mixed[0], full_out, ln2_gain, ln2_bias, slot_row[s], total
        )
        last = (sent,)
        rows.append(exchange(sent, experts, capacity))
        saved.append((mixed, lse, after))

    act_a, gpre_a, out_a, gtok_a = expert_a_call(
        rows[0], cots[0], w_in_local, w_down_local, nz, deps=last
    )
    last = (gtok_a,)
    outs = [exchange(out_a, experts, capacity)]
    gtoks = [exchange(gtok_a, experts, capacity)]

    acts, gpres, gdowns, gins = [], [], [], []
    for first, many in ((0, 1), (1, chunks - 1)):
        act_b, gpre_b, gdown, gin = expert_b_call(
            rows[0],
            cots[0],
            act_a,
            gpre_a,
            rows[1],
            cots[1],
            w_in_local,
            w_down_local,
            nz,
            first,
            many,
            deps=last,
        )
        last = (act_b,)
        acts.append(act_b)
        gpres.append(gpre_b)
        gdowns.append(lax.psum_scatter(gdown, "dp", scatter_dimension=0, tiled=True))
        gins.append(lax.psum_scatter(gin, "dp", scatter_dimension=0, tiled=True))
    gtok_b = expert_c_call(gpres, w_in_local, nz, NT, deps=last)
    gtoks.append(exchange(gtok_b, experts, capacity))
    out_b = expert_c_call(acts, w_down_local, nz, NN, deps=(gtok_b,))
    outs.append(exchange(out_b, experts, capacity))
    last = (out_b,)

    results = []
    gxs = []
    gw_out = jnp.zeros((width, width), f32)
    gw_qkv = None
    sums = 0.0
    for s in range(seqs):
        mixed, lse, after = saved[s]
        ga, gmix, gw_out, sums_two = norm_two_call(
            gtoks[s],
            slot_col[s],
            after,
            cotangent[s],
            mixed[0],
            full_out,
            ln2_gain,
            gw_out,
            deps=last,
        )
        dq, dk, dv = attn_bwd_call(qkv, mixed, gmix[None], lse, HEADS, s)
        gx, gw_qkv, sums_one = norm_one_call(
            dq[0],
            dk[0],
            dv[0],
            tokens_in[s],
            full_qkv,
            ln1_gain,
            ln1_bias,
            ga,
            gw_qkv,
            gw_out,
            nz,
        )
        last = (gx,)
        gxs.append(gx)
        sums = sums + jnp.concatenate([sums_one, sums_two, sums_one, sums_two], axis=0)
    for s in range(seqs):
        results.append(add_back_call(saved[s][2], outs[s], slot_col[s], deps=last))
        last = (results[-1],)

    gq, go, sums = reduce_call(gw_qkv, sums, width, experts, nz)
    mine = lax.dynamic_slice_in_dim(
        sums, lax.axis_index("dp") * (width // nz), width // nz, axis=1
    )
    gdown = jnp.concatenate([g[0] for g in gdowns], axis=0).reshape(1, hidden // nz, width)
    gin = jnp.concatenate([g[0, i] for g in gins for i in range(g.shape[1])], axis=1)[None]
    return (
        jnp.stack(results),
        jnp.stack(gxs),
        mine[0],
        mine[1],
        gq,
        go,
        mine[2],
        mine[3],
        gin.astype(f32),
        gdown.astype(f32),
    )


def solution(mesh):
    placed = (
        P(("dp", "expert"), None, None),
        P(("dp", "expert"), None),
        P(),
        P(),
        P("dp", None),
        P("dp", None),
        P(),
        P(),
        P("expert", None, None),
        P("expert", None, None),
        P(("dp", "expert"), None, None),
    )
    return jax.shard_map(
        on_device,
        mesh=mesh,
        in_specs=placed,
        out_specs=(
            P(("dp", "expert"), None, None),
            P(("dp", "expert"), None, None),
            P("dp"),
            P("dp"),
            P("dp", None),
            P("dp", None),
            P("dp"),
            P("dp"),
            P("expert", None, "dp"),
            P("expert", "dp", None),
        ),
        check_vma=False,
    )
```

```python
import functools

import jax
import jax.numpy as jnp
from jax import lax
from jax.experimental import pallas as pl
from jax.experimental.pallas import tpu as pltpu
from jax.sharding import PartitionSpec as P

HEADS = 12
EPS = 1e-5
NEG = -1e30
bf16 = jnp.bfloat16
f32 = jnp.float32
NN = (((1,), (0,)), ((), ()))
NT = (((1,), (1,)), ((), ()))
TN = (((0,), (0,)), ((), ()))
GELU_A = 0.7978845608028654
GELU_B = 0.044715
BLK = 256
FFT = 256


def dot(a, b, dims=NN):
    return lax.dot_general(a, b, dims, preferred_element_type=f32)


def params(mib=56):
    return pltpu.CompilerParams(vmem_limit_bytes=mib << 20)


def cost(flops, nbytes, trans=0):
    return pl.CostEstimate(flops=int(flops), bytes_accessed=int(nbytes), transcendentals=int(trans))


def sds(shape, dtype):
    return jax.ShapeDtypeStruct(shape, dtype)


VM = pl.BlockSpec(memory_space=pltpu.VMEM)
ANY = pl.BlockSpec(memory_space=pl.ANY)


def kernel_call(body, in_specs, args, deps=(), into=None, **options):
    into = into or {}
    count = len(args)
    extra = len(into) + len(deps)

    def wrapped(*refs):
        body(*refs[:count], *refs[count + extra :])

    return pl.pallas_call(
        wrapped,
        in_specs=list(in_specs) + [ANY] * extra,
        input_output_aliases={count + n: out for n, out in enumerate(into)},
        **options,
    )(*args, *into.values(), *deps)


def norm_parts(v):
    centre = jnp.mean(v, axis=-1, keepdims=True)
    shifted = v - centre
    spread = jnp.mean(shifted * shifted, axis=-1, keepdims=True)
    r = lax.rsqrt(spread + EPS)
    return shifted * r, r


MESH = pl.DeviceIdType.MESH


def greet(peers):
    barrier = pltpu.get_barrier_semaphore()
    for peer in peers:
        pl.semaphore_signal(barrier, inc=1, device_id=peer, device_id_type=MESH)
    return barrier


def find_slots(bucket, experts, capacity):
    length = bucket.shape[1]
    hot = (lax.broadcasted_iota(jnp.int32, (experts, length), 0) == bucket).astype(f32)
    upto = lax.broadcasted_iota(jnp.int32, (length, length), 0) <= lax.broadcasted_iota(
        jnp.int32, (length, length), 1
    )
    count = dot(hot.astype(bf16), upto.astype(bf16))
    rank = jnp.sum(hot * count, axis=0, keepdims=True) - 1.0
    return bucket * capacity + rank.astype(jnp.int32)


def qkv_body(
    x_ref,
    g_ref,
    b_ref,
    wq_ref,
    wo_ref,
    buckets_ref,
    cot_ref,
    qkv_ref,
    fq_ref,
    fo_ref,
    row_ref,
    col_ref,
    cots_ref,
    low,
    acc,
    stage,
    sent,
    up_s,
    dn_s,
    core_s,
    z_r,
    core_r,
    loc,
    a2a_s,
    a2a_r,
    out_s,
    stay_s,
):
    nz = lax.axis_size("dp")
    experts = lax.axis_size("expert")
    z = lax.axis_index("dp")
    e = lax.axis_index("expert")
    core = e % 2
    seqs, length, width = x_ref.shape
    per = width // nz
    half = per // 2
    above = (jnp.minimum(z + 1, nz - 1), e)
    below = (jnp.maximum(z - 1, 0), e)
    mate = (z, e + 1 - 2 * core)
    full = (fq_ref, fo_ref)

    barrier = pltpu.get_barrier_semaphore()

    @pl.when(z + 1 < nz)
    def _():
        pl.semaphore_signal(barrier, inc=1, device_id=above, device_id_type=MESH)

    @pl.when(z > 0)
    def _():
        pl.semaphore_signal(barrier, inc=1, device_id=below, device_id_type=MESH)

    plane = [(z, (e + j) % experts) for j in range(1, experts)]
    plane_back = [(e + experts - j) % experts for j in range(1, experts)]
    for peer in plane:
        pl.semaphore_signal(barrier, inc=1, device_id=peer, device_id_type=MESH)

    @pl.when((z + 1 < nz) & (z > 0))
    def _():
        pl.semaphore_wait(barrier, experts + 1)

    @pl.when((z + 1 >= nz) | (z <= 0))
    def _():
        pl.semaphore_wait(barrier, experts)

    def rows_of(ref, p, c):
        return ref.at[pl.ds(pl.multiple_of(p * per + c * half, 16), half)]

    def hop(t, p, c, src, sem, r_sem, peer):
        return pltpu.make_async_remote_copy(
            src_ref=src,
            dst_ref=rows_of(full[t], p, c),
            send_sem=sem.at[t, p],
            recv_sem=r_sem.at[t, p],
            device_id=peer,
            device_id_type=MESH,
        )

    shard = (wq_ref, wo_ref)
    for t in range(2):
        mine = shard[t].at[pl.ds(pl.multiple_of(core * half, 16), half)]

        @pl.when(z + 1 < nz)
        def _(t=t, mine=mine):
            hop(t, z, core, mine, up_s, z_r, above).start()

        @pl.when(z > 0)
        def _(t=t, mine=mine):
            hop(t, z, core, mine, dn_s, z_r, below).start()

    own = [
        pltpu.make_async_copy(
            shard[t], full[t].at[pl.ds(pl.multiple_of(z * per, 16), per)], loc.at[t]
        )
        for t in range(2)
    ]
    for c in own:
        c.start()

    def trade(s, j):
        return pltpu.make_async_remote_copy(
            src_ref=sent.at[s, plane[j][1]],
            dst_ref=cots_ref.at[s, e],
            send_sem=a2a_s.at[s, j],
            recv_sem=a2a_r.at[s, j],
            device_id=plane[j],
            device_id_type=MESH,
        )

    def traded(s, j):
        return pltpu.make_async_remote_copy(
            src_ref=sent.at[s, plane_back[j]],
            dst_ref=cots_ref.at[s, plane_back[j]],
            send_sem=a2a_s.at[s, j],
            recv_sem=a2a_r.at[s, j],
            device_id=plane[j],
            device_id_type=MESH,
        )

    def stay(s):
        return pltpu.make_async_copy(sent.at[s, e], cots_ref.at[s, e], stay_s.at[s])

    blk = min(BLK, length)

    def prepare(s):
        slot = find_slots(buckets_ref[s], experts, cots_ref.shape[2])
        row_ref[s] = slot
        col_ref[s] = jnp.broadcast_to(slot.astype(f32), (8, length)).T[:, :1].astype(jnp.int32)
        place_rows(cot_ref[s], slot, sent.at[s])
        for j in range(experts - 1):
            trade(s, j).start()
        stay(s).start()

    def first_norm(s):
        for a in range(0, length, blk):
            hat, _ = norm_parts(x_ref[s, a : a + blk].astype(f32))
            v = (hat * g_ref[...] + b_ref[...]).astype(bf16)
            for p in range(nz):
                low[p, s * length + a : s * length + a + blk] = v[:, p * per : (p + 1) * per]

    total = seqs * length
    step = min(512, length)

    def product(p, first):
        w = fq_ref[pl.ds(pl.multiple_of(p * per, 16), per)]
        for a in range(0, total, step):
            term = dot(low[p, a : a + step], w)
            if first:
                acc[a : a + step] = term
            else:
                acc[a : a + step] += term

    def arrive(t, p, forward, sem, peer):
        hop(t, p, core, rows_of(full[t], p, core), sem, z_r, peer).wait_recv()
        hop(t, p, core, rows_of(full[t], p, core), core_s, core_r, mate).start()

        @pl.when(forward)
        def _():
            hop(t, p, core, rows_of(full[t], p, core), sem, z_r, peer).start()

    def got(t, p):
        hop(t, p, 1 - core, rows_of(full[t], p, 1 - core), core_s, core_r, mate).wait_recv()

    def arrivals(t, d):
        @pl.when(z - d >= 0)
        def _():
            arrive(t, z - d, z + 1 < nz, up_s, above)

        @pl.when(z + d < nz)
        def _():
            arrive(t, z + d, z > 0, dn_s, below)

    def products(d):
        @pl.when(z - d >= 0)
        def _():
            got(0, z - d)
            product(z - d, False)

        @pl.when(z + d < nz)
        def _():
            got(0, z + d)
            product(z + d, False)

    prepare(0)
    first_norm(0)
    arrivals(0, 1)
    for s in range(1, seqs):
        first_norm(s)
    own[0].wait()
    own[1].wait()
    product(z, True)
    arrivals(0, 2)
    for s in range(1, seqs):
        prepare(s)
    for d in range(1, nz):
        products(d)
        if d + 2 < nz:
            arrivals(0, d + 2)
        if d == 1:
            arrivals(1, 1)

    flights = []
    for n, a in enumerate(range(0, total, step)):
        if n >= 2:
            flights[n - 2].wait()
        stage[n % 2] = acc[a : a + step].astype(bf16)
        flights.append(
            pltpu.make_async_copy(
                stage.at[n % 2],
                qkv_ref.at[a // length, a % length : a % length + step],
                out_s.at[n % 2],
            )
        )
        flights[n].start()
    for d in range(2, nz):
        arrivals(1, d)

    for d in range(1, nz):
        for ok, p in ((z - d >= 0, z - d), (z + d < nz, z + d)):

            @pl.when(ok)
            def _(p=p):
                got(1, p)

    for t in range(2):
        mine = shard[t].at[pl.ds(pl.multiple_of(core * half, 16), half)]

        @pl.when(z + 1 < nz)
        def _(t=t, mine=mine):
            hop(t, z, core, mine, up_s, z_r, above).wait_send()

        @pl.when(z > 0)
        def _(t=t, mine=mine):
            hop(t, z, core, mine, dn_s, z_r, below).wait_send()

        for d in range(1, nz):
            for ok, p, more, sem, peer in (
                (z - d >= 0, z - d, z + 1 < nz, up_s, above),
                (z + d < nz, z + d, z > 0, dn_s, below),
            ):

                @pl.when(ok)
                def _(t=t, p=p):
                    hop(t, p, core, rows_of(full[t], p, core), core_s, core_r, mate).wait_send()

                @pl.when(ok & more)
                def _(t=t, p=p, sem=sem, peer=peer):
                    hop(t, p, core, rows_of(full[t], p, core), sem, z_r, peer).wait_send()

    for c in flights[-2:]:
        c.wait()
    for s in range(seqs):
        stay(s).wait()
        for j in range(experts - 1):
            trade(s, j).wait_send()
            traded(s, j).wait_recv()


def qkv_call(x, gain, bias, wq, wo, buckets, cot, nz, experts, capacity):
    seqs, length, width = x.shape
    triple = wq.shape[1]
    step = min(512, length)
    dma = pltpu.SemaphoreType.DMA
    return pl.pallas_call(
        qkv_body,
        in_specs=[VM] * 7,
        out_specs=[ANY] + [VM] * 4 + [ANY],
        out_shape=[
            sds((seqs, length, triple), bf16),
            sds((width, triple), bf16),
            sds((width, width), bf16),
            sds((seqs, 1, length), jnp.int32),
            sds((seqs, length, 1), jnp.int32),
            sds((seqs, experts, capacity, width), bf16),
        ],
        scratch_shapes=[
            pltpu.VMEM((nz, seqs * length, width // nz), bf16),
            pltpu.VMEM((seqs * length, triple), f32),
            pltpu.VMEM((2, step, triple), bf16),
            pltpu.VMEM((seqs, experts, capacity, width), bf16),
        ]
        + [dma((2, nz))] * 5
        + [dma((2,))]
        + [dma((seqs, experts - 1))] * 2
        + [dma((2,)), dma((seqs,))],
        compiler_params=pltpu.CompilerParams(
            vmem_limit_bytes=60 << 20, collective_id=0, has_side_effects=True
        ),
        cost_estimate=cost(40 << 30, 30 << 20),
    )(x, gain.reshape(1, -1), bias.reshape(1, -1), wq, wo, buckets, cot)


def attn_fwd_body(q_ref, k_ref, v_ref, o_ref, lse_ref, *, blk, hs, scale, depth):
    length = q_ref.shape[1]
    lane = lax.broadcasted_iota(jnp.int32, (1, 2 * hs), 1) // hs
    v_t = v_ref[0].T
    keys = k_ref[0]
    kh = [jnp.where(lane == h, keys, jnp.zeros_like(keys)) for h in range(2)]
    ones = jnp.ones((16, length), bf16)
    vh = [jnp.concatenate([v_t[h * hs : (h + 1) * hs], ones], axis=0) for h in range(2)]
    future = lax.broadcasted_iota(jnp.int32, (blk, blk), 0) > lax.broadcasted_iota(
        jnp.int32, (blk, blk), 1
    )
    tasks = [(i, h) for i in range(length // blk) for h in range(2)]

    def score(task):
        i, h = task
        top = (i + 1) * blk
        q = q_ref[0, i * blk : top, :] * jnp.asarray(scale, bf16)
        s = dot(kh[h][:top], q, NT)
        diag = jnp.where(future, NEG, s[i * blk :])
        s = jnp.concatenate([s[: i * blk], diag], axis=0) if i else diag
        return s, jnp.max(s, axis=0, keepdims=True)

    queue = [score(t) for t in tasks[:depth]]
    done = {}
    for at, task in enumerate(tasks):
        if at + depth < len(tasks):
            queue.append(score(tasks[at + depth]))
        s, largest = queue.pop(0)
        i, h = task
        top = (i + 1) * blk
        o = dot(vh[h][:, :top], jnp.exp(s - largest).astype(bf16))
        total = o[hs : hs + 1]
        done[task] = o[:hs] * (1.0 / total)
        lse_ref[0, 0, h : h + 1, i * blk : top] = largest + jnp.log(total)
        if h == 1:
            both = jnp.concatenate([done[(i, 0)], done[(i, 1)]], axis=0)
            o_ref[0, i * blk : top, :] = both.T.astype(bf16)


def attn_fwd_call(qkv, heads, at, deps=()):
    n, length, triple = 1, *qkv.shape[1:]
    width = triple // 3
    hs = width // heads
    pairs = heads // 2
    blk = min(BLK, length)

    def spec(o, at=0):
        return pl.BlockSpec((1, length, 2 * hs), lambda s, p: (s + at, 0, o * pairs + p))

    return kernel_call(
        functools.partial(attn_fwd_body, blk=blk, hs=hs, scale=hs**-0.5, depth=3),
        args=[qkv, qkv, qkv],
        deps=deps,
        grid=(n, pairs),
        in_specs=[spec(0, at), spec(1, at), spec(2, at)],
        out_specs=[spec(0), pl.BlockSpec((1, 1, 2, length), lambda s, p: (s, p, 0, 0))],
        out_shape=[sds((n, length, width), bf16), sds((n, pairs, 2, length), f32)],
        compiler_params=params(48),
        cost_estimate=cost(13 << 30, n * length * width * 8),
    )


def attn_bwd_body(
    q_ref, k_ref, v_ref, o_ref, do_ref, lse_ref, d_ref, dqa, doa, *, blk, hs, scale, depth
):
    length = q_ref.shape[1]
    n = length // blk
    lanes = lax.broadcasted_iota(jnp.int32, (1, 2 * hs), 1)
    lane = lanes // hs
    spot = lanes % hs
    keys = k_ref[0]
    vals = v_ref[0]
    k_t = (keys * jnp.asarray(scale, bf16)).T
    kh = [jnp.where(lane == h, keys, jnp.zeros_like(keys)) for h in range(2)]
    vh = [
        jnp.where(lane == h, vals, jnp.where(spot < 2, jnp.ones_like(vals), jnp.zeros_like(vals)))
        for h in range(2)
    ]
    future = lax.broadcasted_iota(jnp.int32, (blk, blk), 0) > lax.broadcasted_iota(
        jnp.int32, (blk, blk), 1
    )
    q = q_ref[0] * jnp.asarray(scale, bf16)
    do = do_ref[0]
    prod = do.astype(f32) * o_ref[0].astype(f32)
    for h in range(2):
        inside = lane == h
        inner = -jnp.sum(jnp.where(inside, prod, 0.0), axis=1, keepdims=True)
        high = inner.astype(bf16)
        rest = (inner - high.astype(f32)).astype(bf16)
        doa[h] = jnp.where(
            inside,
            do,
            jnp.where(spot == 0, high, jnp.where(spot == 1, rest, jnp.zeros_like(high))),
        )
    tasks = [(j, h) for j in range(n) for h in range(2)]

    def score(task):
        j, h = task
        a = j * blk
        return (
            dot(kh[h][a : a + blk], q[a:], NT),
            dot(vh[h][a : a + blk], doa[h, a:], NT),
        )

    queue = [score(t) for t in tasks[:depth]]
    kept = None
    for at, task in enumerate(tasks):
        if at + depth < len(tasks):
            queue.append(score(tasks[at + depth]))
        s, dp = queue.pop(0)
        j, h = task
        a = j * blk
        p = jnp.exp(s - lse_ref[0, 0, h : h + 1, a:])
        diag = jnp.where(future, 0.0, p[:, :blk])
        p = jnp.concatenate([diag, p[:, blk:]], axis=1) if j < n - 1 else diag
        ds = (p * dp).astype(bf16)
        dv = dot(p.astype(bf16), do[a:])
        dk = dot(ds, q[a:])
        dq = dot(k_t[h * hs : (h + 1) * hs, a : a + blk], ds)
        if j == 0:
            dqa[h * hs : (h + 1) * hs, :] = dq
        else:
            dqa[h * hs : (h + 1) * hs, a:] += dq
        if h == 0:
            kept = (dk, dv)
        else:
            d_ref[0, 1, a : a + blk, :] = jnp.where(lane == 0, kept[0], dk).astype(bf16)
            d_ref[0, 2, a : a + blk, :] = jnp.where(lane == 0, kept[1], dv).astype(bf16)
            d_ref[0, 0, a : a + blk, :] = dqa[:, a : a + blk].T.astype(bf16)


def attn_bwd_call(qkv, o, do, lse, heads, at, into=None, deps=()):
    seqs, length, triple = qkv.shape
    n = 1
    width = triple // 3
    hs = width // heads
    pairs = heads // 2
    blk = min(BLK, length)

    def spec(o, at=0):
        return pl.BlockSpec((1, length, 2 * hs), lambda s, p: (s + at, 0, o * pairs + p))

    return kernel_call(
        functools.partial(attn_bwd_body, blk=blk, hs=hs, scale=hs**-0.5, depth=2),
        args=[qkv, qkv, qkv, o, do, lse],
        deps=deps,
        grid=(n, pairs),
        in_specs=[spec(0, at), spec(1, at), spec(2, at), spec(0), spec(0)]
        + [pl.BlockSpec((1, 1, 2, length), lambda s, p: (s, p, 0, 0))],
        out_specs=pl.BlockSpec((1, 3, length, 2 * hs), lambda s, p: (at, 0, 0, p)),
        out_shape=sds((seqs, 3, length, width), bf16),
        into=into,
        scratch_shapes=[
            pltpu.VMEM((2 * hs, length), f32),
            pltpu.VMEM((2, length, 2 * hs), bf16),
        ],
        compiler_params=params(48),
        cost_estimate=cost(27 << 30, n * length * width * 16),
    )


def slot_chunk(total):
    return 256 if total % 256 == 0 else total


def place_rows(rows, slot_row, out_ref):
    experts, capacity, _ = out_ref.shape
    base = lax.broadcasted_iota(jnp.int32, (capacity, rows.shape[0]), 0)
    for e in range(experts):
        hot = jnp.where(base + e * capacity == slot_row, 1.0, 0.0).astype(bf16)
        out_ref[e] = dot(hot, rows).astype(bf16)


def take_rows(slots, slot_col):
    total = slots.shape[0]
    at = lax.broadcasted_iota(jnp.int32, (slot_col.shape[0], total), 1)
    return dot(jnp.where(at == slot_col, 1.0, 0.0).astype(bf16), slots)


def out_body(x_ref, mixed_ref, w_ref, g_ref, b_ref, slot_ref, after_ref, sent_ref, toks):
    size = x_ref.shape[1]
    after = x_ref[0].astype(f32) + dot(mixed_ref[0], w_ref[...])
    after_ref[0] = after
    hat, _ = norm_parts(after)
    step = pl.program_id(0)
    toks[pl.ds(pl.multiple_of(step * size, size), size)] = (
        hat * g_ref[...] + b_ref[...]
    ).astype(bf16)

    @pl.when(step == pl.num_programs(0) - 1)
    def _():
        place_rows(toks[...], slot_ref[0], sent_ref)


def out_call(x, mixed, w, gain, bias, slot_row, experts, capacity, at, into=None):
    seqs, length, width = x.shape
    blk = min(BLK, length)

    def keep(*shape):
        return pl.BlockSpec(shape, lambda r: (0,) * len(shape))

    rows = pl.BlockSpec((1, blk, width), lambda r: (at, r, 0))
    return kernel_call(
        out_body,
        args=[x, mixed, w, gain.reshape(1, -1), bias.reshape(1, -1), slot_row],
        into=into,
        grid=(length // blk,),
        in_specs=[
            rows,
            pl.BlockSpec((1, blk, width), lambda r: (0, r, 0)),
            keep(width, width),
            keep(1, width),
            keep(1, width),
            pl.BlockSpec((1, 1, length), lambda r: (at, 0, 0)),
        ],
        out_specs=[rows, keep(experts, capacity, width)],
        out_shape=[sds((seqs, length, width), f32), sds((experts, capacity, width), bf16)],
        scratch_shapes=[pltpu.VMEM((length, width), bf16)],
        compiler_params=params(40),
        cost_estimate=cost(5 << 30, length * width * 12),
    )


def gelu_parts(pre):
    sq = pre * pre
    half = 0.5 + 0.5 * jnp.tanh(pre * (GELU_A + (GELU_A * GELU_B) * sq))
    act = pre * half
    slope = half + (act - act * half) * (2 * GELU_A + (6 * GELU_A * GELU_B) * sq)
    return act, slope


def hidden_rows(rows_ref, cot_ref, w_in, w_down, act_ref, gpre_ref, use=None):
    total = rows_ref.shape[0]
    step = slot_chunk(total)
    starts = list(range(0, total, step))

    def first(a):
        return dot(rows_ref[a : a + step], w_in), dot(cot_ref[a : a + step], w_down, NT)

    ahead = first(starts[0])
    for at, a in enumerate(starts):
        pre, gact = ahead
        if at + 1 < len(starts):
            ahead = first(starts[at + 1])
        act, slope = gelu_parts(pre)
        act_low = act.astype(bf16)
        gpre_low = (gact * slope).astype(bf16)
        act_ref[0, a : a + step] = act_low
        gpre_ref[0, a : a + step] = gpre_low
        if use is not None:
            use(a, a + step, act_low, gpre_low)


def join_cols(refs):
    return jnp.concatenate([r[...] for r in refs], axis=1)


def join_rows(refs):
    return jnp.concatenate([r[...] for r in refs], axis=0)


def expert_a_body(*refs, nz):
    rows_ref, cot_ref = refs[:2]
    w_in = join_cols(refs[2 : 2 + nz])
    w_down = join_rows(refs[2 + nz : 2 + 2 * nz])
    act_ref, gpre_ref = refs[2 + 2 * nz :]
    hidden_rows(rows_ref, cot_ref.at[0], w_in, w_down, act_ref, gpre_ref)


def weight_specs(width, hidden, nz, first=0):
    per = hidden // (nz * FFT)
    ins = [
        pl.BlockSpec((width, FFT), lambda c, z=z: (0, z * per + c + first)) for z in range(nz)
    ]
    downs = [
        pl.BlockSpec((FFT, width), lambda c, z=z: (z * per + c + first, 0)) for z in range(nz)
    ]
    return ins + downs


def expert_a_call(rows, cot, w_in, w_down, nz, deps=()):
    total, width = rows.shape
    hidden = w_in.shape[1]
    chunks = hidden // (nz * FFT)
    tile = nz * FFT
    keep = pl.BlockSpec((total, width), lambda c: (0, 0))
    cots = pl.BlockSpec((1, total, width), lambda c: (0, 0, 0))
    mid = pl.BlockSpec((1, total, tile), lambda c: (c, 0, 0))
    return kernel_call(
        functools.partial(expert_a_body, nz=nz),
        args=[rows, cot, *([w_in] * nz), *([w_down] * nz)],
        deps=deps,
        grid=(chunks,),
        in_specs=[keep, cots] + weight_specs(width, hidden, nz),
        out_specs=[mid, mid],
        out_shape=[sds((chunks, total, tile), bf16)] * 2,
        compiler_params=params(60),
        cost_estimate=cost(20 << 30, 30 << 20),
    )


def expert_b_body(*refs, nz):
    rows_a, cot_a, act_a, gpre_a, rows_b, cot_b = refs[:6]
    w_in = join_cols(refs[6 : 6 + nz])
    w_down = join_rows(refs[6 + nz : 6 + 2 * nz])
    act_b, gpre_b, gdown_ref, gin_ref = refs[6 + 2 * nz :]
    cot_a, cot_b = cot_a.at[0], cot_b.at[0]
    hidden_rows(rows_b, cot_b, w_in, w_down, act_b, gpre_b)
    for z in range(nz):
        cols = slice(z * FFT, (z + 1) * FFT)
        gdown = dot(act_a[0, :, cols], cot_a[...], TN) + dot(act_b[0, :, cols], cot_b[...], TN)
        gdown_ref[z, 0] = gdown.astype(bf16)
        gin = dot(rows_a[...], gpre_a[0, :, cols], TN) + dot(rows_b[...], gpre_b[0, :, cols], TN)
        gin_ref[z, 0] = gin.astype(bf16)


def expert_b_call(rows_a, act_a, gpre_a, rows_b, cots, w_in, w_down, nz, first, count, deps=()):
    total, width = rows_a.shape
    hidden = w_in.shape[1]
    tile = nz * FFT
    keep = pl.BlockSpec((total, width), lambda c: (0, 0))
    mid = pl.BlockSpec((1, total, tile), lambda c: (c + first, 0, 0))

    def cot(s):
        return pl.BlockSpec((1, total, width), lambda c: (s, 0, 0))

    mid_out = pl.BlockSpec((1, total, tile), lambda c: (c, 0, 0))
    return kernel_call(
        functools.partial(expert_b_body, nz=nz),
        args=[rows_a, cots, act_a, gpre_a, rows_b, cots, *([w_in] * nz), *([w_down] * nz)],
        deps=deps,
        grid=(count,),
        in_specs=[keep, cot(0), mid, mid, keep, cot(1)] + weight_specs(width, hidden, nz, first),
        out_specs=[
            mid_out,
            mid_out,
            pl.BlockSpec((nz, 1, FFT, width), lambda c: (0, c, 0, 0)),
            pl.BlockSpec((nz, 1, width, FFT), lambda c: (0, c, 0, 0)),
        ],
        out_shape=[
            sds((count, total, tile), bf16),
            sds((count, total, tile), bf16),
            sds((nz, count, FFT, width), bf16),
            sds((nz, count, width, FFT), bf16),
        ],
        compiler_params=params(60),
        cost_estimate=cost(20 * count << 30, 30 << 20),
    )


def expert_c_body(*refs, nz, counts, dims):
    parts = len(counts)
    mids = refs[:parts]
    w_refs = refs[parts : parts + nz]
    out_ref, acc = refs[parts + nz :]
    w = join_cols(w_refs) if dims is NT else join_rows(w_refs)
    c = pl.program_id(0)
    total = acc.shape[0]
    step = slot_chunk(total)
    lo = 0
    for m, k in zip(mids, counts):

        @pl.when((c >= lo) & (c < lo + k))
        def _(m=m, lo=lo):
            for a in range(0, total, step):
                term = dot(m[0, a : a + step], w, dims)
                if lo == 0:
                    acc[a : a + step] = jnp.where(c == 0, term, acc[a : a + step] + term)
                else:
                    acc[a : a + step] += term

        lo += k

    @pl.when(c == pl.num_programs(0) - 1)
    def _():
        out_ref[...] = acc[...].astype(bf16)


def expert_c_call(mids, w, nz, dims, deps=()):
    total, tile = mids[0].shape[1:]
    hidden = tile * sum(m.shape[0] for m in mids)
    width = w.shape[0] if dims is NT else w.shape[1]
    chunks = hidden // tile
    specs = weight_specs(width, hidden, nz)
    specs = specs[:nz] if dims is NT else specs[nz:]
    counts = [m.shape[0] for m in mids]
    blocks = []
    for n, k in enumerate(counts):
        lo = sum(counts[:n])
        blocks.append(
            pl.BlockSpec(
                (1, total, tile), lambda c, lo=lo, k=k: (jnp.clip(c - lo, 0, k - 1), 0, 0)
            )
        )
    return kernel_call(
        functools.partial(expert_c_body, nz=nz, counts=counts, dims=dims),
        args=[*mids, *([w] * nz)],
        deps=deps,
        grid=(chunks,),
        in_specs=blocks + specs,
        out_specs=pl.BlockSpec((total, width), lambda c: (0, 0)),
        out_shape=sds((total, width), bf16),
        scratch_shapes=[pltpu.VMEM((total, width), f32)],
        compiler_params=params(60),
        cost_estimate=cost(10 << 30, 14 << 20),
    )


def norm_two_body(
    back_ref, slot_ref, after_ref, cot_ref, mixed_ref, w_ref, g_ref, ga_ref, gmix_ref, gw_ref, sums_ref, low
):
    size = after_ref.shape[1]
    part = size // 2
    starts = [0, part]
    back = back_ref[...]
    gts = [take_rows(back, slot_ref[0, a : a + part]) for a in starts]
    gain_sum = 0.0
    bias_sum = 0.0
    for a, gt in zip(starts, gts):
        rows = slice(a, a + part)
        hat, r = norm_parts(after_ref[0, rows])
        gain_sum = gain_sum + jnp.sum(gt * hat, axis=0, keepdims=True)
        bias_sum = bias_sum + jnp.sum(gt, axis=0, keepdims=True)
        s = gt * g_ref[...]
        ga = cot_ref[0, rows].astype(f32) + r * (
            s
            - jnp.mean(s, axis=-1, keepdims=True)
            - hat * jnp.mean(s * hat, axis=-1, keepdims=True)
        )
        ga_ref[0, rows] = ga
        low[rows] = ga.astype(bf16)
        gmix_ref[0, rows] = dot(low[rows], w_ref[...], NT).astype(bf16)
    gw = dot(mixed_ref[0], low[...], TN)

    @pl.when(pl.program_id(0) == 0)
    def _():
        gw_ref[...] = gw
        sums_ref[0:1] = gain_sum
        sums_ref[1:2] = bias_sum

    @pl.when(pl.program_id(0) > 0)
    def _():
        gw_ref[...] += gw
        sums_ref[0:1] += gain_sum
        sums_ref[1:2] += bias_sum


def norm_two_call(back, slot_col, after, cot, mixed, w, gain, at, into=None, deps=()):
    seqs, length, width = after.shape
    total = back.shape[0]
    blk = min(2 * BLK, length)

    def keep(*shape):
        return pl.BlockSpec(shape, lambda r: (0,) * len(shape))

    rows = pl.BlockSpec((1, blk, width), lambda r: (at, r, 0))
    single = pl.BlockSpec((1, blk, width), lambda r: (0, r, 0))
    return kernel_call(
        norm_two_body,
        args=[back, slot_col, after, cot, mixed, w, gain.reshape(1, -1)],
        deps=deps,
        into=into,
        grid=(length // blk,),
        in_specs=[
            keep(total, width),
            pl.BlockSpec((1, blk, 1), lambda r: (at, r, 0)),
            rows,
            rows,
            single,
            keep(width, width),
            keep(1, width),
        ],
        out_specs=[rows, single, keep(width, width), keep(2, width)],
        out_shape=[
            sds((seqs, length, width), f32),
            sds((1, length, width), bf16),
            sds((width, width), f32),
            sds((2, width), f32),
        ],
        scratch_shapes=[pltpu.VMEM((blk, width), bf16)],
        compiler_params=params(56),
        cost_estimate=cost(9 << 30, length * width * 20),
    )


GROUPS = 4


def last_body(*refs, seqs, per_seq, plan):
    (dw_ref, d_ref, xw_ref, x_ref, w_ref, g_ref, b_ref, ga_ref) = refs[:8]
    gwos = refs[8 : 8 + seqs]
    sums_ref, after_ref = refs[8 + seqs : 10 + seqs]
    backs = refs[10 + seqs : 10 + 2 * seqs]
    slot_ref = refs[10 + 2 * seqs]
    gx_ref, res_ref, gq_ref, go_ref, tot_ref = refs[11 + 2 * seqs : 16 + 2 * seqs]
    acc, low, pay, r1, r2, s2, r3, fin, w0, v1, w1, v2, w2, v3 = refs[16 + 2 * seqs : 30 + 2 * seqs]
    send_s, recv_s, vs_s, vr_s = refs[30 + 2 * seqs :]
    nz = lax.axis_size("dp")
    experts = lax.axis_size("expert")
    z = lax.axis_index("dp")
    e = lax.axis_index("expert")
    chips = experts // 2
    core = e % 2
    chip = e // 2
    mate = (z, chip * 2 + 1 - core)
    others = [(z, lax.rem(chip + j, chips) * 2 + core) for j in range(1, chips)]
    layers = [(lax.rem(z + j, nz), e) for j in range(1, nz)]
    peers = [mate] + others + layers
    width = x_ref.shape[2]
    step = pl.program_id(0)
    last = pl.num_programs(0) - 1
    s1 = r1

    def copy(src, dst, at, peer, sems=None):
        a, b = sems or (send_s, recv_s)
        return pltpu.make_async_remote_copy(
            src_ref=src,
            dst_ref=dst,
            send_sem=a.at[at],
            recv_sem=b.at[at],
            device_id=peer,
            device_id_type=MESH,
        )

    def stage(n, t):
        if n == 1:
            return [copy(pay.at[t, 1 - core], r1.at[t], (t, 0), mate)]
        if n == 2:
            return [
                copy(
                    s1.at[t, lax.rem(chip + j, chips)], r2.at[t, j - 1], (t, j), others[j - 1]
                )
                for j in range(1, chips)
            ]
        if n == 3:
            return [
                copy(
                    s2.at[t, lax.rem(z + j, nz)], r3.at[t, j - 1], (t, chips + j), layers[j - 1]
                )
                for j in range(1, nz)
            ]
        if n == 4:
            here = fin.at[t, core, chip]
            return [
                copy(here, here, (t, chips + nz + j), others[j - 1]) for j in range(1, chips)
            ]
        side = fin.at[t, core]
        return [copy(side, side, (t, 2 * chips + nz), mate)]

    def vector(n):
        sems = (vs_s, vr_s)
        if n == 1:
            return [copy(w0, v1, 0, mate, sems)]
        if n == 2:
            return [copy(w1, v2.at[j - 1], j, others[j - 1], sems) for j in range(1, chips)]
        return [copy(w2, v3.at[j - 1], chips + j, layers[j - 1], sems) for j in range(1, nz)]

    def start(n, t):
        for c in vector(n) if t is None else stage(n, t):
            c.start()

    def finish(n, t):
        for c in vector(n) if t is None else stage(n, t):
            c.wait()
        if t is None:
            if n == 1:
                w1[...] = w0[...] + v1[...]
            elif n == 2:
                line = w1[...]
                for j in range(1, chips):
                    line = line + v2[j - 1]
                w2[...] = line
            else:
                line = w2[...]
                for j in range(1, nz):
                    line = line + v3[j - 1]
                tot_ref[...] = line
            if n < 3:
                start(n + 1, None)
            return
        if n == 1:
            for k in range(chips):
                s1[t, k] = (pay[t, core, k].astype(f32) + r1[t, k].astype(f32)).astype(bf16)
        elif n == 2:
            part = s1[t, chip].astype(f32)
            for j in range(1, chips):
                part = part + r2[t, j - 1].astype(f32)
            s2[t] = part.astype(bf16)
        elif n == 3:
            part = s2[t, z].astype(f32)
            for j in range(1, nz):
                part = part + r3[t, j - 1].astype(f32)
            fin[t, core, chip] = part.astype(bf16)
        elif n == 5:
            piece = fin.shape[3]
            for c in range(2):
                for k in range(chips):
                    at = (c * chips + k) * piece
                    value = fin[t, c, k].astype(f32)
                    if t < 3:
                        gq_ref[at : at + piece, t * width : (t + 1) * width] = value
                    else:
                        go_ref[at : at + piece, :] = value
        if n < 5:
            start(n + 1, t)

    def pack(value, t):
        per = value.shape[0] // nz
        piece = pay.shape[4]
        for zz in range(nz):
            for c in range(2):
                for k in range(chips):
                    at = zz * per + (c * chips + k) * piece
                    pay[t, c, k, zz] = value[at : at + piece].astype(bf16)
        start(1, t)

    @pl.when(step == 0)
    def _():
        pl.semaphore_wait(greet(peers), len(peers))
        gwo = gwos[0][...]
        for s in range(1, seqs):
            gwo = gwo + gwos[s][...]
        pack(gwo, 3)

    for n in range(3 * seqs):
        t, s = n // seqs, n % seqs

        @pl.when(step == n)
        def _(t=t, s=s):
            if t == 0:
                hat, _ = norm_parts(xw_ref[0].astype(f32))
                low[s] = (hat * g_ref[...] + b_ref[...]).astype(bf16)
            term = dot(low[s], dw_ref[0, 0], TN)
            if s == 0:
                acc[...] = term
            elif s < seqs - 1:
                acc[...] += term
            else:
                pack(acc[...] + term, t)

    base = 3 * seqs

    @pl.when(step == base)
    def _():
        w0[0:2] = jnp.zeros((2, width), f32)
        w0[2:8] = sums_ref[2:8]

    @pl.when((step >= base) & (step < base + seqs * per_seq))
    def _():
        hat, r = norm_parts(x_ref[0].astype(f32))
        gn = 0.0
        for t in range(3):
            gn = gn + dot(d_ref[0, t], w_ref[:, t * width : (t + 1) * width], NT)
        w0[0:1] += jnp.sum(gn * hat, axis=0, keepdims=True)
        w0[1:2] += jnp.sum(gn, axis=0, keepdims=True)
        g = gn * g_ref[...]
        gx_ref[0] = ga_ref[0] + r * (
            g
            - jnp.mean(g, axis=-1, keepdims=True)
            - hat * jnp.mean(g * hat, axis=-1, keepdims=True)
        )

    base = base + seqs * per_seq

    @pl.when(step == base - 1)
    def _():
        start(1, None)

    for s in range(seqs):

        @pl.when((step >= base + s * per_seq) & (step < base + (s + 1) * per_seq))
        def _(s=s):
            res_ref[0] = after_ref[0] + take_rows(backs[s][...], slot_ref[0])

    for when, events in plan:

        @pl.when(step == when)
        def _(events=events):
            for n, t in events:
                finish(n, t)


def last_plan(seqs, per_seq):
    dw = 3 * seqs
    end = dw + 2 * seqs * per_seq - 1
    mid = dw + seqs * per_seq
    first = [
        (2, [(1, 3)]),
        (4, [(1, 0)]),
        (dw, [(1, 1)]),
        (dw + 1, [(2, 3)]),
        (dw + 2, [(1, 2)]),
        (dw + 3, [(3, 3)]),
        (dw + 5, [(2, 0)]),
        (dw + 6, [(4, 3)]),
        (dw + 7, [(3, 0)]),
        (mid, [(5, 3)]),
        (mid + 1, [(2, 1), (1, None)]),
        (mid + 2, [(4, 0)]),
        (mid + 3, [(3, 1), (2, None)]),
        (mid + 4, [(5, 0)]),
        (mid + 5, [(3, None)]),
        (mid + 6, [(4, 1)]),
        (end, [(2, 2), (5, 1), (3, 2), (4, 2), (5, 2)]),
    ]
    return [(min(a, end), b) for a, b in first]


def last_call(d, x, w, gain, bias, ga, gwos, sums, after, backs, slot_col, experts, nz, deps=()):
    seqs, length, width = x.shape
    blk = min(BLK, length)
    per_seq = length // blk
    total = backs[0].shape[0]
    dw = 3 * seqs
    mid = dw + seqs * per_seq
    chips = experts // 2
    piece = width // nz // experts
    per = width // nz
    dma = pltpu.SemaphoreType.DMA
    once = pl.Buffered(1)

    def keep(*shape):
        return pl.BlockSpec(shape, lambda r: (0,) * len(shape), pipeline_mode=once)

    def at(first, r):
        n = jnp.clip(r - first, 0, seqs * per_seq - 1)
        return n // per_seq, n % per_seq

    def dw_at(r):
        n = jnp.minimum(r, dw - 1)
        return n % seqs, n // seqs, 0, 0

    def rows(first):
        return pl.BlockSpec((1, blk, width), lambda r: (*at(first, r), 0))

    def d_at(r):
        s, b = at(dw, r)
        return s, 0, b, 0

    steps = mid + seqs * per_seq
    in_specs = [
        pl.BlockSpec((1, 1, length, width), dw_at),
        pl.BlockSpec((1, 3, blk, width), d_at),
        pl.BlockSpec((1, length, width), lambda r: (jnp.minimum(r, seqs - 1), 0, 0)),
        rows(dw),
        keep(width, 3 * width),
        keep(1, width),
        keep(1, width),
        rows(dw),
    ]
    in_specs += [keep(width, width)] * seqs + [keep(8, width), rows(mid)]
    in_specs += [keep(total, width)] * seqs
    in_specs += [pl.BlockSpec((1, blk, 1), lambda r: (*at(mid, r), 0))]
    return pl.pallas_call(
        functools.partial(last_body, seqs=seqs, per_seq=per_seq, plan=last_plan(seqs, per_seq)),
        grid=(steps,),
        in_specs=in_specs,
        out_specs=[rows(dw), rows(mid), keep(per, 3 * width), keep(per, width), keep(8, width)],
        out_shape=[
            sds((seqs, length, width), f32),
            sds((seqs, length, width), f32),
            sds((per, 3 * width), f32),
            sds((per, width), f32),
            sds((8, width), f32),
        ],
        scratch_shapes=[
            pltpu.VMEM((width, width), f32),
            pltpu.VMEM((seqs, length, width), bf16),
            pltpu.VMEM((GROUPS, 2, chips, nz, piece, width), bf16),
            pltpu.VMEM((GROUPS, chips, nz, piece, width), bf16),
            pltpu.VMEM((GROUPS, chips - 1, nz, piece, width), bf16),
            pltpu.VMEM((GROUPS, nz, piece, width), bf16),
            pltpu.VMEM((GROUPS, nz - 1, piece, width), bf16),
            pltpu.VMEM((GROUPS, 2, chips, piece, width), bf16),
            pltpu.VMEM((8, width), f32),
            pltpu.VMEM((8, width), f32),
            pltpu.VMEM((8, width), f32),
            pltpu.VMEM((chips - 1, 8, width), f32),
            pltpu.VMEM((8, width), f32),
            pltpu.VMEM((nz - 1, 8, width), f32),
        ]
        + [dma((GROUPS, 2 * chips + nz + 1))] * 2
        + [dma((chips + nz,))] * 2,
        compiler_params=pltpu.CompilerParams(
            vmem_limit_bytes=62 << 20, collective_id=1, has_side_effects=True
        ),
        cost_estimate=cost(50 << 30, 150 << 20),
    )(
        d,
        d,
        x,
        x,
        w,
        gain.reshape(1, -1),
        bias.reshape(1, -1),
        ga,
        *gwos,
        sums,
        after,
        *backs,
        slot_col,
    )


def exchange(parts):
    got = lax.all_to_all(parts, "expert", split_axis=0, concat_axis=0, tiled=True)
    return got.reshape(-1, parts.shape[-1])


def on_device(
    tokens_in,
    buckets,
    ln1_gain,
    ln1_bias,
    w_qkv,
    w_out,
    ln2_gain,
    ln2_bias,
    w_in,
    w_down,
    cotangent,
):
    experts = lax.axis_size("expert")
    nz = lax.axis_size("dp")
    seqs, length, width = tokens_in.shape
    capacity = 5 * length // (4 * experts)
    total = experts * capacity
    w_in_local = w_in[0]
    w_down_local = w_down[0]
    hidden = w_in_local.shape[1]
    chunks = hidden // (nz * FFT)

    qkv, full_qkv, full_out, slot_row, slot_col, cots = qkv_call(
        tokens_in,
        ln1_gain,
        ln1_bias,
        w_qkv,
        w_out,
        buckets.reshape(seqs, 1, length),
        cotangent,
        nz,
        experts,
        capacity,
    )
    cots = cots.reshape(seqs, total, width)
    saved = []
    rows = []
    last = ()
    after = None
    for s in range(seqs):
        mixed, lse = attn_fwd_call(qkv, HEADS, s, deps=last)
        after, sent = out_call(
            tokens_in,
            mixed,
            full_out,
            ln2_gain,
            ln2_bias,
            slot_row,
            experts,
            capacity,
            s,
            into={0: after} if s else None,
        )
        last = (sent,)
        rows.append(exchange(sent))
        saved.append((mixed, lse))

    act_a, gpre_a = expert_a_call(rows[0], cots, w_in_local, w_down_local, nz, deps=last)
    last = (gpre_a,)
    acts, gpres, gdowns, gins = [], [], [], []
    for first, many in ((0, 1), (1, chunks - 1)):
        act_b, gpre_b, gdown, gin = expert_b_call(
            rows[0],
            act_a,
            gpre_a,
            rows[1],
            cots,
            w_in_local,
            w_down_local,
            nz,
            first,
            many,
            deps=last,
        )
        last = (act_b,)
        acts.append(act_b)
        gpres.append(gpre_b)
        gdowns.append(lax.psum_scatter(gdown, "dp", scatter_dimension=0, tiled=True))
        gins.append(lax.psum_scatter(gin, "dp", scatter_dimension=0, tiled=True))

    def tokens_of(mids, w, dims, last):
        made = expert_c_call(mids, w, nz, dims, deps=last)
        return exchange(made.reshape(experts, capacity, width)), (made,)

    gtok_a, last = tokens_of([gpre_a], w_in_local, NT, last)
    gtok_b, last = tokens_of(gpres, w_in_local, NT, last)
    out_a, last = tokens_of([act_a], w_down_local, NN, last)
    gtoks = [gtok_a, gtok_b]

    d = ga = None
    gwos = []
    sums_two = 0.0
    for s in range(seqs):
        mixed, lse = saved[s]
        ga, gmix, gwo, sums = norm_two_call(
            gtoks[s],
            slot_col,
            after,
            cotangent,
            mixed,
            full_out,
            ln2_gain,
            s,
            into={0: ga} if s else None,
            deps=last,
        )
        sums_two = sums_two + sums
        gwos.append(gwo)
        d = attn_bwd_call(qkv, mixed, gmix, lse, HEADS, s, into={0: d} if s else None)
        if s == 0:
            out_b, last = tokens_of(acts, w_down_local, NN, (gmix,))
    outs = [out_a, out_b]
    sums = jnp.concatenate([sums_two] * 4, axis=0)
    gxs, results, gq, go, sums = last_call(
        d,
        tokens_in,
        full_qkv,
        ln1_gain,
        ln1_bias,
        ga,
        gwos,
        sums,
        after,
        outs,
        slot_col,
        experts,
        nz,
    )
    mine = lax.dynamic_slice_in_dim(
        sums, lax.axis_index("dp") * (width // nz), width // nz, axis=1
    )
    gdown = jnp.concatenate([g[0] for g in gdowns], axis=0).reshape(1, hidden // nz, width)
    gin = jnp.concatenate([g[0, i] for g in gins for i in range(g.shape[1])], axis=1)[None]
    return (
        results,
        gxs,
        mine[0],
        mine[1],
        gq,
        go,
        mine[2],
        mine[3],
        gin.astype(f32),
        gdown.astype(f32),
    )


def solution(mesh):
    placed = (
        P(("dp", "expert"), None, None),
        P(("dp", "expert"), None),
        P(),
        P(),
        P("dp", None),
        P("dp", None),
        P(),
        P(),
        P("expert", None, None),
        P("expert", None, None),
        P(("dp", "expert"), None, None),
    )
    return jax.shard_map(
        on_device,
        mesh=mesh,
        in_specs=placed,
        out_specs=(
            P(("dp", "expert"), None, None),
            P(("dp", "expert"), None, None),
            P("dp"),
            P("dp"),
            P("dp", None),
            P("dp", None),
            P("dp"),
            P("dp"),
            P("expert", None, "dp"),
            P("expert", "dp", None),
        ),
        check_vma=False,
    )
```

```python
import functools

import jax
import jax.numpy as jnp
from jax import lax
from jax.experimental import pallas as pl
from jax.experimental.pallas import tpu as pltpu
from jax.sharding import PartitionSpec as P

HEADS = 12
EPS = 1e-5
NEG = -1e30
bf16 = jnp.bfloat16
f32 = jnp.float32
NN = (((1,), (0,)), ((), ()))
NT = (((1,), (1,)), ((), ()))
TN = (((0,), (0,)), ((), ()))
GELU_A = 0.7978845608028654
GELU_B = 0.044715
BLK = 256
FFT = 256


def dot(a, b, dims=NN):
    return lax.dot_general(a, b, dims, preferred_element_type=f32)


def params(mib=56):
    return pltpu.CompilerParams(vmem_limit_bytes=mib << 20)


def cost(flops, nbytes, trans=0):
    return pl.CostEstimate(flops=int(flops), bytes_accessed=int(nbytes), transcendentals=int(trans))


def sds(shape, dtype):
    return jax.ShapeDtypeStruct(shape, dtype)


VM = pl.BlockSpec(memory_space=pltpu.VMEM)
ANY = pl.BlockSpec(memory_space=pl.ANY)


def kernel_call(body, in_specs, args, deps=(), into=None, **options):
    into = into or {}
    count = len(args)
    extra = len(into) + len(deps)

    def wrapped(*refs):
        body(*refs[:count], *refs[count + extra :])

    return pl.pallas_call(
        wrapped,
        in_specs=list(in_specs) + [ANY] * extra,
        input_output_aliases={count + n: out for n, out in enumerate(into)},
        **options,
    )(*args, *into.values(), *deps)


def norm_parts(v):
    centre = jnp.mean(v, axis=-1, keepdims=True)
    shifted = v - centre
    spread = jnp.mean(shifted * shifted, axis=-1, keepdims=True)
    r = lax.rsqrt(spread + EPS)
    return shifted * r, r


MESH = pl.DeviceIdType.MESH


def greet(peers):
    barrier = pltpu.get_barrier_semaphore()
    for peer in peers:
        pl.semaphore_signal(barrier, inc=1, device_id=peer, device_id_type=MESH)
    return barrier


def find_slots(bucket, experts, capacity):
    length = bucket.shape[1]
    hot = (lax.broadcasted_iota(jnp.int32, (experts, length), 0) == bucket).astype(f32)
    upto = lax.broadcasted_iota(jnp.int32, (length, length), 0) <= lax.broadcasted_iota(
        jnp.int32, (length, length), 1
    )
    count = dot(hot.astype(bf16), upto.astype(bf16))
    rank = jnp.sum(hot * count, axis=0, keepdims=True) - 1.0
    return bucket * capacity + rank.astype(jnp.int32)


def front_body(
    x_ref,
    g1_ref,
    b1_ref,
    g2_ref,
    b2_ref,
    wq_ref,
    wo_ref,
    buckets_ref,
    cot_ref,
    qkv_ref,
    fq_ref,
    fo_ref,
    mixed_ref,
    after_ref,
    lse_ref,
    col_ref,
    cots_ref,
    rows_ref,
    next_ref,
    x_v,
    cot_v,
    fq_v,
    fo_v,
    low,
    qkv_v,
    sent,
    toks,
    mixed_v,
    after_v,
    slots,
    up_s,
    dn_s,
    core_s,
    z_r,
    core_r,
    own_s,
    load_s,
    save_s,
    stay_s,
    a2a_s,
    a2a_r,
    *,
    heads,
):
    nz = lax.axis_size("dp")
    experts = lax.axis_size("expert")
    z = lax.axis_index("dp")
    e = lax.axis_index("expert")
    core = e % 2
    seqs, length, width = x_ref.shape
    capacity = cots_ref.shape[2]
    per = width // nz
    half = per // 2
    above = (jnp.minimum(z + 1, nz - 1), e)
    below = (jnp.maximum(z - 1, 0), e)
    mate = (z, e + 1 - 2 * core)
    full = (fq_v, fo_v)
    shard = (wq_ref, wo_ref)
    blk = min(BLK, length)

    cot_in = [pltpu.make_async_copy(cot_ref.at[s], cot_v.at[s], load_s.at[0, s]) for s in range(seqs)]
    x_in = [pltpu.make_async_copy(x_ref.at[s], x_v.at[s], load_s.at[1, s]) for s in range(seqs)]
    for c in cot_in[:1] + x_in + cot_in[1:]:
        c.start()

    barrier = pltpu.get_barrier_semaphore()

    @pl.when(z + 1 < nz)
    def _():
        pl.semaphore_signal(barrier, inc=1, device_id=above, device_id_type=MESH)

    @pl.when(z > 0)
    def _():
        pl.semaphore_signal(barrier, inc=1, device_id=below, device_id_type=MESH)

    plane = [(z, (e + j) % experts) for j in range(1, experts)]
    plane_back = [(e + experts - j) % experts for j in range(1, experts)]
    for peer in plane:
        pl.semaphore_signal(barrier, inc=1, device_id=peer, device_id_type=MESH)

    @pl.when((z + 1 < nz) & (z > 0))
    def _():
        pl.semaphore_wait(barrier, experts + 1)

    @pl.when((z + 1 >= nz) | (z <= 0))
    def _():
        pl.semaphore_wait(barrier, experts)

    def rows_of(ref, p, c):
        return ref.at[pl.ds(pl.multiple_of(p * per + c * half, 16), half)]

    def hop(t, p, c, src, sem, r_sem, peer):
        return pltpu.make_async_remote_copy(
            src_ref=src,
            dst_ref=rows_of(full[t], p, c),
            send_sem=sem.at[t, p],
            recv_sem=r_sem.at[t, p],
            device_id=peer,
            device_id_type=MESH,
        )

    def mine(t):
        return shard[t].at[pl.ds(pl.multiple_of(core * half, 16), half)]

    def own(t):
        return pltpu.make_async_copy(
            shard[t], full[t].at[pl.ds(pl.multiple_of(z * per, 16), per)], own_s.at[t]
        )

    def begin(t):
        @pl.when(z + 1 < nz)
        def _():
            hop(t, z, core, mine(t), up_s, z_r, above).start()

        @pl.when(z > 0)
        def _():
            hop(t, z, core, mine(t), dn_s, z_r, below).start()

        own(t).start()

    def sides(d):
        return ((z - d >= 0, z - d, z + 1 < nz, up_s, above), (z + d < nz, z + d, z > 0, dn_s, below))

    def held(t, p, sem, r_sem, peer):
        return hop(t, p, core, rows_of(full[t], p, core), sem, r_sem, peer)

    def arrivals(t, d):
        for ok, p, more, sem, peer in sides(d):

            @pl.when(ok)
            def _(p=p, more=more, sem=sem, peer=peer):
                held(t, p, sem, z_r, peer).wait_recv()

                @pl.when(more)
                def _():
                    held(t, p, sem, z_r, peer).start()

                held(t, p, core_s, core_r, mate).start()

    def complete(t):
        own(t).wait()
        for d in range(1, nz):
            for ok, p, _, _, _ in sides(d):

                @pl.when(ok)
                def _(p=p):
                    hop(t, p, 1 - core, rows_of(full[t], p, 1 - core), core_s, core_r, mate).wait_recv()

    def sent_all(t):
        @pl.when(z + 1 < nz)
        def _():
            hop(t, z, core, mine(t), up_s, z_r, above).wait_send()

        @pl.when(z > 0)
        def _():
            hop(t, z, core, mine(t), dn_s, z_r, below).wait_send()

        for d in range(1, nz):
            for ok, p, more, sem, peer in sides(d):

                @pl.when(ok)
                def _(p=p):
                    held(t, p, core_s, core_r, mate).wait_send()

                @pl.when(ok & more)
                def _(p=p, sem=sem, peer=peer):
                    held(t, p, sem, z_r, peer).wait_send()

    def lane(n):
        return (sent.at[n], cots_ref.at[n]) if n < seqs else (toks, rows_ref)

    def trade(n, j, at):
        src, dst = lane(n)
        return pltpu.make_async_remote_copy(
            src_ref=src.at[plane[j][1]],
            dst_ref=dst.at[at],
            send_sem=a2a_s.at[n, j],
            recv_sem=a2a_r.at[n, j],
            device_id=plane[j],
            device_id_type=MESH,
        )

    def stay(n):
        src, dst = lane(n)
        return pltpu.make_async_copy(src.at[e], dst.at[e], stay_s.at[n])

    def spread(n):
        for j in range(experts - 1):
            trade(n, j, e).start()
        stay(n).start()

    def settle(n):
        stay(n).wait()
        for j in range(experts - 1):
            trade(n, j, e).wait_send()
            trade(n, j, plane_back[j]).wait_recv()

    def prepare(s):
        slot = find_slots(buckets_ref[s : s + 1, :], experts, capacity)
        slots[s] = slot
        col_ref[s] = jnp.broadcast_to(slot.astype(f32), (8, length)).T[:, :1].astype(jnp.int32)
        cot_in[s].wait()
        place_rows(cot_v[s], slot, sent.at[s])
        spread(s)

    def first_norm(s):
        x_in[s].wait()
        for a in range(0, length, blk):
            hat, _ = norm_parts(x_v[s, a : a + blk].astype(f32))
            low[s, a : a + blk] = (hat * row(g1_ref) + row(b1_ref)).astype(bf16)

    def save(n, src, dst):
        return pltpu.make_async_copy(src, dst, save_s.at[n])

    saves = [save(0, fq_v, fq_ref), save(1, fo_v, fo_ref)]
    for s in range(seqs):
        saves += [
            save(2 + 3 * s, qkv_v.at[s], qkv_ref.at[s]),
            save(3 + 3 * s, mixed_v.at[s], mixed_ref.at[s]),
            save(4 + 3 * s, after_v.at[s], after_ref.at[s]),
        ]

    def project(s):
        rows = min(512, length)
        for a in range(0, length, rows):
            qkv_v[s, a : a + rows] = dot(low[s, a : a + rows], fq_v[...]).astype(bf16)
        saves[2 + 3 * s].start()

    hs = width // heads
    pairs = heads // 2

    def attend(s):
        def pair(p, carry):
            def cols(t):
                return pl.ds(pl.multiple_of(t * width + p * 2 * hs, 128), 2 * hs)

            one = pl.ds(s, 1)
            attn_fwd_body(
                qkv_v.at[one, :, cols(0)],
                qkv_v.at[one, :, cols(1)],
                qkv_v.at[one, :, cols(2)],
                mixed_v.at[one, :, cols(0)],
                lse_ref.at[one, pl.ds(p, 1)],
                blk=blk,
                hs=hs,
                scale=hs**-0.5,
                depth=3,
            )
            return carry

        lax.fori_loop(0, pairs, pair, 0)
        saves[3 + 3 * s].start()

    def finish(s, out):
        for a in range(0, length, blk):
            rows = slice(a, a + blk)
            after = x_v[s, rows].astype(f32) + dot(mixed_v[s, rows], fo_v[...])
            after_v[s, rows] = after.astype(bf16)
            hat, _ = norm_parts(after)
            low[s, rows] = (hat * row(g2_ref) + row(b2_ref)).astype(bf16)
        saves[4 + 3 * s].start()
        place_rows(low[s], slots[s], out)

    begin(0)
    prepare(0)
    first_norm(0)
    arrivals(0, 1)
    for s in range(1, seqs):
        first_norm(s)
    for d in range(2, nz - 1):
        arrivals(0, d)
    begin(1)
    for s in range(1, seqs):
        prepare(s)
    arrivals(0, nz - 1)
    complete(0)
    saves[0].start()
    project(0)
    arrivals(1, 1)
    for s in range(1, seqs):
        project(s)
    if nz > 2:
        arrivals(1, 2)
    attend(0)
    for d in range(3, nz):
        arrivals(1, d)
    complete(1)
    saves[1].start()
    finish(0, toks)
    spread(seqs)
    for s in range(1, seqs):
        attend(s)
        finish(s, next_ref)
    for t in range(2):
        sent_all(t)
    for n in range(seqs + 1):
        settle(n)
    for c in saves:
        c.wait()


def row(ref):
    return ref[...].reshape(1, -1)


def front_call(x, g1, b1, g2, b2, wq, wo, buckets, cot, heads, nz, experts, capacity):
    seqs, length, width = x.shape
    triple = wq.shape[1]
    dma = pltpu.SemaphoreType.DMA
    slab = (experts, capacity, width)
    pairs = heads // 2
    return pl.pallas_call(
        functools.partial(front_body, heads=heads),
        in_specs=[ANY] + [VM] * 4 + [ANY] * 2 + [VM, ANY],
        out_specs=[ANY] * 5 + [VM] * 2 + [ANY] * 2 + [VM],
        out_shape=[
            sds((seqs, length, triple), bf16),
            sds((width, triple), bf16),
            sds((width, width), bf16),
            sds((seqs, length, width), bf16),
            sds((seqs, length, width), bf16),
            sds((seqs, pairs, 2, length), f32),
            sds((seqs, length, 1), jnp.int32),
            sds((seqs,) + slab, bf16),
            sds(slab, bf16),
            sds(slab, bf16),
        ],
        scratch_shapes=[
            pltpu.VMEM((seqs, length, width), bf16),
            pltpu.VMEM((seqs, length, width), bf16),
            pltpu.VMEM((width, triple), bf16),
            pltpu.VMEM((width, width), bf16),
            pltpu.VMEM((seqs, length, width), bf16),
            pltpu.VMEM((seqs, length, triple), bf16),
            pltpu.VMEM((seqs,) + slab, bf16),
            pltpu.VMEM(slab, bf16),
            pltpu.VMEM((seqs, length, width), bf16),
            pltpu.VMEM((seqs, length, width), bf16),
            pltpu.VMEM((seqs, 1, length), jnp.int32),
        ]
        + [dma((2, nz))] * 5
        + [dma((2,)), dma((2, seqs)), dma((2 + 3 * seqs,)), dma((seqs + 1,))]
        + [dma((seqs + 1, experts - 1))] * 2,
        compiler_params=pltpu.CompilerParams(
            vmem_limit_bytes=62 << 20, collective_id=0, has_side_effects=True
        ),
        cost_estimate=cost(90 << 30, 30 << 20),
    )(x, g1, b1, g2, b2, wq, wo, buckets, cot)


def attn_fwd_body(q_ref, k_ref, v_ref, o_ref, lse_ref, *, blk, hs, scale, depth):
    length = q_ref.shape[1]
    lane = lax.broadcasted_iota(jnp.int32, (1, 2 * hs), 1) // hs
    v_t = v_ref[0].T
    keys = k_ref[0]
    kh = [jnp.where(lane == h, keys, jnp.zeros_like(keys)) for h in range(2)]
    ones = jnp.ones((16, length), bf16)
    vh = [jnp.concatenate([v_t[h * hs : (h + 1) * hs], ones], axis=0) for h in range(2)]
    future = lax.broadcasted_iota(jnp.int32, (blk, blk), 0) > lax.broadcasted_iota(
        jnp.int32, (blk, blk), 1
    )
    tasks = [(i, h) for i in range(length // blk) for h in range(2)]

    def score(task):
        i, h = task
        top = (i + 1) * blk
        q = q_ref[0, i * blk : top, :] * jnp.asarray(scale, bf16)
        s = dot(kh[h][:top], q, NT)
        diag = jnp.where(future, NEG, s[i * blk :])
        s = jnp.concatenate([s[: i * blk], diag], axis=0) if i else diag
        return s, jnp.max(s, axis=0, keepdims=True)

    queue = [score(t) for t in tasks[:depth]]
    done = {}
    for at, task in enumerate(tasks):
        if at + depth < len(tasks):
            queue.append(score(tasks[at + depth]))
        s, largest = queue.pop(0)
        i, h = task
        top = (i + 1) * blk
        o = dot(vh[h][:, :top], jnp.exp(s - largest).astype(bf16))
        total = o[hs : hs + 1]
        done[task] = o[:hs] * (1.0 / total)
        lse_ref[0, 0, h : h + 1, i * blk : top] = largest + jnp.log(total)
        if h == 1:
            both = jnp.concatenate([done[(i, 0)], done[(i, 1)]], axis=0)
            o_ref[0, i * blk : top, :] = both.T.astype(bf16)


def attn_bwd_body(
    q_ref, k_ref, v_ref, o_ref, do_ref, lse_ref, d_ref, dqa, doa, *, blk, hs, scale, depth
):
    length = q_ref.shape[1]
    n = length // blk
    lanes = lax.broadcasted_iota(jnp.int32, (1, 2 * hs), 1)
    lane = lanes // hs
    spot = lanes % hs
    keys = k_ref[0]
    vals = v_ref[0]
    k_t = (keys * jnp.asarray(scale, bf16)).T
    kh = [jnp.where(lane == h, keys, jnp.zeros_like(keys)) for h in range(2)]
    vh = [
        jnp.where(lane == h, vals, jnp.where(spot < 2, jnp.ones_like(vals), jnp.zeros_like(vals)))
        for h in range(2)
    ]
    future = lax.broadcasted_iota(jnp.int32, (blk, blk), 0) > lax.broadcasted_iota(
        jnp.int32, (blk, blk), 1
    )
    q = q_ref[0] * jnp.asarray(scale, bf16)
    do = do_ref[0]
    prod = do.astype(f32) * o_ref[0].astype(f32)
    for h in range(2):
        inside = lane == h
        inner = -jnp.sum(jnp.where(inside, prod, 0.0), axis=1, keepdims=True)
        high = inner.astype(bf16)
        rest = (inner - high.astype(f32)).astype(bf16)
        doa[h] = jnp.where(
            inside,
            do,
            jnp.where(spot == 0, high, jnp.where(spot == 1, rest, jnp.zeros_like(high))),
        )
    tasks = [(j, h) for j in range(n) for h in range(2)]

    def score(task):
        j, h = task
        a = j * blk
        return (
            dot(kh[h][a : a + blk], q[a:], NT),
            dot(vh[h][a : a + blk], doa[h, a:], NT),
        )

    queue = [score(t) for t in tasks[:depth]]
    kept = None
    for at, task in enumerate(tasks):
        if at + depth < len(tasks):
            queue.append(score(tasks[at + depth]))
        s, dp = queue.pop(0)
        j, h = task
        a = j * blk
        p = jnp.exp(s - lse_ref[0, 0, h : h + 1, a:])
        diag = jnp.where(future, 0.0, p[:, :blk])
        p = jnp.concatenate([diag, p[:, blk:]], axis=1) if j < n - 1 else diag
        ds = (p * dp).astype(bf16)
        dv = dot(p.astype(bf16), do[a:])
        dk = dot(ds, q[a:])
        dq = dot(k_t[h * hs : (h + 1) * hs, a : a + blk], ds)
        if j == 0:
            dqa[h * hs : (h + 1) * hs, :] = dq
        else:
            dqa[h * hs : (h + 1) * hs, a:] += dq
        if h == 0:
            kept = (dk, dv)
        else:
            d_ref[0, 1, a : a + blk, :] = jnp.where(lane == 0, kept[0], dk).astype(bf16)
            d_ref[0, 2, a : a + blk, :] = jnp.where(lane == 0, kept[1], dv).astype(bf16)
            d_ref[0, 0, a : a + blk, :] = dqa[:, a : a + blk].T.astype(bf16)


def attn_bwd_call(qkv, o, do, lse, heads, at, into=None, deps=()):
    seqs, length, triple = qkv.shape
    n = 1
    width = triple // 3
    hs = width // heads
    pairs = heads // 2
    blk = min(BLK, length)

    def spec(o, at=0):
        return pl.BlockSpec((1, length, 2 * hs), lambda s, p: (s + at, 0, o * pairs + p))

    return kernel_call(
        functools.partial(attn_bwd_body, blk=blk, hs=hs, scale=hs**-0.5, depth=2),
        args=[qkv, qkv, qkv, o, do, lse],
        deps=deps,
        grid=(n, pairs),
        in_specs=[spec(0, at), spec(1, at), spec(2, at), spec(0, at), spec(0)]
        + [pl.BlockSpec((1, 1, 2, length), lambda s, p: (at, p, 0, 0))],
        out_specs=pl.BlockSpec((1, 3, length, 2 * hs), lambda s, p: (at, 0, 0, p)),
        out_shape=sds((seqs, 3, length, width), bf16),
        into=into,
        scratch_shapes=[
            pltpu.VMEM((2 * hs, length), f32),
            pltpu.VMEM((2, length, 2 * hs), bf16),
        ],
        compiler_params=params(60),
        cost_estimate=cost(27 << 30, n * length * width * 16),
    )


def slot_chunk(total):
    return 256 if total % 256 == 0 else total


def place_rows(rows, slot_row, out_ref):
    experts, capacity, _ = out_ref.shape
    base = lax.broadcasted_iota(jnp.int32, (capacity, rows.shape[0]), 0)
    for e in range(experts):
        hot = jnp.where(base + e * capacity == slot_row, 1.0, 0.0).astype(bf16)
        out_ref[e] = dot(hot, rows).astype(bf16)


def take_rows(slots, slot_col):
    total = slots.shape[0]
    at = lax.broadcasted_iota(jnp.int32, (slot_col.shape[0], total), 1)
    return dot(jnp.where(at == slot_col, 1.0, 0.0).astype(bf16), slots)


def gelu_parts(pre):
    sq = pre * pre
    half = 0.5 + 0.5 * jnp.tanh(pre * (GELU_A + (GELU_A * GELU_B) * sq))
    act = pre * half
    slope = half + (act - act * half) * (2 * GELU_A + (6 * GELU_A * GELU_B) * sq)
    return act, slope


def hidden_rows(rows_ref, cot_ref, w_in, w_down, act_ref, gpre_ref, use=None):
    total = rows_ref.shape[0]
    step = slot_chunk(total)
    starts = list(range(0, total, step))

    def first(a):
        return dot(rows_ref[a : a + step], w_in), dot(cot_ref[a : a + step], w_down, NT)

    ahead = first(starts[0])
    for at, a in enumerate(starts):
        pre, gact = ahead
        if at + 1 < len(starts):
            ahead = first(starts[at + 1])
        act, slope = gelu_parts(pre)
        act_low = act.astype(bf16)
        gpre_low = (gact * slope).astype(bf16)
        act_ref[0, a : a + step] = act_low
        gpre_ref[0, a : a + step] = gpre_low
        if use is not None:
            use(a, a + step, act_low, gpre_low)


def join_cols(refs):
    return jnp.concatenate([r[...] for r in refs], axis=1)


def join_rows(refs):
    return jnp.concatenate([r[...] for r in refs], axis=0)


def expert_a_body(*refs, nz):
    rows_ref, cot_ref = refs[:2]
    w_in = join_cols(refs[2 : 2 + nz])
    w_down = join_rows(refs[2 + nz : 2 + 2 * nz])
    act_ref, gpre_ref = refs[2 + 2 * nz :]
    hidden_rows(rows_ref, cot_ref.at[0], w_in, w_down, act_ref, gpre_ref)


def weight_specs(width, hidden, nz, first=0):
    per = hidden // (nz * FFT)
    ins = [
        pl.BlockSpec((width, FFT), lambda c, z=z: (0, z * per + c + first)) for z in range(nz)
    ]
    downs = [
        pl.BlockSpec((FFT, width), lambda c, z=z: (z * per + c + first, 0)) for z in range(nz)
    ]
    return ins + downs


def expert_a_call(rows, cot, w_in, w_down, nz):
    total, width = rows.shape
    hidden = w_in.shape[1]
    chunks = hidden // (nz * FFT)
    tile = nz * FFT
    keep = pl.BlockSpec((total, width), lambda c: (0, 0))
    cots = pl.BlockSpec((1, total, width), lambda c: (0, 0, 0))
    mid = pl.BlockSpec((1, total, tile), lambda c: (c, 0, 0))
    return pl.pallas_call(
        functools.partial(expert_a_body, nz=nz),
        grid=(chunks,),
        in_specs=[keep, cots] + weight_specs(width, hidden, nz),
        out_specs=[mid, mid],
        out_shape=[sds((chunks, total, tile), bf16)] * 2,
        compiler_params=params(60),
        cost_estimate=cost(22 << 30, 30 << 20),
    )(rows, cot, *([w_in] * nz), *([w_down] * nz))


def expert_b_body(*refs, nz):
    rows_a, cot_a, act_a, gpre_a, rows_b, cot_b = refs[:6]
    w_in = join_cols(refs[6 : 6 + nz])
    w_down = join_rows(refs[6 + nz : 6 + 2 * nz])
    act_b, gpre_b, gdown_ref, gin_ref = refs[6 + 2 * nz :]
    cot_a, cot_b = cot_a.at[0], cot_b.at[0]
    hidden_rows(rows_b, cot_b, w_in, w_down, act_b, gpre_b)
    for z in range(nz):
        cols = slice(z * FFT, (z + 1) * FFT)
        gdown = dot(act_a[0, :, cols], cot_a[...], TN) + dot(act_b[0, :, cols], cot_b[...], TN)
        gdown_ref[z, 0] = gdown.astype(bf16)
        gin = dot(rows_a[...], gpre_a[0, :, cols], TN) + dot(rows_b[...], gpre_b[0, :, cols], TN)
        gin_ref[z, 0] = gin.astype(bf16)


def expert_b_call(rows_a, act_a, gpre_a, rows_b, cots, w_in, w_down, nz, first, count, deps=()):
    total, width = rows_a.shape
    hidden = w_in.shape[1]
    tile = nz * FFT
    keep = pl.BlockSpec((total, width), lambda c: (0, 0))
    mid = pl.BlockSpec((1, total, tile), lambda c: (c + first, 0, 0))

    def cot(s):
        return pl.BlockSpec((1, total, width), lambda c: (s, 0, 0))

    mid_out = pl.BlockSpec((1, total, tile), lambda c: (c, 0, 0))
    return kernel_call(
        functools.partial(expert_b_body, nz=nz),
        args=[rows_a, cots, act_a, gpre_a, rows_b, cots, *([w_in] * nz), *([w_down] * nz)],
        deps=deps,
        grid=(count,),
        in_specs=[keep, cot(0), mid, mid, keep, cot(1)] + weight_specs(width, hidden, nz, first),
        out_specs=[
            mid_out,
            mid_out,
            pl.BlockSpec((nz, 1, FFT, width), lambda c: (0, c, 0, 0)),
            pl.BlockSpec((nz, 1, width, FFT), lambda c: (0, c, 0, 0)),
        ],
        out_shape=[
            sds((count, total, tile), bf16),
            sds((count, total, tile), bf16),
            sds((nz, count, FFT, width), bf16),
            sds((nz, count, width, FFT), bf16),
        ],
        compiler_params=params(60),
        cost_estimate=cost(20 * count << 30, 30 << 20),
    )


def expert_c_body(*refs, nz, counts, dims):
    parts = len(counts)
    mids = refs[:parts]
    w_refs = refs[parts : parts + nz]
    out_ref, acc = refs[parts + nz :]
    w = join_cols(w_refs) if dims is NT else join_rows(w_refs)
    c = pl.program_id(0)
    total = acc.shape[0]
    step = slot_chunk(total)
    lo = 0
    for m, k in zip(mids, counts):

        @pl.when((c >= lo) & (c < lo + k))
        def _(m=m, lo=lo):
            for a in range(0, total, step):
                term = dot(m[0, a : a + step], w, dims)
                if lo == 0:
                    acc[a : a + step] = jnp.where(c == 0, term, acc[a : a + step] + term)
                else:
                    acc[a : a + step] += term

        lo += k

    @pl.when(c == pl.num_programs(0) - 1)
    def _():
        out_ref[...] = acc[...].astype(bf16)


def expert_c_call(mids, w, nz, dims, deps=()):
    total, tile = mids[0].shape[1:]
    hidden = tile * sum(m.shape[0] for m in mids)
    width = w.shape[0] if dims is NT else w.shape[1]
    chunks = hidden // tile
    specs = weight_specs(width, hidden, nz)
    specs = specs[:nz] if dims is NT else specs[nz:]
    counts = [m.shape[0] for m in mids]
    blocks = []
    for n, k in enumerate(counts):
        lo = sum(counts[:n])
        blocks.append(
            pl.BlockSpec(
                (1, total, tile), lambda c, lo=lo, k=k: (jnp.clip(c - lo, 0, k - 1), 0, 0)
            )
        )
    return kernel_call(
        functools.partial(expert_c_body, nz=nz, counts=counts, dims=dims),
        args=[*mids, *([w] * nz)],
        deps=deps,
        grid=(chunks,),
        in_specs=blocks + specs,
        out_specs=pl.BlockSpec((total, width), lambda c: (0, 0)),
        out_shape=sds((total, width), bf16),
        scratch_shapes=[pltpu.VMEM((total, width), f32)],
        compiler_params=params(60),
        cost_estimate=cost(10 << 30, 14 << 20),
    )


def norm_two_body(
    back_ref, slot_ref, after_ref, cot_ref, mixed_ref, w_ref, g_ref, ga_ref, gmix_ref, gw_ref, sums_ref, acc
):
    size = after_ref.shape[1]
    part = size // 2
    starts = [0, part]
    back = back_ref[...]
    gts = [take_rows(back, slot_ref[0, a : a + part]) for a in starts]
    gain_sum = 0.0
    bias_sum = 0.0
    for a, gt in zip(starts, gts):
        rows = slice(a, a + part)
        hat, r = norm_parts(after_ref[0, rows].astype(f32))
        gain_sum = gain_sum + jnp.sum(gt * hat, axis=0, keepdims=True)
        bias_sum = bias_sum + jnp.sum(gt, axis=0, keepdims=True)
        s = gt * g_ref[...]
        ga = cot_ref[0, rows].astype(f32) + r * (
            s
            - jnp.mean(s, axis=-1, keepdims=True)
            - hat * jnp.mean(s * hat, axis=-1, keepdims=True)
        )
        ga_ref[0, rows] = ga.astype(bf16)
        gmix_ref[0, rows] = dot(ga_ref[0, rows], w_ref[...], NT).astype(bf16)
    gw = dot(mixed_ref[0], ga_ref[0], TN)
    last = pl.num_programs(0) - 1

    @pl.when(pl.program_id(0) == 0)
    def _():
        acc[...] = gw
        sums_ref[0:1] = gain_sum
        sums_ref[1:2] = bias_sum

    @pl.when(pl.program_id(0) > 0)
    def _():
        acc[...] += gw
        sums_ref[0:1] += gain_sum
        sums_ref[1:2] += bias_sum

    @pl.when(pl.program_id(0) == last)
    def _():
        gw_ref[...] = acc[...].astype(bf16)


def norm_two_call(back, slot_col, after, cot, mixed, w, gain, at, into=None, deps=()):
    seqs, length, width = after.shape
    total = back.shape[0]
    blk = min(2 * BLK, length)

    def keep(*shape):
        return pl.BlockSpec(shape, lambda r: (0,) * len(shape))

    rows = pl.BlockSpec((1, blk, width), lambda r: (at, r, 0))
    single = pl.BlockSpec((1, blk, width), lambda r: (0, r, 0))
    return kernel_call(
        norm_two_body,
        args=[back, slot_col, after, cot, mixed, w, gain.reshape(1, -1)],
        deps=deps,
        into=into,
        grid=(length // blk,),
        in_specs=[
            keep(total, width),
            pl.BlockSpec((1, blk, 1), lambda r: (at, r, 0)),
            rows,
            rows,
            rows,
            keep(width, width),
            keep(1, width),
        ],
        out_specs=[rows, single, keep(width, width), keep(2, width)],
        out_shape=[
            sds((seqs, length, width), bf16),
            sds((1, length, width), bf16),
            sds((width, width), bf16),
            sds((2, width), f32),
        ],
        scratch_shapes=[pltpu.VMEM((width, width), f32)],
        compiler_params=params(60),
        cost_estimate=cost(9 << 30, length * width * 20),
    )


GROUPS = 4


def last_body(*refs, seqs, per_seq, plan):
    (dw_ref, d_ref, xw_ref, x_ref, w_any, g_ref, b_ref) = refs[:7]
    gwos = refs[7 : 7 + seqs]
    sums_ref = refs[7 + seqs]
    backs_any = refs[8 + seqs : 8 + 2 * seqs]
    slot_ref = refs[8 + 2 * seqs]
    gx_ref, res_ref, gq_ref, go_ref, tot_ref = refs[9 + 2 * seqs : 14 + 2 * seqs]
    rest = refs[14 + 2 * seqs :]
    acc, low, pay, r1, r2, s2, r3, fin, w0, v1, w1, v2, w2, v3, w_ref, backs = rest[:16]
    send_s, recv_s, vs_s, vr_s, load_s = rest[16:]
    nz = lax.axis_size("dp")
    experts = lax.axis_size("expert")
    z = lax.axis_index("dp")
    e = lax.axis_index("expert")
    chips = experts // 2
    core = e % 2
    chip = e // 2
    mate = (z, chip * 2 + 1 - core)
    others = [(z, lax.rem(chip + j, chips) * 2 + core) for j in range(1, chips)]
    layers = [(lax.rem(z + j, nz), e) for j in range(1, nz)]
    peers = [mate] + others + layers
    width = x_ref.shape[2]
    step = pl.program_id(0)
    last = pl.num_programs(0) - 1
    s1 = r1

    def copy(src, dst, at, peer, sems=None):
        a, b = sems or (send_s, recv_s)
        return pltpu.make_async_remote_copy(
            src_ref=src,
            dst_ref=dst,
            send_sem=a.at[at],
            recv_sem=b.at[at],
            device_id=peer,
            device_id_type=MESH,
        )

    def stage(n, t):
        if n == 1:
            return [copy(pay.at[t, 1 - core], r1.at[t], (t, 0), mate)]
        if n == 2:
            return [
                copy(
                    s1.at[t, lax.rem(chip + j, chips)], r2.at[t, j - 1], (t, j), others[j - 1]
                )
                for j in range(1, chips)
            ]
        if n == 3:
            return [
                copy(
                    s2.at[t, lax.rem(z + j, nz)], r3.at[t, j - 1], (t, chips + j), layers[j - 1]
                )
                for j in range(1, nz)
            ]
        if n == 4:
            here = fin.at[t, core, chip]
            return [
                copy(here, here, (t, chips + nz + j), others[j - 1]) for j in range(1, chips)
            ]
        side = fin.at[t, core]
        return [copy(side, side, (t, 2 * chips + nz), mate)]

    def vector(n):
        sems = (vs_s, vr_s)
        if n == 1:
            return [copy(w0, v1, 0, mate, sems)]
        if n == 2:
            return [copy(w1, v2.at[j - 1], j, others[j - 1], sems) for j in range(1, chips)]
        return [copy(w2, v3.at[j - 1], chips + j, layers[j - 1], sems) for j in range(1, nz)]

    def start(n, t):
        for c in vector(n) if t is None else stage(n, t):
            c.start()

    def finish(n, t):
        for c in vector(n) if t is None else stage(n, t):
            c.wait()
        if t is None:
            if n == 1:
                w1[...] = w0[...] + v1[...]
            elif n == 2:
                line = w1[...]
                for j in range(1, chips):
                    line = line + v2[j - 1]
                w2[...] = line
            else:
                line = w2[...]
                for j in range(1, nz):
                    line = line + v3[j - 1]
                tot_ref[...] = line
            if n < 3:
                start(n + 1, None)
            return
        if n == 1:
            for k in range(chips):
                s1[t, k] = (pay[t, core, k].astype(f32) + r1[t, k].astype(f32)).astype(bf16)
        elif n == 2:
            part = s1[t, chip].astype(f32)
            for j in range(1, chips):
                part = part + r2[t, j - 1].astype(f32)
            s2[t] = part.astype(bf16)
        elif n == 3:
            part = s2[t, z].astype(f32)
            for j in range(1, nz):
                part = part + r3[t, j - 1].astype(f32)
            fin[t, core, chip] = part.astype(bf16)
        elif n == 5:
            piece = fin.shape[3]
            for c in range(2):
                for k in range(chips):
                    at = (c * chips + k) * piece
                    value = fin[t, c, k].astype(f32)
                    if t < 3:
                        gq_ref[at : at + piece, t * width : (t + 1) * width] = value
                    else:
                        go_ref[at : at + piece, :] = value
        if n < 5:
            start(n + 1, t)

    def pack(value, t):
        per = value.shape[0] // nz
        piece = pay.shape[4]
        for zz in range(nz):
            for c in range(2):
                for k in range(chips):
                    at = zz * per + (c * chips + k) * piece
                    pay[t, c, k, zz] = value[at : at + piece].astype(bf16)
        start(1, t)

    loads = [pltpu.make_async_copy(w_any, w_ref, load_s.at[0])]
    loads += [
        pltpu.make_async_copy(backs_any[s], backs.at[s], load_s.at[1 + s]) for s in range(seqs)
    ]

    @pl.when(step == 0)
    def _():
        for c in loads:
            c.start()
        pl.semaphore_wait(greet(peers), len(peers))
        gwo = gwos[0][...].astype(f32)
        for s in range(1, seqs):
            gwo = gwo + gwos[s][...].astype(f32)
        pack(gwo, 3)

    for n in range(3 * seqs):
        t, s = n // seqs, n % seqs

        @pl.when(step == n)
        def _(t=t, s=s):
            if t == 0:
                hat, _ = norm_parts(xw_ref[0].astype(f32))
                low[s] = (hat * g_ref[...] + b_ref[...]).astype(bf16)
            term = dot(low[s], dw_ref[0, 0], TN)
            if s == 0:
                acc[...] = term
            elif s < seqs - 1:
                acc[...] += term
            else:
                pack(acc[...] + term, t)

    base = 3 * seqs

    @pl.when(step == base)
    def _():
        loads[0].wait()
        w0[0:2] = jnp.zeros((2, width), f32)
        w0[2:8] = sums_ref[2:8]

    @pl.when((step >= base) & (step < base + seqs * per_seq))
    def _():
        hat, r = norm_parts(x_ref[0].astype(f32))
        gn = 0.0
        for t in range(3):
            gn = gn + dot(d_ref[0, t], w_ref[:, t * width : (t + 1) * width], NT)
        w0[0:1] += jnp.sum(gn * hat, axis=0, keepdims=True)
        w0[1:2] += jnp.sum(gn, axis=0, keepdims=True)
        g = gn * g_ref[...]
        gx_ref[0] = (
            r
            * (
                g
                - jnp.mean(g, axis=-1, keepdims=True)
                - hat * jnp.mean(g * hat, axis=-1, keepdims=True)
            )
        ).astype(bf16)

    base = base + seqs * per_seq

    @pl.when(step == base)
    def _():
        for c in loads[1:]:
            c.wait()

    @pl.when(step == base - 1)
    def _():
        start(1, None)

    for s in range(seqs):

        @pl.when((step >= base + s * per_seq) & (step < base + (s + 1) * per_seq))
        def _(s=s):
            res_ref[0] = take_rows(backs[s], slot_ref[0]).astype(bf16)

    for when, events in plan:

        @pl.when(step == when)
        def _(events=events):
            for n, t in events:
                finish(n, t)


def last_plan(seqs, per_seq):
    dw = 3 * seqs
    end = dw + 2 * seqs * per_seq - 1
    mid = dw + seqs * per_seq
    first = [
        (2, [(1, 3)]),
        (4, [(1, 0)]),
        (dw, [(1, 1)]),
        (dw + 2, [(1, 2)]),
        (dw + 4, [(2, 3)]),
        (dw + 6, [(2, 0)]),
        (dw + 7, [(3, 3)]),
        (mid, [(2, 1)]),
        (mid + 1, [(3, 0)]),
        (mid + 2, [(1, None), (2, 2), (4, 3)]),
        (mid + 3, [(3, 1)]),
        (mid + 4, [(2, None), (4, 0), (5, 3)]),
        (mid + 5, [(3, 2)]),
        (mid + 6, [(3, None), (4, 1), (5, 0)]),
        (end, [(4, 2), (5, 1), (5, 2)]),
    ]
    return [(min(a, end), b) for a, b in first]


def last_call(d, x, w, gain, bias, gwos, sums, backs, slot_col, experts, nz):
    seqs, length, width = x.shape
    blk = min(BLK, length)
    per_seq = length // blk
    total = backs[0].shape[0]
    dw = 3 * seqs
    mid = dw + seqs * per_seq
    chips = experts // 2
    piece = width // nz // experts
    per = width // nz
    dma = pltpu.SemaphoreType.DMA
    once = pl.Buffered(1)

    def keep(*shape):
        return pl.BlockSpec(shape, lambda r: (0,) * len(shape), pipeline_mode=once)

    def at(first, r):
        n = jnp.clip(r - first, 0, seqs * per_seq - 1)
        return n // per_seq, n % per_seq

    def dw_at(r):
        n = jnp.minimum(r, dw - 1)
        return n % seqs, n // seqs, 0, 0

    def rows(first):
        return pl.BlockSpec((1, blk, width), lambda r: (*at(first, r), 0))

    def d_at(r):
        s, b = at(dw, r)
        return s, 0, b, 0

    steps = mid + seqs * per_seq
    in_specs = [
        pl.BlockSpec((1, 1, length, width), dw_at),
        pl.BlockSpec((1, 3, blk, width), d_at),
        pl.BlockSpec((1, length, width), lambda r: (jnp.minimum(r, seqs - 1), 0, 0)),
        rows(dw),
        ANY,
        keep(1, width),
        keep(1, width),
    ]
    in_specs += [keep(width, width)] * seqs + [keep(8, width)]
    in_specs += [ANY] * seqs
    in_specs += [pl.BlockSpec((1, blk, 1), lambda r: (*at(mid, r), 0))]
    return pl.pallas_call(
        functools.partial(last_body, seqs=seqs, per_seq=per_seq, plan=last_plan(seqs, per_seq)),
        grid=(steps,),
        in_specs=in_specs,
        out_specs=[rows(dw), rows(mid), keep(per, 3 * width), keep(per, width), keep(8, width)],
        out_shape=[
            sds((seqs, length, width), bf16),
            sds((seqs, length, width), bf16),
            sds((per, 3 * width), f32),
            sds((per, width), f32),
            sds((8, width), f32),
        ],
        scratch_shapes=[
            pltpu.VMEM((width, width), f32),
            pltpu.VMEM((seqs, length, width), bf16),
            pltpu.VMEM((GROUPS, 2, chips, nz, piece, width), bf16),
            pltpu.VMEM((GROUPS, chips, nz, piece, width), bf16),
            pltpu.VMEM((GROUPS, chips - 1, nz, piece, width), bf16),
            pltpu.VMEM((GROUPS, nz, piece, width), bf16),
            pltpu.VMEM((GROUPS, nz - 1, piece, width), bf16),
            pltpu.VMEM((GROUPS, 2, chips, piece, width), bf16),
            pltpu.VMEM((8, width), f32),
            pltpu.VMEM((8, width), f32),
            pltpu.VMEM((8, width), f32),
            pltpu.VMEM((chips - 1, 8, width), f32),
            pltpu.VMEM((8, width), f32),
            pltpu.VMEM((nz - 1, 8, width), f32),
            pltpu.VMEM((width, 3 * width), bf16),
            pltpu.VMEM((seqs, total, width), bf16),
        ]
        + [dma((GROUPS, 2 * chips + nz + 1))] * 2
        + [dma((chips + nz,))] * 2
        + [dma((1 + seqs,))],
        compiler_params=pltpu.CompilerParams(
            vmem_limit_bytes=62 << 20, collective_id=1, has_side_effects=True
        ),
        cost_estimate=cost(50 << 30, 150 << 20),
    )(
        d,
        d,
        x,
        x,
        w,
        gain.reshape(1, -1),
        bias.reshape(1, -1),
        *gwos,
        sums,
        *backs,
        slot_col,
    )


def close_body(*refs, counts):
    ga_ref, dx_ref, after_ref, back_ref, gq_ref, go_ref = refs[:6]
    n = len(counts)
    downs, ins = refs[6 : 6 + n], refs[6 + n : 6 + 2 * n]
    gx_out, res_out, gq_out, go_out, down_out, in_out = refs[6 + 2 * n :]
    gx_out[...] = ga_ref[...].astype(f32) + dx_ref[...].astype(f32)
    res_out[...] = after_ref[...].astype(f32) + back_ref[...].astype(f32)
    gq_out[...] = gq_ref[...]
    go_out[...] = go_ref[...]
    at = 0
    for k, down, gin in zip(counts, downs, ins):
        down_out[at : at + k] = down[0].astype(f32)
        for i in range(k):
            in_out[:, (at + i) * FFT : (at + i + 1) * FFT] = gin[0, i].astype(f32)
        at += k


def close_call(ga, dx, after, back, gq, go, downs, ins):
    seqs, length, width = ga.shape
    blk = min(BLK, length)
    per_seq = length // blk
    steps = seqs * per_seq
    counts = [v.shape[1] for v in downs]
    chunks = sum(counts)
    rows = pl.BlockSpec((1, blk, width), lambda r: (r // per_seq, r % per_seq, 0))

    def split(v):
        return pl.BlockSpec((v.shape[0] // steps, v.shape[1]), lambda r: (r, 0))

    def part(v):
        return pl.BlockSpec(
            (1, v.shape[1], v.shape[2] // steps, v.shape[3]), lambda r: (0, 0, r, 0)
        )

    side = ins[0].shape[2]
    return pl.pallas_call(
        functools.partial(close_body, counts=counts),
        grid=(steps,),
        in_specs=[rows] * 4 + [split(gq), split(go)] + [part(v) for v in downs + ins],
        out_specs=[
            rows,
            rows,
            split(gq),
            split(go),
            pl.BlockSpec((chunks, FFT // steps, width), lambda r: (0, r, 0)),
            pl.BlockSpec((side // steps, chunks * FFT), lambda r: (r, 0)),
        ],
        out_shape=[
            sds((seqs, length, width), f32),
            sds((seqs, length, width), f32),
            sds(gq.shape, f32),
            sds(go.shape, f32),
            sds((chunks, FFT, width), f32),
            sds((side, chunks * FFT), f32),
        ],
        compiler_params=params(60),
        cost_estimate=cost(8 << 30, 40 << 20),
    )(ga, dx, after, back, gq, go, *downs, *ins)


def exchange(parts):
    got = lax.all_to_all(parts, "expert", split_axis=0, concat_axis=0, tiled=True)
    return got.reshape(-1, parts.shape[-1])


def on_device(
    tokens_in,
    buckets,
    ln1_gain,
    ln1_bias,
    w_qkv,
    w_out,
    ln2_gain,
    ln2_bias,
    w_in,
    w_down,
    cotangent,
):
    experts = lax.axis_size("expert")
    nz = lax.axis_size("dp")
    seqs, length, width = tokens_in.shape
    capacity = 5 * length // (4 * experts)
    total = experts * capacity
    w_in_local = w_in[0]
    w_down_local = w_down[0]
    hidden = w_in_local.shape[1]
    chunks = hidden // (nz * FFT)

    qkv, full_qkv, full_out, mixed, after, lse, slot_col, cots, rows_a, give = front_call(
        tokens_in,
        ln1_gain,
        ln1_bias,
        ln2_gain,
        ln2_bias,
        w_qkv,
        w_out,
        buckets,
        cotangent,
        HEADS,
        nz,
        experts,
        capacity,
    )
    cots = cots.reshape(seqs, total, width)
    rows_a = rows_a.reshape(total, width)
    rows = [rows_a, exchange(give)]
    act_a, gpre_a = expert_a_call(rows_a, cots, w_in_local, w_down_local, nz)
    last = (gpre_a,)
    acts, gpres, gdowns, gins = [], [], [], []
    for first, many in ((0, 1), (1, chunks - 1)):
        act_b, gpre_b, gdown, gin = expert_b_call(
            rows[0],
            act_a,
            gpre_a,
            rows[1],
            cots,
            w_in_local,
            w_down_local,
            nz,
            first,
            many,
            deps=last,
        )
        last = (act_b,)
        acts.append(act_b)
        gpres.append(gpre_b)
        gdowns.append(lax.psum_scatter(gdown, "dp", scatter_dimension=0, tiled=True))
        gins.append(lax.psum_scatter(gin, "dp", scatter_dimension=0, tiled=True))

    def tokens_of(mids, w, dims, last):
        made = expert_c_call(mids, w, nz, dims, deps=last)
        return exchange(made.reshape(experts, capacity, width)), (made,)

    gtok_a, last = tokens_of([gpre_a], w_in_local, NT, last)
    gtok_b, last = tokens_of(gpres, w_in_local, NT, last)
    out_a, last = tokens_of([act_a], w_down_local, NN, last)
    gtoks = [gtok_a, gtok_b]

    d = ga = None
    gwos = []
    sums_two = 0.0
    for s in range(seqs):
        ga, gmix, gwo, sums = norm_two_call(
            gtoks[s],
            slot_col,
            after,
            cotangent,
            mixed,
            full_out,
            ln2_gain,
            s,
            into={0: ga} if s else None,
            deps=last,
        )
        sums_two = sums_two + sums
        gwos.append(gwo)
        d = attn_bwd_call(qkv, mixed, gmix, lse, HEADS, s, into={0: d} if s else None)
        if s == 0:
            out_b, last = tokens_of(acts, w_down_local, NN, (gmix,))
    outs = [out_a, out_b]
    sums = jnp.concatenate([sums_two] * 4, axis=0)
    dx, back, gq, go, sums = last_call(
        d,
        tokens_in,
        full_qkv,
        ln1_gain,
        ln1_bias,
        gwos,
        sums,
        outs,
        slot_col,
        experts,
        nz,
    )
    gxs, results, gq, go, gdown, gin = close_call(ga, dx, after, back, gq, go, gdowns, gins)
    mine = lax.dynamic_slice_in_dim(
        sums, lax.axis_index("dp") * (width // nz), width // nz, axis=1
    )
    return (
        results,
        gxs,
        mine[0],
        mine[1],
        gq,
        go,
        mine[2],
        mine[3],
        gin[None],
        gdown.reshape(1, hidden // nz, width),
    )


def solution(mesh):
    placed = (
        P(("dp", "expert"), None, None),
        P(("dp", "expert"), None),
        P(),
        P(),
        P("dp", None),
        P("dp", None),
        P(),
        P(),
        P("expert", None, None),
        P("expert", None, None),
        P(("dp", "expert"), None, None),
    )
    return jax.shard_map(
        on_device,
        mesh=mesh,
        in_specs=placed,
        out_specs=(
            P(("dp", "expert"), None, None),
            P(("dp", "expert"), None, None),
            P("dp"),
            P("dp"),
            P("dp", None),
            P("dp", None),
            P("dp"),
            P("dp"),
            P("expert", None, "dp"),
            P("expert", "dp", None),
        ),
        check_vma=False,
    )
```

```python
import functools

import jax
import jax.numpy as jnp
from jax import lax
from jax.experimental import pallas as pl
from jax.experimental.pallas import tpu as pltpu
from jax.sharding import PartitionSpec as P

HEADS = 12
EPS = 1e-5
NEG = -1e30
bf16 = jnp.bfloat16
f32 = jnp.float32
NN = (((1,), (0,)), ((), ()))
NT = (((1,), (1,)), ((), ()))
TN = (((0,), (0,)), ((), ()))
GELU_A = 0.7978845608028654
GELU_B = 0.044715
BLK = 256
FFT = 256


def dot(a, b, dims=NN):
    return lax.dot_general(a, b, dims, preferred_element_type=f32)


def params(mib=56):
    return pltpu.CompilerParams(vmem_limit_bytes=mib << 20)


def cost(flops, nbytes, trans=0):
    return pl.CostEstimate(flops=int(flops), bytes_accessed=int(nbytes), transcendentals=int(trans))


def sds(shape, dtype):
    return jax.ShapeDtypeStruct(shape, dtype)


VM = pl.BlockSpec(memory_space=pltpu.VMEM)
ANY = pl.BlockSpec(memory_space=pl.ANY)


def kernel_call(body, in_specs, args, deps=(), into=None, **options):
    into = into or {}
    count = len(args)
    extra = len(into) + len(deps)

    def wrapped(*refs):
        body(*refs[:count], *refs[count + extra :])

    return pl.pallas_call(
        wrapped,
        in_specs=list(in_specs) + [ANY] * extra,
        input_output_aliases={count + n: out for n, out in enumerate(into)},
        **options,
    )(*args, *into.values(), *deps)


def norm_parts(v):
    centre = jnp.mean(v, axis=-1, keepdims=True)
    shifted = v - centre
    spread = jnp.mean(shifted * shifted, axis=-1, keepdims=True)
    r = lax.rsqrt(spread + EPS)
    return shifted * r, r


MESH = pl.DeviceIdType.MESH


def greet(peers):
    barrier = pltpu.get_barrier_semaphore()
    for peer in peers:
        pl.semaphore_signal(barrier, inc=1, device_id=peer, device_id_type=MESH)
    return barrier


def find_slots(bucket, experts, capacity):
    length = bucket.shape[1]
    hot = (lax.broadcasted_iota(jnp.int32, (experts, length), 0) == bucket).astype(f32)
    upto = lax.broadcasted_iota(jnp.int32, (length, length), 0) <= lax.broadcasted_iota(
        jnp.int32, (length, length), 1
    )
    count = dot(hot.astype(bf16), upto.astype(bf16))
    rank = jnp.sum(hot * count, axis=0, keepdims=True) - 1.0
    return bucket * capacity + rank.astype(jnp.int32)


GATHERS = 3


def front_body(*refs, heads, capacity):
    nz = lax.axis_size("dp")
    n = 9 + 2 * nz
    (x_ref, g1_ref, b1_ref, g2_ref, b2_ref, wq_ref, wo_ref, buckets_ref, cot_ref) = refs[:9]
    w_ins, w_downs = refs[9 : 9 + nz], refs[9 + nz : n]
    (
        qkv_ref,
        fq_ref,
        fo_ref,
        mixed_ref,
        after_ref,
        lse_ref,
        col_ref,
        cots_ref,
        rows_ref,
        act_ref,
        gpre_ref,
    ) = refs[n : n + 11]
    (
        fq_v,
        fo_v,
        sent,
        toks,
        slots,
        rows_v,
        cot_a,
        up_s,
        dn_s,
        core_s,
        z_r,
        core_r,
        own_s,
        load_s,
        save_s,
        stay_s,
        a2a_s,
        a2a_r,
    ) = refs[n + 11 :]
    seqs, length, width = x_ref.shape

    def work(x_v, cot_v, low, qkv_v, mixed_v, after_v):
        return front_work(
            x_ref, g1_ref, b1_ref, g2_ref, b2_ref, wq_ref, wo_ref, buckets_ref, cot_ref,
            qkv_ref, fq_ref, fo_ref, mixed_ref, after_ref, lse_ref, col_ref, cots_ref, rows_ref,
            x_v, cot_v, fq_v, fo_v, low, qkv_v, sent, toks, mixed_v, after_v, slots,
            up_s, dn_s, core_s, z_r, core_r, own_s, load_s, save_s, stay_s, a2a_s, a2a_r,
            heads=heads, capacity=capacity,
        )

    one = pltpu.VMEM((seqs, length, width), bf16)
    pl.run_scoped(work, one, one, one, pltpu.VMEM((seqs, length, 3 * width), bf16), one, one)
    settle = front_lanes(sent, toks, cots_ref, rows_ref, stay_s, a2a_s, a2a_r, capacity)[1]
    for k in range(seqs + 1):
        settle(k)
    load = [
        pltpu.make_async_copy(rows_ref.at[0], rows_v, load_s.at[0, 0]),
        pltpu.make_async_copy(cots_ref.at[0], cot_a, load_s.at[1, 0]),
    ]
    for c in load:
        c.start()
    for c in load:
        c.wait()
    hidden = w_ins[0].shape[1]
    total = rows_v.shape[0]

    def step(*blocks):
        hidden_rows(
            rows_v, cot_a, join_cols(blocks[:nz]), join_rows(blocks[nz : 2 * nz]), *blocks[2 * nz :]
        )

    mid = pl.BlockSpec((1, total, nz * FFT), lambda c: (c, 0, 0))
    pltpu.emit_pipeline(
        step,
        grid=(hidden // (nz * FFT),),
        in_specs=weight_specs(width, hidden, nz),
        out_specs=[mid, mid],
    )(*w_ins, *w_downs, act_ref, gpre_ref)
    for k in range(seqs + 1, 2 * seqs):
        settle(k)


def front_lanes(sent, toks, cots_ref, rows_ref, stay_s, a2a_s, a2a_r, capacity):
    experts = lax.axis_size("expert")
    z = lax.axis_index("dp")
    e = lax.axis_index("expert")
    seqs = cots_ref.shape[0]
    plane = [(e + j) % experts for j in range(1, experts)]
    back = [(e + experts - j) % experts for j in range(1, experts)]

    def lane(n, at):
        src, dst = (sent, cots_ref) if n < seqs else (toks, rows_ref)
        k = n % seqs
        return src.at[k], dst.at[k, pl.ds(pl.multiple_of(at * capacity, 8), capacity)]

    def trade(n, j, at):
        src, dst = lane(n, at)
        return pltpu.make_async_remote_copy(
            src_ref=src.at[plane[j]],
            dst_ref=dst,
            send_sem=a2a_s.at[n, j],
            recv_sem=a2a_r.at[n, j],
            device_id=(z, plane[j]),
            device_id_type=MESH,
        )

    def stay(n):
        src, dst = lane(n, e)
        return pltpu.make_async_copy(src.at[e], dst, stay_s.at[n])

    def spread(n):
        for j in range(experts - 1):
            trade(n, j, e).start()
        stay(n).start()

    def settle(n):
        stay(n).wait()
        for j in range(experts - 1):
            trade(n, j, e).wait_send()
            trade(n, j, back[j]).wait_recv()

    return spread, settle


def front_work(
    x_ref,
    g1_ref,
    b1_ref,
    g2_ref,
    b2_ref,
    wq_ref,
    wo_ref,
    buckets_ref,
    cot_ref,
    qkv_ref,
    fq_ref,
    fo_ref,
    mixed_ref,
    after_ref,
    lse_ref,
    col_ref,
    cots_ref,
    rows_ref,
    x_v,
    cot_v,
    fq_v,
    fo_v,
    low,
    qkv_v,
    sent,
    toks,
    mixed_v,
    after_v,
    slots,
    up_s,
    dn_s,
    core_s,
    z_r,
    core_r,
    own_s,
    load_s,
    save_s,
    stay_s,
    a2a_s,
    a2a_r,
    *,
    heads,
    capacity,
):
    nz = lax.axis_size("dp")
    experts = lax.axis_size("expert")
    z = lax.axis_index("dp")
    e = lax.axis_index("expert")
    core = e % 2
    seqs, length, width = x_ref.shape
    spread = front_lanes(sent, toks, cots_ref, rows_ref, stay_s, a2a_s, a2a_r, capacity)[0]
    per = width // nz
    half = per // 2
    above = (jnp.minimum(z + 1, nz - 1), e)
    below = (jnp.maximum(z - 1, 0), e)
    mate = (z, e + 1 - 2 * core)
    full = (fq_v, fo_v)
    shard = (wq_ref, wo_ref)
    blk = min(BLK, length)

    cot_in = [pltpu.make_async_copy(cot_ref.at[s], cot_v.at[s], load_s.at[0, s]) for s in range(seqs)]
    x_in = [pltpu.make_async_copy(x_ref.at[s], x_v.at[s], load_s.at[1, s]) for s in range(seqs)]
    for c in cot_in[:1] + x_in + cot_in[1:]:
        c.start()

    barrier = pltpu.get_barrier_semaphore()

    @pl.when(z + 1 < nz)
    def _():
        pl.semaphore_signal(barrier, inc=1, device_id=above, device_id_type=MESH)

    @pl.when(z > 0)
    def _():
        pl.semaphore_signal(barrier, inc=1, device_id=below, device_id_type=MESH)

    plane = [(z, (e + j) % experts) for j in range(1, experts)]
    for peer in plane:
        pl.semaphore_signal(barrier, inc=1, device_id=peer, device_id_type=MESH)

    @pl.when((z + 1 < nz) & (z > 0))
    def _():
        pl.semaphore_wait(barrier, experts + 1)

    @pl.when((z + 1 >= nz) | (z <= 0))
    def _():
        pl.semaphore_wait(barrier, experts)

    hs = width // heads
    pairs = heads // 2
    groups = min(GATHERS, pairs)
    wide = width // groups
    lanes = [[(3 * g + m, 0, m * width + g * wide, wide) for m in range(3)] for g in range(groups)]
    lanes.append([(3 * groups, 1, 0, width)])

    def half_rows(ref, at, piece):
        return ref.at[pl.ds(pl.multiple_of(at, 16), half), pl.ds(piece[2], piece[3])]

    def held(piece, p, c):
        return half_rows(full[piece[1]], p * per + c * half, piece)

    def mine(piece):
        return half_rows(shard[piece[1]], core * half, piece)

    def hop(piece, p, c, src, sem, r_sem, peer):
        return pltpu.make_async_remote_copy(
            src_ref=src,
            dst_ref=held(piece, p, c),
            send_sem=sem.at[piece[0], p],
            recv_sem=r_sem.at[piece[0], p],
            device_id=peer,
            device_id_type=MESH,
        )

    def pass_on(piece, p, sem, r_sem, peer):
        return hop(piece, p, core, held(piece, p, core), sem, r_sem, peer)

    def own(piece):
        cols = pl.ds(piece[2], piece[3])
        return pltpu.make_async_copy(
            shard[piece[1]].at[:, cols],
            full[piece[1]].at[pl.ds(pl.multiple_of(z * per, 16), per), cols],
            own_s.at[piece[0]],
        )

    def begin(i):
        for piece in lanes[i]:

            @pl.when(z + 1 < nz)
            def _(piece=piece):
                hop(piece, z, core, mine(piece), up_s, z_r, above).start()

            @pl.when(z > 0)
            def _(piece=piece):
                hop(piece, z, core, mine(piece), dn_s, z_r, below).start()

            own(piece).start()

    def sides(d):
        return ((z - d >= 0, z - d, z + 1 < nz, up_s, above), (z + d < nz, z + d, z > 0, dn_s, below))

    def arrivals(i, d):
        for ok, p, more, sem, peer in sides(d):

            @pl.when(ok)
            def _(p=p, more=more, sem=sem, peer=peer):
                for piece in lanes[i]:
                    pass_on(piece, p, sem, z_r, peer).wait_recv()

                    @pl.when(more)
                    def _(piece=piece):
                        pass_on(piece, p, sem, z_r, peer).start()

                    pass_on(piece, p, core_s, core_r, mate).start()

    def wave(w):
        for i in range(len(lanes)):
            if 0 < w - i < nz:
                arrivals(i, w - i)
            if w == i:
                begin(i)

    def complete(i):
        for piece in lanes[i]:
            own(piece).wait()
            for d in range(1, nz):
                for ok, p, _, _, _ in sides(d):

                    @pl.when(ok)
                    def _(piece=piece, p=p):
                        hop(
                            piece, p, 1 - core, held(piece, p, 1 - core), core_s, core_r, mate
                        ).wait_recv()

    def sent_all(i):
        for piece in lanes[i]:

            @pl.when(z + 1 < nz)
            def _(piece=piece):
                hop(piece, z, core, mine(piece), up_s, z_r, above).wait_send()

            @pl.when(z > 0)
            def _(piece=piece):
                hop(piece, z, core, mine(piece), dn_s, z_r, below).wait_send()

            for d in range(1, nz):
                for ok, p, more, sem, peer in sides(d):

                    @pl.when(ok)
                    def _(piece=piece, p=p):
                        pass_on(piece, p, core_s, core_r, mate).wait_send()

                    @pl.when(ok & more)
                    def _(piece=piece, p=p, sem=sem, peer=peer):
                        pass_on(piece, p, sem, z_r, peer).wait_send()

    def prepare(s):
        slot = find_slots(buckets_ref[s : s + 1, :], experts, capacity)
        slots[s] = slot
        col_ref[s] = jnp.broadcast_to(slot.astype(f32), (8, length)).T[:, :1].astype(jnp.int32)
        cot_in[s].wait()
        place_rows(cot_v[s], slot, sent.at[s])
        spread(s)

    def first_norm(s):
        x_in[s].wait()
        for a in range(0, length, blk):
            hat, _ = norm_parts(x_v[s, a : a + blk].astype(f32))
            low[s, a : a + blk] = (hat * row(g1_ref) + row(b1_ref)).astype(bf16)

    def save(n, src, dst):
        return pltpu.make_async_copy(src, dst, save_s.at[n])

    saves = [save(0, fq_v, fq_ref), save(1, fo_v, fo_ref)]
    for s in range(seqs):
        saves += [
            save(2 + 3 * s, qkv_v.at[s], qkv_ref.at[s]),
            save(3 + 3 * s, mixed_v.at[s], mixed_ref.at[s]),
            save(4 + 3 * s, after_v.at[s], after_ref.at[s]),
        ]

    def project(s, g):
        for _, _, at, size in lanes[g]:
            w = fq_v[:, at : at + size]
            rows = min(512, length)
            for a in range(0, length, rows):
                qkv_v[s, a : a + rows, at : at + size] = dot(low[s, a : a + rows], w).astype(bf16)

    each = pairs // groups

    def attend(g, first, many):
        def pair(n, carry):
            s = first + n // each
            p = g * each + n % each

            def cols(t):
                return pl.ds(pl.multiple_of(t * width + p * 2 * hs, 128), 2 * hs)

            one = pl.ds(s, 1)
            attn_fwd_body(
                qkv_v.at[one, :, cols(0)],
                qkv_v.at[one, :, cols(1)],
                qkv_v.at[one, :, cols(2)],
                mixed_v.at[one, :, cols(0)],
                lse_ref.at[one, pl.ds(p, 1)],
                blk=blk,
                hs=hs,
                scale=hs**-0.5,
                depth=3,
            )
            return carry

        lax.fori_loop(0, many * each, pair, 0)

    def finish(s, out):
        for a in range(0, length, blk):
            rows = slice(a, a + blk)
            after = x_v[s, rows].astype(f32) + dot(mixed_v[s, rows], fo_v[...])
            after_v[s, rows] = after.astype(bf16)
            hat, _ = norm_parts(after)
            low[s, rows] = (hat * row(g2_ref) + row(b2_ref)).astype(bf16)
        saves[4 + 3 * s].start()
        place_rows(low[s], slots[s], out)

    todo = list(range(1, groups + nz))

    def waves(upto):
        while todo and todo[0] <= upto:
            wave(todo.pop(0))

    wave(0)
    prepare(0)
    waves(1)
    for s in range(seqs):
        first_norm(s)
    waves(2)
    for s in range(1, seqs):
        prepare(s)
    for g in range(groups):
        waves(g + nz - 1)
        complete(g)
        for s in range(seqs):
            project(s, g)
        if g < groups - 1:
            attend(g, 0, seqs)
    saves[0].start()
    for s in range(seqs):
        saves[2 + 3 * s].start()
    attend(groups - 1, 0, 1)
    waves(groups + nz - 1)
    complete(groups)
    saves[1].start()
    saves[3].start()
    finish(0, toks.at[0])
    spread(seqs)
    for s in range(1, seqs):
        attend(groups - 1, s, 1)
        saves[3 + 3 * s].start()
        finish(s, toks.at[s])
        spread(seqs + s)
    for i in range(groups + 1):
        sent_all(i)
    for c in saves:
        c.wait()


def row(ref):
    return ref[...].reshape(1, -1)


def front_call(x, g1, b1, g2, b2, wq, wo, buckets, cot, w_in, w_down, heads, nz, experts, capacity):
    seqs, length, width = x.shape
    triple = wq.shape[1]
    dma = pltpu.SemaphoreType.DMA
    slab = (seqs, experts, capacity, width)
    total = experts * capacity
    pairs = heads // 2
    tile = nz * FFT
    chunks = w_in.shape[1] // tile
    return pl.pallas_call(
        functools.partial(front_body, heads=heads, capacity=capacity),
        in_specs=[ANY] + [VM] * 4 + [ANY] * 2 + [VM, ANY] + [ANY] * (2 * nz),
        out_specs=[ANY] * 5 + [VM] * 2 + [ANY] * 4,
        out_shape=[
            sds((seqs, length, triple), bf16),
            sds((width, triple), bf16),
            sds((width, width), bf16),
            sds((seqs, length, width), bf16),
            sds((seqs, length, width), bf16),
            sds((seqs, pairs, 2, length), f32),
            sds((seqs, length, 1), jnp.int32),
            sds((seqs, total, width), bf16),
            sds((seqs, total, width), bf16),
            sds((chunks, total, tile), bf16),
            sds((chunks, total, tile), bf16),
        ],
        scratch_shapes=[
            pltpu.VMEM((width, triple), bf16),
            pltpu.VMEM((width, width), bf16),
            pltpu.VMEM(slab, bf16),
            pltpu.VMEM(slab, bf16),
            pltpu.VMEM((seqs, 1, length), jnp.int32),
            pltpu.VMEM((total, width), bf16),
            pltpu.VMEM((total, width), bf16),
        ]
        + [dma((3 * GATHERS + 1, nz))] * 5
        + [dma((3 * GATHERS + 1,)), dma((2, seqs)), dma((2 + 3 * seqs,)), dma((2 * seqs,))]
        + [dma((2 * seqs, experts - 1))] * 2,
        compiler_params=pltpu.CompilerParams(
            vmem_limit_bytes=62 << 20, collective_id=0, has_side_effects=True
        ),
        cost_estimate=cost(110 << 30, 40 << 20),
    )(x, g1, b1, g2, b2, wq, wo, buckets, cot, *([w_in] * nz), *([w_down] * nz))


def attn_fwd_body(q_ref, k_ref, v_ref, o_ref, lse_ref, *, blk, hs, scale, depth):
    length = q_ref.shape[1]
    lane = lax.broadcasted_iota(jnp.int32, (1, 2 * hs), 1) // hs
    v_t = v_ref[0].T
    keys = k_ref[0]
    kh = [jnp.where(lane == h, keys, jnp.zeros_like(keys)) for h in range(2)]
    ones = jnp.ones((16, length), bf16)
    vh = [jnp.concatenate([v_t[h * hs : (h + 1) * hs], ones], axis=0) for h in range(2)]
    future = lax.broadcasted_iota(jnp.int32, (blk, blk), 0) > lax.broadcasted_iota(
        jnp.int32, (blk, blk), 1
    )
    tasks = [(i, h) for i in range(length // blk) for h in range(2)]

    def score(task):
        i, h = task
        top = (i + 1) * blk
        q = q_ref[0, i * blk : top, :] * jnp.asarray(scale, bf16)
        s = dot(kh[h][:top], q, NT)
        diag = jnp.where(future, NEG, s[i * blk :])
        s = jnp.concatenate([s[: i * blk], diag], axis=0) if i else diag
        return s, jnp.max(s, axis=0, keepdims=True)

    queue = [score(t) for t in tasks[:depth]]
    done = {}
    for at, task in enumerate(tasks):
        if at + depth < len(tasks):
            queue.append(score(tasks[at + depth]))
        s, largest = queue.pop(0)
        i, h = task
        top = (i + 1) * blk
        o = dot(vh[h][:, :top], jnp.exp(s - largest).astype(bf16))
        total = o[hs : hs + 1]
        done[task] = o[:hs] * (1.0 / total)
        lse_ref[0, 0, h : h + 1, i * blk : top] = largest + jnp.log(total)
        if h == 1:
            both = jnp.concatenate([done[(i, 0)], done[(i, 1)]], axis=0)
            o_ref[0, i * blk : top, :] = both.T.astype(bf16)


def attn_bwd_body(
    q_ref, k_ref, v_ref, o_ref, do_ref, lse_ref, d_ref, dqa, doa, *, blk, hs, scale, depth
):
    length = q_ref.shape[1]
    n = length // blk
    lanes = lax.broadcasted_iota(jnp.int32, (1, 2 * hs), 1)
    lane = lanes // hs
    spot = lanes % hs
    keys = k_ref[0]
    vals = v_ref[0]
    k_t = (keys * jnp.asarray(scale, bf16)).T
    kh = [jnp.where(lane == h, keys, jnp.zeros_like(keys)) for h in range(2)]
    vh = [
        jnp.where(lane == h, vals, jnp.where(spot < 2, jnp.ones_like(vals), jnp.zeros_like(vals)))
        for h in range(2)
    ]
    future = lax.broadcasted_iota(jnp.int32, (blk, blk), 0) > lax.broadcasted_iota(
        jnp.int32, (blk, blk), 1
    )
    q = q_ref[0] * jnp.asarray(scale, bf16)
    do = do_ref[0]
    prod = do.astype(f32) * o_ref[0].astype(f32)
    for h in range(2):
        inside = lane == h
        inner = -jnp.sum(jnp.where(inside, prod, 0.0), axis=1, keepdims=True)
        high = inner.astype(bf16)
        rest = (inner - high.astype(f32)).astype(bf16)
        doa[h] = jnp.where(
            inside,
            do,
            jnp.where(spot == 0, high, jnp.where(spot == 1, rest, jnp.zeros_like(high))),
        )
    tasks = [(j, h) for j in range(n) for h in range(2)]

    def score(task):
        j, h = task
        a = j * blk
        return (
            dot(kh[h][a : a + blk], q[a:], NT),
            dot(vh[h][a : a + blk], doa[h, a:], NT),
        )

    queue = [score(t) for t in tasks[:depth]]
    kept = None
    for at, task in enumerate(tasks):
        if at + depth < len(tasks):
            queue.append(score(tasks[at + depth]))
        s, dp = queue.pop(0)
        j, h = task
        a = j * blk
        p = jnp.exp(s - lse_ref[0, 0, h : h + 1, a:])
        diag = jnp.where(future, 0.0, p[:, :blk])
        p = jnp.concatenate([diag, p[:, blk:]], axis=1) if j < n - 1 else diag
        ds = (p * dp).astype(bf16)
        dv = dot(p.astype(bf16), do[a:])
        dk = dot(ds, q[a:])
        dq = dot(k_t[h * hs : (h + 1) * hs, a : a + blk], ds)
        if j == 0:
            dqa[h * hs : (h + 1) * hs, :] = dq
        else:
            dqa[h * hs : (h + 1) * hs, a:] += dq
        if h == 0:
            kept = (dk, dv)
        else:
            d_ref[0, 1, a : a + blk, :] = jnp.where(lane == 0, kept[0], dk).astype(bf16)
            d_ref[0, 2, a : a + blk, :] = jnp.where(lane == 0, kept[1], dv).astype(bf16)
            d_ref[0, 0, a : a + blk, :] = dqa[:, a : a + blk].T.astype(bf16)


def attn_bwd_call(qkv, o, do, lse, heads, at, into=None, deps=()):
    seqs, length, triple = qkv.shape
    n = 1
    width = triple // 3
    hs = width // heads
    pairs = heads // 2
    blk = min(BLK, length)

    def spec(o, at=0):
        return pl.BlockSpec((1, length, 2 * hs), lambda s, p: (s + at, 0, o * pairs + p))

    return kernel_call(
        functools.partial(attn_bwd_body, blk=blk, hs=hs, scale=hs**-0.5, depth=2),
        args=[qkv, qkv, qkv, o, do, lse],
        deps=deps,
        grid=(n, pairs),
        in_specs=[spec(0, at), spec(1, at), spec(2, at), spec(0, at), spec(0)]
        + [pl.BlockSpec((1, 1, 2, length), lambda s, p: (at, p, 0, 0))],
        out_specs=pl.BlockSpec((1, 3, length, 2 * hs), lambda s, p: (at, 0, 0, p)),
        out_shape=sds((seqs, 3, length, width), bf16),
        into=into,
        scratch_shapes=[
            pltpu.VMEM((2 * hs, length), f32),
            pltpu.VMEM((2, length, 2 * hs), bf16),
        ],
        compiler_params=params(60),
        cost_estimate=cost(27 << 30, n * length * width * 16),
    )


def slot_chunk(total):
    return 256 if total % 256 == 0 else total


def place_rows(rows, slot_row, out_ref):
    experts, capacity, _ = out_ref.shape
    base = lax.broadcasted_iota(jnp.int32, (capacity, rows.shape[0]), 0)
    for e in range(experts):
        hot = jnp.where(base + e * capacity == slot_row, 1.0, 0.0).astype(bf16)
        out_ref[e] = dot(hot, rows).astype(bf16)


def take_rows(slots, slot_col):
    total = slots.shape[0]
    at = lax.broadcasted_iota(jnp.int32, (slot_col.shape[0], total), 1)
    return dot(jnp.where(at == slot_col, 1.0, 0.0).astype(bf16), slots)


def gelu_parts(pre):
    sq = pre * pre
    half = 0.5 + 0.5 * jnp.tanh(pre * (GELU_A + (GELU_A * GELU_B) * sq))
    act = pre * half
    slope = half + (act - act * half) * (2 * GELU_A + (6 * GELU_A * GELU_B) * sq)
    return act, slope


def hidden_rows(rows_ref, cot_ref, w_in, w_down, act_ref, gpre_ref, use=None):
    total = rows_ref.shape[0]
    step = slot_chunk(total)
    starts = list(range(0, total, step))

    def first(a):
        return dot(rows_ref[a : a + step], w_in), dot(cot_ref[a : a + step], w_down, NT)

    ahead = first(starts[0])
    for at, a in enumerate(starts):
        pre, gact = ahead
        if at + 1 < len(starts):
            ahead = first(starts[at + 1])
        act, slope = gelu_parts(pre)
        act_low = act.astype(bf16)
        gpre_low = (gact * slope).astype(bf16)
        act_ref[0, a : a + step] = act_low
        gpre_ref[0, a : a + step] = gpre_low
        if use is not None:
            use(a, a + step, act_low, gpre_low)


def join_cols(refs):
    return jnp.concatenate([r[...] for r in refs], axis=1)


def join_rows(refs):
    return jnp.concatenate([r[...] for r in refs], axis=0)


def weight_specs(width, hidden, nz, first=0):
    per = hidden // (nz * FFT)
    ins = [
        pl.BlockSpec((width, FFT), lambda c, z=z: (0, z * per + c + first)) for z in range(nz)
    ]
    downs = [
        pl.BlockSpec((FFT, width), lambda c, z=z: (z * per + c + first, 0)) for z in range(nz)
    ]
    return ins + downs


def expert_b_body(*refs, nz):
    rows_a, cot_a, act_a, gpre_a, rows_b, cot_b = refs[:6]
    rows_a, rows_b = rows_a.at[0], rows_b.at[0]
    w_in = join_cols(refs[6 : 6 + nz])
    w_down = join_rows(refs[6 + nz : 6 + 2 * nz])
    act_b, gpre_b, gdown_ref, gin_ref = refs[6 + 2 * nz :]
    cot_a, cot_b = cot_a.at[0], cot_b.at[0]
    hidden_rows(rows_b, cot_b, w_in, w_down, act_b, gpre_b)
    for z in range(nz):
        cols = slice(z * FFT, (z + 1) * FFT)
        gdown = dot(act_a[0, :, cols], cot_a[...], TN) + dot(act_b[0, :, cols], cot_b[...], TN)
        gdown_ref[z, 0] = gdown.astype(bf16)
        gin = dot(rows_a[...], gpre_a[0, :, cols], TN) + dot(rows_b[...], gpre_b[0, :, cols], TN)
        gin_ref[z, 0] = gin.astype(bf16)


def expert_b_call(rows, act_a, gpre_a, cots, w_in, w_down, nz, first, count, deps=()):
    _, total, width = rows.shape
    tile = nz * FFT
    hidden = w_in.shape[1]
    mid = pl.BlockSpec((1, total, tile), lambda c: (c + first, 0, 0))

    def cot(s):
        return pl.BlockSpec((1, total, width), lambda c: (s, 0, 0))

    mid_out = pl.BlockSpec((1, total, tile), lambda c: (c, 0, 0))
    return kernel_call(
        functools.partial(expert_b_body, nz=nz),
        args=[rows, cots, act_a, gpre_a, rows, cots, *([w_in] * nz), *([w_down] * nz)],
        deps=deps,
        grid=(count,),
        in_specs=[cot(0), cot(0), mid, mid, cot(1), cot(1)] + weight_specs(width, hidden, nz, first),
        out_specs=[
            mid_out,
            mid_out,
            pl.BlockSpec((nz, 1, FFT, width), lambda c: (0, c, 0, 0)),
            pl.BlockSpec((nz, 1, width, FFT), lambda c: (0, c, 0, 0)),
        ],
        out_shape=[
            sds((count, total, tile), bf16),
            sds((count, total, tile), bf16),
            sds((nz, count, FFT, width), bf16),
            sds((nz, count, width, FFT), bf16),
        ],
        compiler_params=params(60),
        cost_estimate=cost(20 * count << 30, 30 << 20),
    )


def expert_c_body(*refs, nz, counts, dims):
    parts = len(counts)
    mids = refs[:parts]
    w_refs = refs[parts : parts + nz]
    out_ref, acc = refs[parts + nz :]
    w = join_cols(w_refs) if dims is NT else join_rows(w_refs)
    c = pl.program_id(0)
    total = acc.shape[0]
    step = slot_chunk(total)
    lo = 0
    for m, k in zip(mids, counts):

        @pl.when((c >= lo) & (c < lo + k))
        def _(m=m, lo=lo):
            for a in range(0, total, step):
                term = dot(m[0, a : a + step], w, dims)
                if lo == 0:
                    acc[a : a + step] = jnp.where(c == 0, term, acc[a : a + step] + term)
                else:
                    acc[a : a + step] += term

        lo += k

    @pl.when(c == pl.num_programs(0) - 1)
    def _():
        out_ref[...] = acc[...].astype(bf16)


def expert_c_call(mids, w, nz, dims, deps=()):
    total, tile = mids[0].shape[1:]
    hidden = tile * sum(m.shape[0] for m in mids)
    width = w.shape[0] if dims is NT else w.shape[1]
    chunks = hidden // tile
    specs = weight_specs(width, hidden, nz)
    specs = specs[:nz] if dims is NT else specs[nz:]
    counts = [m.shape[0] for m in mids]
    blocks = []
    for n, k in enumerate(counts):
        lo = sum(counts[:n])
        blocks.append(
            pl.BlockSpec(
                (1, total, tile), lambda c, lo=lo, k=k: (jnp.clip(c - lo, 0, k - 1), 0, 0)
            )
        )
    return kernel_call(
        functools.partial(expert_c_body, nz=nz, counts=counts, dims=dims),
        args=[*mids, *([w] * nz)],
        deps=deps,
        grid=(chunks,),
        in_specs=blocks + specs,
        out_specs=pl.BlockSpec((total, width), lambda c: (0, 0)),
        out_shape=sds((total, width), bf16),
        scratch_shapes=[pltpu.VMEM((total, width), f32)],
        compiler_params=params(60),
        cost_estimate=cost(10 << 30, 14 << 20),
    )


def norm_two_body(
    back_ref, slot_ref, after_ref, cot_ref, mixed_ref, w_ref, g_ref, ga_ref, gmix_ref, gw_ref, sums_ref, acc
):
    size = after_ref.shape[1]
    part = size // 2
    starts = [0, part]
    back = back_ref[...]
    gts = [take_rows(back, slot_ref[0, a : a + part]) for a in starts]
    gain_sum = 0.0
    bias_sum = 0.0
    for a, gt in zip(starts, gts):
        rows = slice(a, a + part)
        hat, r = norm_parts(after_ref[0, rows].astype(f32))
        gain_sum = gain_sum + jnp.sum(gt * hat, axis=0, keepdims=True)
        bias_sum = bias_sum + jnp.sum(gt, axis=0, keepdims=True)
        s = gt * g_ref[...]
        ga = cot_ref[0, rows].astype(f32) + r * (
            s
            - jnp.mean(s, axis=-1, keepdims=True)
            - hat * jnp.mean(s * hat, axis=-1, keepdims=True)
        )
        ga_ref[0, rows] = ga.astype(bf16)
        gmix_ref[0, rows] = dot(ga_ref[0, rows], w_ref[...], NT).astype(bf16)
    gw = dot(mixed_ref[0], ga_ref[0], TN)
    last = pl.num_programs(0) - 1

    @pl.when(pl.program_id(0) == 0)
    def _():
        acc[...] = gw
        sums_ref[0:1] = gain_sum
        sums_ref[1:2] = bias_sum

    @pl.when(pl.program_id(0) > 0)
    def _():
        acc[...] += gw
        sums_ref[0:1] += gain_sum
        sums_ref[1:2] += bias_sum

    @pl.when(pl.program_id(0) == last)
    def _():
        gw_ref[...] = acc[...].astype(bf16)


def norm_two_call(back, slot_col, after, cot, mixed, w, gain, at, into=None, deps=()):
    seqs, length, width = after.shape
    total = back.shape[0]
    blk = min(2 * BLK, length)

    def keep(*shape):
        return pl.BlockSpec(shape, lambda r: (0,) * len(shape))

    rows = pl.BlockSpec((1, blk, width), lambda r: (at, r, 0))
    single = pl.BlockSpec((1, blk, width), lambda r: (0, r, 0))
    return kernel_call(
        norm_two_body,
        args=[back, slot_col, after, cot, mixed, w, gain.reshape(1, -1)],
        deps=deps,
        into=into,
        grid=(length // blk,),
        in_specs=[
            keep(total, width),
            pl.BlockSpec((1, blk, 1), lambda r: (at, r, 0)),
            rows,
            rows,
            rows,
            keep(width, width),
            keep(1, width),
        ],
        out_specs=[rows, single, keep(width, width), keep(2, width)],
        out_shape=[
            sds((seqs, length, width), bf16),
            sds((1, length, width), bf16),
            sds((width, width), bf16),
            sds((2, width), f32),
        ],
        scratch_shapes=[pltpu.VMEM((width, width), f32)],
        compiler_params=params(60),
        cost_estimate=cost(9 << 30, length * width * 20),
    )


GROUPS = 4


def last_body(*refs, seqs, per_seq, plan):
    (dw_ref, d_ref, xw_ref, x_ref, w_any, g_ref, b_ref) = refs[:7]
    gwos = refs[7 : 7 + seqs]
    sums_ref = refs[7 + seqs]
    backs_any = refs[8 + seqs : 8 + 2 * seqs]
    slot_ref = refs[8 + 2 * seqs]
    gx_ref, res_ref, gq_ref, go_ref, tot_ref = refs[9 + 2 * seqs : 14 + 2 * seqs]
    rest = refs[14 + 2 * seqs :]
    acc, low, pay, r1, r2, s2, r3, fin, w0, v1, w1, v2, w2, v3, w_ref, backs = rest[:16]
    send_s, recv_s, vs_s, vr_s, load_s = rest[16:]
    nz = lax.axis_size("dp")
    experts = lax.axis_size("expert")
    z = lax.axis_index("dp")
    e = lax.axis_index("expert")
    chips = experts // 2
    core = e % 2
    chip = e // 2
    mate = (z, chip * 2 + 1 - core)
    others = [(z, lax.rem(chip + j, chips) * 2 + core) for j in range(1, chips)]
    layers = [(lax.rem(z + j, nz), e) for j in range(1, nz)]
    peers = [mate] + others + layers
    width = x_ref.shape[2]
    step = pl.program_id(0)
    last = pl.num_programs(0) - 1
    s1 = r1

    def copy(src, dst, at, peer, sems=None):
        a, b = sems or (send_s, recv_s)
        return pltpu.make_async_remote_copy(
            src_ref=src,
            dst_ref=dst,
            send_sem=a.at[at],
            recv_sem=b.at[at],
            device_id=peer,
            device_id_type=MESH,
        )

    def stage(n, t):
        if n == 1:
            return [copy(pay.at[t, 1 - core], r1.at[t], (t, 0), mate)]
        if n == 2:
            return [
                copy(
                    s1.at[t, lax.rem(chip + j, chips)], r2.at[t, j - 1], (t, j), others[j - 1]
                )
                for j in range(1, chips)
            ]
        if n == 3:
            return [
                copy(
                    s2.at[t, lax.rem(z + j, nz)], r3.at[t, j - 1], (t, chips + j), layers[j - 1]
                )
                for j in range(1, nz)
            ]
        if n == 4:
            here = fin.at[t, core, chip]
            return [
                copy(here, here, (t, chips + nz + j), others[j - 1]) for j in range(1, chips)
            ]
        side = fin.at[t, core]
        return [copy(side, side, (t, 2 * chips + nz), mate)]

    def vector(n):
        sems = (vs_s, vr_s)
        if n == 1:
            return [copy(w0, v1, 0, mate, sems)]
        if n == 2:
            return [copy(w1, v2.at[j - 1], j, others[j - 1], sems) for j in range(1, chips)]
        return [copy(w2, v3.at[j - 1], chips + j, layers[j - 1], sems) for j in range(1, nz)]

    def start(n, t):
        for c in vector(n) if t is None else stage(n, t):
            c.start()

    def finish(n, t):
        for c in vector(n) if t is None else stage(n, t):
            c.wait()
        if t is None:
            if n == 1:
                w1[...] = w0[...] + v1[...]
            elif n == 2:
                line = w1[...]
                for j in range(1, chips):
                    line = line + v2[j - 1]
                w2[...] = line
            else:
                line = w2[...]
                for j in range(1, nz):
                    line = line + v3[j - 1]
                tot_ref[...] = line
            if n < 3:
                start(n + 1, None)
            return
        if n == 1:
            for k in range(chips):
                s1[t, k] = (pay[t, core, k].astype(f32) + r1[t, k].astype(f32)).astype(bf16)
        elif n == 2:
            part = s1[t, chip].astype(f32)
            for j in range(1, chips):
                part = part + r2[t, j - 1].astype(f32)
            s2[t] = part.astype(bf16)
        elif n == 3:
            part = s2[t, z].astype(f32)
            for j in range(1, nz):
                part = part + r3[t, j - 1].astype(f32)
            fin[t, core, chip] = part.astype(bf16)
        elif n == 5:
            piece = fin.shape[3]
            for c in range(2):
                for k in range(chips):
                    at = (c * chips + k) * piece
                    value = fin[t, c, k].astype(f32)
                    if t < 3:
                        gq_ref[at : at + piece, t * width : (t + 1) * width] = value
                    else:
                        go_ref[at : at + piece, :] = value
        if n < 5:
            start(n + 1, t)

    def pack(value, t):
        per = value.shape[0] // nz
        piece = pay.shape[4]
        for zz in range(nz):
            for c in range(2):
                for k in range(chips):
                    at = zz * per + (c * chips + k) * piece
                    pay[t, c, k, zz] = value[at : at + piece].astype(bf16)
        start(1, t)

    loads = [pltpu.make_async_copy(w_any, w_ref, load_s.at[0])]
    loads += [
        pltpu.make_async_copy(backs_any[s], backs.at[s], load_s.at[1 + s]) for s in range(seqs)
    ]

    @pl.when(step == 0)
    def _():
        for c in loads:
            c.start()
        pl.semaphore_wait(greet(peers), len(peers))
        gwo = gwos[0][...].astype(f32)
        for s in range(1, seqs):
            gwo = gwo + gwos[s][...].astype(f32)
        pack(gwo, 3)

    for n in range(3 * seqs):
        t, s = n // seqs, n % seqs

        @pl.when(step == n)
        def _(t=t, s=s):
            if t == 0:
                hat, _ = norm_parts(xw_ref[0].astype(f32))
                low[s] = (hat * g_ref[...] + b_ref[...]).astype(bf16)
            term = dot(low[s], dw_ref[0, 0], TN)
            if s == 0:
                acc[...] = term
            elif s < seqs - 1:
                acc[...] += term
            else:
                pack(acc[...] + term, t)

    base = 3 * seqs

    @pl.when(step == base)
    def _():
        loads[0].wait()
        w0[0:2] = jnp.zeros((2, width), f32)
        w0[2:8] = sums_ref[2:8]

    @pl.when((step >= base) & (step < base + seqs * per_seq))
    def _():
        hat, r = norm_parts(x_ref[0].astype(f32))
        gn = 0.0
        for t in range(3):
            gn = gn + dot(d_ref[0, t], w_ref[:, t * width : (t + 1) * width], NT)
        w0[0:1] += jnp.sum(gn * hat, axis=0, keepdims=True)
        w0[1:2] += jnp.sum(gn, axis=0, keepdims=True)
        g = gn * g_ref[...]
        gx_ref[0] = (
            r
            * (
                g
                - jnp.mean(g, axis=-1, keepdims=True)
                - hat * jnp.mean(g * hat, axis=-1, keepdims=True)
            )
        ).astype(bf16)

    base = base + seqs * per_seq

    @pl.when(step == base)
    def _():
        for c in loads[1:]:
            c.wait()

    @pl.when(step == base - 1)
    def _():
        start(1, None)

    for s in range(seqs):

        @pl.when((step >= base + s * per_seq) & (step < base + (s + 1) * per_seq))
        def _(s=s):
            res_ref[0] = take_rows(backs[s], slot_ref[0]).astype(bf16)

    for when, events in plan:

        @pl.when(step == when)
        def _(events=events):
            for n, t in events:
                finish(n, t)


def last_plan(seqs, per_seq):
    dw = 3 * seqs
    end = dw + 2 * seqs * per_seq - 1
    mid = dw + seqs * per_seq
    first = [
        (2, [(1, 3)]),
        (4, [(1, 0)]),
        (dw, [(1, 1)]),
        (dw + 2, [(1, 2)]),
        (dw + 4, [(2, 3)]),
        (dw + 6, [(2, 0)]),
        (dw + 7, [(3, 3)]),
        (mid, [(2, 1)]),
        (mid + 1, [(3, 0)]),
        (mid + 2, [(1, None), (2, 2), (4, 3)]),
        (mid + 3, [(3, 1)]),
        (mid + 4, [(2, None), (4, 0), (5, 3)]),
        (mid + 5, [(3, 2)]),
        (mid + 6, [(3, None), (4, 1), (5, 0)]),
        (end, [(4, 2), (5, 1), (5, 2)]),
    ]
    return [(min(a, end), b) for a, b in first]


def last_call(d, x, w, gain, bias, gwos, sums, backs, slot_col, experts, nz):
    seqs, length, width = x.shape
    blk = min(BLK, length)
    per_seq = length // blk
    total = backs[0].shape[0]
    dw = 3 * seqs
    mid = dw + seqs * per_seq
    chips = experts // 2
    piece = width // nz // experts
    per = width // nz
    dma = pltpu.SemaphoreType.DMA
    once = pl.Buffered(1)

    def keep(*shape):
        return pl.BlockSpec(shape, lambda r: (0,) * len(shape), pipeline_mode=once)

    def at(first, r):
        n = jnp.clip(r - first, 0, seqs * per_seq - 1)
        return n // per_seq, n % per_seq

    def dw_at(r):
        n = jnp.minimum(r, dw - 1)
        return n % seqs, n // seqs, 0, 0

    def rows(first):
        return pl.BlockSpec((1, blk, width), lambda r: (*at(first, r), 0))

    def d_at(r):
        s, b = at(dw, r)
        return s, 0, b, 0

    steps = mid + seqs * per_seq
    in_specs = [
        pl.BlockSpec((1, 1, length, width), dw_at),
        pl.BlockSpec((1, 3, blk, width), d_at),
        pl.BlockSpec((1, length, width), lambda r: (jnp.minimum(r, seqs - 1), 0, 0)),
        rows(dw),
        ANY,
        keep(1, width),
        keep(1, width),
    ]
    in_specs += [keep(width, width)] * seqs + [keep(8, width)]
    in_specs += [ANY] * seqs
    in_specs += [pl.BlockSpec((1, blk, 1), lambda r: (*at(mid, r), 0))]
    return pl.pallas_call(
        functools.partial(last_body, seqs=seqs, per_seq=per_seq, plan=last_plan(seqs, per_seq)),
        grid=(steps,),
        in_specs=in_specs,
        out_specs=[rows(dw), rows(mid), keep(per, 3 * width), keep(per, width), keep(8, width)],
        out_shape=[
            sds((seqs, length, width), bf16),
            sds((seqs, length, width), bf16),
            sds((per, 3 * width), f32),
            sds((per, width), f32),
            sds((8, width), f32),
        ],
        scratch_shapes=[
            pltpu.VMEM((width, width), f32),
            pltpu.VMEM((seqs, length, width), bf16),
            pltpu.VMEM((GROUPS, 2, chips, nz, piece, width), bf16),
            pltpu.VMEM((GROUPS, chips, nz, piece, width), bf16),
            pltpu.VMEM((GROUPS, chips - 1, nz, piece, width), bf16),
            pltpu.VMEM((GROUPS, nz, piece, width), bf16),
            pltpu.VMEM((GROUPS, nz - 1, piece, width), bf16),
            pltpu.VMEM((GROUPS, 2, chips, piece, width), bf16),
            pltpu.VMEM((8, width), f32),
            pltpu.VMEM((8, width), f32),
            pltpu.VMEM((8, width), f32),
            pltpu.VMEM((chips - 1, 8, width), f32),
            pltpu.VMEM((8, width), f32),
            pltpu.VMEM((nz - 1, 8, width), f32),
            pltpu.VMEM((width, 3 * width), bf16),
            pltpu.VMEM((seqs, total, width), bf16),
        ]
        + [dma((GROUPS, 2 * chips + nz + 1))] * 2
        + [dma((chips + nz,))] * 2
        + [dma((1 + seqs,))],
        compiler_params=pltpu.CompilerParams(
            vmem_limit_bytes=62 << 20, collective_id=1, has_side_effects=True
        ),
        cost_estimate=cost(50 << 30, 150 << 20),
    )(
        d,
        d,
        x,
        x,
        w,
        gain.reshape(1, -1),
        bias.reshape(1, -1),
        *gwos,
        sums,
        *backs,
        slot_col,
    )


def close_body(*refs, counts):
    ga_ref, dx_ref, after_ref, back_ref, gq_ref, go_ref = refs[:6]
    n = len(counts)
    downs, ins = refs[6 : 6 + n], refs[6 + n : 6 + 2 * n]
    gx_out, res_out, gq_out, go_out, down_out, in_out = refs[6 + 2 * n :]
    gx_out[...] = ga_ref[...].astype(f32) + dx_ref[...].astype(f32)
    res_out[...] = after_ref[...].astype(f32) + back_ref[...].astype(f32)
    gq_out[...] = gq_ref[...]
    go_out[...] = go_ref[...]
    at = 0
    for k, down, gin in zip(counts, downs, ins):
        down_out[at : at + k] = down[0].astype(f32)
        for i in range(k):
            in_out[:, (at + i) * FFT : (at + i + 1) * FFT] = gin[0, i].astype(f32)
        at += k


def close_call(ga, dx, after, back, gq, go, downs, ins):
    seqs, length, width = ga.shape
    blk = min(BLK, length)
    per_seq = length // blk
    steps = seqs * per_seq
    counts = [v.shape[1] for v in downs]
    chunks = sum(counts)
    rows = pl.BlockSpec((1, blk, width), lambda r: (r // per_seq, r % per_seq, 0))

    def split(v):
        return pl.BlockSpec((v.shape[0] // steps, v.shape[1]), lambda r: (r, 0))

    def part(v):
        return pl.BlockSpec(
            (1, v.shape[1], v.shape[2] // steps, v.shape[3]), lambda r: (0, 0, r, 0)
        )

    side = ins[0].shape[2]
    return pl.pallas_call(
        functools.partial(close_body, counts=counts),
        grid=(steps,),
        in_specs=[rows] * 4 + [split(gq), split(go)] + [part(v) for v in downs + ins],
        out_specs=[
            rows,
            rows,
            split(gq),
            split(go),
            pl.BlockSpec((chunks, FFT // steps, width), lambda r: (0, r, 0)),
            pl.BlockSpec((side // steps, chunks * FFT), lambda r: (r, 0)),
        ],
        out_shape=[
            sds((seqs, length, width), f32),
            sds((seqs, length, width), f32),
            sds(gq.shape, f32),
            sds(go.shape, f32),
            sds((chunks, FFT, width), f32),
            sds((side, chunks * FFT), f32),
        ],
        compiler_params=params(60),
        cost_estimate=cost(8 << 30, 40 << 20),
    )(ga, dx, after, back, gq, go, *downs, *ins)


def exchange(parts):
    got = lax.all_to_all(parts, "expert", split_axis=0, concat_axis=0, tiled=True)
    return got.reshape(-1, parts.shape[-1])


def on_device(
    tokens_in,
    buckets,
    ln1_gain,
    ln1_bias,
    w_qkv,
    w_out,
    ln2_gain,
    ln2_bias,
    w_in,
    w_down,
    cotangent,
):
    experts = lax.axis_size("expert")
    nz = lax.axis_size("dp")
    seqs, length, width = tokens_in.shape
    capacity = 5 * length // (4 * experts)
    total = experts * capacity
    w_in_local = w_in[0]
    w_down_local = w_down[0]
    hidden = w_in_local.shape[1]
    chunks = hidden // (nz * FFT)

    qkv, full_qkv, full_out, mixed, after, lse, slot_col, cots, rows, act_a, gpre_a = front_call(
        tokens_in,
        ln1_gain,
        ln1_bias,
        ln2_gain,
        ln2_bias,
        w_qkv,
        w_out,
        buckets,
        cotangent,
        w_in_local,
        w_down_local,
        HEADS,
        nz,
        experts,
        capacity,
    )
    last = ()
    acts, gpres, gdowns, gins = [], [], [], []
    for first, many in ((0, 1), (1, chunks - 1)):
        act_b, gpre_b, gdown, gin = expert_b_call(
            rows,
            act_a,
            gpre_a,
            cots,
            w_in_local,
            w_down_local,
            nz,
            first,
            many,
            deps=last,
        )
        last = (act_b,)
        acts.append(act_b)
        gpres.append(gpre_b)
        gdowns.append(lax.psum_scatter(gdown, "dp", scatter_dimension=0, tiled=True))
        gins.append(lax.psum_scatter(gin, "dp", scatter_dimension=0, tiled=True))

    def tokens_of(mids, w, dims, last):
        made = expert_c_call(mids, w, nz, dims, deps=last)
        return exchange(made.reshape(experts, capacity, width)), (made,)

    gtok_a, last = tokens_of([gpre_a], w_in_local, NT, last)
    gtok_b, last = tokens_of(gpres, w_in_local, NT, last)
    out_a, last = tokens_of([act_a], w_down_local, NN, last)
    gtoks = [gtok_a, gtok_b]

    d = ga = None
    gwos = []
    sums_two = 0.0
    for s in range(seqs):
        ga, gmix, gwo, sums = norm_two_call(
            gtoks[s],
            slot_col,
            after,
            cotangent,
            mixed,
            full_out,
            ln2_gain,
            s,
            into={0: ga} if s else None,
            deps=last,
        )
        sums_two = sums_two + sums
        gwos.append(gwo)
        d = attn_bwd_call(qkv, mixed, gmix, lse, HEADS, s, into={0: d} if s else None)
        if s == 0:
            out_b, last = tokens_of(acts, w_down_local, NN, (gmix,))
    outs = [out_a, out_b]
    sums = jnp.concatenate([sums_two] * 4, axis=0)
    dx, back, gq, go, sums = last_call(
        d,
        tokens_in,
        full_qkv,
        ln1_gain,
        ln1_bias,
        gwos,
        sums,
        outs,
        slot_col,
        experts,
        nz,
    )
    gxs, results, gq, go, gdown, gin = close_call(ga, dx, after, back, gq, go, gdowns, gins)
    mine = lax.dynamic_slice_in_dim(
        sums, lax.axis_index("dp") * (width // nz), width // nz, axis=1
    )
    return (
        results,
        gxs,
        mine[0],
        mine[1],
        gq,
        go,
        mine[2],
        mine[3],
        gin[None],
        gdown.reshape(1, hidden // nz, width),
    )


def solution(mesh):
    placed = (
        P(("dp", "expert"), None, None),
        P(("dp", "expert"), None),
        P(),
        P(),
        P("dp", None),
        P("dp", None),
        P(),
        P(),
        P("expert", None, None),
        P("expert", None, None),
        P(("dp", "expert"), None, None),
    )
    return jax.shard_map(
        on_device,
        mesh=mesh,
        in_specs=placed,
        out_specs=(
            P(("dp", "expert"), None, None),
            P(("dp", "expert"), None, None),
            P("dp"),
            P("dp"),
            P("dp", None),
            P("dp", None),
            P("dp"),
            P("dp"),
            P("expert", None, "dp"),
            P("expert", "dp", None),
        ),
        check_vma=False,
    )
```

```python
import functools

import jax
import jax.numpy as jnp
from jax import lax
from jax.experimental import pallas as pl
from jax.experimental.pallas import tpu as pltpu
from jax.sharding import PartitionSpec as P

HEADS = 12
EPS = 1e-5
NEG = -1e30
bf16 = jnp.bfloat16
f32 = jnp.float32
NN = (((1,), (0,)), ((), ()))
NT = (((1,), (1,)), ((), ()))
TN = (((0,), (0,)), ((), ()))
GELU_A = 0.7978845608028654
GELU_B = 0.044715
BLK = 256
FFT = 256


def dot(a, b, dims=NN):
    return lax.dot_general(a, b, dims, preferred_element_type=f32)


def params(mib=56):
    return pltpu.CompilerParams(vmem_limit_bytes=mib << 20)


def cost(flops, nbytes, trans=0):
    return pl.CostEstimate(flops=int(flops), bytes_accessed=int(nbytes), transcendentals=int(trans))


def sds(shape, dtype):
    return jax.ShapeDtypeStruct(shape, dtype)


VM = pl.BlockSpec(memory_space=pltpu.VMEM)
ANY = pl.BlockSpec(memory_space=pl.ANY)


def kernel_call(body, in_specs, args, deps=(), into=None, **options):
    into = into or {}
    count = len(args)
    extra = len(into) + len(deps)

    def wrapped(*refs):
        body(*refs[:count], *refs[count + extra :])

    return pl.pallas_call(
        wrapped,
        in_specs=list(in_specs) + [ANY] * extra,
        input_output_aliases={count + n: out for n, out in enumerate(into)},
        **options,
    )(*args, *into.values(), *deps)


def norm_parts(v):
    centre = jnp.mean(v, axis=-1, keepdims=True)
    shifted = v - centre
    spread = jnp.mean(shifted * shifted, axis=-1, keepdims=True)
    r = lax.rsqrt(spread + EPS)
    return shifted * r, r


MESH = pl.DeviceIdType.MESH


def greet(peers):
    barrier = pltpu.get_barrier_semaphore()
    for peer in peers:
        pl.semaphore_signal(barrier, inc=1, device_id=peer, device_id_type=MESH)
    return barrier


def find_slots(bucket, experts, capacity):
    length = bucket.shape[1]
    hot = (lax.broadcasted_iota(jnp.int32, (experts, length), 0) == bucket).astype(f32)
    upto = lax.broadcasted_iota(jnp.int32, (length, length), 0) <= lax.broadcasted_iota(
        jnp.int32, (length, length), 1
    )
    count = dot(hot.astype(bf16), upto.astype(bf16))
    rank = jnp.sum(hot * count, axis=0, keepdims=True) - 1.0
    return bucket * capacity + rank.astype(jnp.int32)


GATHERS = 3


def front_body(*refs, heads, capacity):
    nz = lax.axis_size("dp")
    n = 9 + 2 * nz
    (x_ref, g1_ref, b1_ref, g2_ref, b2_ref, wq_ref, wo_ref, buckets_ref, cot_ref) = refs[:9]
    w_ins, w_downs = refs[9 : 9 + nz], refs[9 + nz : n]
    (
        qkv_ref,
        fq_ref,
        fo_ref,
        mixed_ref,
        after_ref,
        lse_ref,
        col_ref,
        cots_ref,
        rows_ref,
        act_ref,
        gpre_ref,
    ) = refs[n : n + 11]
    (
        fq_v,
        fo_v,
        sent,
        toks,
        slots,
        rows_v,
        cot_a,
        up_s,
        dn_s,
        core_s,
        z_r,
        core_r,
        own_s,
        load_s,
        save_s,
        stay_s,
        a2a_s,
        a2a_r,
    ) = refs[n + 11 :]
    seqs, length, width = x_ref.shape

    def work(x_v, cot_v, low, qkv_v, mixed_v, after_v):
        return front_work(
            x_ref, g1_ref, b1_ref, g2_ref, b2_ref, wq_ref, wo_ref, buckets_ref, cot_ref,
            qkv_ref, fq_ref, fo_ref, mixed_ref, after_ref, lse_ref, col_ref, cots_ref, rows_ref,
            x_v, cot_v, fq_v, fo_v, low, qkv_v, sent, toks, mixed_v, after_v, slots,
            up_s, dn_s, core_s, z_r, core_r, own_s, load_s, save_s, stay_s, a2a_s, a2a_r,
            heads=heads, capacity=capacity,
        )

    one = pltpu.VMEM((seqs, length, width), bf16)
    pl.run_scoped(work, one, one, one, pltpu.VMEM((seqs, length, 3 * width), bf16), one, one)
    settle = front_lanes(sent, toks, cots_ref, rows_ref, stay_s, a2a_s, a2a_r, capacity)[1]
    for k in range(seqs + 1):
        settle(k)
    load = [
        pltpu.make_async_copy(rows_ref.at[0], rows_v, load_s.at[0, 0]),
        pltpu.make_async_copy(cots_ref.at[0], cot_a, load_s.at[1, 0]),
    ]
    for c in load:
        c.start()
    for c in load:
        c.wait()
    hidden = w_ins[0].shape[1]
    total = rows_v.shape[0]

    def step(*blocks):
        hidden_rows(
            rows_v, cot_a, join_cols(blocks[:nz]), join_rows(blocks[nz : 2 * nz]), *blocks[2 * nz :]
        )

    mid = pl.BlockSpec((1, total, nz * FFT), lambda c: (c, 0, 0))
    pltpu.emit_pipeline(
        step,
        grid=(hidden // (nz * FFT),),
        in_specs=weight_specs(width, hidden, nz),
        out_specs=[mid, mid],
    )(*w_ins, *w_downs, act_ref, gpre_ref)
    for k in range(seqs + 1, 2 * seqs):
        settle(k)


def front_lanes(sent, toks, cots_ref, rows_ref, stay_s, a2a_s, a2a_r, capacity):
    experts = lax.axis_size("expert")
    z = lax.axis_index("dp")
    e = lax.axis_index("expert")
    seqs = cots_ref.shape[0]
    plane = [(e + j) % experts for j in range(1, experts)]
    back = [(e + experts - j) % experts for j in range(1, experts)]

    def lane(n, at):
        src, dst = (sent, cots_ref) if n < seqs else (toks, rows_ref)
        k = n % seqs
        return src.at[k], dst.at[k, pl.ds(pl.multiple_of(at * capacity, 8), capacity)]

    def trade(n, j, at):
        src, dst = lane(n, at)
        return pltpu.make_async_remote_copy(
            src_ref=src.at[plane[j]],
            dst_ref=dst,
            send_sem=a2a_s.at[n, j],
            recv_sem=a2a_r.at[n, j],
            device_id=(z, plane[j]),
            device_id_type=MESH,
        )

    def stay(n):
        src, dst = lane(n, e)
        return pltpu.make_async_copy(src.at[e], dst, stay_s.at[n])

    def spread(n):
        for j in range(experts - 1):
            trade(n, j, e).start()
        stay(n).start()

    def settle(n):
        stay(n).wait()
        for j in range(experts - 1):
            trade(n, j, e).wait_send()
            trade(n, j, back[j]).wait_recv()

    return spread, settle


def front_work(
    x_ref,
    g1_ref,
    b1_ref,
    g2_ref,
    b2_ref,
    wq_ref,
    wo_ref,
    buckets_ref,
    cot_ref,
    qkv_ref,
    fq_ref,
    fo_ref,
    mixed_ref,
    after_ref,
    lse_ref,
    col_ref,
    cots_ref,
    rows_ref,
    x_v,
    cot_v,
    fq_v,
    fo_v,
    low,
    qkv_v,
    sent,
    toks,
    mixed_v,
    after_v,
    slots,
    up_s,
    dn_s,
    core_s,
    z_r,
    core_r,
    own_s,
    load_s,
    save_s,
    stay_s,
    a2a_s,
    a2a_r,
    *,
    heads,
    capacity,
):
    nz = lax.axis_size("dp")
    experts = lax.axis_size("expert")
    z = lax.axis_index("dp")
    e = lax.axis_index("expert")
    core = e % 2
    seqs, length, width = x_ref.shape
    spread = front_lanes(sent, toks, cots_ref, rows_ref, stay_s, a2a_s, a2a_r, capacity)[0]
    per = width // nz
    half = per // 2
    above = (jnp.minimum(z + 1, nz - 1), e)
    below = (jnp.maximum(z - 1, 0), e)
    mate = (z, e + 1 - 2 * core)
    full = (fq_v, fo_v)
    shard = (wq_ref, wo_ref)
    blk = min(BLK, length)

    cot_in = [pltpu.make_async_copy(cot_ref.at[s], cot_v.at[s], load_s.at[0, s]) for s in range(seqs)]
    x_in = [pltpu.make_async_copy(x_ref.at[s], x_v.at[s], load_s.at[1, s]) for s in range(seqs)]
    for c in cot_in[:1] + x_in + cot_in[1:]:
        c.start()

    barrier = pltpu.get_barrier_semaphore()

    @pl.when(z + 1 < nz)
    def _():
        pl.semaphore_signal(barrier, inc=1, device_id=above, device_id_type=MESH)

    @pl.when(z > 0)
    def _():
        pl.semaphore_signal(barrier, inc=1, device_id=below, device_id_type=MESH)

    plane = [(z, (e + j) % experts) for j in range(1, experts)]
    for peer in plane:
        pl.semaphore_signal(barrier, inc=1, device_id=peer, device_id_type=MESH)

    @pl.when((z + 1 < nz) & (z > 0))
    def _():
        pl.semaphore_wait(barrier, experts + 1)

    @pl.when((z + 1 >= nz) | (z <= 0))
    def _():
        pl.semaphore_wait(barrier, experts)

    hs = width // heads
    pairs = heads // 2
    groups = min(GATHERS, pairs)
    wide = width // groups
    lanes = [[(3 * g + m, 0, m * width + g * wide, wide) for m in range(3)] for g in range(groups)]
    lanes.append([(3 * groups, 1, 0, width)])

    def half_rows(ref, at, piece):
        return ref.at[pl.ds(pl.multiple_of(at, 16), half), pl.ds(piece[2], piece[3])]

    def held(piece, p, c):
        return half_rows(full[piece[1]], p * per + c * half, piece)

    def mine(piece):
        return half_rows(shard[piece[1]], core * half, piece)

    def hop(piece, p, c, src, sem, r_sem, peer):
        return pltpu.make_async_remote_copy(
            src_ref=src,
            dst_ref=held(piece, p, c),
            send_sem=sem.at[piece[0], p],
            recv_sem=r_sem.at[piece[0], p],
            device_id=peer,
            device_id_type=MESH,
        )

    def pass_on(piece, p, sem, r_sem, peer):
        return hop(piece, p, core, held(piece, p, core), sem, r_sem, peer)

    def own(piece):
        cols = pl.ds(piece[2], piece[3])
        return pltpu.make_async_copy(
            shard[piece[1]].at[:, cols],
            full[piece[1]].at[pl.ds(pl.multiple_of(z * per, 16), per), cols],
            own_s.at[piece[0]],
        )

    def begin(i):
        for piece in lanes[i]:

            @pl.when(z + 1 < nz)
            def _(piece=piece):
                hop(piece, z, core, mine(piece), up_s, z_r, above).start()

            @pl.when(z > 0)
            def _(piece=piece):
                hop(piece, z, core, mine(piece), dn_s, z_r, below).start()

            own(piece).start()

    def sides(d):
        return ((z - d >= 0, z - d, z + 1 < nz, up_s, above), (z + d < nz, z + d, z > 0, dn_s, below))

    def arrivals(i, d):
        for ok, p, more, sem, peer in sides(d):

            @pl.when(ok)
            def _(p=p, more=more, sem=sem, peer=peer):
                for piece in lanes[i]:
                    pass_on(piece, p, sem, z_r, peer).wait_recv()

                    @pl.when(more)
                    def _(piece=piece):
                        pass_on(piece, p, sem, z_r, peer).start()

                    pass_on(piece, p, core_s, core_r, mate).start()

    def wave(w):
        for i in range(len(lanes)):
            if 0 < w - i < nz:
                arrivals(i, w - i)
            if w == i:
                begin(i)

    def complete(i):
        for piece in lanes[i]:
            own(piece).wait()
            for d in range(1, nz):
                for ok, p, _, _, _ in sides(d):

                    @pl.when(ok)
                    def _(piece=piece, p=p):
                        hop(
                            piece, p, 1 - core, held(piece, p, 1 - core), core_s, core_r, mate
                        ).wait_recv()

    def sent_all(i):
        for piece in lanes[i]:

            @pl.when(z + 1 < nz)
            def _(piece=piece):
                hop(piece, z, core, mine(piece), up_s, z_r, above).wait_send()

            @pl.when(z > 0)
            def _(piece=piece):
                hop(piece, z, core, mine(piece), dn_s, z_r, below).wait_send()

            for d in range(1, nz):
                for ok, p, more, sem, peer in sides(d):

                    @pl.when(ok)
                    def _(piece=piece, p=p):
                        pass_on(piece, p, core_s, core_r, mate).wait_send()

                    @pl.when(ok & more)
                    def _(piece=piece, p=p, sem=sem, peer=peer):
                        pass_on(piece, p, sem, z_r, peer).wait_send()

    def prepare(s):
        slot = find_slots(buckets_ref[s : s + 1, :], experts, capacity)
        slots[s] = slot
        col_ref[s] = jnp.broadcast_to(slot.astype(f32), (8, length)).T[:, :1].astype(jnp.int32)
        cot_in[s].wait()
        place_rows(cot_v[s], slot, sent.at[s])
        spread(s)

    def first_norm(s):
        x_in[s].wait()
        for a in range(0, length, blk):
            hat, _ = norm_parts(x_v[s, a : a + blk].astype(f32))
            low[s, a : a + blk] = (hat * row(g1_ref) + row(b1_ref)).astype(bf16)

    def save(n, src, dst):
        return pltpu.make_async_copy(src, dst, save_s.at[n])

    saves = [save(0, fq_v, fq_ref), save(1, fo_v, fo_ref)]
    for s in range(seqs):
        saves += [
            save(2 + 3 * s, qkv_v.at[s], qkv_ref.at[s]),
            save(3 + 3 * s, mixed_v.at[s], mixed_ref.at[s]),
            save(4 + 3 * s, after_v.at[s], after_ref.at[s]),
        ]

    def project(s, g):
        for _, _, at, size in lanes[g]:
            w = fq_v[:, at : at + size]
            rows = min(512, length)
            for a in range(0, length, rows):
                qkv_v[s, a : a + rows, at : at + size] = dot(low[s, a : a + rows], w).astype(bf16)

    each = pairs // groups

    def attend(g, first, many):
        def pair(n, carry):
            s = first + n // each
            p = g * each + n % each

            def cols(t):
                return pl.ds(pl.multiple_of(t * width + p * 2 * hs, 128), 2 * hs)

            one = pl.ds(s, 1)
            attn_fwd_body(
                qkv_v.at[one, :, cols(0)],
                qkv_v.at[one, :, cols(1)],
                qkv_v.at[one, :, cols(2)],
                mixed_v.at[one, :, cols(0)],
                lse_ref.at[one, pl.ds(p, 1)],
                blk=blk,
                hs=hs,
                scale=hs**-0.5,
                depth=3,
            )
            return carry

        lax.fori_loop(0, many * each, pair, 0)

    def finish(s, out):
        for a in range(0, length, blk):
            rows = slice(a, a + blk)
            after = x_v[s, rows].astype(f32) + dot(mixed_v[s, rows], fo_v[...])
            after_v[s, rows] = after.astype(bf16)
            hat, _ = norm_parts(after)
            low[s, rows] = (hat * row(g2_ref) + row(b2_ref)).astype(bf16)
        saves[4 + 3 * s].start()
        place_rows(low[s], slots[s], out)

    todo = list(range(1, groups + nz))

    def waves(upto):
        while todo and todo[0] <= upto:
            wave(todo.pop(0))

    wave(0)
    prepare(0)
    waves(1)
    for s in range(seqs):
        first_norm(s)
    waves(2)
    for s in range(1, seqs):
        prepare(s)
    for g in range(groups):
        waves(g + nz - 1)
        complete(g)
        for s in range(seqs):
            project(s, g)
        if g < groups - 1:
            attend(g, 0, seqs)
    saves[0].start()
    for s in range(seqs):
        saves[2 + 3 * s].start()
    attend(groups - 1, 0, 1)
    waves(groups + nz - 1)
    complete(groups)
    saves[1].start()
    saves[3].start()
    finish(0, toks.at[0])
    spread(seqs)
    for s in range(1, seqs):
        attend(groups - 1, s, 1)
        saves[3 + 3 * s].start()
        finish(s, toks.at[s])
        spread(seqs + s)
    for i in range(groups + 1):
        sent_all(i)
    for c in saves:
        c.wait()


def row(ref):
    return ref[...].reshape(1, -1)


def front_call(x, g1, b1, g2, b2, wq, wo, buckets, cot, w_in, w_down, heads, nz, experts, capacity):
    seqs, length, width = x.shape
    triple = wq.shape[1]
    dma = pltpu.SemaphoreType.DMA
    slab = (seqs, experts, capacity, width)
    total = experts * capacity
    pairs = heads // 2
    tile = nz * FFT
    chunks = w_in.shape[1] // tile
    return pl.pallas_call(
        functools.partial(front_body, heads=heads, capacity=capacity),
        in_specs=[ANY] + [VM] * 4 + [ANY] * 2 + [VM, ANY] + [ANY] * (2 * nz),
        out_specs=[ANY] * 5 + [VM] * 2 + [ANY] * 4,
        out_shape=[
            sds((seqs, length, triple), bf16),
            sds((width, triple), bf16),
            sds((width, width), bf16),
            sds((seqs, length, width), bf16),
            sds((seqs, length, width), bf16),
            sds((seqs, pairs, 2, length), f32),
            sds((seqs, length, 1), jnp.int32),
            sds((seqs, total, width), bf16),
            sds((seqs, total, width), bf16),
            sds((chunks, total, tile), bf16),
            sds((chunks, total, tile), bf16),
        ],
        scratch_shapes=[
            pltpu.VMEM((width, triple), bf16),
            pltpu.VMEM((width, width), bf16),
            pltpu.VMEM(slab, bf16),
            pltpu.VMEM(slab, bf16),
            pltpu.VMEM((seqs, 1, length), jnp.int32),
            pltpu.VMEM((total, width), bf16),
            pltpu.VMEM((total, width), bf16),
        ]
        + [dma((3 * GATHERS + 1, nz))] * 5
        + [dma((3 * GATHERS + 1,)), dma((2, seqs)), dma((2 + 3 * seqs,)), dma((2 * seqs,))]
        + [dma((2 * seqs, experts - 1))] * 2,
        compiler_params=pltpu.CompilerParams(
            vmem_limit_bytes=62 << 20, collective_id=0, has_side_effects=True
        ),
        cost_estimate=cost(110 << 30, 40 << 20),
    )(x, g1, b1, g2, b2, wq, wo, buckets, cot, *([w_in] * nz), *([w_down] * nz))


def attn_fwd_body(q_ref, k_ref, v_ref, o_ref, lse_ref, *, blk, hs, scale, depth):
    length = q_ref.shape[1]
    lane = lax.broadcasted_iota(jnp.int32, (1, 2 * hs), 1) // hs
    v_t = v_ref[0].T
    keys = k_ref[0]
    kh = [jnp.where(lane == h, keys, jnp.zeros_like(keys)) for h in range(2)]
    ones = jnp.ones((16, length), bf16)
    vh = [jnp.concatenate([v_t[h * hs : (h + 1) * hs], ones], axis=0) for h in range(2)]
    future = lax.broadcasted_iota(jnp.int32, (blk, blk), 0) > lax.broadcasted_iota(
        jnp.int32, (blk, blk), 1
    )
    tasks = [(i, h) for i in range(length // blk) for h in range(2)]

    def score(task):
        i, h = task
        top = (i + 1) * blk
        q = q_ref[0, i * blk : top, :] * jnp.asarray(scale, bf16)
        s = dot(kh[h][:top], q, NT)
        diag = jnp.where(future, NEG, s[i * blk :])
        s = jnp.concatenate([s[: i * blk], diag], axis=0) if i else diag
        return s, jnp.max(s, axis=0, keepdims=True)

    queue = [score(t) for t in tasks[:depth]]
    done = {}
    for at, task in enumerate(tasks):
        if at + depth < len(tasks):
            queue.append(score(tasks[at + depth]))
        s, largest = queue.pop(0)
        i, h = task
        top = (i + 1) * blk
        o = dot(vh[h][:, :top], jnp.exp(s - largest).astype(bf16))
        total = o[hs : hs + 1]
        done[task] = o[:hs] * (1.0 / total)
        lse_ref[0, 0, h : h + 1, i * blk : top] = largest + jnp.log(total)
        if h == 1:
            both = jnp.concatenate([done[(i, 0)], done[(i, 1)]], axis=0)
            o_ref[0, i * blk : top, :] = both.T.astype(bf16)


def attn_bwd_body(
    q_ref, k_ref, v_ref, o_ref, do_ref, lse_ref, d_ref, dqa, doa, *, blk, hs, scale, depth
):
    length = q_ref.shape[1]
    n = length // blk
    lanes = lax.broadcasted_iota(jnp.int32, (1, 2 * hs), 1)
    lane = lanes // hs
    spot = lanes % hs
    keys = k_ref[0]
    vals = v_ref[0]
    k_t = (keys * jnp.asarray(scale, bf16)).T
    kh = [jnp.where(lane == h, keys, jnp.zeros_like(keys)) for h in range(2)]
    vh = [
        jnp.where(lane == h, vals, jnp.where(spot < 2, jnp.ones_like(vals), jnp.zeros_like(vals)))
        for h in range(2)
    ]
    future = lax.broadcasted_iota(jnp.int32, (blk, blk), 0) > lax.broadcasted_iota(
        jnp.int32, (blk, blk), 1
    )
    q = q_ref[0] * jnp.asarray(scale, bf16)
    do = do_ref[0]
    prod = do.astype(f32) * o_ref[0].astype(f32)
    for h in range(2):
        inside = lane == h
        inner = -jnp.sum(jnp.where(inside, prod, 0.0), axis=1, keepdims=True)
        high = inner.astype(bf16)
        rest = (inner - high.astype(f32)).astype(bf16)
        doa[h] = jnp.where(
            inside,
            do,
            jnp.where(spot == 0, high, jnp.where(spot == 1, rest, jnp.zeros_like(high))),
        )
    tasks = [(j, h) for j in range(n) for h in range(2)]

    def score(task):
        j, h = task
        a = j * blk
        return (
            dot(kh[h][a : a + blk], q[a:], NT),
            dot(vh[h][a : a + blk], doa[h, a:], NT),
        )

    queue = [score(t) for t in tasks[:depth]]
    kept = None
    for at, task in enumerate(tasks):
        if at + depth < len(tasks):
            queue.append(score(tasks[at + depth]))
        s, dp = queue.pop(0)
        j, h = task
        a = j * blk
        p = jnp.exp(s - lse_ref[0, 0, h : h + 1, a:])
        diag = jnp.where(future, 0.0, p[:, :blk])
        p = jnp.concatenate([diag, p[:, blk:]], axis=1) if j < n - 1 else diag
        ds = (p * dp).astype(bf16)
        dv = dot(p.astype(bf16), do[a:])
        dk = dot(ds, q[a:])
        dq = dot(k_t[h * hs : (h + 1) * hs, a : a + blk], ds)
        if j == 0:
            dqa[h * hs : (h + 1) * hs, :] = dq
        else:
            dqa[h * hs : (h + 1) * hs, a:] += dq
        if h == 0:
            kept = (dk, dv)
        else:
            d_ref[0, 1, a : a + blk, :] = jnp.where(lane == 0, kept[0], dk).astype(bf16)
            d_ref[0, 2, a : a + blk, :] = jnp.where(lane == 0, kept[1], dv).astype(bf16)
            d_ref[0, 0, a : a + blk, :] = dqa[:, a : a + blk].T.astype(bf16)


def slot_chunk(total):
    return 256 if total % 256 == 0 else total


def place_rows(rows, slot_row, out_ref):
    experts, capacity, _ = out_ref.shape
    base = lax.broadcasted_iota(jnp.int32, (capacity, rows.shape[0]), 0)
    for e in range(experts):
        hot = jnp.where(base + e * capacity == slot_row, 1.0, 0.0).astype(bf16)
        out_ref[e] = dot(hot, rows).astype(bf16)


def take_rows(slots, slot_col):
    total = slots.shape[0]
    at = lax.broadcasted_iota(jnp.int32, (slot_col.shape[0], total), 1)
    return dot(jnp.where(at == slot_col, 1.0, 0.0).astype(bf16), slots)


def gelu_parts(pre):
    sq = pre * pre
    half = 0.5 + 0.5 * jnp.tanh(pre * (GELU_A + (GELU_A * GELU_B) * sq))
    act = pre * half
    slope = half + (act - act * half) * (2 * GELU_A + (6 * GELU_A * GELU_B) * sq)
    return act, slope


def hidden_rows(rows_ref, cot_ref, w_in, w_down, act_ref, gpre_ref, use=None):
    total = rows_ref.shape[0]
    step = slot_chunk(total)
    starts = list(range(0, total, step))

    def first(a):
        return dot(rows_ref[a : a + step], w_in), dot(cot_ref[a : a + step], w_down, NT)

    ahead = first(starts[0])
    for at, a in enumerate(starts):
        pre, gact = ahead
        if at + 1 < len(starts):
            ahead = first(starts[at + 1])
        act, slope = gelu_parts(pre)
        act_low = act.astype(bf16)
        gpre_low = (gact * slope).astype(bf16)
        act_ref[0, a : a + step] = act_low
        gpre_ref[0, a : a + step] = gpre_low
        if use is not None:
            use(a, a + step, act_low, gpre_low)


def join_cols(refs):
    return jnp.concatenate([r[...] for r in refs], axis=1)


def join_rows(refs):
    return jnp.concatenate([r[...] for r in refs], axis=0)


def weight_specs(width, hidden, nz, first=0):
    per = hidden // (nz * FFT)
    ins = [
        pl.BlockSpec((width, FFT), lambda c, z=z: (0, z * per + c + first)) for z in range(nz)
    ]
    downs = [
        pl.BlockSpec((FFT, width), lambda c, z=z: (z * per + c + first, 0)) for z in range(nz)
    ]
    return ins + downs


def expert_b_body(*refs, nz):
    rows_a, cot_a, act_a, gpre_a, rows_b, cot_b = refs[:6]
    rows_a, rows_b = rows_a.at[0], rows_b.at[0]
    w_in = join_cols(refs[6 : 6 + nz])
    w_down = join_rows(refs[6 + nz : 6 + 2 * nz])
    act_b, gpre_b, gdown_ref, gin_ref = refs[6 + 2 * nz :]
    cot_a, cot_b = cot_a.at[0], cot_b.at[0]
    hidden_rows(rows_b, cot_b, w_in, w_down, act_b, gpre_b)
    for z in range(nz):
        cols = slice(z * FFT, (z + 1) * FFT)
        gdown = dot(act_a[0, :, cols], cot_a[...], TN) + dot(act_b[0, :, cols], cot_b[...], TN)
        gdown_ref[z, 0] = gdown.astype(bf16)
        gin = dot(rows_a[...], gpre_a[0, :, cols], TN) + dot(rows_b[...], gpre_b[0, :, cols], TN)
        gin_ref[z, 0] = gin.astype(bf16)


def expert_b_call(rows, act_a, gpre_a, cots, w_in, w_down, nz, first, count, deps=()):
    _, total, width = rows.shape
    tile = nz * FFT
    hidden = w_in.shape[1]
    mid = pl.BlockSpec((1, total, tile), lambda c: (c + first, 0, 0))

    def cot(s):
        return pl.BlockSpec((1, total, width), lambda c: (s, 0, 0))

    mid_out = pl.BlockSpec((1, total, tile), lambda c: (c, 0, 0))
    return kernel_call(
        functools.partial(expert_b_body, nz=nz),
        args=[rows, cots, act_a, gpre_a, rows, cots, *([w_in] * nz), *([w_down] * nz)],
        deps=deps,
        grid=(count,),
        in_specs=[cot(0), cot(0), mid, mid, cot(1), cot(1)] + weight_specs(width, hidden, nz, first),
        out_specs=[
            mid_out,
            mid_out,
            pl.BlockSpec((nz, 1, FFT, width), lambda c: (0, c, 0, 0)),
            pl.BlockSpec((nz, 1, width, FFT), lambda c: (0, c, 0, 0)),
        ],
        out_shape=[
            sds((count, total, tile), bf16),
            sds((count, total, tile), bf16),
            sds((nz, count, FFT, width), bf16),
            sds((nz, count, width, FFT), bf16),
        ],
        compiler_params=params(60),
        cost_estimate=cost(20 * count << 30, 30 << 20),
    )


def back_body(*refs, heads, capacity, split):
    pieces = len(split)
    acts_a, gpres_a = refs[:2]
    acts_b, gpres_b = refs[2 : 2 + pieces], refs[2 + pieces : 2 + 2 * pieces]
    (
        w_in,
        w_down,
        qkv_ref,
        mixed_ref,
        after_ref,
        cot_ref,
        fo_ref,
        lse_ref,
        slot_ref,
        g_ref,
        d_ref,
        ga_ref,
        gtoks_ref,
        outs_ref,
        gw_ref,
        sums_ref,
        slab_g,
        slab_o,
        qkv_v,
        mixed_v,
        after_v,
        cot_v,
        fo_v,
        load_s,
        mid_s,
        w_s,
        save_s,
        stay_s,
        a2a_s,
        a2a_r,
    ) = refs[2 + 2 * pieces :]
    nz = lax.axis_size("dp")
    experts = lax.axis_size("expert")
    z = lax.axis_index("dp")
    e = lax.axis_index("expert")
    seqs, total, width = gtoks_ref.shape
    length = after_ref.shape[1]
    hidden = w_in.shape[1]
    tile = nz * FFT
    chunks = hidden // tile
    peers = [(z, (e + j) % experts) for j in range(1, experts)]

    def load(n, src, dst):
        return pltpu.make_async_copy(src, dst, load_s.at[n])

    early = [load(0, fo_ref, fo_v), load(1, qkv_ref.at[0], qkv_v.at[0])]
    for s in range(seqs):
        early += [
            load(2 + 3 * s, after_ref.at[s], after_v.at[s]),
            load(3 + 3 * s, cot_ref.at[s], cot_v.at[s]),
            load(4 + 3 * s, mixed_ref.at[s], mixed_v.at[s]),
        ]
    pl.semaphore_wait(greet(peers), len(peers))
    spread, settle = front_lanes(
        slab_g, slab_o, gtoks_ref, outs_ref, stay_s, a2a_s, a2a_r, capacity
    )

    def second(arrays, c):
        for arr, k in zip(arrays, split):
            if c < k:
                return arr.at[c]
            c -= k

    def products(mid_v, in_v, down_v, acc):
        jobs = []
        for n in range(2 * seqs):
            for c in range(chunks):
                first = n % seqs == 0
                if n < seqs:
                    src = gpres_a.at[c] if first else second(gpres_b, c)
                else:
                    src = acts_a.at[c] if first else second(acts_b, c)
                jobs.append((n, c, src))

        def fetch(k):
            n, c, src = jobs[k]
            slot = k % 2
            got = [pltpu.make_async_copy(src, mid_v.at[slot], mid_s.at[slot])]
            for zz in range(nz):
                at = (zz * chunks + c) * FFT
                if n < seqs:
                    pair = (w_in.at[:, at : at + FFT], in_v.at[slot, :, zz * FFT : (zz + 1) * FFT])
                else:
                    pair = (w_down.at[at : at + FFT], down_v.at[slot, zz * FFT : (zz + 1) * FFT])
                got.append(pltpu.make_async_copy(*pair, w_s.at[slot, zz]))
            return got

        step = slot_chunk(total)
        for c in fetch(0):
            c.start()
        for k, (n, c, _) in enumerate(jobs):
            if k + 1 < len(jobs):
                for v in fetch(k + 1):
                    v.start()
            for v in fetch(k):
                v.wait()
            slot = k % 2
            w, dims = (in_v[slot], NT) if n < seqs else (down_v[slot], NN)
            for a in range(0, total, step):
                term = dot(mid_v[slot, a : a + step], w, dims)
                if c == 0:
                    acc[a : a + step] = term
                else:
                    acc[a : a + step] += term
            if c == chunks - 1:
                slab = slab_g if n < seqs else slab_o
                for ee in range(experts):
                    slab[n % seqs, ee] = acc[ee * capacity : (ee + 1) * capacity].astype(bf16)
                spread(n)
            if k == 1:
                for v in early:
                    v.start()

    pl.run_scoped(
        products,
        pltpu.VMEM((2, total, tile), bf16),
        pltpu.VMEM((2, width, tile), bf16),
        pltpu.VMEM((2, tile, width), bf16),
        pltpu.VMEM((total, width), f32),
    )
    hs = width // heads
    pairs = heads // 2
    blk = min(BLK, length)

    def backward(back_v, ga_v, gm_v, d_v, dqa, doa):
        sums_ref[...] = jnp.zeros_like(sums_ref)
        saves = {}
        for s in range(seqs):
            settle(s)
            fill = load(2 + 3 * seqs, gtoks_ref.at[s], back_v)
            fill.start()
            if s:
                again = load(1, qkv_ref.at[s], qkv_v.at[0])
                again.start()
            else:
                for v in early:
                    v.wait()
            fill.wait()
            starts = list(range(0, length, blk))

            def take(a, s=s):
                return take_rows(back_v[...], slot_ref[s, a : a + blk])

            ahead = take(0)
            for at, a in enumerate(starts):
                gt = ahead
                if at + 1 < len(starts):
                    ahead = take(starts[at + 1])
                rows = slice(a, a + blk)
                hat, r = norm_parts(after_v[s, rows].astype(f32))
                sums_ref[2:3] += jnp.sum(gt * hat, axis=0, keepdims=True)
                sums_ref[3:4] += jnp.sum(gt, axis=0, keepdims=True)
                g = gt * row(g_ref)
                ga = cot_v[s, rows].astype(f32) + r * (
                    g
                    - jnp.mean(g, axis=-1, keepdims=True)
                    - hat * jnp.mean(g * hat, axis=-1, keepdims=True)
                )
                ga_v[s, rows] = ga.astype(bf16)
                gm_v[0, rows] = dot(ga_v[s, rows], fo_v[...], NT).astype(bf16)
            gw = dot(mixed_v[s], ga_v[s], TN)
            if s == 0:
                gw_ref[...] = gw
            else:
                gw_ref[...] += gw
                again.wait()
                saves[s - 1].wait()
            keep = pltpu.make_async_copy(ga_v.at[s], ga_ref.at[s], save_s.at[0, s])
            keep.start()

            def pair(p, carry, s=s):
                def cols(t):
                    return pl.ds(pl.multiple_of(t * width + p * 2 * hs, 128), 2 * hs)

                one = pl.ds(s, 1)
                attn_bwd_body(
                    qkv_v.at[:, :, cols(0)],
                    qkv_v.at[:, :, cols(1)],
                    qkv_v.at[:, :, cols(2)],
                    mixed_v.at[one, :, cols(0)],
                    gm_v.at[:, :, cols(0)],
                    lse_ref.at[one, pl.ds(p, 1)],
                    d_v.at[:, :, :, cols(0)],
                    dqa,
                    doa,
                    blk=blk,
                    hs=hs,
                    scale=hs**-0.5,
                    depth=2,
                )
                return carry

            lax.fori_loop(0, pairs, pair, 0)
            saves[s] = pltpu.make_async_copy(d_v.at[0], d_ref.at[s], save_s.at[1, s])
            saves[s].start()
            keep.wait()
        saves[seqs - 1].wait()

    pl.run_scoped(
        backward,
        pltpu.VMEM((total, width), bf16),
        pltpu.VMEM((seqs, length, width), bf16),
        pltpu.VMEM((1, length, width), bf16),
        pltpu.VMEM((1, 3, length, width), bf16),
        pltpu.VMEM((2 * hs, length), f32),
        pltpu.VMEM((2, length, 2 * hs), bf16),
    )
    for n in range(seqs, 2 * seqs):
        settle(n)


def back_call(
    acts_a, gpres_a, acts_b, gpres_b, w_in, w_down, qkv, mixed, after, cot, fo, lse, slot_col, gain, heads, nz, experts, capacity
):
    seqs, length, width = after.shape
    total = experts * capacity
    dma = pltpu.SemaphoreType.DMA
    slab = (seqs, experts, capacity, width)
    split = [v.shape[0] for v in acts_b]
    three = pltpu.VMEM((seqs, length, width), bf16)
    return pl.pallas_call(
        functools.partial(back_body, heads=heads, capacity=capacity, split=split),
        in_specs=[ANY] * (2 + 2 * len(split) + 7) + [VM] * 3,
        out_specs=[ANY] * 4 + [VM] * 2,
        out_shape=[
            sds((seqs, 3, length, width), bf16),
            sds((seqs, length, width), bf16),
            sds((seqs, total, width), bf16),
            sds((seqs, total, width), bf16),
            sds((width, width), f32),
            sds((8, width), f32),
        ],
        scratch_shapes=[
            pltpu.VMEM(slab, bf16),
            pltpu.VMEM(slab, bf16),
            pltpu.VMEM((1, length, 3 * width), bf16),
            three,
            three,
            three,
            pltpu.VMEM((width, width), bf16),
            dma((3 + 3 * seqs,)),
            dma((2,)),
            dma((2, nz)),
            dma((2, seqs)),
            dma((2 * seqs,)),
            dma((2 * seqs, experts - 1)),
            dma((2 * seqs, experts - 1)),
        ],
        compiler_params=pltpu.CompilerParams(
            vmem_limit_bytes=62 << 20, collective_id=2, has_side_effects=True
        ),
        cost_estimate=cost(110 << 30, 60 << 20),
    )(
        acts_a, gpres_a, *acts_b, *gpres_b, w_in, w_down, qkv, mixed, after, cot, fo, lse, slot_col, gain
    )


GROUPS = 4


def last_body(*refs, seqs, per_seq, plan):
    (dw_ref, d_ref, xw_ref, x_ref, w_any, g_ref, b_ref) = refs[:7]
    gwo_ref, sums_ref, backs_any, slot_ref = refs[7:11]
    gx_ref, res_ref, gq_ref, go_ref, tot_ref = refs[11:16]
    rest = refs[16:]
    acc, low, pay, r1, r2, s2, r3, fin, w0, v1, w1, v2, w2, v3, w_ref, backs = rest[:16]
    send_s, recv_s, vs_s, vr_s, load_s = rest[16:]
    nz = lax.axis_size("dp")
    experts = lax.axis_size("expert")
    z = lax.axis_index("dp")
    e = lax.axis_index("expert")
    chips = experts // 2
    core = e % 2
    chip = e // 2
    mate = (z, chip * 2 + 1 - core)
    others = [(z, lax.rem(chip + j, chips) * 2 + core) for j in range(1, chips)]
    layers = [(lax.rem(z + j, nz), e) for j in range(1, nz)]
    peers = [mate] + others + layers
    width = x_ref.shape[2]
    step = pl.program_id(0)
    last = pl.num_programs(0) - 1
    s1 = r1

    def copy(src, dst, at, peer, sems=None):
        a, b = sems or (send_s, recv_s)
        return pltpu.make_async_remote_copy(
            src_ref=src,
            dst_ref=dst,
            send_sem=a.at[at],
            recv_sem=b.at[at],
            device_id=peer,
            device_id_type=MESH,
        )

    def stage(n, t):
        if n == 1:
            return [copy(pay.at[t, 1 - core], r1.at[t], (t, 0), mate)]
        if n == 2:
            return [
                copy(
                    s1.at[t, lax.rem(chip + j, chips)], r2.at[t, j - 1], (t, j), others[j - 1]
                )
                for j in range(1, chips)
            ]
        if n == 3:
            return [
                copy(
                    s2.at[t, lax.rem(z + j, nz)], r3.at[t, j - 1], (t, chips + j), layers[j - 1]
                )
                for j in range(1, nz)
            ]
        if n == 4:
            here = fin.at[t, core, chip]
            return [
                copy(here, here, (t, chips + nz + j), others[j - 1]) for j in range(1, chips)
            ]
        side = fin.at[t, core]
        return [copy(side, side, (t, 2 * chips + nz), mate)]

    def vector(n):
        sems = (vs_s, vr_s)
        if n == 1:
            return [copy(w0, v1, 0, mate, sems)]
        if n == 2:
            return [copy(w1, v2.at[j - 1], j, others[j - 1], sems) for j in range(1, chips)]
        return [copy(w2, v3.at[j - 1], chips + j, layers[j - 1], sems) for j in range(1, nz)]

    def start(n, t):
        for c in vector(n) if t is None else stage(n, t):
            c.start()

    def finish(n, t):
        for c in vector(n) if t is None else stage(n, t):
            c.wait()
        if t is None:
            if n == 1:
                w1[...] = w0[...] + v1[...]
            elif n == 2:
                line = w1[...]
                for j in range(1, chips):
                    line = line + v2[j - 1]
                w2[...] = line
            else:
                line = w2[...]
                for j in range(1, nz):
                    line = line + v3[j - 1]
                tot_ref[...] = line
            if n < 3:
                start(n + 1, None)
            return
        if n == 1:
            for k in range(chips):
                s1[t, k] = (pay[t, core, k].astype(f32) + r1[t, k].astype(f32)).astype(bf16)
        elif n == 2:
            part = s1[t, chip].astype(f32)
            for j in range(1, chips):
                part = part + r2[t, j - 1].astype(f32)
            s2[t] = part.astype(bf16)
        elif n == 3:
            part = s2[t, z].astype(f32)
            for j in range(1, nz):
                part = part + r3[t, j - 1].astype(f32)
            fin[t, core, chip] = part.astype(bf16)
        elif n == 5:
            piece = fin.shape[3]
            for c in range(2):
                for k in range(chips):
                    at = (c * chips + k) * piece
                    value = fin[t, c, k].astype(f32)
                    if t < 3:
                        gq_ref[at : at + piece, t * width : (t + 1) * width] = value
                    else:
                        go_ref[at : at + piece, :] = value
        if n < 5:
            start(n + 1, t)

    def pack(value, t):
        per = value.shape[0] // nz
        piece = pay.shape[4]
        for zz in range(nz):
            for c in range(2):
                for k in range(chips):
                    at = zz * per + (c * chips + k) * piece
                    pay[t, c, k, zz] = value[at : at + piece].astype(bf16)
        start(1, t)

    loads = [pltpu.make_async_copy(w_any, w_ref, load_s.at[0])]
    loads += [
        pltpu.make_async_copy(backs_any.at[s], backs.at[s], load_s.at[1 + s]) for s in range(seqs)
    ]

    @pl.when(step == 0)
    def _():
        for c in loads:
            c.start()
        pl.semaphore_wait(greet(peers), len(peers))
        pack(gwo_ref[...], 3)

    for n in range(3 * seqs):
        t, s = n // seqs, n % seqs

        @pl.when(step == n)
        def _(t=t, s=s):
            if t == 0:
                hat, _ = norm_parts(xw_ref[0].astype(f32))
                low[s] = (hat * g_ref[...] + b_ref[...]).astype(bf16)
            term = dot(low[s], dw_ref[0, 0], TN)
            if s == 0:
                acc[...] = term
            elif s < seqs - 1:
                acc[...] += term
            else:
                pack(acc[...] + term, t)

    base = 3 * seqs

    @pl.when(step == base)
    def _():
        loads[0].wait()
        w0[0:2] = jnp.zeros((2, width), f32)
        w0[2:8] = sums_ref[2:8]

    @pl.when((step >= base) & (step < base + seqs * per_seq))
    def _():
        hat, r = norm_parts(x_ref[0].astype(f32))
        gn = 0.0
        for t in range(3):
            gn = gn + dot(d_ref[0, t], w_ref[:, t * width : (t + 1) * width], NT)
        w0[0:1] += jnp.sum(gn * hat, axis=0, keepdims=True)
        w0[1:2] += jnp.sum(gn, axis=0, keepdims=True)
        g = gn * g_ref[...]
        gx_ref[0] = (
            r
            * (
                g
                - jnp.mean(g, axis=-1, keepdims=True)
                - hat * jnp.mean(g * hat, axis=-1, keepdims=True)
            )
        ).astype(bf16)

    base = base + seqs * per_seq

    @pl.when(step == base)
    def _():
        for c in loads[1:]:
            c.wait()

    @pl.when(step == base - 1)
    def _():
        start(1, None)

    for s in range(seqs):

        @pl.when((step >= base + s * per_seq) & (step < base + (s + 1) * per_seq))
        def _(s=s):
            res_ref[0] = take_rows(backs[s], slot_ref[0]).astype(bf16)

    for when, events in plan:

        @pl.when(step == when)
        def _(events=events):
            for n, t in events:
                finish(n, t)


def last_plan(seqs, per_seq):
    dw = 3 * seqs
    end = dw + 2 * seqs * per_seq - 1
    mid = dw + seqs * per_seq
    first = [
        (2, [(1, 3)]),
        (4, [(1, 0)]),
        (dw, [(1, 1)]),
        (dw + 2, [(1, 2)]),
        (dw + 4, [(2, 3)]),
        (dw + 6, [(2, 0)]),
        (dw + 7, [(3, 3)]),
        (mid, [(2, 1)]),
        (mid + 1, [(3, 0)]),
        (mid + 2, [(1, None), (2, 2), (4, 3)]),
        (mid + 3, [(3, 1)]),
        (mid + 4, [(2, None), (4, 0), (5, 3)]),
        (mid + 5, [(3, 2)]),
        (mid + 6, [(3, None), (4, 1), (5, 0)]),
        (end, [(4, 2), (5, 1), (5, 2)]),
    ]
    return [(min(a, end), b) for a, b in first]


def last_call(d, x, w, gain, bias, gwo, sums, backs, slot_col, experts, nz):
    seqs, length, width = x.shape
    blk = min(BLK, length)
    per_seq = length // blk
    total = backs.shape[1]
    dw = 3 * seqs
    mid = dw + seqs * per_seq
    chips = experts // 2
    piece = width // nz // experts
    per = width // nz
    dma = pltpu.SemaphoreType.DMA
    once = pl.Buffered(1)

    def keep(*shape):
        return pl.BlockSpec(shape, lambda r: (0,) * len(shape), pipeline_mode=once)

    def at(first, r):
        n = jnp.clip(r - first, 0, seqs * per_seq - 1)
        return n // per_seq, n % per_seq

    def dw_at(r):
        n = jnp.minimum(r, dw - 1)
        return n % seqs, n // seqs, 0, 0

    def rows(first):
        return pl.BlockSpec((1, blk, width), lambda r: (*at(first, r), 0))

    def d_at(r):
        s, b = at(dw, r)
        return s, 0, b, 0

    steps = mid + seqs * per_seq
    in_specs = [
        pl.BlockSpec((1, 1, length, width), dw_at),
        pl.BlockSpec((1, 3, blk, width), d_at),
        pl.BlockSpec((1, length, width), lambda r: (jnp.minimum(r, seqs - 1), 0, 0)),
        rows(dw),
        ANY,
        keep(1, width),
        keep(1, width),
    ]
    in_specs += [keep(width, width), keep(8, width), ANY]
    in_specs += [pl.BlockSpec((1, blk, 1), lambda r: (*at(mid, r), 0))]
    return pl.pallas_call(
        functools.partial(last_body, seqs=seqs, per_seq=per_seq, plan=last_plan(seqs, per_seq)),
        grid=(steps,),
        in_specs=in_specs,
        out_specs=[rows(dw), rows(mid), keep(per, 3 * width), keep(per, width), keep(8, width)],
        out_shape=[
            sds((seqs, length, width), bf16),
            sds((seqs, length, width), bf16),
            sds((per, 3 * width), f32),
            sds((per, width), f32),
            sds((8, width), f32),
        ],
        scratch_shapes=[
            pltpu.VMEM((width, width), f32),
            pltpu.VMEM((seqs, length, width), bf16),
            pltpu.VMEM((GROUPS, 2, chips, nz, piece, width), bf16),
            pltpu.VMEM((GROUPS, chips, nz, piece, width), bf16),
            pltpu.VMEM((GROUPS, chips - 1, nz, piece, width), bf16),
            pltpu.VMEM((GROUPS, nz, piece, width), bf16),
            pltpu.VMEM((GROUPS, nz - 1, piece, width), bf16),
            pltpu.VMEM((GROUPS, 2, chips, piece, width), bf16),
            pltpu.VMEM((8, width), f32),
            pltpu.VMEM((8, width), f32),
            pltpu.VMEM((8, width), f32),
            pltpu.VMEM((chips - 1, 8, width), f32),
            pltpu.VMEM((8, width), f32),
            pltpu.VMEM((nz - 1, 8, width), f32),
            pltpu.VMEM((width, 3 * width), bf16),
            pltpu.VMEM((seqs, total, width), bf16),
        ]
        + [dma((GROUPS, 2 * chips + nz + 1))] * 2
        + [dma((chips + nz,))] * 2
        + [dma((1 + seqs,))],
        compiler_params=pltpu.CompilerParams(
            vmem_limit_bytes=62 << 20, collective_id=1, has_side_effects=True
        ),
        cost_estimate=cost(50 << 30, 150 << 20),
    )(
        d,
        d,
        x,
        x,
        w,
        gain.reshape(1, -1),
        bias.reshape(1, -1),
        gwo,
        sums,
        backs,
        slot_col,
    )


def close_body(*refs, counts):
    ga_ref, dx_ref, after_ref, back_ref, gq_ref, go_ref = refs[:6]
    n = len(counts)
    downs, ins = refs[6 : 6 + n], refs[6 + n : 6 + 2 * n]
    gx_out, res_out, gq_out, go_out, down_out, in_out = refs[6 + 2 * n :]
    gx_out[...] = ga_ref[...].astype(f32) + dx_ref[...].astype(f32)
    res_out[...] = after_ref[...].astype(f32) + back_ref[...].astype(f32)
    gq_out[...] = gq_ref[...]
    go_out[...] = go_ref[...]
    at = 0
    for k, down, gin in zip(counts, downs, ins):
        down_out[at : at + k] = down[0].astype(f32)
        for i in range(k):
            in_out[:, (at + i) * FFT : (at + i + 1) * FFT] = gin[0, i].astype(f32)
        at += k


def close_call(ga, dx, after, back, gq, go, downs, ins):
    seqs, length, width = ga.shape
    blk = min(BLK, length)
    per_seq = length // blk
    steps = seqs * per_seq
    counts = [v.shape[1] for v in downs]
    chunks = sum(counts)
    rows = pl.BlockSpec((1, blk, width), lambda r: (r // per_seq, r % per_seq, 0))

    def split(v):
        return pl.BlockSpec((v.shape[0] // steps, v.shape[1]), lambda r: (r, 0))

    def part(v):
        return pl.BlockSpec(
            (1, v.shape[1], v.shape[2] // steps, v.shape[3]), lambda r: (0, 0, r, 0)
        )

    side = ins[0].shape[2]
    return pl.pallas_call(
        functools.partial(close_body, counts=counts),
        grid=(steps,),
        in_specs=[rows] * 4 + [split(gq), split(go)] + [part(v) for v in downs + ins],
        out_specs=[
            rows,
            rows,
            split(gq),
            split(go),
            pl.BlockSpec((chunks, FFT // steps, width), lambda r: (0, r, 0)),
            pl.BlockSpec((side // steps, chunks * FFT), lambda r: (r, 0)),
        ],
        out_shape=[
            sds((seqs, length, width), f32),
            sds((seqs, length, width), f32),
            sds(gq.shape, f32),
            sds(go.shape, f32),
            sds((chunks, FFT, width), f32),
            sds((side, chunks * FFT), f32),
        ],
        compiler_params=params(60),
        cost_estimate=cost(8 << 30, 40 << 20),
    )(ga, dx, after, back, gq, go, *downs, *ins)


def exchange(parts):
    got = lax.all_to_all(parts, "expert", split_axis=0, concat_axis=0, tiled=True)
    return got.reshape(-1, parts.shape[-1])


def on_device(
    tokens_in,
    buckets,
    ln1_gain,
    ln1_bias,
    w_qkv,
    w_out,
    ln2_gain,
    ln2_bias,
    w_in,
    w_down,
    cotangent,
):
    experts = lax.axis_size("expert")
    nz = lax.axis_size("dp")
    seqs, length, width = tokens_in.shape
    capacity = 5 * length // (4 * experts)
    total = experts * capacity
    w_in_local = w_in[0]
    w_down_local = w_down[0]
    hidden = w_in_local.shape[1]
    chunks = hidden // (nz * FFT)

    qkv, full_qkv, full_out, mixed, after, lse, slot_col, cots, rows, act_a, gpre_a = front_call(
        tokens_in,
        ln1_gain,
        ln1_bias,
        ln2_gain,
        ln2_bias,
        w_qkv,
        w_out,
        buckets,
        cotangent,
        w_in_local,
        w_down_local,
        HEADS,
        nz,
        experts,
        capacity,
    )
    last = ()
    acts, gpres, gdowns, gins = [], [], [], []
    for first, many in ((0, 1), (1, chunks - 1)):
        act_b, gpre_b, gdown, gin = expert_b_call(
            rows,
            act_a,
            gpre_a,
            cots,
            w_in_local,
            w_down_local,
            nz,
            first,
            many,
            deps=last,
        )
        last = (act_b,)
        acts.append(act_b)
        gpres.append(gpre_b)
        gdowns.append(lax.psum_scatter(gdown, "dp", scatter_dimension=0, tiled=True))
        gins.append(lax.psum_scatter(gin, "dp", scatter_dimension=0, tiled=True))

    d, ga, _, outs, gwo, sums = back_call(
        act_a,
        gpre_a,
        acts,
        gpres,
        w_in_local,
        w_down_local,
        qkv,
        mixed,
        after,
        cotangent,
        full_out,
        lse,
        slot_col,
        ln2_gain,
        HEADS,
        nz,
        experts,
        capacity,
    )
    dx, back, gq, go, sums = last_call(
        d,
        tokens_in,
        full_qkv,
        ln1_gain,
        ln1_bias,
        gwo,
        sums,
        outs,
        slot_col,
        experts,
        nz,
    )
    gxs, results, gq, go, gdown, gin = close_call(ga, dx, after, back, gq, go, gdowns, gins)
    mine = lax.dynamic_slice_in_dim(
        sums, lax.axis_index("dp") * (width // nz), width // nz, axis=1
    )
    return (
        results,
        gxs,
        mine[0],
        mine[1],
        gq,
        go,
        mine[2],
        mine[3],
        gin[None],
        gdown.reshape(1, hidden // nz, width),
    )


def solution(mesh):
    placed = (
        P(("dp", "expert"), None, None),
        P(("dp", "expert"), None),
        P(),
        P(),
        P("dp", None),
        P("dp", None),
        P(),
        P(),
        P("expert", None, None),
        P("expert", None, None),
        P(("dp", "expert"), None, None),
    )
    return jax.shard_map(
        on_device,
        mesh=mesh,
        in_specs=placed,
        out_specs=(
            P(("dp", "expert"), None, None),
            P(("dp", "expert"), None, None),
            P("dp"),
            P("dp"),
            P("dp", None),
            P("dp", None),
            P("dp"),
            P("dp"),
            P("expert", None, "dp"),
            P("expert", "dp", None),
        ),
        check_vma=False,
    )
```

```python
import functools

import jax
import jax.numpy as jnp
from jax import lax
from jax.experimental import pallas as pl
from jax.experimental.pallas import tpu as pltpu
from jax.sharding import PartitionSpec as P

HEADS = 12
EPS = 1e-5
NEG = -1e30
bf16 = jnp.bfloat16
f32 = jnp.float32
NN = (((1,), (0,)), ((), ()))
NT = (((1,), (1,)), ((), ()))
TN = (((0,), (0,)), ((), ()))
GELU_A = 0.7978845608028654
GELU_B = 0.044715
BLK = 256
FFT = 256


def dot(a, b, dims=NN):
    return lax.dot_general(a, b, dims, preferred_element_type=f32)


def params(mib=56):
    return pltpu.CompilerParams(vmem_limit_bytes=mib << 20)


def cost(flops, nbytes, trans=0):
    return pl.CostEstimate(flops=int(flops), bytes_accessed=int(nbytes), transcendentals=int(trans))


def sds(shape, dtype):
    return jax.ShapeDtypeStruct(shape, dtype)


VM = pl.BlockSpec(memory_space=pltpu.VMEM)
ANY = pl.BlockSpec(memory_space=pl.ANY)


def kernel_call(body, in_specs, args, deps=(), into=None, **options):
    into = into or {}
    count = len(args)
    extra = len(into) + len(deps)

    def wrapped(*refs):
        body(*refs[:count], *refs[count + extra :])

    return pl.pallas_call(
        wrapped,
        in_specs=list(in_specs) + [ANY] * extra,
        input_output_aliases={count + n: out for n, out in enumerate(into)},
        **options,
    )(*args, *into.values(), *deps)


def norm_parts(v):
    centre = jnp.mean(v, axis=-1, keepdims=True)
    shifted = v - centre
    spread = jnp.mean(shifted * shifted, axis=-1, keepdims=True)
    r = lax.rsqrt(spread + EPS)
    return shifted * r, r


MESH = pl.DeviceIdType.MESH


def greet(peers):
    barrier = pltpu.get_barrier_semaphore()
    for peer in peers:
        pl.semaphore_signal(barrier, inc=1, device_id=peer, device_id_type=MESH)
    return barrier


def find_slots(bucket, experts, capacity):
    length = bucket.shape[1]
    hot = (lax.broadcasted_iota(jnp.int32, (experts, length), 0) == bucket).astype(f32)
    upto = lax.broadcasted_iota(jnp.int32, (length, length), 0) <= lax.broadcasted_iota(
        jnp.int32, (length, length), 1
    )
    count = dot(hot.astype(bf16), upto.astype(bf16))
    rank = jnp.sum(hot * count, axis=0, keepdims=True) - 1.0
    return bucket * capacity + rank.astype(jnp.int32)


GATHERS = 3


def front_body(*refs, heads, capacity):
    nz = lax.axis_size("dp")
    n = 9 + 2 * nz
    (x_ref, g1_ref, b1_ref, g2_ref, b2_ref, wq_ref, wo_ref, buckets_ref, cot_ref) = refs[:9]
    w_ins, w_downs = refs[9 : 9 + nz], refs[9 + nz : n]
    (
        qkv_ref,
        fq_ref,
        fo_ref,
        mixed_ref,
        after_ref,
        lse_ref,
        col_ref,
        cots_ref,
        rows_ref,
        act_ref,
        gpre_ref,
        give_ref,
    ) = refs[n : n + 12]
    (
        fq_v,
        fo_v,
        sent,
        toks,
        slots,
        rows_v,
        cot_a,
        up_s,
        dn_s,
        core_s,
        z_r,
        core_r,
        own_s,
        load_s,
        save_s,
        stay_s,
        a2a_s,
        a2a_r,
    ) = refs[n + 12 :]
    seqs, length, width = x_ref.shape

    def work(x_v, cot_v, low, qkv_v, mixed_v, after_v):
        return front_work(
            x_ref, g1_ref, b1_ref, g2_ref, b2_ref, wq_ref, wo_ref, buckets_ref, cot_ref,
            qkv_ref, fq_ref, fo_ref, mixed_ref, after_ref, lse_ref, col_ref, cots_ref, rows_ref,
            x_v, cot_v, fq_v, fo_v, low, qkv_v, sent, toks, mixed_v, after_v, slots,
            up_s, dn_s, core_s, z_r, core_r, own_s, load_s, save_s, stay_s, a2a_s, a2a_r,
            heads=heads, capacity=capacity,
        )

    one = pltpu.VMEM((seqs, length, width), bf16)
    pl.run_scoped(work, one, one, one, pltpu.VMEM((seqs, length, 3 * width), bf16), one, one)
    settle = front_lanes(sent, toks, cots_ref, rows_ref, stay_s, a2a_s, a2a_r, capacity)[1]
    for k in range(seqs + 1):
        settle(k)
    load = [
        pltpu.make_async_copy(rows_ref.at[0], rows_v, load_s.at[0, 0]),
        pltpu.make_async_copy(cots_ref.at[0], cot_a, load_s.at[1, 0]),
    ]
    for c in load:
        c.start()
    for c in load:
        c.wait()
    hidden = w_ins[0].shape[1]
    total = rows_v.shape[0]

    mid = pl.BlockSpec((1, total, nz * FFT), lambda c: (c, 0, 0))

    def expert(acc):
        acc[...] = jnp.zeros_like(acc)

        def step(*blocks):
            w_in = join_cols(blocks[:nz])

            def use(a, b, act_low, gpre_low):
                acc[a:b] += dot(gpre_low, w_in, NT)

            w_down = join_rows(blocks[nz : 2 * nz])
            hidden_rows(rows_v, cot_a, w_in, w_down, *blocks[2 * nz :], use)

        pltpu.emit_pipeline(
            step,
            grid=(hidden // (nz * FFT),),
            in_specs=weight_specs(width, hidden, nz),
            out_specs=[mid, mid],
        )(*w_ins, *w_downs, act_ref, gpre_ref)
        for k in range(sent.shape[1]):
            sent[0, k] = acc[k * capacity : (k + 1) * capacity].astype(bf16)
        out = pltpu.make_async_copy(sent.at[0], give_ref.at[0], load_s.at[0, 0])
        out.start()
        out.wait()

    pl.run_scoped(expert, pltpu.VMEM((total, width), f32))
    for k in range(seqs + 1, 2 * seqs):
        settle(k)


def front_lanes(sent, toks, cots_ref, rows_ref, stay_s, a2a_s, a2a_r, capacity):
    experts = lax.axis_size("expert")
    z = lax.axis_index("dp")
    e = lax.axis_index("expert")
    seqs = cots_ref.shape[0]
    plane = [(e + j) % experts for j in range(1, experts)]
    back = [(e + experts - j) % experts for j in range(1, experts)]

    def lane(n, at):
        src, dst = (sent, cots_ref) if n < seqs else (toks, rows_ref)
        k = n % seqs
        return src.at[k], dst.at[k, pl.ds(pl.multiple_of(at * capacity, 8), capacity)]

    def trade(n, j, at):
        src, dst = lane(n, at)
        return pltpu.make_async_remote_copy(
            src_ref=src.at[plane[j]],
            dst_ref=dst,
            send_sem=a2a_s.at[n, j],
            recv_sem=a2a_r.at[n, j],
            device_id=(z, plane[j]),
            device_id_type=MESH,
        )

    def stay(n):
        src, dst = lane(n, e)
        return pltpu.make_async_copy(src.at[e], dst, stay_s.at[n])

    def spread(n):
        for j in range(experts - 1):
            trade(n, j, e).start()
        stay(n).start()

    def settle(n):
        stay(n).wait()
        for j in range(experts - 1):
            trade(n, j, e).wait_send()
            trade(n, j, back[j]).wait_recv()

    return spread, settle


def front_work(
    x_ref,
    g1_ref,
    b1_ref,
    g2_ref,
    b2_ref,
    wq_ref,
    wo_ref,
    buckets_ref,
    cot_ref,
    qkv_ref,
    fq_ref,
    fo_ref,
    mixed_ref,
    after_ref,
    lse_ref,
    col_ref,
    cots_ref,
    rows_ref,
    x_v,
    cot_v,
    fq_v,
    fo_v,
    low,
    qkv_v,
    sent,
    toks,
    mixed_v,
    after_v,
    slots,
    up_s,
    dn_s,
    core_s,
    z_r,
    core_r,
    own_s,
    load_s,
    save_s,
    stay_s,
    a2a_s,
    a2a_r,
    *,
    heads,
    capacity,
):
    nz = lax.axis_size("dp")
    experts = lax.axis_size("expert")
    z = lax.axis_index("dp")
    e = lax.axis_index("expert")
    core = e % 2
    seqs, length, width = x_ref.shape
    spread = front_lanes(sent, toks, cots_ref, rows_ref, stay_s, a2a_s, a2a_r, capacity)[0]
    per = width // nz
    half = per // 2
    above = (jnp.minimum(z + 1, nz - 1), e)
    below = (jnp.maximum(z - 1, 0), e)
    mate = (z, e + 1 - 2 * core)
    full = (fq_v, fo_v)
    shard = (wq_ref, wo_ref)
    blk = min(BLK, length)

    cot_in = [pltpu.make_async_copy(cot_ref.at[s], cot_v.at[s], load_s.at[0, s]) for s in range(seqs)]
    x_in = [pltpu.make_async_copy(x_ref.at[s], x_v.at[s], load_s.at[1, s]) for s in range(seqs)]
    for c in cot_in[:1] + x_in + cot_in[1:]:
        c.start()

    barrier = pltpu.get_barrier_semaphore()

    @pl.when(z + 1 < nz)
    def _():
        pl.semaphore_signal(barrier, inc=1, device_id=above, device_id_type=MESH)

    @pl.when(z > 0)
    def _():
        pl.semaphore_signal(barrier, inc=1, device_id=below, device_id_type=MESH)

    plane = [(z, (e + j) % experts) for j in range(1, experts)]
    for peer in plane:
        pl.semaphore_signal(barrier, inc=1, device_id=peer, device_id_type=MESH)

    @pl.when((z + 1 < nz) & (z > 0))
    def _():
        pl.semaphore_wait(barrier, experts + 1)

    @pl.when((z + 1 >= nz) | (z <= 0))
    def _():
        pl.semaphore_wait(barrier, experts)

    hs = width // heads
    pairs = heads // 2
    groups = min(GATHERS, pairs)
    wide = width // groups
    lanes = [[(3 * g + m, 0, m * width + g * wide, wide) for m in range(3)] for g in range(groups)]
    lanes.append([(3 * groups, 1, 0, width)])

    def half_rows(ref, at, piece):
        return ref.at[pl.ds(pl.multiple_of(at, 16), half), pl.ds(piece[2], piece[3])]

    def held(piece, p, c):
        return half_rows(full[piece[1]], p * per + c * half, piece)

    def mine(piece):
        return half_rows(shard[piece[1]], core * half, piece)

    def hop(piece, p, c, src, sem, r_sem, peer):
        return pltpu.make_async_remote_copy(
            src_ref=src,
            dst_ref=held(piece, p, c),
            send_sem=sem.at[piece[0], p],
            recv_sem=r_sem.at[piece[0], p],
            device_id=peer,
            device_id_type=MESH,
        )

    def pass_on(piece, p, sem, r_sem, peer):
        return hop(piece, p, core, held(piece, p, core), sem, r_sem, peer)

    def own(piece):
        cols = pl.ds(piece[2], piece[3])
        return pltpu.make_async_copy(
            shard[piece[1]].at[:, cols],
            full[piece[1]].at[pl.ds(pl.multiple_of(z * per, 16), per), cols],
            own_s.at[piece[0]],
        )

    def begin(i):
        for piece in lanes[i]:

            @pl.when(z + 1 < nz)
            def _(piece=piece):
                hop(piece, z, core, mine(piece), up_s, z_r, above).start()

            @pl.when(z > 0)
            def _(piece=piece):
                hop(piece, z, core, mine(piece), dn_s, z_r, below).start()

            own(piece).start()

    def sides(d):
        return ((z - d >= 0, z - d, z + 1 < nz, up_s, above), (z + d < nz, z + d, z > 0, dn_s, below))

    def arrivals(i, d):
        for ok, p, more, sem, peer in sides(d):

            @pl.when(ok)
            def _(p=p, more=more, sem=sem, peer=peer):
                for piece in lanes[i]:
                    pass_on(piece, p, sem, z_r, peer).wait_recv()

                    @pl.when(more)
                    def _(piece=piece):
                        pass_on(piece, p, sem, z_r, peer).start()

                    pass_on(piece, p, core_s, core_r, mate).start()

    def wave(w):
        for i in range(len(lanes)):
            if 0 < w - i < nz:
                arrivals(i, w - i)
            if w == i:
                begin(i)

    def complete(i):
        for piece in lanes[i]:
            own(piece).wait()
            for d in range(1, nz):
                for ok, p, _, _, _ in sides(d):

                    @pl.when(ok)
                    def _(piece=piece, p=p):
                        hop(
                            piece, p, 1 - core, held(piece, p, 1 - core), core_s, core_r, mate
                        ).wait_recv()

    def sent_all(i):
        for piece in lanes[i]:

            @pl.when(z + 1 < nz)
            def _(piece=piece):
                hop(piece, z, core, mine(piece), up_s, z_r, above).wait_send()

            @pl.when(z > 0)
            def _(piece=piece):
                hop(piece, z, core, mine(piece), dn_s, z_r, below).wait_send()

            for d in range(1, nz):
                for ok, p, more, sem, peer in sides(d):

                    @pl.when(ok)
                    def _(piece=piece, p=p):
                        pass_on(piece, p, core_s, core_r, mate).wait_send()

                    @pl.when(ok & more)
                    def _(piece=piece, p=p, sem=sem, peer=peer):
                        pass_on(piece, p, sem, z_r, peer).wait_send()

    def prepare(s):
        slot = find_slots(buckets_ref[s : s + 1, :], experts, capacity)
        slots[s] = slot
        col_ref[s] = jnp.broadcast_to(slot.astype(f32), (8, length)).T[:, :1].astype(jnp.int32)
        cot_in[s].wait()
        place_rows(cot_v[s], slot, sent.at[s])
        spread(s)

    def first_norm(s):
        x_in[s].wait()
        for a in range(0, length, blk):
            hat, _ = norm_parts(x_v[s, a : a + blk].astype(f32))
            low[s, a : a + blk] = (hat * row(g1_ref) + row(b1_ref)).astype(bf16)

    def save(n, src, dst):
        return pltpu.make_async_copy(src, dst, save_s.at[n])

    saves = [save(0, fq_v, fq_ref), save(1, fo_v, fo_ref)]
    for s in range(seqs):
        saves += [
            save(2 + 3 * s, qkv_v.at[s], qkv_ref.at[s]),
            save(3 + 3 * s, mixed_v.at[s], mixed_ref.at[s]),
            save(4 + 3 * s, after_v.at[s], after_ref.at[s]),
        ]

    def project(s, g):
        for _, _, at, size in lanes[g]:
            w = fq_v[:, at : at + size]
            rows = min(512, length)
            for a in range(0, length, rows):
                qkv_v[s, a : a + rows, at : at + size] = dot(low[s, a : a + rows], w).astype(bf16)

    each = pairs // groups

    def attend(g, first, many):
        def pair(n, carry):
            s = first + n // each
            p = g * each + n % each

            def cols(t):
                return pl.ds(pl.multiple_of(t * width + p * 2 * hs, 128), 2 * hs)

            one = pl.ds(s, 1)
            attn_fwd_body(
                qkv_v.at[one, :, cols(0)],
                qkv_v.at[one, :, cols(1)],
                qkv_v.at[one, :, cols(2)],
                mixed_v.at[one, :, cols(0)],
                lse_ref.at[one, pl.ds(p, 1)],
                blk=blk,
                hs=hs,
                scale=hs**-0.5,
                depth=3,
            )
            return carry

        lax.fori_loop(0, many * each, pair, 0)

    def finish(s, out):
        for a in range(0, length, blk):
            rows = slice(a, a + blk)
            after = x_v[s, rows].astype(f32) + dot(mixed_v[s, rows], fo_v[...])
            after_v[s, rows] = after.astype(bf16)
            hat, _ = norm_parts(after)
            low[s, rows] = (hat * row(g2_ref) + row(b2_ref)).astype(bf16)
        saves[4 + 3 * s].start()
        place_rows(low[s], slots[s], out)

    todo = list(range(1, groups + nz))

    def waves(upto):
        while todo and todo[0] <= upto:
            wave(todo.pop(0))

    wave(0)
    prepare(0)
    waves(1)
    for s in range(seqs):
        first_norm(s)
    waves(2)
    for s in range(1, seqs):
        prepare(s)
    for g in range(groups):
        waves(g + nz - 1)
        complete(g)
        for s in range(seqs):
            project(s, g)
        if g < groups - 1:
            attend(g, 0, seqs)
    saves[0].start()
    for s in range(seqs):
        saves[2 + 3 * s].start()
    attend(groups - 1, 0, 1)
    waves(groups + nz - 1)
    complete(groups)
    saves[1].start()
    saves[3].start()
    finish(0, toks.at[0])
    spread(seqs)
    for s in range(1, seqs):
        attend(groups - 1, s, 1)
        saves[3 + 3 * s].start()
        finish(s, toks.at[s])
        spread(seqs + s)
    for i in range(groups + 1):
        sent_all(i)
    for c in saves:
        c.wait()


def row(ref):
    return ref[...].reshape(1, -1)


def front_call(x, g1, b1, g2, b2, wq, wo, buckets, cot, w_in, w_down, heads, nz, experts, capacity):
    seqs, length, width = x.shape
    triple = wq.shape[1]
    dma = pltpu.SemaphoreType.DMA
    slab = (seqs, experts, capacity, width)
    total = experts * capacity
    pairs = heads // 2
    tile = nz * FFT
    chunks = w_in.shape[1] // tile
    return pl.pallas_call(
        functools.partial(front_body, heads=heads, capacity=capacity),
        in_specs=[ANY] + [VM] * 4 + [ANY] * 2 + [VM, ANY] + [ANY] * (2 * nz),
        out_specs=[ANY] * 5 + [VM] * 2 + [ANY] * 5,
        out_shape=[
            sds((seqs, length, triple), bf16),
            sds((width, triple), bf16),
            sds((width, width), bf16),
            sds((seqs, length, width), bf16),
            sds((seqs, length, width), bf16),
            sds((seqs, pairs, 2, length), f32),
            sds((seqs, length, 1), jnp.int32),
            sds((seqs, total, width), bf16),
            sds((seqs, total, width), bf16),
            sds((chunks, total, tile), bf16),
            sds((chunks, total, tile), bf16),
            sds((1, experts, capacity, width), bf16),
        ],
        scratch_shapes=[
            pltpu.VMEM((width, triple), bf16),
            pltpu.VMEM((width, width), bf16),
            pltpu.VMEM(slab, bf16),
            pltpu.VMEM(slab, bf16),
            pltpu.VMEM((seqs, 1, length), jnp.int32),
            pltpu.VMEM((total, width), bf16),
            pltpu.VMEM((total, width), bf16),
        ]
        + [dma((3 * GATHERS + 1, nz))] * 5
        + [dma((3 * GATHERS + 1,)), dma((2, seqs)), dma((2 + 3 * seqs,)), dma((2 * seqs,))]
        + [dma((2 * seqs, experts - 1))] * 2,
        compiler_params=pltpu.CompilerParams(
            vmem_limit_bytes=62 << 20, collective_id=0, has_side_effects=True
        ),
        cost_estimate=cost(110 << 30, 40 << 20),
    )(x, g1, b1, g2, b2, wq, wo, buckets, cot, *([w_in] * nz), *([w_down] * nz))


def attn_fwd_body(q_ref, k_ref, v_ref, o_ref, lse_ref, *, blk, hs, scale, depth):
    length = q_ref.shape[1]
    lane = lax.broadcasted_iota(jnp.int32, (1, 2 * hs), 1) // hs
    v_t = v_ref[0].T
    keys = k_ref[0]
    kh = [jnp.where(lane == h, keys, jnp.zeros_like(keys)) for h in range(2)]
    ones = jnp.ones((16, length), bf16)
    vh = [jnp.concatenate([v_t[h * hs : (h + 1) * hs], ones], axis=0) for h in range(2)]
    future = lax.broadcasted_iota(jnp.int32, (blk, blk), 0) > lax.broadcasted_iota(
        jnp.int32, (blk, blk), 1
    )
    tasks = [(i, h) for i in range(length // blk) for h in range(2)]

    def score(task):
        i, h = task
        top = (i + 1) * blk
        q = q_ref[0, i * blk : top, :] * jnp.asarray(scale, bf16)
        s = dot(kh[h][:top], q, NT)
        diag = jnp.where(future, NEG, s[i * blk :])
        s = jnp.concatenate([s[: i * blk], diag], axis=0) if i else diag
        return s, jnp.max(s, axis=0, keepdims=True)

    queue = [score(t) for t in tasks[:depth]]
    done = {}
    for at, task in enumerate(tasks):
        if at + depth < len(tasks):
            queue.append(score(tasks[at + depth]))
        s, largest = queue.pop(0)
        i, h = task
        top = (i + 1) * blk
        o = dot(vh[h][:, :top], jnp.exp(s - largest).astype(bf16))
        total = o[hs : hs + 1]
        done[task] = o[:hs] * (1.0 / total)
        lse_ref[0, 0, h : h + 1, i * blk : top] = largest + jnp.log(total)
        if h == 1:
            both = jnp.concatenate([done[(i, 0)], done[(i, 1)]], axis=0)
            o_ref[0, i * blk : top, :] = both.T.astype(bf16)


def attn_bwd_body(
    q_ref, k_ref, v_ref, o_ref, do_ref, lse_ref, d_ref, dqa, doa, *, blk, hs, scale, depth
):
    length = q_ref.shape[1]
    n = length // blk
    lanes = lax.broadcasted_iota(jnp.int32, (1, 2 * hs), 1)
    lane = lanes // hs
    spot = lanes % hs
    keys = k_ref[0]
    vals = v_ref[0]
    k_t = (keys * jnp.asarray(scale, bf16)).T
    kh = [jnp.where(lane == h, keys, jnp.zeros_like(keys)) for h in range(2)]
    vh = [
        jnp.where(lane == h, vals, jnp.where(spot < 2, jnp.ones_like(vals), jnp.zeros_like(vals)))
        for h in range(2)
    ]
    future = lax.broadcasted_iota(jnp.int32, (blk, blk), 0) > lax.broadcasted_iota(
        jnp.int32, (blk, blk), 1
    )
    q = q_ref[0] * jnp.asarray(scale, bf16)
    do = do_ref[0]
    prod = do.astype(f32) * o_ref[0].astype(f32)
    for h in range(2):
        inside = lane == h
        inner = -jnp.sum(jnp.where(inside, prod, 0.0), axis=1, keepdims=True)
        high = inner.astype(bf16)
        rest = (inner - high.astype(f32)).astype(bf16)
        doa[h] = jnp.where(
            inside,
            do,
            jnp.where(spot == 0, high, jnp.where(spot == 1, rest, jnp.zeros_like(high))),
        )
    tasks = [(j, h) for j in range(n) for h in range(2)]

    def score(task):
        j, h = task
        a = j * blk
        return (
            dot(kh[h][a : a + blk], q[a:], NT),
            dot(vh[h][a : a + blk], doa[h, a:], NT),
        )

    queue = [score(t) for t in tasks[:depth]]
    kept = None
    for at, task in enumerate(tasks):
        if at + depth < len(tasks):
            queue.append(score(tasks[at + depth]))
        s, dp = queue.pop(0)
        j, h = task
        a = j * blk
        p = jnp.exp(s - lse_ref[0, 0, h : h + 1, a:])
        diag = jnp.where(future, 0.0, p[:, :blk])
        p = jnp.concatenate([diag, p[:, blk:]], axis=1) if j < n - 1 else diag
        ds = (p * dp).astype(bf16)
        dv = dot(p.astype(bf16), do[a:])
        dk = dot(ds, q[a:])
        dq = dot(k_t[h * hs : (h + 1) * hs, a : a + blk], ds)
        if j == 0:
            dqa[h * hs : (h + 1) * hs, :] = dq
        else:
            dqa[h * hs : (h + 1) * hs, a:] += dq
        if h == 0:
            kept = (dk, dv)
        else:
            d_ref[0, 1, a : a + blk, :] = jnp.where(lane == 0, kept[0], dk).astype(bf16)
            d_ref[0, 2, a : a + blk, :] = jnp.where(lane == 0, kept[1], dv).astype(bf16)
            d_ref[0, 0, a : a + blk, :] = dqa[:, a : a + blk].T.astype(bf16)


def slot_chunk(total):
    return 256 if total % 256 == 0 else total


def place_rows(rows, slot_row, out_ref):
    experts, capacity, _ = out_ref.shape
    base = lax.broadcasted_iota(jnp.int32, (capacity, rows.shape[0]), 0)
    for e in range(experts):
        hot = jnp.where(base + e * capacity == slot_row, 1.0, 0.0).astype(bf16)
        out_ref[e] = dot(hot, rows).astype(bf16)


def take_rows(slots, slot_col):
    total = slots.shape[0]
    at = lax.broadcasted_iota(jnp.int32, (slot_col.shape[0], total), 1)
    return dot(jnp.where(at == slot_col, 1.0, 0.0).astype(bf16), slots)


def gelu_parts(pre):
    sq = pre * pre
    half = 0.5 + 0.5 * jnp.tanh(pre * (GELU_A + (GELU_A * GELU_B) * sq))
    act = pre * half
    slope = half + (act - act * half) * (2 * GELU_A + (6 * GELU_A * GELU_B) * sq)
    return act, slope


def hidden_rows(rows_ref, cot_ref, w_in, w_down, act_ref, gpre_ref, use=None):
    total = rows_ref.shape[0]
    step = slot_chunk(total)
    starts = list(range(0, total, step))

    def first(a):
        return dot(rows_ref[a : a + step], w_in), dot(cot_ref[a : a + step], w_down, NT)

    ahead = first(starts[0])
    for at, a in enumerate(starts):
        pre, gact = ahead
        if at + 1 < len(starts):
            ahead = first(starts[at + 1])
        act, slope = gelu_parts(pre)
        act_low = act.astype(bf16)
        gpre_low = (gact * slope).astype(bf16)
        act_ref[0, a : a + step] = act_low
        gpre_ref[0, a : a + step] = gpre_low
        if use is not None:
            use(a, a + step, act_low, gpre_low)


def join_cols(refs):
    return jnp.concatenate([r[...] for r in refs], axis=1)


def join_rows(refs):
    return jnp.concatenate([r[...] for r in refs], axis=0)


def weight_specs(width, hidden, nz, first=0):
    per = hidden // (nz * FFT)
    ins = [
        pl.BlockSpec((width, FFT), lambda c, z=z: (0, z * per + c + first)) for z in range(nz)
    ]
    downs = [
        pl.BlockSpec((FFT, width), lambda c, z=z: (z * per + c + first, 0)) for z in range(nz)
    ]
    return ins + downs


def expert_b_body(*refs, nz, carry):
    rows_a, cot_a, act_a, gpre_a, rows_b, cot_b = refs[:6]
    rows_a, rows_b = rows_a.at[0], rows_b.at[0]
    w_in = join_cols(refs[6 : 6 + nz])
    w_down = join_rows(refs[6 + nz : 6 + 2 * nz])
    rest = refs[6 + 2 * nz :]
    if carry:
        give_ref, act_b, gpre_b, sum_ref, take_ref, stay_s, a2a_s, a2a_r = rest
        experts = lax.axis_size("expert")
        e = lax.axis_index("expert")
        peers = [(lax.axis_index("dp"), (e + j) % experts) for j in range(1, experts)]
        spread, settle = front_lanes(
            give_ref, None, take_ref, None, stay_s, a2a_s, a2a_r, give_ref.shape[2]
        )

        @pl.when(pl.program_id(0) == 0)
        def _():
            pl.semaphore_wait(greet(peers), len(peers))
            spread(0)

    else:
        act_b, gpre_b, sum_ref = rest
    cot_a, cot_b = cot_a.at[0], cot_b.at[0]
    hidden_rows(rows_b, cot_b, w_in, w_down, act_b, gpre_b)
    for z in range(nz):
        cols = slice(z * FFT, (z + 1) * FFT)
        gdown = dot(act_a[0, :, cols], cot_a[...], TN) + dot(act_b[0, :, cols], cot_b[...], TN)
        sum_ref[z, 0, :FFT] = gdown.astype(bf16)
        gin = dot(gpre_a[0, :, cols], rows_a[...], TN) + dot(gpre_b[0, :, cols], rows_b[...], TN)
        sum_ref[z, 0, FFT:] = gin.astype(bf16)
    if carry:

        @pl.when(pl.program_id(0) == pl.num_programs(0) - 1)
        def _():
            settle(0)


def expert_b_call(rows, act_a, gpre_a, cots, w_in, w_down, nz, first, count, give=None, deps=()):
    _, total, width = rows.shape
    tile = nz * FFT
    hidden = w_in.shape[1]
    mid = pl.BlockSpec((1, total, tile), lambda c: (c + first, 0, 0))

    def cot(s):
        return pl.BlockSpec((1, total, width), lambda c: (s, 0, 0))

    mid_out = pl.BlockSpec((1, total, tile), lambda c: (c, 0, 0))
    carry = give is not None
    args = [rows, cots, act_a, gpre_a, rows, cots, *([w_in] * nz), *([w_down] * nz)]
    in_specs = [cot(0), cot(0), mid, mid, cot(1), cot(1)] + weight_specs(width, hidden, nz, first)
    out_specs = [
        mid_out,
        mid_out,
        pl.BlockSpec((nz, 1, 2 * FFT, width), lambda c: (0, c, 0, 0)),
    ]
    out_shape = [
        sds((count, total, tile), bf16),
        sds((count, total, tile), bf16),
        sds((nz, count, 2 * FFT, width), bf16),
    ]
    scratch = []
    options = dict(vmem_limit_bytes=60 << 20)
    if carry:
        experts = give.shape[1]
        dma = pltpu.SemaphoreType.DMA
        args.append(give)
        in_specs.append(ANY)
        out_specs.append(ANY)
        out_shape.append(sds((1, total, width), bf16))
        scratch = [dma((1,)), dma((1, experts - 1)), dma((1, experts - 1))]
        options.update(collective_id=3, has_side_effects=True)
    return kernel_call(
        functools.partial(expert_b_body, nz=nz, carry=carry),
        args=args,
        deps=deps,
        grid=(count,),
        in_specs=in_specs,
        out_specs=out_specs,
        out_shape=out_shape,
        scratch_shapes=scratch,
        compiler_params=pltpu.CompilerParams(**options),
        cost_estimate=cost(20 * count << 30, 30 << 20),
    )


def back_body(*refs, heads, capacity, split):
    pieces = len(split)
    acts_a = refs[0]
    acts_b, gpres_b = refs[1 : 1 + pieces], refs[1 + pieces : 1 + 2 * pieces]
    gtok_ref = refs[1 + 2 * pieces]
    (
        w_in,
        w_down,
        qkv_ref,
        mixed_ref,
        after_ref,
        cot_ref,
        fo_ref,
        lse_ref,
        slot_ref,
        g_ref,
        d_ref,
        ga_ref,
        gtoks_ref,
        outs_ref,
        gw_ref,
        sums_ref,
        slab_g,
        slab_o,
        qkv_v,
        mixed_v,
        after_v,
        cot_v,
        fo_v,
        load_s,
        mid_s,
        w_s,
        save_s,
        stay_s,
        a2a_s,
        a2a_r,
    ) = refs[2 + 2 * pieces :]
    nz = lax.axis_size("dp")
    experts = lax.axis_size("expert")
    z = lax.axis_index("dp")
    e = lax.axis_index("expert")
    seqs, total, width = gtoks_ref.shape
    length = after_ref.shape[1]
    hidden = w_in.shape[1]
    tile = nz * FFT
    chunks = hidden // tile
    peers = [(z, (e + j) % experts) for j in range(1, experts)]

    def load(n, src, dst):
        return pltpu.make_async_copy(src, dst, load_s.at[n])

    early = [load(0, fo_ref, fo_v), load(1, qkv_ref.at[0], qkv_v.at[0])]
    for s in range(seqs):
        early += [
            load(2 + 3 * s, after_ref.at[s], after_v.at[s]),
            load(3 + 3 * s, cot_ref.at[s], cot_v.at[s]),
            load(4 + 3 * s, mixed_ref.at[s], mixed_v.at[s]),
        ]
    pl.semaphore_wait(greet(peers), len(peers))
    spread, settle = front_lanes(
        slab_g, slab_o, gtoks_ref, outs_ref, stay_s, a2a_s, a2a_r, capacity
    )

    def second(arrays, c):
        for arr, k in zip(arrays, split):
            if c < k:
                return arr.at[c]
            c -= k

    def products(mid_v, in_v, down_v, acc):
        jobs = []
        for n in range(1, 2 * seqs):
            for c in range(chunks):
                first = n % seqs == 0
                if n < seqs:
                    src = second(gpres_b, c)
                else:
                    src = acts_a.at[c] if first else second(acts_b, c)
                jobs.append((n, c, src))

        def fetch(k):
            n, c, src = jobs[k]
            slot = k % 2
            got = [pltpu.make_async_copy(src, mid_v.at[slot], mid_s.at[slot])]
            for zz in range(nz):
                at = (zz * chunks + c) * FFT
                if n < seqs:
                    pair = (w_in.at[:, at : at + FFT], in_v.at[slot, :, zz * FFT : (zz + 1) * FFT])
                else:
                    pair = (w_down.at[at : at + FFT], down_v.at[slot, zz * FFT : (zz + 1) * FFT])
                got.append(pltpu.make_async_copy(*pair, w_s.at[slot, zz]))
            return got

        step = slot_chunk(total)
        for c in fetch(0):
            c.start()
        for k, (n, c, _) in enumerate(jobs):
            if k + 1 < len(jobs):
                for v in fetch(k + 1):
                    v.start()
            for v in fetch(k):
                v.wait()
            slot = k % 2
            w, dims = (in_v[slot], NT) if n < seqs else (down_v[slot], NN)
            for a in range(0, total, step):
                term = dot(mid_v[slot, a : a + step], w, dims)
                if c == 0:
                    acc[a : a + step] = term
                else:
                    acc[a : a + step] += term
            if c == chunks - 1:
                slab = slab_g if n < seqs else slab_o
                for ee in range(experts):
                    slab[n % seqs, ee] = acc[ee * capacity : (ee + 1) * capacity].astype(bf16)
                spread(n)
            if k == 1:
                for v in early:
                    v.start()

    pl.run_scoped(
        products,
        pltpu.VMEM((2, total, tile), bf16),
        pltpu.VMEM((2, width, tile), bf16),
        pltpu.VMEM((2, tile, width), bf16),
        pltpu.VMEM((total, width), f32),
    )
    hs = width // heads
    pairs = heads // 2
    blk = min(BLK, length)

    def backward(back_v, ga_v, gm_v, d_v, dqa, doa):
        sums_ref[...] = jnp.zeros_like(sums_ref)
        saves = {}
        for s in range(seqs):
            if s:
                settle(s)
            fill = load(2 + 3 * seqs, gtoks_ref.at[s] if s else gtok_ref.at[0], back_v)
            fill.start()
            if s:
                again = load(1, qkv_ref.at[s], qkv_v.at[0])
                again.start()
            else:
                for v in early:
                    v.wait()
            fill.wait()
            starts = list(range(0, length, blk))

            def take(a, s=s):
                return take_rows(back_v[...], slot_ref[s, a : a + blk])

            ahead = take(0)
            for at, a in enumerate(starts):
                gt = ahead
                if at + 1 < len(starts):
                    ahead = take(starts[at + 1])
                rows = slice(a, a + blk)
                hat, r = norm_parts(after_v[s, rows].astype(f32))
                sums_ref[2:3] += jnp.sum(gt * hat, axis=0, keepdims=True)
                sums_ref[3:4] += jnp.sum(gt, axis=0, keepdims=True)
                g = gt * row(g_ref)
                ga = cot_v[s, rows].astype(f32) + r * (
                    g
                    - jnp.mean(g, axis=-1, keepdims=True)
                    - hat * jnp.mean(g * hat, axis=-1, keepdims=True)
                )
                ga_v[s, rows] = ga.astype(bf16)
                gm_v[0, rows] = dot(ga_v[s, rows], fo_v[...], NT).astype(bf16)
            gw = dot(mixed_v[s], ga_v[s], TN)
            if s == 0:
                gw_ref[...] = gw
            else:
                gw_ref[...] += gw
                again.wait()
                saves[s - 1].wait()
            keep = pltpu.make_async_copy(ga_v.at[s], ga_ref.at[s], save_s.at[0, s])
            keep.start()

            def pair(p, carry, s=s):
                def cols(t):
                    return pl.ds(pl.multiple_of(t * width + p * 2 * hs, 128), 2 * hs)

                one = pl.ds(s, 1)
                attn_bwd_body(
                    qkv_v.at[:, :, cols(0)],
                    qkv_v.at[:, :, cols(1)],
                    qkv_v.at[:, :, cols(2)],
                    mixed_v.at[one, :, cols(0)],
                    gm_v.at[:, :, cols(0)],
                    lse_ref.at[one, pl.ds(p, 1)],
                    d_v.at[:, :, :, cols(0)],
                    dqa,
                    doa,
                    blk=blk,
                    hs=hs,
                    scale=hs**-0.5,
                    depth=2,
                )
                return carry

            lax.fori_loop(0, pairs, pair, 0)
            saves[s] = pltpu.make_async_copy(d_v.at[0], d_ref.at[s], save_s.at[1, s])
            saves[s].start()
            keep.wait()
        saves[seqs - 1].wait()

    pl.run_scoped(
        backward,
        pltpu.VMEM((total, width), bf16),
        pltpu.VMEM((seqs, length, width), bf16),
        pltpu.VMEM((1, length, width), bf16),
        pltpu.VMEM((1, 3, length, width), bf16),
        pltpu.VMEM((2 * hs, length), f32),
        pltpu.VMEM((2, length, 2 * hs), bf16),
    )
    for n in range(seqs, 2 * seqs):
        settle(n)


def back_call(
    acts_a, acts_b, gpres_b, gtok, w_in, w_down, qkv, mixed, after, cot, fo, lse, slot_col, gain, heads, nz, experts, capacity
):
    seqs, length, width = after.shape
    total = experts * capacity
    dma = pltpu.SemaphoreType.DMA
    slab = (seqs, experts, capacity, width)
    split = [v.shape[0] for v in acts_b]
    three = pltpu.VMEM((seqs, length, width), bf16)
    return pl.pallas_call(
        functools.partial(back_body, heads=heads, capacity=capacity, split=split),
        in_specs=[ANY] * (2 + 2 * len(split) + 7) + [VM] * 3,
        out_specs=[ANY] * 4 + [VM] * 2,
        out_shape=[
            sds((seqs, 3, length, width), bf16),
            sds((seqs, length, width), bf16),
            sds((seqs, total, width), bf16),
            sds((seqs, total, width), bf16),
            sds((width, width), f32),
            sds((8, width), f32),
        ],
        scratch_shapes=[
            pltpu.VMEM(slab, bf16),
            pltpu.VMEM(slab, bf16),
            pltpu.VMEM((1, length, 3 * width), bf16),
            three,
            three,
            three,
            pltpu.VMEM((width, width), bf16),
            dma((3 + 3 * seqs,)),
            dma((2,)),
            dma((2, nz)),
            dma((2, seqs)),
            dma((2 * seqs,)),
            dma((2 * seqs, experts - 1)),
            dma((2 * seqs, experts - 1)),
        ],
        compiler_params=pltpu.CompilerParams(
            vmem_limit_bytes=62 << 20, collective_id=2, has_side_effects=True
        ),
        cost_estimate=cost(110 << 30, 60 << 20),
    )(
        acts_a, *acts_b, *gpres_b, gtok, w_in, w_down, qkv, mixed, after, cot, fo, lse, slot_col, gain
    )


GROUPS = 4


def last_body(*refs, seqs, per_seq, plan):
    (dw_ref, d_ref, xw_ref, x_ref, w_any, g_ref, b_ref) = refs[:7]
    gwo_ref, sums_ref, backs_any, slot_ref = refs[7:11]
    gx_ref, res_ref, gq_ref, go_ref, tot_ref = refs[11:16]
    rest = refs[16:]
    acc, low, pay, r1, r2, s2, r3, fin, w0, v1, w1, v2, w2, v3, w_ref, backs = rest[:16]
    send_s, recv_s, vs_s, vr_s, load_s = rest[16:]
    nz = lax.axis_size("dp")
    experts = lax.axis_size("expert")
    z = lax.axis_index("dp")
    e = lax.axis_index("expert")
    chips = experts // 2
    core = e % 2
    chip = e // 2
    mate = (z, chip * 2 + 1 - core)
    others = [(z, lax.rem(chip + j, chips) * 2 + core) for j in range(1, chips)]
    layers = [(lax.rem(z + j, nz), e) for j in range(1, nz)]
    peers = [mate] + others + layers
    width = x_ref.shape[2]
    step = pl.program_id(0)
    last = pl.num_programs(0) - 1
    s1 = r1

    def copy(src, dst, at, peer, sems=None):
        a, b = sems or (send_s, recv_s)
        return pltpu.make_async_remote_copy(
            src_ref=src,
            dst_ref=dst,
            send_sem=a.at[at],
            recv_sem=b.at[at],
            device_id=peer,
            device_id_type=MESH,
        )

    def stage(n, t):
        if n == 1:
            return [copy(pay.at[t, 1 - core], r1.at[t], (t, 0), mate)]
        if n == 2:
            return [
                copy(
                    s1.at[t, lax.rem(chip + j, chips)], r2.at[t, j - 1], (t, j), others[j - 1]
                )
                for j in range(1, chips)
            ]
        if n == 3:
            return [
                copy(
                    s2.at[t, lax.rem(z + j, nz)], r3.at[t, j - 1], (t, chips + j), layers[j - 1]
                )
                for j in range(1, nz)
            ]
        if n == 4:
            here = fin.at[t, core, chip]
            return [
                copy(here, here, (t, chips + nz + j), others[j - 1]) for j in range(1, chips)
            ]
        side = fin.at[t, core]
        return [copy(side, side, (t, 2 * chips + nz), mate)]

    def vector(n):
        sems = (vs_s, vr_s)
        if n == 1:
            return [copy(w0, v1, 0, mate, sems)]
        if n == 2:
            return [copy(w1, v2.at[j - 1], j, others[j - 1], sems) for j in range(1, chips)]
        return [copy(w2, v3.at[j - 1], chips + j, layers[j - 1], sems) for j in range(1, nz)]

    def start(n, t):
        for c in vector(n) if t is None else stage(n, t):
            c.start()

    def finish(n, t):
        for c in vector(n) if t is None else stage(n, t):
            c.wait()
        if t is None:
            if n == 1:
                w1[...] = w0[...] + v1[...]
            elif n == 2:
                line = w1[...]
                for j in range(1, chips):
                    line = line + v2[j - 1]
                w2[...] = line
            else:
                line = w2[...]
                for j in range(1, nz):
                    line = line + v3[j - 1]
                tot_ref[...] = line
            if n < 3:
                start(n + 1, None)
            return
        if n == 1:
            for k in range(chips):
                s1[t, k] = (pay[t, core, k].astype(f32) + r1[t, k].astype(f32)).astype(bf16)
        elif n == 2:
            part = s1[t, chip].astype(f32)
            for j in range(1, chips):
                part = part + r2[t, j - 1].astype(f32)
            s2[t] = part.astype(bf16)
        elif n == 3:
            part = s2[t, z].astype(f32)
            for j in range(1, nz):
                part = part + r3[t, j - 1].astype(f32)
            fin[t, core, chip] = part.astype(bf16)
        elif n == 5:
            piece = fin.shape[3]
            for c in range(2):
                for k in range(chips):
                    at = (c * chips + k) * piece
                    value = fin[t, c, k].astype(f32)
                    if t < 3:
                        gq_ref[at : at + piece, t * width : (t + 1) * width] = value
                    else:
                        go_ref[at : at + piece, :] = value
        if n < 5:
            start(n + 1, t)

    def pack(value, t):
        per = value.shape[0] // nz
        piece = pay.shape[4]
        for zz in range(nz):
            for c in range(2):
                for k in range(chips):
                    at = zz * per + (c * chips + k) * piece
                    pay[t, c, k, zz] = value[at : at + piece].astype(bf16)
        start(1, t)

    loads = [pltpu.make_async_copy(w_any, w_ref, load_s.at[0])]
    loads += [
        pltpu.make_async_copy(backs_any.at[s], backs.at[s], load_s.at[1 + s]) for s in range(seqs)
    ]

    @pl.when(step == 0)
    def _():
        for c in loads:
            c.start()
        pl.semaphore_wait(greet(peers), len(peers))
        pack(gwo_ref[...], 3)

    for n in range(3 * seqs):
        t, s = n // seqs, n % seqs

        @pl.when(step == n)
        def _(t=t, s=s):
            if t == 0:
                hat, _ = norm_parts(xw_ref[0].astype(f32))
                low[s] = (hat * g_ref[...] + b_ref[...]).astype(bf16)
            term = dot(low[s], dw_ref[0, 0], TN)
            if s == 0:
                acc[...] = term
            elif s < seqs - 1:
                acc[...] += term
            else:
                pack(acc[...] + term, t)

    base = 3 * seqs

    @pl.when(step == base)
    def _():
        loads[0].wait()
        w0[0:2] = jnp.zeros((2, width), f32)
        w0[2:8] = sums_ref[2:8]

    @pl.when((step >= base) & (step < base + seqs * per_seq))
    def _():
        hat, r = norm_parts(x_ref[0].astype(f32))
        gn = 0.0
        for t in range(3):
            gn = gn + dot(d_ref[0, t], w_ref[:, t * width : (t + 1) * width], NT)
        w0[0:1] += jnp.sum(gn * hat, axis=0, keepdims=True)
        w0[1:2] += jnp.sum(gn, axis=0, keepdims=True)
        g = gn * g_ref[...]
        gx_ref[0] = (
            r
            * (
                g
                - jnp.mean(g, axis=-1, keepdims=True)
                - hat * jnp.mean(g * hat, axis=-1, keepdims=True)
            )
        ).astype(bf16)

    base = base + seqs * per_seq

    @pl.when(step == base)
    def _():
        for c in loads[1:]:
            c.wait()

    @pl.when(step == base - 1)
    def _():
        start(1, None)

    for s in range(seqs):

        @pl.when((step >= base + s * per_seq) & (step < base + (s + 1) * per_seq))
        def _(s=s):
            res_ref[0] = take_rows(backs[s], slot_ref[0]).astype(bf16)

    for when, events in plan:

        @pl.when(step == when)
        def _(events=events):
            for n, t in events:
                finish(n, t)


def last_plan(seqs, per_seq):
    dw = 3 * seqs
    end = dw + 2 * seqs * per_seq - 1
    mid = dw + seqs * per_seq
    first = [
        (2, [(1, 3)]),
        (4, [(1, 0)]),
        (dw, [(1, 1)]),
        (dw + 2, [(1, 2)]),
        (dw + 4, [(2, 3)]),
        (dw + 6, [(2, 0)]),
        (dw + 7, [(3, 3)]),
        (mid, [(2, 1)]),
        (mid + 1, [(3, 0)]),
        (mid + 2, [(1, None), (2, 2), (4, 3)]),
        (mid + 3, [(3, 1)]),
        (mid + 4, [(2, None), (4, 0), (5, 3)]),
        (mid + 5, [(3, 2)]),
        (mid + 6, [(3, None), (4, 1), (5, 0)]),
        (end, [(4, 2), (5, 1), (5, 2)]),
    ]
    return [(min(a, end), b) for a, b in first]


def last_call(d, x, w, gain, bias, gwo, sums, backs, slot_col, experts, nz):
    seqs, length, width = x.shape
    blk = min(BLK, length)
    per_seq = length // blk
    total = backs.shape[1]
    dw = 3 * seqs
    mid = dw + seqs * per_seq
    chips = experts // 2
    piece = width // nz // experts
    per = width // nz
    dma = pltpu.SemaphoreType.DMA
    once = pl.Buffered(1)

    def keep(*shape):
        return pl.BlockSpec(shape, lambda r: (0,) * len(shape), pipeline_mode=once)

    def at(first, r):
        n = jnp.clip(r - first, 0, seqs * per_seq - 1)
        return n // per_seq, n % per_seq

    def dw_at(r):
        n = jnp.minimum(r, dw - 1)
        return n % seqs, n // seqs, 0, 0

    def rows(first):
        return pl.BlockSpec((1, blk, width), lambda r: (*at(first, r), 0))

    def d_at(r):
        s, b = at(dw, r)
        return s, 0, b, 0

    steps = mid + seqs * per_seq
    in_specs = [
        pl.BlockSpec((1, 1, length, width), dw_at),
        pl.BlockSpec((1, 3, blk, width), d_at),
        pl.BlockSpec((1, length, width), lambda r: (jnp.minimum(r, seqs - 1), 0, 0)),
        rows(dw),
        ANY,
        keep(1, width),
        keep(1, width),
    ]
    in_specs += [keep(width, width), keep(8, width), ANY]
    in_specs += [pl.BlockSpec((1, blk, 1), lambda r: (*at(mid, r), 0))]
    return pl.pallas_call(
        functools.partial(last_body, seqs=seqs, per_seq=per_seq, plan=last_plan(seqs, per_seq)),
        grid=(steps,),
        in_specs=in_specs,
        out_specs=[rows(dw), rows(mid), keep(per, 3 * width), keep(per, width), keep(8, width)],
        out_shape=[
            sds((seqs, length, width), bf16),
            sds((seqs, length, width), bf16),
            sds((per, 3 * width), f32),
            sds((per, width), f32),
            sds((8, width), f32),
        ],
        scratch_shapes=[
            pltpu.VMEM((width, width), f32),
            pltpu.VMEM((seqs, length, width), bf16),
            pltpu.VMEM((GROUPS, 2, chips, nz, piece, width), bf16),
            pltpu.VMEM((GROUPS, chips, nz, piece, width), bf16),
            pltpu.VMEM((GROUPS, chips - 1, nz, piece, width), bf16),
            pltpu.VMEM((GROUPS, nz, piece, width), bf16),
            pltpu.VMEM((GROUPS, nz - 1, piece, width), bf16),
            pltpu.VMEM((GROUPS, 2, chips, piece, width), bf16),
            pltpu.VMEM((8, width), f32),
            pltpu.VMEM((8, width), f32),
            pltpu.VMEM((8, width), f32),
            pltpu.VMEM((chips - 1, 8, width), f32),
            pltpu.VMEM((8, width), f32),
            pltpu.VMEM((nz - 1, 8, width), f32),
            pltpu.VMEM((width, 3 * width), bf16),
            pltpu.VMEM((seqs, total, width), bf16),
        ]
        + [dma((GROUPS, 2 * chips + nz + 1))] * 2
        + [dma((chips + nz,))] * 2
        + [dma((1 + seqs,))],
        compiler_params=pltpu.CompilerParams(
            vmem_limit_bytes=62 << 20, collective_id=1, has_side_effects=True
        ),
        cost_estimate=cost(50 << 30, 150 << 20),
    )(
        d,
        d,
        x,
        x,
        w,
        gain.reshape(1, -1),
        bias.reshape(1, -1),
        gwo,
        sums,
        backs,
        slot_col,
    )


def close_body(*refs, counts):
    ga_ref, dx_ref, after_ref, back_ref, gq_ref, go_ref = refs[:6]
    n = len(counts)
    downs, ins = refs[6 : 6 + n], refs[6 + n : 6 + 2 * n]
    gx_out, res_out, gq_out, go_out, down_out, in_out = refs[6 + 2 * n :]
    step = pl.program_id(0)
    gx_out[...] = ga_ref[...].astype(f32) + dx_ref[...].astype(f32)
    res_out[...] = after_ref[...].astype(f32) + back_ref[...].astype(f32)
    gq_out[...] = gq_ref[...]
    go_out[...] = go_ref[...]
    at = 0
    for k, down, gin in zip(counts, downs, ins):
        down_out[at : at + k] = down[0].astype(f32)

        @pl.when((step >= at) & (step < at + k))
        def _(gin=gin):
            in_out[...] = gin[0, 0].astype(f32).T

        at += k


def close_call(ga, dx, after, back, gq, go, sums):
    seqs, length, width = ga.shape
    blk = min(BLK, length)
    per_seq = length // blk
    steps = seqs * per_seq
    counts = [v.shape[1] for v in sums]
    chunks = sum(counts)
    rows = pl.BlockSpec((1, blk, width), lambda r: (r // per_seq, r % per_seq, 0))

    def split(v):
        return pl.BlockSpec((v.shape[0] // steps, v.shape[1]), lambda r: (r, 0))

    def down(v):
        return pl.BlockSpec((1, v.shape[1], FFT // steps, width), lambda r: (0, 0, r, 0))

    def inward(n):
        lo = sum(counts[:n])
        return pl.BlockSpec(
            (1, 1, FFT, width), lambda r: (0, jnp.clip(r - lo, 0, counts[n] - 1), 1, 0)
        )

    return pl.pallas_call(
        functools.partial(close_body, counts=counts),
        grid=(steps,),
        in_specs=[rows] * 4
        + [split(gq), split(go)]
        + [down(v) for v in sums]
        + [inward(n) for n in range(len(sums))],
        out_specs=[
            rows,
            rows,
            split(gq),
            split(go),
            pl.BlockSpec((chunks, FFT // steps, width), lambda r: (0, r, 0)),
            pl.BlockSpec((width, FFT), lambda r: (0, jnp.minimum(r, chunks - 1))),
        ],
        out_shape=[
            sds((seqs, length, width), f32),
            sds((seqs, length, width), f32),
            sds(gq.shape, f32),
            sds(go.shape, f32),
            sds((chunks, FFT, width), f32),
            sds((width, chunks * FFT), f32),
        ],
        compiler_params=params(60),
        cost_estimate=cost(8 << 30, 40 << 20),
    )(ga, dx, after, back, gq, go, *sums, *sums)


def exchange(parts):
    got = lax.all_to_all(parts, "expert", split_axis=0, concat_axis=0, tiled=True)
    return got.reshape(-1, parts.shape[-1])


def on_device(
    tokens_in,
    buckets,
    ln1_gain,
    ln1_bias,
    w_qkv,
    w_out,
    ln2_gain,
    ln2_bias,
    w_in,
    w_down,
    cotangent,
):
    experts = lax.axis_size("expert")
    nz = lax.axis_size("dp")
    seqs, length, width = tokens_in.shape
    capacity = 5 * length // (4 * experts)
    total = experts * capacity
    w_in_local = w_in[0]
    w_down_local = w_down[0]
    hidden = w_in_local.shape[1]
    chunks = hidden // (nz * FFT)

    qkv, full_qkv, full_out, mixed, after, lse, slot_col, cots, rows, act_a, gpre_a, give = front_call(
        tokens_in,
        ln1_gain,
        ln1_bias,
        ln2_gain,
        ln2_bias,
        w_qkv,
        w_out,
        buckets,
        cotangent,
        w_in_local,
        w_down_local,
        HEADS,
        nz,
        experts,
        capacity,
    )
    last = ()
    acts, gpres, totals = [], [], []
    for first, many in ((0, 1), (1, chunks - 1)):
        made = expert_b_call(
            rows,
            act_a,
            gpre_a,
            cots,
            w_in_local,
            w_down_local,
            nz,
            first,
            many,
            give=give if first else None,
            deps=last,
        )
        last = (made[0],)
        acts.append(made[0])
        gpres.append(made[1])
        totals.append(lax.psum_scatter(made[2], "dp", scatter_dimension=0, tiled=True))
    gtok_a = made[3]
    d, ga, _, outs, gwo, sums = back_call(
        act_a,
        acts,
        gpres,
        gtok_a,
        w_in_local,
        w_down_local,
        qkv,
        mixed,
        after,
        cotangent,
        full_out,
        lse,
        slot_col,
        ln2_gain,
        HEADS,
        nz,
        experts,
        capacity,
    )
    dx, back, gq, go, sums = last_call(
        d,
        tokens_in,
        full_qkv,
        ln1_gain,
        ln1_bias,
        gwo,
        sums,
        outs,
        slot_col,
        experts,
        nz,
    )
    gxs, results, gq, go, gdown, gin = close_call(ga, dx, after, back, gq, go, totals)
    mine = lax.dynamic_slice_in_dim(
        sums, lax.axis_index("dp") * (width // nz), width // nz, axis=1
    )
    return (
        results,
        gxs,
        mine[0],
        mine[1],
        gq,
        go,
        mine[2],
        mine[3],
        gin[None],
        gdown.reshape(1, hidden // nz, width),
    )


def solution(mesh):
    placed = (
        P(("dp", "expert"), None, None),
        P(("dp", "expert"), None),
        P(),
        P(),
        P("dp", None),
        P("dp", None),
        P(),
        P(),
        P("expert", None, None),
        P("expert", None, None),
        P(("dp", "expert"), None, None),
    )
    return jax.shard_map(
        on_device,
        mesh=mesh,
        in_specs=placed,
        out_specs=(
            P(("dp", "expert"), None, None),
            P(("dp", "expert"), None, None),
            P("dp"),
            P("dp"),
            P("dp", None),
            P("dp", None),
            P("dp"),
            P("dp"),
            P("expert", None, "dp"),
            P("expert", "dp", None),
        ),
        check_vma=False,
    )
```

```python
import functools

import jax
import jax.numpy as jnp
from jax import lax
from jax.experimental import pallas as pl
from jax.experimental.pallas import tpu as pltpu
from jax.sharding import PartitionSpec as P

HEADS = 12
EPS = 1e-5
NEG = -1e30
bf16 = jnp.bfloat16
f32 = jnp.float32
NN = (((1,), (0,)), ((), ()))
NT = (((1,), (1,)), ((), ()))
TN = (((0,), (0,)), ((), ()))
GELU_A = 0.7978845608028654
GELU_B = 0.044715
BLK = 256
FFT = 256


def dot(a, b, dims=NN):
    return lax.dot_general(a, b, dims, preferred_element_type=f32)


def params(mib=56):
    return pltpu.CompilerParams(vmem_limit_bytes=mib << 20)


def cost(flops, nbytes, trans=0):
    return pl.CostEstimate(flops=int(flops), bytes_accessed=int(nbytes), transcendentals=int(trans))


def sds(shape, dtype):
    return jax.ShapeDtypeStruct(shape, dtype)


VM = pl.BlockSpec(memory_space=pltpu.VMEM)
ANY = pl.BlockSpec(memory_space=pl.ANY)


def kernel_call(body, in_specs, args, deps=(), into=None, **options):
    into = into or {}
    count = len(args)
    extra = len(into) + len(deps)

    def wrapped(*refs):
        body(*refs[:count], *refs[count + extra :])

    return pl.pallas_call(
        wrapped,
        in_specs=list(in_specs) + [ANY] * extra,
        input_output_aliases={count + n: out for n, out in enumerate(into)},
        **options,
    )(*args, *into.values(), *deps)


def norm_parts(v):
    centre = jnp.mean(v, axis=-1, keepdims=True)
    shifted = v - centre
    spread = jnp.mean(shifted * shifted, axis=-1, keepdims=True)
    r = lax.rsqrt(spread + EPS)
    return shifted * r, r


MESH = pl.DeviceIdType.MESH


def greet(peers):
    barrier = pltpu.get_barrier_semaphore()
    for peer in peers:
        pl.semaphore_signal(barrier, inc=1, device_id=peer, device_id_type=MESH)
    return barrier


def find_slots(bucket, experts, capacity):
    length = bucket.shape[1]
    hot = (lax.broadcasted_iota(jnp.int32, (experts, length), 0) == bucket).astype(f32)
    upto = lax.broadcasted_iota(jnp.int32, (length, length), 0) <= lax.broadcasted_iota(
        jnp.int32, (length, length), 1
    )
    count = dot(hot.astype(bf16), upto.astype(bf16))
    rank = jnp.sum(hot * count, axis=0, keepdims=True) - 1.0
    return bucket * capacity + rank.astype(jnp.int32)


GATHERS = 3


def front_body(*refs, heads, capacity):
    nz = lax.axis_size("dp")
    n = 9 + 2 * nz
    (x_ref, g1_ref, b1_ref, g2_ref, b2_ref, wq_ref, wo_ref, buckets_ref, cot_ref) = refs[:9]
    w_ins, w_downs = refs[9 : 9 + nz], refs[9 + nz : n]
    (
        qkv_ref,
        fq_ref,
        fo_ref,
        mixed_ref,
        after_ref,
        lse_ref,
        col_ref,
        cots_ref,
        rows_ref,
        act_ref,
        gpre_ref,
        give_ref,
    ) = refs[n : n + 12]
    (
        fq_v,
        fo_v,
        sent,
        toks,
        slots,
        rows_v,
        cot_a,
        up_s,
        dn_s,
        core_s,
        z_r,
        core_r,
        own_s,
        load_s,
        save_s,
        stay_s,
        a2a_s,
        a2a_r,
    ) = refs[n + 12 :]
    seqs, length, width = x_ref.shape

    def work(x_v, cot_v, low, qkv_v, mixed_v, after_v):
        return front_work(
            x_ref, g1_ref, b1_ref, g2_ref, b2_ref, wq_ref, wo_ref, buckets_ref, cot_ref,
            qkv_ref, fq_ref, fo_ref, mixed_ref, after_ref, lse_ref, col_ref, cots_ref, rows_ref,
            x_v, cot_v, fq_v, fo_v, low, qkv_v, sent, toks, mixed_v, after_v, slots,
            up_s, dn_s, core_s, z_r, core_r, own_s, load_s, save_s, stay_s, a2a_s, a2a_r,
            heads=heads, capacity=capacity,
        )

    one = pltpu.VMEM((seqs, length, width), bf16)
    pl.run_scoped(work, one, one, one, pltpu.VMEM((seqs, length, 3 * width), bf16), one, one)
    settle = front_lanes(sent, toks, cots_ref, rows_ref, stay_s, a2a_s, a2a_r, capacity)[1]
    hidden = w_ins[0].shape[1]
    total = rows_v.shape[0]
    chunks = hidden // (nz * FFT)
    specs = weight_specs(width, hidden, nz)
    mid = pl.BlockSpec((1, total, nz * FFT), lambda c: (c, 0, 0))

    def fill(src, dst, n):
        load = pltpu.make_async_copy(src, dst, load_s.at[n, 0])
        load.start()
        load.wait()

    def expert(acc, gact):
        settle(0)
        fill(cots_ref.at[0], cot_a, 1)
        size = slot_chunk(total)

        def early(*blocks):
            c = pl.program_id(0)
            w_down = join_rows(blocks)
            for a in range(0, total, size):
                gact[c, a : a + size] = dot(cot_a[a : a + size], w_down, NT).astype(bf16)

        pltpu.emit_pipeline(early, grid=(chunks,), in_specs=specs[nz:])(*w_downs)
        for k in range(1, seqs + 1):
            settle(k)
        fill(rows_ref.at[0], rows_v, 0)
        acc[...] = jnp.zeros_like(acc)

        def step(*blocks):
            w_in = join_cols(blocks[:nz])

            def use(a, b, act_low, gpre_low):
                acc[a:b] += dot(gpre_low, w_in, NT)

            hidden_rows(rows_v, gact.at[pl.program_id(0)], w_in, None, *blocks[nz:], use)

        pltpu.emit_pipeline(
            step, grid=(chunks,), in_specs=specs[:nz], out_specs=[mid, mid]
        )(*w_ins, act_ref, gpre_ref)
        for k in range(sent.shape[1]):
            sent[0, k] = acc[k * capacity : (k + 1) * capacity].astype(bf16)
        fill(sent.at[0], give_ref.at[0], 0)

    pl.run_scoped(
        expert, pltpu.VMEM((total, width), f32), pltpu.VMEM((chunks, total, nz * FFT), bf16)
    )
    for k in range(seqs + 1, 2 * seqs):
        settle(k)


def front_lanes(sent, toks, cots_ref, rows_ref, stay_s, a2a_s, a2a_r, capacity):
    experts = lax.axis_size("expert")
    z = lax.axis_index("dp")
    e = lax.axis_index("expert")
    seqs = cots_ref.shape[0]
    plane = [(e + j) % experts for j in range(1, experts)]
    back = [(e + experts - j) % experts for j in range(1, experts)]

    def lane(n, at):
        src, dst = (sent, cots_ref) if n < seqs else (toks, rows_ref)
        k = n % seqs
        return src.at[k], dst.at[k, pl.ds(pl.multiple_of(at * capacity, 8), capacity)]

    def trade(n, j, at):
        src, dst = lane(n, at)
        return pltpu.make_async_remote_copy(
            src_ref=src.at[plane[j]],
            dst_ref=dst,
            send_sem=a2a_s.at[n, j],
            recv_sem=a2a_r.at[n, j],
            device_id=(z, plane[j]),
            device_id_type=MESH,
        )

    def stay(n):
        src, dst = lane(n, e)
        return pltpu.make_async_copy(src.at[e], dst, stay_s.at[n])

    def spread(n):
        for j in range(experts - 1):
            trade(n, j, e).start()
        stay(n).start()

    def settle(n):
        stay(n).wait()
        for j in range(experts - 1):
            trade(n, j, e).wait_send()
            trade(n, j, back[j]).wait_recv()

    return spread, settle


def front_work(
    x_ref,
    g1_ref,
    b1_ref,
    g2_ref,
    b2_ref,
    wq_ref,
    wo_ref,
    buckets_ref,
    cot_ref,
    qkv_ref,
    fq_ref,
    fo_ref,
    mixed_ref,
    after_ref,
    lse_ref,
    col_ref,
    cots_ref,
    rows_ref,
    x_v,
    cot_v,
    fq_v,
    fo_v,
    low,
    qkv_v,
    sent,
    toks,
    mixed_v,
    after_v,
    slots,
    up_s,
    dn_s,
    core_s,
    z_r,
    core_r,
    own_s,
    load_s,
    save_s,
    stay_s,
    a2a_s,
    a2a_r,
    *,
    heads,
    capacity,
):
    nz = lax.axis_size("dp")
    experts = lax.axis_size("expert")
    z = lax.axis_index("dp")
    e = lax.axis_index("expert")
    core = e % 2
    seqs, length, width = x_ref.shape
    spread = front_lanes(sent, toks, cots_ref, rows_ref, stay_s, a2a_s, a2a_r, capacity)[0]
    per = width // nz
    half = per // 2
    above = (jnp.minimum(z + 1, nz - 1), e)
    below = (jnp.maximum(z - 1, 0), e)
    mate = (z, e + 1 - 2 * core)
    full = (fq_v, fo_v)
    shard = (wq_ref, wo_ref)
    blk = min(BLK, length)

    cot_in = [pltpu.make_async_copy(cot_ref.at[s], cot_v.at[s], load_s.at[0, s]) for s in range(seqs)]
    x_in = [pltpu.make_async_copy(x_ref.at[s], x_v.at[s], load_s.at[1, s]) for s in range(seqs)]
    for c in cot_in[:1] + x_in + cot_in[1:]:
        c.start()

    barrier = pltpu.get_barrier_semaphore()

    @pl.when(z + 1 < nz)
    def _():
        pl.semaphore_signal(barrier, inc=1, device_id=above, device_id_type=MESH)

    @pl.when(z > 0)
    def _():
        pl.semaphore_signal(barrier, inc=1, device_id=below, device_id_type=MESH)

    plane = [(z, (e + j) % experts) for j in range(1, experts)]
    for peer in plane:
        pl.semaphore_signal(barrier, inc=1, device_id=peer, device_id_type=MESH)

    @pl.when((z + 1 < nz) & (z > 0))
    def _():
        pl.semaphore_wait(barrier, experts + 1)

    @pl.when((z + 1 >= nz) | (z <= 0))
    def _():
        pl.semaphore_wait(barrier, experts)

    hs = width // heads
    pairs = heads // 2
    groups = min(GATHERS, pairs)
    wide = width // groups
    lanes = [[(3 * g + m, 0, m * width + g * wide, wide) for m in range(3)] for g in range(groups)]
    lanes.append([(3 * groups, 1, 0, width)])

    def half_rows(ref, at, piece):
        return ref.at[pl.ds(pl.multiple_of(at, 16), half), pl.ds(piece[2], piece[3])]

    def held(piece, p, c):
        return half_rows(full[piece[1]], p * per + c * half, piece)

    def mine(piece):
        return half_rows(shard[piece[1]], core * half, piece)

    def hop(piece, p, c, src, sem, r_sem, peer):
        return pltpu.make_async_remote_copy(
            src_ref=src,
            dst_ref=held(piece, p, c),
            send_sem=sem.at[piece[0], p],
            recv_sem=r_sem.at[piece[0], p],
            device_id=peer,
            device_id_type=MESH,
        )

    def pass_on(piece, p, sem, r_sem, peer):
        return hop(piece, p, core, held(piece, p, core), sem, r_sem, peer)

    def own(piece):
        cols = pl.ds(piece[2], piece[3])
        return pltpu.make_async_copy(
            shard[piece[1]].at[:, cols],
            full[piece[1]].at[pl.ds(pl.multiple_of(z * per, 16), per), cols],
            own_s.at[piece[0]],
        )

    def begin(i):
        for piece in lanes[i]:

            @pl.when(z + 1 < nz)
            def _(piece=piece):
                hop(piece, z, core, mine(piece), up_s, z_r, above).start()

            @pl.when(z > 0)
            def _(piece=piece):
                hop(piece, z, core, mine(piece), dn_s, z_r, below).start()

            own(piece).start()

    def sides(d):
        return ((z - d >= 0, z - d, z + 1 < nz, up_s, above), (z + d < nz, z + d, z > 0, dn_s, below))

    def arrivals(i, d):
        for ok, p, more, sem, peer in sides(d):

            @pl.when(ok)
            def _(p=p, more=more, sem=sem, peer=peer):
                for piece in lanes[i]:
                    pass_on(piece, p, sem, z_r, peer).wait_recv()

                    @pl.when(more)
                    def _(piece=piece):
                        pass_on(piece, p, sem, z_r, peer).start()

                    pass_on(piece, p, core_s, core_r, mate).start()

    def wave(w):
        for i in range(len(lanes)):
            if 0 < w - i < nz:
                arrivals(i, w - i)
            if w == i:
                begin(i)

    def complete(i):
        for piece in lanes[i]:
            own(piece).wait()
            for d in range(1, nz):
                for ok, p, _, _, _ in sides(d):

                    @pl.when(ok)
                    def _(piece=piece, p=p):
                        hop(
                            piece, p, 1 - core, held(piece, p, 1 - core), core_s, core_r, mate
                        ).wait_recv()

    def sent_all(i):
        for piece in lanes[i]:

            @pl.when(z + 1 < nz)
            def _(piece=piece):
                hop(piece, z, core, mine(piece), up_s, z_r, above).wait_send()

            @pl.when(z > 0)
            def _(piece=piece):
                hop(piece, z, core, mine(piece), dn_s, z_r, below).wait_send()

            for d in range(1, nz):
                for ok, p, more, sem, peer in sides(d):

                    @pl.when(ok)
                    def _(piece=piece, p=p):
                        pass_on(piece, p, core_s, core_r, mate).wait_send()

                    @pl.when(ok & more)
                    def _(piece=piece, p=p, sem=sem, peer=peer):
                        pass_on(piece, p, sem, z_r, peer).wait_send()

    def prepare(s):
        slot = find_slots(buckets_ref[s : s + 1, :], experts, capacity)
        slots[s] = slot
        col_ref[s] = jnp.broadcast_to(slot.astype(f32), (8, length)).T[:, :1].astype(jnp.int32)
        cot_in[s].wait()
        place_rows(cot_v[s], slot, sent.at[s])
        spread(s)

    def first_norm(s):
        x_in[s].wait()
        for a in range(0, length, blk):
            hat, _ = norm_parts(x_v[s, a : a + blk].astype(f32))
            low[s, a : a + blk] = (hat * row(g1_ref) + row(b1_ref)).astype(bf16)

    def save(n, src, dst):
        return pltpu.make_async_copy(src, dst, save_s.at[n])

    saves = [save(0, fq_v, fq_ref), save(1, fo_v, fo_ref)]
    for s in range(seqs):
        saves += [
            save(2 + 3 * s, qkv_v.at[s], qkv_ref.at[s]),
            save(3 + 3 * s, mixed_v.at[s], mixed_ref.at[s]),
            save(4 + 3 * s, after_v.at[s], after_ref.at[s]),
        ]

    def project(s, g):
        for _, _, at, size in lanes[g]:
            w = fq_v[:, at : at + size]
            rows = min(512, length)
            for a in range(0, length, rows):
                qkv_v[s, a : a + rows, at : at + size] = dot(low[s, a : a + rows], w).astype(bf16)

    each = pairs // groups

    def attend(g, first, many):
        def pair(n, carry):
            s = first + n // each
            p = g * each + n % each

            def cols(t):
                return pl.ds(pl.multiple_of(t * width + p * 2 * hs, 128), 2 * hs)

            one = pl.ds(s, 1)
            attn_fwd_body(
                qkv_v.at[one, :, cols(0)],
                qkv_v.at[one, :, cols(1)],
                qkv_v.at[one, :, cols(2)],
                mixed_v.at[one, :, cols(0)],
                lse_ref.at[one, pl.ds(p, 1)],
                blk=blk,
                hs=hs,
                scale=hs**-0.5,
                depth=3,
            )
            return carry

        lax.fori_loop(0, many * each, pair, 0)

    def finish(s, out):
        for a in range(0, length, blk):
            rows = slice(a, a + blk)
            after = x_v[s, rows].astype(f32) + dot(mixed_v[s, rows], fo_v[...])
            after_v[s, rows] = after.astype(bf16)
            hat, _ = norm_parts(after)
            low[s, rows] = (hat * row(g2_ref) + row(b2_ref)).astype(bf16)
        saves[4 + 3 * s].start()
        place_rows(low[s], slots[s], out)

    todo = list(range(1, groups + nz))

    def waves(upto):
        while todo and todo[0] <= upto:
            wave(todo.pop(0))

    wave(0)
    prepare(0)
    waves(1)
    for s in range(seqs):
        first_norm(s)
    waves(2)
    for s in range(1, seqs):
        prepare(s)
    for g in range(groups):
        waves(g + nz - 1)
        complete(g)
        for s in range(seqs):
            project(s, g)
        if g < groups - 1:
            attend(g, 0, seqs)
    saves[0].start()
    for s in range(seqs):
        saves[2 + 3 * s].start()
    attend(groups - 1, 0, 1)
    waves(groups + nz - 1)
    complete(groups)
    saves[1].start()
    saves[3].start()
    finish(0, toks.at[0])
    spread(seqs)
    for s in range(1, seqs):
        attend(groups - 1, s, 1)
        saves[3 + 3 * s].start()
        finish(s, toks.at[s])
        spread(seqs + s)
    for i in range(groups + 1):
        sent_all(i)
    for c in saves:
        c.wait()


def row(ref):
    return ref[...].reshape(1, -1)


def front_call(x, g1, b1, g2, b2, wq, wo, buckets, cot, w_in, w_down, heads, nz, experts, capacity):
    seqs, length, width = x.shape
    triple = wq.shape[1]
    dma = pltpu.SemaphoreType.DMA
    slab = (seqs, experts, capacity, width)
    total = experts * capacity
    pairs = heads // 2
    tile = nz * FFT
    chunks = w_in.shape[1] // tile
    return pl.pallas_call(
        functools.partial(front_body, heads=heads, capacity=capacity),
        in_specs=[ANY] + [VM] * 4 + [ANY] * 2 + [VM, ANY] + [ANY] * (2 * nz),
        out_specs=[ANY] * 5 + [VM] * 2 + [ANY] * 5,
        out_shape=[
            sds((seqs, length, triple), bf16),
            sds((width, triple), bf16),
            sds((width, width), bf16),
            sds((seqs, length, width), bf16),
            sds((seqs, length, width), bf16),
            sds((seqs, pairs, 2, length), f32),
            sds((seqs, length, 1), jnp.int32),
            sds((seqs, total, width), bf16),
            sds((seqs, total, width), bf16),
            sds((chunks, total, tile), bf16),
            sds((chunks, total, tile), bf16),
            sds((1, experts, capacity, width), bf16),
        ],
        scratch_shapes=[
            pltpu.VMEM((width, triple), bf16),
            pltpu.VMEM((width, width), bf16),
            pltpu.VMEM(slab, bf16),
            pltpu.VMEM(slab, bf16),
            pltpu.VMEM((seqs, 1, length), jnp.int32),
            pltpu.VMEM((total, width), bf16),
            pltpu.VMEM((total, width), bf16),
        ]
        + [dma((3 * GATHERS + 1, nz))] * 5
        + [dma((3 * GATHERS + 1,)), dma((2, seqs)), dma((2 + 3 * seqs,)), dma((2 * seqs,))]
        + [dma((2 * seqs, experts - 1))] * 2,
        compiler_params=pltpu.CompilerParams(
            vmem_limit_bytes=62 << 20, collective_id=0, has_side_effects=True
        ),
        cost_estimate=cost(110 << 30, 40 << 20),
    )(x, g1, b1, g2, b2, wq, wo, buckets, cot, *([w_in] * nz), *([w_down] * nz))


def attn_fwd_body(q_ref, k_ref, v_ref, o_ref, lse_ref, *, blk, hs, scale, depth):
    length = q_ref.shape[1]
    lane = lax.broadcasted_iota(jnp.int32, (1, 2 * hs), 1) // hs
    v_t = v_ref[0].T
    keys = k_ref[0]
    kh = [jnp.where(lane == h, keys, jnp.zeros_like(keys)) for h in range(2)]
    ones = jnp.ones((16, length), bf16)
    vh = [jnp.concatenate([v_t[h * hs : (h + 1) * hs], ones], axis=0) for h in range(2)]
    future = lax.broadcasted_iota(jnp.int32, (blk, blk), 0) > lax.broadcasted_iota(
        jnp.int32, (blk, blk), 1
    )
    tasks = [(i, h) for i in range(length // blk) for h in range(2)]

    def score(task):
        i, h = task
        top = (i + 1) * blk
        q = q_ref[0, i * blk : top, :] * jnp.asarray(scale, bf16)
        s = dot(kh[h][:top], q, NT)
        diag = jnp.where(future, NEG, s[i * blk :])
        s = jnp.concatenate([s[: i * blk], diag], axis=0) if i else diag
        return s, jnp.max(s, axis=0, keepdims=True)

    queue = [score(t) for t in tasks[:depth]]
    done = {}
    for at, task in enumerate(tasks):
        if at + depth < len(tasks):
            queue.append(score(tasks[at + depth]))
        s, largest = queue.pop(0)
        i, h = task
        top = (i + 1) * blk
        o = dot(vh[h][:, :top], jnp.exp(s - largest).astype(bf16))
        total = o[hs : hs + 1]
        done[task] = o[:hs] * (1.0 / total)
        lse_ref[0, 0, h : h + 1, i * blk : top] = largest + jnp.log(total)
        if h == 1:
            both = jnp.concatenate([done[(i, 0)], done[(i, 1)]], axis=0)
            o_ref[0, i * blk : top, :] = both.T.astype(bf16)


def attn_bwd_body(
    q_ref, k_ref, v_ref, o_ref, do_ref, lse_ref, d_ref, dqa, doa, *, blk, hs, scale, depth
):
    length = q_ref.shape[1]
    n = length // blk
    lanes = lax.broadcasted_iota(jnp.int32, (1, 2 * hs), 1)
    lane = lanes // hs
    spot = lanes % hs
    keys = k_ref[0]
    vals = v_ref[0]
    k_t = (keys * jnp.asarray(scale, bf16)).T
    kh = [jnp.where(lane == h, keys, jnp.zeros_like(keys)) for h in range(2)]
    vh = [
        jnp.where(lane == h, vals, jnp.where(spot < 2, jnp.ones_like(vals), jnp.zeros_like(vals)))
        for h in range(2)
    ]
    future = lax.broadcasted_iota(jnp.int32, (blk, blk), 0) > lax.broadcasted_iota(
        jnp.int32, (blk, blk), 1
    )
    q = q_ref[0] * jnp.asarray(scale, bf16)
    do = do_ref[0]
    prod = do.astype(f32) * o_ref[0].astype(f32)
    for h in range(2):
        inside = lane == h
        inner = -jnp.sum(jnp.where(inside, prod, 0.0), axis=1, keepdims=True)
        high = inner.astype(bf16)
        rest = (inner - high.astype(f32)).astype(bf16)
        doa[h] = jnp.where(
            inside,
            do,
            jnp.where(spot == 0, high, jnp.where(spot == 1, rest, jnp.zeros_like(high))),
        )
    tasks = [(j, h) for j in range(n) for h in range(2)]

    def score(task):
        j, h = task
        a = j * blk
        return (
            dot(kh[h][a : a + blk], q[a:], NT),
            dot(vh[h][a : a + blk], doa[h, a:], NT),
        )

    queue = [score(t) for t in tasks[:depth]]
    kept = None
    for at, task in enumerate(tasks):
        if at + depth < len(tasks):
            queue.append(score(tasks[at + depth]))
        s, dp = queue.pop(0)
        j, h = task
        a = j * blk
        p = jnp.exp(s - lse_ref[0, 0, h : h + 1, a:])
        diag = jnp.where(future, 0.0, p[:, :blk])
        p = jnp.concatenate([diag, p[:, blk:]], axis=1) if j < n - 1 else diag
        ds = (p * dp).astype(bf16)
        dv = dot(p.astype(bf16), do[a:])
        dk = dot(ds, q[a:])
        dq = dot(k_t[h * hs : (h + 1) * hs, a : a + blk], ds)
        if j == 0:
            dqa[h * hs : (h + 1) * hs, :] = dq
        else:
            dqa[h * hs : (h + 1) * hs, a:] += dq
        if h == 0:
            kept = (dk, dv)
        else:
            d_ref[0, 1, a : a + blk, :] = jnp.where(lane == 0, kept[0], dk).astype(bf16)
            d_ref[0, 2, a : a + blk, :] = jnp.where(lane == 0, kept[1], dv).astype(bf16)
            d_ref[0, 0, a : a + blk, :] = dqa[:, a : a + blk].T.astype(bf16)


def slot_chunk(total):
    return 256 if total % 256 == 0 else total


def place_rows(rows, slot_row, out_ref):
    experts, capacity, _ = out_ref.shape
    base = lax.broadcasted_iota(jnp.int32, (capacity, rows.shape[0]), 0)
    for e in range(experts):
        hot = jnp.where(base + e * capacity == slot_row, 1.0, 0.0).astype(bf16)
        out_ref[e] = dot(hot, rows).astype(bf16)


def take_rows(slots, slot_col):
    total = slots.shape[0]
    at = lax.broadcasted_iota(jnp.int32, (slot_col.shape[0], total), 1)
    return dot(jnp.where(at == slot_col, 1.0, 0.0).astype(bf16), slots)


def gelu_parts(pre):
    sq = pre * pre
    half = 0.5 + 0.5 * jnp.tanh(pre * (GELU_A + (GELU_A * GELU_B) * sq))
    act = pre * half
    slope = half + (act - act * half) * (2 * GELU_A + (6 * GELU_A * GELU_B) * sq)
    return act, slope


def hidden_rows(rows_ref, cot_ref, w_in, w_down, act_ref, gpre_ref, use=None):
    total = rows_ref.shape[0]
    step = slot_chunk(total)
    starts = list(range(0, total, step))

    def first(a):
        pre = dot(rows_ref[a : a + step], w_in)
        if w_down is None:
            return pre, cot_ref[a : a + step].astype(f32)
        return pre, dot(cot_ref[a : a + step], w_down, NT)

    ahead = first(starts[0])
    for at, a in enumerate(starts):
        pre, gact = ahead
        if at + 1 < len(starts):
            ahead = first(starts[at + 1])
        act, slope = gelu_parts(pre)
        act_low = act.astype(bf16)
        gpre_low = (gact * slope).astype(bf16)
        act_ref[0, a : a + step] = act_low
        gpre_ref[0, a : a + step] = gpre_low
        if use is not None:
            use(a, a + step, act_low, gpre_low)


def join_cols(refs):
    return jnp.concatenate([r[...] for r in refs], axis=1)


def join_rows(refs):
    return jnp.concatenate([r[...] for r in refs], axis=0)


def weight_specs(width, hidden, nz, first=0):
    per = hidden // (nz * FFT)
    ins = [
        pl.BlockSpec((width, FFT), lambda c, z=z: (0, z * per + c + first)) for z in range(nz)
    ]
    downs = [
        pl.BlockSpec((FFT, width), lambda c, z=z: (z * per + c + first, 0)) for z in range(nz)
    ]
    return ins + downs


def expert_b_body(*refs, nz, carry, first):
    rows_any, cot_any, act_any, gpre_any, rows_b, cot_b = refs[:6]
    rows_a, cot_a, act_a, gpre_a, load_s = refs[-5:]
    refs = refs[:-5]
    c = pl.program_id(0)
    loads = [
        pltpu.make_async_copy(act_any.at[c + first], act_a, load_s.at[0]),
        pltpu.make_async_copy(gpre_any.at[c + first], gpre_a, load_s.at[1]),
    ]
    once = [
        pltpu.make_async_copy(rows_any.at[0], rows_a, load_s.at[2]),
        pltpu.make_async_copy(cot_any.at[0], cot_a, load_s.at[3]),
    ]
    for v in loads:
        v.start()

    @pl.when(c == 0)
    def _():
        for v in once:
            v.start()

    rows_b = rows_b.at[0]
    w_in = join_cols(refs[6 : 6 + nz])
    w_down = join_rows(refs[6 + nz : 6 + 2 * nz])
    rest = refs[6 + 2 * nz :]
    if carry:
        give_ref, act_b, gpre_b, sum_ref, take_ref, stay_s, a2a_s, a2a_r = rest
        experts = lax.axis_size("expert")
        e = lax.axis_index("expert")
        peers = [(lax.axis_index("dp"), (e + j) % experts) for j in range(1, experts)]
        spread, settle = front_lanes(
            give_ref, None, take_ref, None, stay_s, a2a_s, a2a_r, give_ref.shape[2]
        )

        @pl.when(pl.program_id(0) == 0)
        def _():
            pl.semaphore_wait(greet(peers), len(peers))
            spread(0)

    else:
        act_b, gpre_b, sum_ref = rest
    cot_b = cot_b.at[0]
    hidden_rows(rows_b, cot_b, w_in, w_down, act_b, gpre_b)
    for v in loads:
        v.wait()

    @pl.when(c == 0)
    def _():
        for v in once:
            v.wait()

    for z in range(nz):
        cols = slice(z * FFT, (z + 1) * FFT)
        gdown = dot(act_a[:, cols], cot_a[...], TN) + dot(act_b[0, :, cols], cot_b[...], TN)
        sum_ref[z, 0, :FFT] = gdown.astype(bf16)
        gin = dot(gpre_a[:, cols], rows_a[...], TN) + dot(gpre_b[0, :, cols], rows_b[...], TN)
        sum_ref[z, 0, FFT:] = gin.astype(bf16)
    if carry:

        @pl.when(pl.program_id(0) == pl.num_programs(0) - 1)
        def _():
            settle(0)


def expert_b_call(rows, act_a, gpre_a, cots, w_in, w_down, nz, first, count, give=None, deps=()):
    _, total, width = rows.shape
    tile = nz * FFT
    hidden = w_in.shape[1]

    def cot(s):
        return pl.BlockSpec((1, total, width), lambda c: (s, 0, 0))

    mid_out = pl.BlockSpec((1, total, tile), lambda c: (c, 0, 0))
    carry = give is not None
    args = [rows, cots, act_a, gpre_a, rows, cots, *([w_in] * nz), *([w_down] * nz)]
    in_specs = [ANY] * 4 + [cot(1), cot(1)] + weight_specs(width, hidden, nz, first)
    out_specs = [
        mid_out,
        mid_out,
        pl.BlockSpec((nz, 1, 2 * FFT, width), lambda c: (0, c, 0, 0)),
    ]
    out_shape = [
        sds((count, total, tile), bf16),
        sds((count, total, tile), bf16),
        sds((nz, count, 2 * FFT, width), bf16),
    ]
    dma = pltpu.SemaphoreType.DMA
    scratch = []
    options = dict(vmem_limit_bytes=60 << 20)
    if carry:
        experts = give.shape[1]
        args.append(give)
        in_specs.append(ANY)
        out_specs.append(ANY)
        out_shape.append(sds((1, total, width), bf16))
        scratch = [dma((1,)), dma((1, experts - 1)), dma((1, experts - 1))]
        options.update(collective_id=3, has_side_effects=True)
    scratch += [pltpu.VMEM((total, width), bf16)] * 2
    scratch += [pltpu.VMEM((total, tile), bf16)] * 2 + [dma((4,))]
    return kernel_call(
        functools.partial(expert_b_body, nz=nz, carry=carry, first=first),
        args=args,
        deps=deps,
        grid=(count,),
        in_specs=in_specs,
        out_specs=out_specs,
        out_shape=out_shape,
        scratch_shapes=scratch,
        compiler_params=pltpu.CompilerParams(**options),
        cost_estimate=cost(20 * count << 30, 30 << 20),
    )


def back_body(*refs, heads, capacity, split):
    pieces = len(split)
    acts_a = refs[0]
    acts_b, gpres_b = refs[1 : 1 + pieces], refs[1 + pieces : 1 + 2 * pieces]
    gtok_ref = refs[1 + 2 * pieces]
    (
        w_in,
        w_down,
        qkv_ref,
        mixed_ref,
        after_ref,
        cot_ref,
        fo_ref,
        lse_ref,
        slot_ref,
        g_ref,
        d_ref,
        ga_ref,
        gtoks_ref,
        outs_ref,
        gw_ref,
        sums_ref,
        slab_g,
        slab_o,
        qkv_v,
        mixed_v,
        after_v,
        cot_v,
        fo_v,
        load_s,
        mid_s,
        w_s,
        save_s,
        stay_s,
        a2a_s,
        a2a_r,
    ) = refs[2 + 2 * pieces :]
    nz = lax.axis_size("dp")
    experts = lax.axis_size("expert")
    z = lax.axis_index("dp")
    e = lax.axis_index("expert")
    seqs, total, width = gtoks_ref.shape
    length = after_ref.shape[1]
    hidden = w_in.shape[1]
    tile = nz * FFT
    chunks = hidden // tile
    peers = [(z, (e + j) % experts) for j in range(1, experts)]

    def load(n, src, dst):
        return pltpu.make_async_copy(src, dst, load_s.at[n])

    early = [load(0, fo_ref, fo_v), load(1, qkv_ref.at[0], qkv_v.at[0])]
    for s in range(seqs):
        early += [
            load(2 + 3 * s, after_ref.at[s], after_v.at[s]),
            load(3 + 3 * s, cot_ref.at[s], cot_v.at[s]),
            load(4 + 3 * s, mixed_ref.at[s], mixed_v.at[s]),
        ]
    pl.semaphore_wait(greet(peers), len(peers))
    spread, settle = front_lanes(
        slab_g, slab_o, gtoks_ref, outs_ref, stay_s, a2a_s, a2a_r, capacity
    )

    def second(arrays, c):
        for arr, k in zip(arrays, split):
            if c < k:
                return arr.at[c]
            c -= k

    def products(mid_v, in_v, down_v, acc):
        jobs = []
        for n in range(1, 2 * seqs):
            for c in range(chunks):
                first = n % seqs == 0
                if n < seqs:
                    src = second(gpres_b, c)
                else:
                    src = acts_a.at[c] if first else second(acts_b, c)
                jobs.append((n, c, src))

        def fetch(k):
            n, c, src = jobs[k]
            slot = k % 2
            got = [pltpu.make_async_copy(src, mid_v.at[slot], mid_s.at[slot])]
            for zz in range(nz):
                at = (zz * chunks + c) * FFT
                if n < seqs:
                    pair = (w_in.at[:, at : at + FFT], in_v.at[slot, :, zz * FFT : (zz + 1) * FFT])
                else:
                    pair = (w_down.at[at : at + FFT], down_v.at[slot, zz * FFT : (zz + 1) * FFT])
                got.append(pltpu.make_async_copy(*pair, w_s.at[slot, zz]))
            return got

        step = slot_chunk(total)
        for c in fetch(0):
            c.start()
        for k, (n, c, _) in enumerate(jobs):
            if k + 1 < len(jobs):
                for v in fetch(k + 1):
                    v.start()
            for v in fetch(k):
                v.wait()
            slot = k % 2
            w, dims = (in_v[slot], NT) if n < seqs else (down_v[slot], NN)
            for a in range(0, total, step):
                term = dot(mid_v[slot, a : a + step], w, dims)
                if c == 0:
                    acc[a : a + step] = term
                else:
                    acc[a : a + step] += term
            if c == chunks - 1:
                slab = slab_g if n < seqs else slab_o
                for ee in range(experts):
                    slab[n % seqs, ee] = acc[ee * capacity : (ee + 1) * capacity].astype(bf16)
                spread(n)
            if k == 1:
                for v in early:
                    v.start()

    pl.run_scoped(
        products,
        pltpu.VMEM((2, total, tile), bf16),
        pltpu.VMEM((2, width, tile), bf16),
        pltpu.VMEM((2, tile, width), bf16),
        pltpu.VMEM((total, width), f32),
    )
    hs = width // heads
    pairs = heads // 2
    blk = min(BLK, length)

    def backward(back_v, ga_v, gm_v, d_v, dqa, doa):
        sums_ref[...] = jnp.zeros_like(sums_ref)
        saves = {}
        for s in range(seqs):
            if s:
                settle(s)
            fill = load(2 + 3 * seqs, gtoks_ref.at[s] if s else gtok_ref.at[0], back_v)
            fill.start()
            if s:
                again = load(1, qkv_ref.at[s], qkv_v.at[0])
                again.start()
            else:
                for v in early:
                    v.wait()
            fill.wait()
            starts = list(range(0, length, blk))

            def take(a, s=s):
                return take_rows(back_v[...], slot_ref[s, a : a + blk])

            ahead = take(0)
            for at, a in enumerate(starts):
                gt = ahead
                if at + 1 < len(starts):
                    ahead = take(starts[at + 1])
                rows = slice(a, a + blk)
                hat, r = norm_parts(after_v[s, rows].astype(f32))
                sums_ref[2:3] += jnp.sum(gt * hat, axis=0, keepdims=True)
                sums_ref[3:4] += jnp.sum(gt, axis=0, keepdims=True)
                g = gt * row(g_ref)
                ga = cot_v[s, rows].astype(f32) + r * (
                    g
                    - jnp.mean(g, axis=-1, keepdims=True)
                    - hat * jnp.mean(g * hat, axis=-1, keepdims=True)
                )
                ga_v[s, rows] = ga.astype(bf16)
                gm_v[0, rows] = dot(ga_v[s, rows], fo_v[...], NT).astype(bf16)
            gw = dot(mixed_v[s], ga_v[s], TN)
            if s == 0:
                gw_ref[...] = gw
            else:
                gw_ref[...] += gw
                again.wait()
                saves[s - 1].wait()
            keep = pltpu.make_async_copy(ga_v.at[s], ga_ref.at[s], save_s.at[0, s])
            keep.start()

            def pair(p, carry, s=s):
                def cols(t):
                    return pl.ds(pl.multiple_of(t * width + p * 2 * hs, 128), 2 * hs)

                one = pl.ds(s, 1)
                attn_bwd_body(
                    qkv_v.at[:, :, cols(0)],
                    qkv_v.at[:, :, cols(1)],
                    qkv_v.at[:, :, cols(2)],
                    mixed_v.at[one, :, cols(0)],
                    gm_v.at[:, :, cols(0)],
                    lse_ref.at[one, pl.ds(p, 1)],
                    d_v.at[:, :, :, cols(0)],
                    dqa,
                    doa,
                    blk=blk,
                    hs=hs,
                    scale=hs**-0.5,
                    depth=2,
                )
                return carry

            lax.fori_loop(0, pairs, pair, 0)
            saves[s] = pltpu.make_async_copy(d_v.at[0], d_ref.at[s], save_s.at[1, s])
            saves[s].start()
            keep.wait()
        saves[seqs - 1].wait()

    pl.run_scoped(
        backward,
        pltpu.VMEM((total, width), bf16),
        pltpu.VMEM((seqs, length, width), bf16),
        pltpu.VMEM((1, length, width), bf16),
        pltpu.VMEM((1, 3, length, width), bf16),
        pltpu.VMEM((2 * hs, length), f32),
        pltpu.VMEM((2, length, 2 * hs), bf16),
    )
    for n in range(seqs, 2 * seqs):
        settle(n)


def back_call(
    acts_a, acts_b, gpres_b, gtok, w_in, w_down, qkv, mixed, after, cot, fo, lse, slot_col, gain, heads, nz, experts, capacity
):
    seqs, length, width = after.shape
    total = experts * capacity
    dma = pltpu.SemaphoreType.DMA
    slab = (seqs, experts, capacity, width)
    split = [v.shape[0] for v in acts_b]
    three = pltpu.VMEM((seqs, length, width), bf16)
    return pl.pallas_call(
        functools.partial(back_body, heads=heads, capacity=capacity, split=split),
        in_specs=[ANY] * (2 + 2 * len(split) + 7) + [VM] * 3,
        out_specs=[ANY] * 4 + [VM] * 2,
        out_shape=[
            sds((seqs, 3, length, width), bf16),
            sds((seqs, length, width), bf16),
            sds((seqs, total, width), bf16),
            sds((seqs, total, width), bf16),
            sds((width, width), f32),
            sds((8, width), f32),
        ],
        scratch_shapes=[
            pltpu.VMEM(slab, bf16),
            pltpu.VMEM(slab, bf16),
            pltpu.VMEM((1, length, 3 * width), bf16),
            three,
            three,
            three,
            pltpu.VMEM((width, width), bf16),
            dma((3 + 3 * seqs,)),
            dma((2,)),
            dma((2, nz)),
            dma((2, seqs)),
            dma((2 * seqs,)),
            dma((2 * seqs, experts - 1)),
            dma((2 * seqs, experts - 1)),
        ],
        compiler_params=pltpu.CompilerParams(
            vmem_limit_bytes=62 << 20, collective_id=2, has_side_effects=True
        ),
        cost_estimate=cost(110 << 30, 60 << 20),
    )(
        acts_a, *acts_b, *gpres_b, gtok, w_in, w_down, qkv, mixed, after, cot, fo, lse, slot_col, gain
    )


GROUPS = 4


def last_body(*refs, seqs, per_seq, plan):
    (dw_ref, d_ref, xw_ref, x_ref, w_any, g_ref, b_ref) = refs[:7]
    gwo_ref, sums_ref, backs_any, slot_ref = refs[7:11]
    gx_ref, res_ref, gq_ref, go_ref, tot_ref = refs[11:16]
    rest = refs[16:]
    acc, low, pay, r1, r2, s2, r3, fin, w0, v1, w1, v2, w2, v3, w_ref, backs = rest[:16]
    send_s, recv_s, vs_s, vr_s, load_s = rest[16:]
    nz = lax.axis_size("dp")
    experts = lax.axis_size("expert")
    z = lax.axis_index("dp")
    e = lax.axis_index("expert")
    chips = experts // 2
    core = e % 2
    chip = e // 2
    mate = (z, chip * 2 + 1 - core)
    others = [(z, lax.rem(chip + j, chips) * 2 + core) for j in range(1, chips)]
    layers = [(lax.rem(z + j, nz), e) for j in range(1, nz)]
    peers = [mate] + others + layers
    width = x_ref.shape[2]
    step = pl.program_id(0)
    last = pl.num_programs(0) - 1
    s1 = r1

    def copy(src, dst, at, peer, sems=None):
        a, b = sems or (send_s, recv_s)
        return pltpu.make_async_remote_copy(
            src_ref=src,
            dst_ref=dst,
            send_sem=a.at[at],
            recv_sem=b.at[at],
            device_id=peer,
            device_id_type=MESH,
        )

    def stage(n, t):
        if n == 1:
            return [copy(pay.at[t, 1 - core], r1.at[t], (t, 0), mate)]
        if n == 2:
            return [
                copy(
                    s1.at[t, lax.rem(chip + j, chips)], r2.at[t, j - 1], (t, j), others[j - 1]
                )
                for j in range(1, chips)
            ]
        if n == 3:
            return [
                copy(
                    s2.at[t, lax.rem(z + j, nz)], r3.at[t, j - 1], (t, chips + j), layers[j - 1]
                )
                for j in range(1, nz)
            ]
        if n == 4:
            here = fin.at[t, core, chip]
            return [
                copy(here, here, (t, chips + nz + j), others[j - 1]) for j in range(1, chips)
            ]
        side = fin.at[t, core]
        return [copy(side, side, (t, 2 * chips + nz), mate)]

    def vector(n):
        sems = (vs_s, vr_s)
        if n == 1:
            return [copy(w0, v1, 0, mate, sems)]
        if n == 2:
            return [copy(w1, v2.at[j - 1], j, others[j - 1], sems) for j in range(1, chips)]
        return [copy(w2, v3.at[j - 1], chips + j, layers[j - 1], sems) for j in range(1, nz)]

    def start(n, t):
        for c in vector(n) if t is None else stage(n, t):
            c.start()

    def finish(n, t):
        for c in vector(n) if t is None else stage(n, t):
            c.wait()
        if t is None:
            if n == 1:
                w1[...] = w0[...] + v1[...]
            elif n == 2:
                line = w1[...]
                for j in range(1, chips):
                    line = line + v2[j - 1]
                w2[...] = line
            else:
                line = w2[...]
                for j in range(1, nz):
                    line = line + v3[j - 1]
                tot_ref[...] = line
            if n < 3:
                start(n + 1, None)
            return
        if n == 1:
            for k in range(chips):
                s1[t, k] = (pay[t, core, k].astype(f32) + r1[t, k].astype(f32)).astype(bf16)
        elif n == 2:
            part = s1[t, chip].astype(f32)
            for j in range(1, chips):
                part = part + r2[t, j - 1].astype(f32)
            s2[t] = part.astype(bf16)
        elif n == 3:
            part = s2[t, z].astype(f32)
            for j in range(1, nz):
                part = part + r3[t, j - 1].astype(f32)
            fin[t, core, chip] = part.astype(bf16)
        elif n == 5:
            piece = fin.shape[3]
            for c in range(2):
                for k in range(chips):
                    at = (c * chips + k) * piece
                    value = fin[t, c, k].astype(f32)
                    if t < 3:
                        gq_ref[at : at + piece, t * width : (t + 1) * width] = value
                    else:
                        go_ref[at : at + piece, :] = value
        if n < 5:
            start(n + 1, t)

    def pack(value, t):
        per = value.shape[0] // nz
        piece = pay.shape[4]
        for zz in range(nz):
            for c in range(2):
                for k in range(chips):
                    at = zz * per + (c * chips + k) * piece
                    pay[t, c, k, zz] = value[at : at + piece].astype(bf16)
        start(1, t)

    loads = [pltpu.make_async_copy(w_any, w_ref, load_s.at[0])]
    loads += [
        pltpu.make_async_copy(backs_any.at[s], backs.at[s], load_s.at[1 + s]) for s in range(seqs)
    ]

    @pl.when(step == 0)
    def _():
        for c in loads:
            c.start()
        pl.semaphore_wait(greet(peers), len(peers))
        pack(gwo_ref[...], 3)

    for n in range(3 * seqs):
        t, s = n // seqs, n % seqs

        @pl.when(step == n)
        def _(t=t, s=s):
            if t == 0:
                hat, _ = norm_parts(xw_ref[0].astype(f32))
                low[s] = (hat * g_ref[...] + b_ref[...]).astype(bf16)
            term = dot(low[s], dw_ref[0, 0], TN)
            if s == 0:
                acc[...] = term
            elif s < seqs - 1:
                acc[...] += term
            else:
                pack(acc[...] + term, t)

    base = 3 * seqs

    @pl.when(step == base)
    def _():
        loads[0].wait()
        w0[0:2] = jnp.zeros((2, width), f32)
        w0[2:8] = sums_ref[2:8]

    @pl.when((step >= base) & (step < base + seqs * per_seq))
    def _():
        hat, r = norm_parts(x_ref[0].astype(f32))
        gn = 0.0
        for t in range(3):
            gn = gn + dot(d_ref[0, t], w_ref[:, t * width : (t + 1) * width], NT)
        w0[0:1] += jnp.sum(gn * hat, axis=0, keepdims=True)
        w0[1:2] += jnp.sum(gn, axis=0, keepdims=True)
        g = gn * g_ref[...]
        gx_ref[0] = (
            r
            * (
                g
                - jnp.mean(g, axis=-1, keepdims=True)
                - hat * jnp.mean(g * hat, axis=-1, keepdims=True)
            )
        ).astype(bf16)

    base = base + seqs * per_seq

    @pl.when(step == base)
    def _():
        for c in loads[1:]:
            c.wait()

    @pl.when(step == base - 1)
    def _():
        start(1, None)

    for s in range(seqs):

        @pl.when((step >= base + s * per_seq) & (step < base + (s + 1) * per_seq))
        def _(s=s):
            res_ref[0] = take_rows(backs[s], slot_ref[0]).astype(bf16)

    for when, events in plan:

        @pl.when(step == when)
        def _(events=events):
            for n, t in events:
                finish(n, t)


def last_plan(seqs, per_seq):
    dw = 3 * seqs
    end = dw + 2 * seqs * per_seq - 1
    mid = dw + seqs * per_seq
    first = [
        (2, [(1, 3)]),
        (4, [(1, 0)]),
        (dw, [(1, 1)]),
        (dw + 2, [(1, 2)]),
        (dw + 4, [(2, 3)]),
        (dw + 6, [(2, 0)]),
        (dw + 7, [(3, 3)]),
        (mid, [(2, 1)]),
        (mid + 1, [(3, 0)]),
        (mid + 2, [(1, None), (2, 2), (4, 3)]),
        (mid + 3, [(3, 1)]),
        (mid + 4, [(2, None), (4, 0), (5, 3)]),
        (mid + 5, [(3, 2)]),
        (mid + 6, [(3, None), (4, 1), (5, 0)]),
        (end, [(4, 2), (5, 1), (5, 2)]),
    ]
    return [(min(a, end), b) for a, b in first]


def last_call(d, x, w, gain, bias, gwo, sums, backs, slot_col, experts, nz):
    seqs, length, width = x.shape
    blk = min(BLK, length)
    per_seq = length // blk
    total = backs.shape[1]
    dw = 3 * seqs
    mid = dw + seqs * per_seq
    chips = experts // 2
    piece = width // nz // experts
    per = width // nz
    dma = pltpu.SemaphoreType.DMA
    once = pl.Buffered(1)

    def keep(*shape):
        return pl.BlockSpec(shape, lambda r: (0,) * len(shape), pipeline_mode=once)

    def at(first, r):
        n = jnp.clip(r - first, 0, seqs * per_seq - 1)
        return n // per_seq, n % per_seq

    def dw_at(r):
        n = jnp.minimum(r, dw - 1)
        return n % seqs, n // seqs, 0, 0

    def rows(first):
        return pl.BlockSpec((1, blk, width), lambda r: (*at(first, r), 0))

    def d_at(r):
        s, b = at(dw, r)
        return s, 0, b, 0

    steps = mid + seqs * per_seq
    in_specs = [
        pl.BlockSpec((1, 1, length, width), dw_at),
        pl.BlockSpec((1, 3, blk, width), d_at),
        pl.BlockSpec((1, length, width), lambda r: (jnp.minimum(r, seqs - 1), 0, 0)),
        rows(dw),
        ANY,
        keep(1, width),
        keep(1, width),
    ]
    in_specs += [keep(width, width), keep(8, width), ANY]
    in_specs += [pl.BlockSpec((1, blk, 1), lambda r: (*at(mid, r), 0))]
    return pl.pallas_call(
        functools.partial(last_body, seqs=seqs, per_seq=per_seq, plan=last_plan(seqs, per_seq)),
        grid=(steps,),
        in_specs=in_specs,
        out_specs=[rows(dw), rows(mid), keep(per, 3 * width), keep(per, width), keep(8, width)],
        out_shape=[
            sds((seqs, length, width), bf16),
            sds((seqs, length, width), bf16),
            sds((per, 3 * width), f32),
            sds((per, width), f32),
            sds((8, width), f32),
        ],
        scratch_shapes=[
            pltpu.VMEM((width, width), f32),
            pltpu.VMEM((seqs, length, width), bf16),
            pltpu.VMEM((GROUPS, 2, chips, nz, piece, width), bf16),
            pltpu.VMEM((GROUPS, chips, nz, piece, width), bf16),
            pltpu.VMEM((GROUPS, chips - 1, nz, piece, width), bf16),
            pltpu.VMEM((GROUPS, nz, piece, width), bf16),
            pltpu.VMEM((GROUPS, nz - 1, piece, width), bf16),
            pltpu.VMEM((GROUPS, 2, chips, piece, width), bf16),
            pltpu.VMEM((8, width), f32),
            pltpu.VMEM((8, width), f32),
            pltpu.VMEM((8, width), f32),
            pltpu.VMEM((chips - 1, 8, width), f32),
            pltpu.VMEM((8, width), f32),
            pltpu.VMEM((nz - 1, 8, width), f32),
            pltpu.VMEM((width, 3 * width), bf16),
            pltpu.VMEM((seqs, total, width), bf16),
        ]
        + [dma((GROUPS, 2 * chips + nz + 1))] * 2
        + [dma((chips + nz,))] * 2
        + [dma((1 + seqs,))],
        compiler_params=pltpu.CompilerParams(
            vmem_limit_bytes=62 << 20, collective_id=1, has_side_effects=True
        ),
        cost_estimate=cost(50 << 30, 150 << 20),
    )(
        d,
        d,
        x,
        x,
        w,
        gain.reshape(1, -1),
        bias.reshape(1, -1),
        gwo,
        sums,
        backs,
        slot_col,
    )


def close_body(*refs, counts):
    ga_ref, dx_ref, after_ref, back_ref, gq_ref, go_ref = refs[:6]
    n = len(counts)
    downs, ins = refs[6 : 6 + n], refs[6 + n : 6 + 2 * n]
    gx_out, res_out, gq_out, go_out, down_out, in_out = refs[6 + 2 * n :]
    step = pl.program_id(0)
    gx_out[...] = ga_ref[...].astype(f32) + dx_ref[...].astype(f32)
    res_out[...] = after_ref[...].astype(f32) + back_ref[...].astype(f32)
    gq_out[...] = gq_ref[...]
    go_out[...] = go_ref[...]
    at = 0
    for k, down, gin in zip(counts, downs, ins):
        down_out[at : at + k] = down[0].astype(f32)

        @pl.when((step >= at) & (step < at + k))
        def _(gin=gin):
            in_out[...] = gin[0, 0].astype(f32).T

        at += k


def close_call(ga, dx, after, back, gq, go, sums):
    seqs, length, width = ga.shape
    blk = min(BLK, length)
    per_seq = length // blk
    steps = seqs * per_seq
    counts = [v.shape[1] for v in sums]
    chunks = sum(counts)
    rows = pl.BlockSpec((1, blk, width), lambda r: (r // per_seq, r % per_seq, 0))

    def split(v):
        return pl.BlockSpec((v.shape[0] // steps, v.shape[1]), lambda r: (r, 0))

    def down(v):
        return pl.BlockSpec((1, v.shape[1], FFT // steps, width), lambda r: (0, 0, r, 0))

    def inward(n):
        lo = sum(counts[:n])
        return pl.BlockSpec(
            (1, 1, FFT, width), lambda r: (0, jnp.clip(r - lo, 0, counts[n] - 1), 1, 0)
        )

    return pl.pallas_call(
        functools.partial(close_body, counts=counts),
        grid=(steps,),
        in_specs=[rows] * 4
        + [split(gq), split(go)]
        + [down(v) for v in sums]
        + [inward(n) for n in range(len(sums))],
        out_specs=[
            rows,
            rows,
            split(gq),
            split(go),
            pl.BlockSpec((chunks, FFT // steps, width), lambda r: (0, r, 0)),
            pl.BlockSpec((width, FFT), lambda r: (0, jnp.minimum(r, chunks - 1))),
        ],
        out_shape=[
            sds((seqs, length, width), f32),
            sds((seqs, length, width), f32),
            sds(gq.shape, f32),
            sds(go.shape, f32),
            sds((chunks, FFT, width), f32),
            sds((width, chunks * FFT), f32),
        ],
        compiler_params=params(60),
        cost_estimate=cost(8 << 30, 40 << 20),
    )(ga, dx, after, back, gq, go, *sums, *sums)


def exchange(parts):
    got = lax.all_to_all(parts, "expert", split_axis=0, concat_axis=0, tiled=True)
    return got.reshape(-1, parts.shape[-1])


def on_device(
    tokens_in,
    buckets,
    ln1_gain,
    ln1_bias,
    w_qkv,
    w_out,
    ln2_gain,
    ln2_bias,
    w_in,
    w_down,
    cotangent,
):
    experts = lax.axis_size("expert")
    nz = lax.axis_size("dp")
    seqs, length, width = tokens_in.shape
    capacity = 5 * length // (4 * experts)
    total = experts * capacity
    w_in_local = w_in[0]
    w_down_local = w_down[0]
    hidden = w_in_local.shape[1]
    chunks = hidden // (nz * FFT)

    qkv, full_qkv, full_out, mixed, after, lse, slot_col, cots, rows, act_a, gpre_a, give = front_call(
        tokens_in,
        ln1_gain,
        ln1_bias,
        ln2_gain,
        ln2_bias,
        w_qkv,
        w_out,
        buckets,
        cotangent,
        w_in_local,
        w_down_local,
        HEADS,
        nz,
        experts,
        capacity,
    )
    last = ()
    acts, gpres, totals = [], [], []
    for first, many in ((0, 1), (1, chunks - 1)):
        made = expert_b_call(
            rows,
            act_a,
            gpre_a,
            cots,
            w_in_local,
            w_down_local,
            nz,
            first,
            many,
            give=give if first else None,
            deps=last,
        )
        last = (made[0],)
        acts.append(made[0])
        gpres.append(made[1])
        totals.append(lax.psum_scatter(made[2], "dp", scatter_dimension=0, tiled=True))
    gtok_a = made[3]
    d, ga, _, outs, gwo, sums = back_call(
        act_a,
        acts,
        gpres,
        gtok_a,
        w_in_local,
        w_down_local,
        qkv,
        mixed,
        after,
        cotangent,
        full_out,
        lse,
        slot_col,
        ln2_gain,
        HEADS,
        nz,
        experts,
        capacity,
    )
    dx, back, gq, go, sums = last_call(
        d,
        tokens_in,
        full_qkv,
        ln1_gain,
        ln1_bias,
        gwo,
        sums,
        outs,
        slot_col,
        experts,
        nz,
    )
    gxs, results, gq, go, gdown, gin = close_call(ga, dx, after, back, gq, go, totals)
    mine = lax.dynamic_slice_in_dim(
        sums, lax.axis_index("dp") * (width // nz), width // nz, axis=1
    )
    return (
        results,
        gxs,
        mine[0],
        mine[1],
        gq,
        go,
        mine[2],
        mine[3],
        gin[None],
        gdown.reshape(1, hidden // nz, width),
    )


def solution(mesh):
    placed = (
        P(("dp", "expert"), None, None),
        P(("dp", "expert"), None),
        P(),
        P(),
        P("dp", None),
        P("dp", None),
        P(),
        P(),
        P("expert", None, None),
        P("expert", None, None),
        P(("dp", "expert"), None, None),
    )
    return jax.shard_map(
        on_device,
        mesh=mesh,
        in_specs=placed,
        out_specs=(
            P(("dp", "expert"), None, None),
            P(("dp", "expert"), None, None),
            P("dp"),
            P("dp"),
            P("dp", None),
            P("dp", None),
            P("dp"),
            P("dp"),
            P("expert", None, "dp"),
            P("expert", "dp", None),
        ),
        check_vma=False,
    )
```

```python
import functools

import jax
import jax.numpy as jnp
from jax import lax
from jax.experimental import pallas as pl
from jax.experimental.pallas import tpu as pltpu
from jax.sharding import PartitionSpec as P

HEADS = 12
EPS = 1e-5
NEG = -1e30
bf16 = jnp.bfloat16
f32 = jnp.float32
NN = (((1,), (0,)), ((), ()))
NT = (((1,), (1,)), ((), ()))
TN = (((0,), (0,)), ((), ()))
GELU_A = 0.7978845608028654
GELU_B = 0.044715
BLK = 256
FFT = 256


def dot(a, b, dims=NN):
    return lax.dot_general(a, b, dims, preferred_element_type=f32)


def params(mib=56):
    return pltpu.CompilerParams(vmem_limit_bytes=mib << 20)


def cost(flops, nbytes, trans=0):
    return pl.CostEstimate(flops=int(flops), bytes_accessed=int(nbytes), transcendentals=int(trans))


def sds(shape, dtype):
    return jax.ShapeDtypeStruct(shape, dtype)


VM = pl.BlockSpec(memory_space=pltpu.VMEM)
ANY = pl.BlockSpec(memory_space=pl.ANY)


def kernel_call(body, in_specs, args, deps=(), into=None, **options):
    into = into or {}
    count = len(args)
    extra = len(into) + len(deps)

    def wrapped(*refs):
        body(*refs[:count], *refs[count + extra :])

    return pl.pallas_call(
        wrapped,
        in_specs=list(in_specs) + [ANY] * extra,
        input_output_aliases={count + n: out for n, out in enumerate(into)},
        **options,
    )(*args, *into.values(), *deps)


def norm_parts(v):
    centre = jnp.mean(v, axis=-1, keepdims=True)
    shifted = v - centre
    spread = jnp.mean(shifted * shifted, axis=-1, keepdims=True)
    r = lax.rsqrt(spread + EPS)
    return shifted * r, r


MESH = pl.DeviceIdType.MESH


def greet(peers):
    barrier = pltpu.get_barrier_semaphore()
    for peer in peers:
        pl.semaphore_signal(barrier, inc=1, device_id=peer, device_id_type=MESH)
    return barrier


def find_slots(bucket, experts, capacity):
    length = bucket.shape[1]
    hot = (lax.broadcasted_iota(jnp.int32, (experts, length), 0) == bucket).astype(f32)
    upto = lax.broadcasted_iota(jnp.int32, (length, length), 0) <= lax.broadcasted_iota(
        jnp.int32, (length, length), 1
    )
    count = dot(hot.astype(bf16), upto.astype(bf16))
    rank = jnp.sum(hot * count, axis=0, keepdims=True) - 1.0
    return bucket * capacity + rank.astype(jnp.int32)


GATHERS = 3


def front_body(*refs, heads, capacity):
    nz = lax.axis_size("dp")
    n = 9 + 2 * nz
    (x_ref, g1_ref, b1_ref, g2_ref, b2_ref, wq_ref, wo_ref, buckets_ref, cot_ref) = refs[:9]
    w_ins, w_downs = refs[9 : 9 + nz], refs[9 + nz : n]
    (
        qkv_ref,
        fq_ref,
        fo_ref,
        mixed_ref,
        after_ref,
        lse_ref,
        col_ref,
        cots_ref,
        rows_ref,
        act_ref,
        gpre_ref,
        give_ref,
    ) = refs[n : n + 12]
    (
        fq_v,
        fo_v,
        sent,
        toks,
        slots,
        rows_v,
        cot_a,
        up_s,
        dn_s,
        core_s,
        z_r,
        core_r,
        own_s,
        load_s,
        save_s,
        stay_s,
        a2a_s,
        a2a_r,
    ) = refs[n + 12 :]
    seqs, length, width = x_ref.shape

    def work(x_v, cot_v, low, qkv_v, mixed_v, after_v):
        return front_work(
            x_ref, g1_ref, b1_ref, g2_ref, b2_ref, wq_ref, wo_ref, buckets_ref, cot_ref,
            qkv_ref, fq_ref, fo_ref, mixed_ref, after_ref, lse_ref, col_ref, cots_ref, rows_ref,
            x_v, cot_v, fq_v, fo_v, low, qkv_v, sent, toks, mixed_v, after_v, slots,
            up_s, dn_s, core_s, z_r, core_r, own_s, load_s, save_s, stay_s, a2a_s, a2a_r,
            heads=heads, capacity=capacity,
        )

    one = pltpu.VMEM((seqs, length, width), bf16)
    pl.run_scoped(work, one, one, one, pltpu.VMEM((seqs, length, 3 * width), bf16), one, one)
    settle = front_lanes(sent, toks, cots_ref, rows_ref, stay_s, a2a_s, a2a_r, capacity)[1]
    hidden = w_ins[0].shape[1]
    total = rows_v.shape[0]
    chunks = hidden // (nz * FFT)
    specs = weight_specs(width, hidden, nz)
    mid = pl.BlockSpec((1, total, nz * FFT), lambda c: (c, 0, 0))

    def fill(src, dst, n):
        load = pltpu.make_async_copy(src, dst, load_s.at[n, 0])
        load.start()
        load.wait()

    def expert(acc, gact):
        settle(0)
        fill(cots_ref.at[0], cot_a, 1)
        size = slot_chunk(total)

        def early(*blocks):
            c = pl.program_id(0)
            w_down = join_rows(blocks)
            for a in range(0, total, size):
                gact[c, a : a + size] = dot(cot_a[a : a + size], w_down, NT).astype(bf16)

        pltpu.emit_pipeline(early, grid=(chunks,), in_specs=specs[nz:])(*w_downs)
        acc[...] = jnp.zeros_like(acc)
        for k in range(1, seqs + 1):
            settle(k)
        fill(rows_ref.at[0], rows_v, 0)

        def step(*blocks):
            w_in = join_cols(blocks[:nz])

            def use(a, b, act_low, gpre_low):
                acc[a:b] += dot(gpre_low, w_in, NT)

            hidden_rows(rows_v, gact.at[pl.program_id(0)], w_in, None, *blocks[nz:], use)

        pltpu.emit_pipeline(
            step, grid=(chunks,), in_specs=specs[:nz], out_specs=[mid, mid]
        )(*w_ins, act_ref, gpre_ref)
        for k in range(sent.shape[1]):
            sent[0, k] = acc[k * capacity : (k + 1) * capacity].astype(bf16)
        out = pltpu.make_async_copy(sent.at[0], give_ref.at[0], load_s.at[0, 0])
        out.start()
        for k in range(seqs + 1, 2 * seqs):
            settle(k)
        out.wait()

    pl.run_scoped(
        expert, pltpu.VMEM((total, width), f32), pltpu.VMEM((chunks, total, nz * FFT), bf16)
    )


def front_lanes(sent, toks, cots_ref, rows_ref, stay_s, a2a_s, a2a_r, capacity):
    experts = lax.axis_size("expert")
    z = lax.axis_index("dp")
    e = lax.axis_index("expert")
    seqs = cots_ref.shape[0]
    plane = [(e + j) % experts for j in range(1, experts)]
    back = [(e + experts - j) % experts for j in range(1, experts)]

    def lane(n, at):
        src, dst = (sent, cots_ref) if n < seqs else (toks, rows_ref)
        k = n % seqs
        return src.at[k], dst.at[k, pl.ds(pl.multiple_of(at * capacity, 8), capacity)]

    def trade(n, j, at):
        src, dst = lane(n, at)
        return pltpu.make_async_remote_copy(
            src_ref=src.at[plane[j]],
            dst_ref=dst,
            send_sem=a2a_s.at[n, j],
            recv_sem=a2a_r.at[n, j],
            device_id=(z, plane[j]),
            device_id_type=MESH,
        )

    def stay(n):
        src, dst = lane(n, e)
        return pltpu.make_async_copy(src.at[e], dst, stay_s.at[n])

    def spread(n):
        for j in range(experts - 1):
            trade(n, j, e).start()
        stay(n).start()

    def settle(n):
        stay(n).wait()
        for j in range(experts - 1):
            trade(n, j, e).wait_send()
            trade(n, j, back[j]).wait_recv()

    return spread, settle


def front_work(
    x_ref,
    g1_ref,
    b1_ref,
    g2_ref,
    b2_ref,
    wq_ref,
    wo_ref,
    buckets_ref,
    cot_ref,
    qkv_ref,
    fq_ref,
    fo_ref,
    mixed_ref,
    after_ref,
    lse_ref,
    col_ref,
    cots_ref,
    rows_ref,
    x_v,
    cot_v,
    fq_v,
    fo_v,
    low,
    qkv_v,
    sent,
    toks,
    mixed_v,
    after_v,
    slots,
    up_s,
    dn_s,
    core_s,
    z_r,
    core_r,
    own_s,
    load_s,
    save_s,
    stay_s,
    a2a_s,
    a2a_r,
    *,
    heads,
    capacity,
):
    nz = lax.axis_size("dp")
    experts = lax.axis_size("expert")
    z = lax.axis_index("dp")
    e = lax.axis_index("expert")
    core = e % 2
    seqs, length, width = x_ref.shape
    spread = front_lanes(sent, toks, cots_ref, rows_ref, stay_s, a2a_s, a2a_r, capacity)[0]
    per = width // nz
    half = per // 2
    above = (jnp.minimum(z + 1, nz - 1), e)
    below = (jnp.maximum(z - 1, 0), e)
    mate = (z, e + 1 - 2 * core)
    full = (fq_v, fo_v)
    shard = (wq_ref, wo_ref)
    blk = min(BLK, length)

    cot_in = [pltpu.make_async_copy(cot_ref.at[s], cot_v.at[s], load_s.at[0, s]) for s in range(seqs)]
    x_in = [pltpu.make_async_copy(x_ref.at[s], x_v.at[s], load_s.at[1, s]) for s in range(seqs)]
    for c in cot_in[:1] + x_in + cot_in[1:]:
        c.start()

    barrier = pltpu.get_barrier_semaphore()

    @pl.when(z + 1 < nz)
    def _():
        pl.semaphore_signal(barrier, inc=1, device_id=above, device_id_type=MESH)

    @pl.when(z > 0)
    def _():
        pl.semaphore_signal(barrier, inc=1, device_id=below, device_id_type=MESH)

    plane = [(z, (e + j) % experts) for j in range(1, experts)]
    for peer in plane:
        pl.semaphore_signal(barrier, inc=1, device_id=peer, device_id_type=MESH)

    @pl.when((z + 1 < nz) & (z > 0))
    def _():
        pl.semaphore_wait(barrier, experts + 1)

    @pl.when((z + 1 >= nz) | (z <= 0))
    def _():
        pl.semaphore_wait(barrier, experts)

    hs = width // heads
    pairs = heads // 2
    groups = min(GATHERS, pairs)
    wide = width // groups
    lanes = [[(3 * g + m, 0, m * width + g * wide, wide) for m in range(3)] for g in range(groups)]
    lanes.append([(3 * groups, 1, 0, width)])

    def half_rows(ref, at, piece):
        return ref.at[pl.ds(pl.multiple_of(at, 16), half), pl.ds(piece[2], piece[3])]

    def held(piece, p, c):
        return half_rows(full[piece[1]], p * per + c * half, piece)

    def mine(piece):
        return half_rows(shard[piece[1]], core * half, piece)

    def hop(piece, p, c, src, sem, r_sem, peer):
        return pltpu.make_async_remote_copy(
            src_ref=src,
            dst_ref=held(piece, p, c),
            send_sem=sem.at[piece[0], p],
            recv_sem=r_sem.at[piece[0], p],
            device_id=peer,
            device_id_type=MESH,
        )

    def pass_on(piece, p, sem, r_sem, peer):
        return hop(piece, p, core, held(piece, p, core), sem, r_sem, peer)

    def own(piece):
        cols = pl.ds(piece[2], piece[3])
        return pltpu.make_async_copy(
            shard[piece[1]].at[:, cols],
            full[piece[1]].at[pl.ds(pl.multiple_of(z * per, 16), per), cols],
            own_s.at[piece[0]],
        )

    def begin(i):
        for piece in lanes[i]:

            @pl.when(z + 1 < nz)
            def _(piece=piece):
                hop(piece, z, core, mine(piece), up_s, z_r, above).start()

            @pl.when(z > 0)
            def _(piece=piece):
                hop(piece, z, core, mine(piece), dn_s, z_r, below).start()

            own(piece).start()

    def sides(d):
        return ((z - d >= 0, z - d, z + 1 < nz, up_s, above), (z + d < nz, z + d, z > 0, dn_s, below))

    def arrivals(i, d):
        for ok, p, more, sem, peer in sides(d):

            @pl.when(ok)
            def _(p=p, more=more, sem=sem, peer=peer):
                for piece in lanes[i]:
                    pass_on(piece, p, sem, z_r, peer).wait_recv()

                    @pl.when(more)
                    def _(piece=piece):
                        pass_on(piece, p, sem, z_r, peer).start()

                    pass_on(piece, p, core_s, core_r, mate).start()

    def wave(w):
        for i in range(len(lanes)):
            if 0 < w - i < nz:
                arrivals(i, w - i)
            if w == i:
                begin(i)

    def complete(i):
        for piece in lanes[i]:
            own(piece).wait()
            for d in range(1, nz):
                for ok, p, _, _, _ in sides(d):

                    @pl.when(ok)
                    def _(piece=piece, p=p):
                        hop(
                            piece, p, 1 - core, held(piece, p, 1 - core), core_s, core_r, mate
                        ).wait_recv()

    def sent_all(i):
        for piece in lanes[i]:

            @pl.when(z + 1 < nz)
            def _(piece=piece):
                hop(piece, z, core, mine(piece), up_s, z_r, above).wait_send()

            @pl.when(z > 0)
            def _(piece=piece):
                hop(piece, z, core, mine(piece), dn_s, z_r, below).wait_send()

            for d in range(1, nz):
                for ok, p, more, sem, peer in sides(d):

                    @pl.when(ok)
                    def _(piece=piece, p=p):
                        pass_on(piece, p, core_s, core_r, mate).wait_send()

                    @pl.when(ok & more)
                    def _(piece=piece, p=p, sem=sem, peer=peer):
                        pass_on(piece, p, sem, z_r, peer).wait_send()

    def prepare(s):
        slot = find_slots(buckets_ref[s : s + 1, :], experts, capacity)
        slots[s] = slot
        col_ref[s] = jnp.broadcast_to(slot.astype(f32), (8, length)).T[:, :1].astype(jnp.int32)
        cot_in[s].wait()
        place_rows(cot_v[s], slot, sent.at[s])
        spread(s)

    def first_norm(s):
        x_in[s].wait()
        for a in range(0, length, blk):
            hat, _ = norm_parts(x_v[s, a : a + blk].astype(f32))
            low[s, a : a + blk] = (hat * row(g1_ref) + row(b1_ref)).astype(bf16)

    def save(n, src, dst):
        return pltpu.make_async_copy(src, dst, save_s.at[n])

    saves = [save(0, fq_v, fq_ref), save(1, fo_v, fo_ref)]
    for s in range(seqs):
        saves += [
            save(2 + 3 * s, qkv_v.at[s], qkv_ref.at[s]),
            save(3 + 3 * s, mixed_v.at[s], mixed_ref.at[s]),
            save(4 + 3 * s, after_v.at[s], after_ref.at[s]),
        ]

    def project(s, g):
        for _, _, at, size in lanes[g]:
            w = fq_v[:, at : at + size]
            rows = min(512, length)
            for a in range(0, length, rows):
                qkv_v[s, a : a + rows, at : at + size] = dot(low[s, a : a + rows], w).astype(bf16)

    each = pairs // groups

    def attend(g, first, many):
        def pair(n, carry):
            s = first + n // each
            p = g * each + n % each

            def cols(t):
                return pl.ds(pl.multiple_of(t * width + p * 2 * hs, 128), 2 * hs)

            one = pl.ds(s, 1)
            attn_fwd_body(
                qkv_v.at[one, :, cols(0)],
                qkv_v.at[one, :, cols(1)],
                qkv_v.at[one, :, cols(2)],
                mixed_v.at[one, :, cols(0)],
                lse_ref.at[one, pl.ds(p, 1)],
                blk=blk,
                hs=hs,
                scale=hs**-0.5,
                depth=3,
            )
            return carry

        lax.fori_loop(0, many * each, pair, 0)

    def finish(s, out):
        for a in range(0, length, blk):
            rows = slice(a, a + blk)
            after = x_v[s, rows].astype(f32) + dot(mixed_v[s, rows], fo_v[...])
            after_v[s, rows] = after.astype(bf16)
            hat, _ = norm_parts(after)
            low[s, rows] = (hat * row(g2_ref) + row(b2_ref)).astype(bf16)
        saves[4 + 3 * s].start()
        place_rows(low[s], slots[s], out)

    todo = list(range(1, groups + nz))

    def waves(upto):
        while todo and todo[0] <= upto:
            wave(todo.pop(0))

    wave(0)
    prepare(0)
    waves(1)
    for s in range(seqs):
        first_norm(s)
    waves(2)
    for s in range(1, seqs):
        prepare(s)
    for g in range(groups):
        waves(g + nz - 1)
        complete(g)
        for s in range(seqs):
            project(s, g)
        if g < groups - 1:
            attend(g, 0, seqs)
    saves[0].start()
    for s in range(seqs):
        saves[2 + 3 * s].start()
    attend(groups - 1, 0, 1)
    waves(groups + nz - 1)
    complete(groups)
    saves[1].start()
    saves[3].start()
    finish(0, toks.at[0])
    spread(seqs)
    for s in range(1, seqs):
        attend(groups - 1, s, 1)
        saves[3 + 3 * s].start()
        finish(s, toks.at[s])
        spread(seqs + s)
    for i in range(groups + 1):
        sent_all(i)
    for c in saves:
        c.wait()


def row(ref):
    return ref[...].reshape(1, -1)


def front_call(x, g1, b1, g2, b2, wq, wo, buckets, cot, w_in, w_down, heads, nz, experts, capacity):
    seqs, length, width = x.shape
    triple = wq.shape[1]
    dma = pltpu.SemaphoreType.DMA
    slab = (seqs, experts, capacity, width)
    total = experts * capacity
    pairs = heads // 2
    tile = nz * FFT
    chunks = w_in.shape[1] // tile
    return pl.pallas_call(
        functools.partial(front_body, heads=heads, capacity=capacity),
        in_specs=[ANY] + [VM] * 4 + [ANY] * 2 + [VM, ANY] + [ANY] * (2 * nz),
        out_specs=[ANY] * 5 + [VM] * 2 + [ANY] * 5,
        out_shape=[
            sds((seqs, length, triple), bf16),
            sds((width, triple), bf16),
            sds((width, width), bf16),
            sds((seqs, length, width), bf16),
            sds((seqs, length, width), bf16),
            sds((seqs, pairs, 2, length), f32),
            sds((seqs, length, 1), jnp.int32),
            sds((seqs, total, width), bf16),
            sds((seqs, total, width), bf16),
            sds((chunks, total, tile), bf16),
            sds((chunks, total, tile), bf16),
            sds((1, experts, capacity, width), bf16),
        ],
        scratch_shapes=[
            pltpu.VMEM((width, triple), bf16),
            pltpu.VMEM((width, width), bf16),
            pltpu.VMEM(slab, bf16),
            pltpu.VMEM(slab, bf16),
            pltpu.VMEM((seqs, 1, length), jnp.int32),
            pltpu.VMEM((total, width), bf16),
            pltpu.VMEM((total, width), bf16),
        ]
        + [dma((3 * GATHERS + 1, nz))] * 5
        + [dma((3 * GATHERS + 1,)), dma((2, seqs)), dma((2 + 3 * seqs,)), dma((2 * seqs,))]
        + [dma((2 * seqs, experts - 1))] * 2,
        compiler_params=pltpu.CompilerParams(
            vmem_limit_bytes=62 << 20, collective_id=0, has_side_effects=True
        ),
        cost_estimate=cost(110 << 30, 40 << 20),
    )(x, g1, b1, g2, b2, wq, wo, buckets, cot, *([w_in] * nz), *([w_down] * nz))


def attn_fwd_body(q_ref, k_ref, v_ref, o_ref, lse_ref, *, blk, hs, scale, depth):
    length = q_ref.shape[1]
    lane = lax.broadcasted_iota(jnp.int32, (1, 2 * hs), 1) // hs
    v_t = v_ref[0].T
    keys = k_ref[0]
    kh = [jnp.where(lane == h, keys, jnp.zeros_like(keys)) for h in range(2)]
    ones = jnp.ones((16, length), bf16)
    vh = [jnp.concatenate([v_t[h * hs : (h + 1) * hs], ones], axis=0) for h in range(2)]
    future = lax.broadcasted_iota(jnp.int32, (blk, blk), 0) > lax.broadcasted_iota(
        jnp.int32, (blk, blk), 1
    )
    tasks = [(i, h) for i in range(length // blk) for h in range(2)]

    def score(task):
        i, h = task
        top = (i + 1) * blk
        q = q_ref[0, i * blk : top, :] * jnp.asarray(scale, bf16)
        s = dot(kh[h][:top], q, NT)
        diag = jnp.where(future, NEG, s[i * blk :])
        s = jnp.concatenate([s[: i * blk], diag], axis=0) if i else diag
        return s, jnp.max(s, axis=0, keepdims=True)

    queue = [score(t) for t in tasks[:depth]]
    done = {}
    for at, task in enumerate(tasks):
        if at + depth < len(tasks):
            queue.append(score(tasks[at + depth]))
        s, largest = queue.pop(0)
        i, h = task
        top = (i + 1) * blk
        o = dot(vh[h][:, :top], jnp.exp(s - largest).astype(bf16))
        total = o[hs : hs + 1]
        done[task] = o[:hs] * (1.0 / total)
        lse_ref[0, 0, h : h + 1, i * blk : top] = largest + jnp.log(total)
        if h == 1:
            both = jnp.concatenate([done[(i, 0)], done[(i, 1)]], axis=0)
            o_ref[0, i * blk : top, :] = both.T.astype(bf16)


def attn_bwd_body(
    q_ref, k_ref, v_ref, o_ref, do_ref, lse_ref, d_ref, dqa, doa, *, blk, hs, scale, depth
):
    length = q_ref.shape[1]
    n = length // blk
    lanes = lax.broadcasted_iota(jnp.int32, (1, 2 * hs), 1)
    lane = lanes // hs
    spot = lanes % hs
    keys = k_ref[0]
    vals = v_ref[0]
    k_t = (keys * jnp.asarray(scale, bf16)).T
    kh = [jnp.where(lane == h, keys, jnp.zeros_like(keys)) for h in range(2)]
    vh = [
        jnp.where(lane == h, vals, jnp.where(spot < 2, jnp.ones_like(vals), jnp.zeros_like(vals)))
        for h in range(2)
    ]
    future = lax.broadcasted_iota(jnp.int32, (blk, blk), 0) > lax.broadcasted_iota(
        jnp.int32, (blk, blk), 1
    )
    q = q_ref[0] * jnp.asarray(scale, bf16)
    do = do_ref[0]
    prod = do.astype(f32) * o_ref[0].astype(f32)
    for h in range(2):
        inside = lane == h
        inner = -jnp.sum(jnp.where(inside, prod, 0.0), axis=1, keepdims=True)
        high = inner.astype(bf16)
        rest = (inner - high.astype(f32)).astype(bf16)
        doa[h] = jnp.where(
            inside,
            do,
            jnp.where(spot == 0, high, jnp.where(spot == 1, rest, jnp.zeros_like(high))),
        )
    tasks = [(j, h) for j in range(n) for h in range(2)]

    def score(task):
        j, h = task
        a = j * blk
        return (
            dot(kh[h][a : a + blk], q[a:], NT),
            dot(vh[h][a : a + blk], doa[h, a:], NT),
        )

    queue = [score(t) for t in tasks[:depth]]
    kept = None
    for at, task in enumerate(tasks):
        if at + depth < len(tasks):
            queue.append(score(tasks[at + depth]))
        s, dp = queue.pop(0)
        j, h = task
        a = j * blk
        p = jnp.exp(s - lse_ref[0, 0, h : h + 1, a:])
        diag = jnp.where(future, 0.0, p[:, :blk])
        p = jnp.concatenate([diag, p[:, blk:]], axis=1) if j < n - 1 else diag
        ds = (p * dp).astype(bf16)
        dv = dot(p.astype(bf16), do[a:])
        dk = dot(ds, q[a:])
        dq = dot(k_t[h * hs : (h + 1) * hs, a : a + blk], ds)
        if j == 0:
            dqa[h * hs : (h + 1) * hs, :] = dq
        else:
            dqa[h * hs : (h + 1) * hs, a:] += dq
        if h == 0:
            kept = (dk, dv)
        else:
            d_ref[0, 1, a : a + blk, :] = jnp.where(lane == 0, kept[0], dk).astype(bf16)
            d_ref[0, 2, a : a + blk, :] = jnp.where(lane == 0, kept[1], dv).astype(bf16)
            d_ref[0, 0, a : a + blk, :] = dqa[:, a : a + blk].T.astype(bf16)


def slot_chunk(total):
    return 256 if total % 256 == 0 else total


def place_rows(rows, slot_row, out_ref):
    experts, capacity, _ = out_ref.shape
    base = lax.broadcasted_iota(jnp.int32, (capacity, rows.shape[0]), 0)
    for e in range(experts):
        hot = jnp.where(base + e * capacity == slot_row, 1.0, 0.0).astype(bf16)
        out_ref[e] = dot(hot, rows).astype(bf16)


def take_rows(slots, slot_col):
    total = slots.shape[0]
    at = lax.broadcasted_iota(jnp.int32, (slot_col.shape[0], total), 1)
    return dot(jnp.where(at == slot_col, 1.0, 0.0).astype(bf16), slots)


def gelu_parts(pre):
    sq = pre * pre
    half = 0.5 + 0.5 * jnp.tanh(pre * (GELU_A + (GELU_A * GELU_B) * sq))
    act = pre * half
    slope = half + (act - act * half) * (2 * GELU_A + (6 * GELU_A * GELU_B) * sq)
    return act, slope


def hidden_rows(rows_ref, cot_ref, w_in, w_down, act_ref, gpre_ref, use=None):
    total = rows_ref.shape[0]
    step = slot_chunk(total)
    starts = list(range(0, total, step))

    def first(a):
        pre = dot(rows_ref[a : a + step], w_in)
        if w_down is None:
            return pre, cot_ref[a : a + step].astype(f32)
        return pre, dot(cot_ref[a : a + step], w_down, NT)

    ahead = first(starts[0])
    for at, a in enumerate(starts):
        pre, gact = ahead
        if at + 1 < len(starts):
            ahead = first(starts[at + 1])
        act, slope = gelu_parts(pre)
        act_low = act.astype(bf16)
        gpre_low = (gact * slope).astype(bf16)
        act_ref[0, a : a + step] = act_low
        gpre_ref[0, a : a + step] = gpre_low
        if use is not None:
            use(a, a + step, act_low, gpre_low)


def join_cols(refs):
    return jnp.concatenate([r[...] for r in refs], axis=1)


def join_rows(refs):
    return jnp.concatenate([r[...] for r in refs], axis=0)


def weight_specs(width, hidden, nz, first=0):
    per = hidden // (nz * FFT)
    ins = [
        pl.BlockSpec((width, FFT), lambda c, z=z: (0, z * per + c + first)) for z in range(nz)
    ]
    downs = [
        pl.BlockSpec((FFT, width), lambda c, z=z: (z * per + c + first, 0)) for z in range(nz)
    ]
    return ins + downs


def expert_b_body(*refs, nz, carry, first):
    rows_any, cot_any, act_any, gpre_any, rows_b, cot_b = refs[:6]
    rows_a, cot_a, act_a, gpre_a, load_s = refs[-5:]
    refs = refs[:-5]
    c = pl.program_id(0)
    loads = [
        pltpu.make_async_copy(act_any.at[c + first], act_a, load_s.at[0]),
        pltpu.make_async_copy(gpre_any.at[c + first], gpre_a, load_s.at[1]),
    ]
    once = [
        pltpu.make_async_copy(rows_any.at[0], rows_a, load_s.at[2]),
        pltpu.make_async_copy(cot_any.at[0], cot_a, load_s.at[3]),
    ]
    for v in loads:
        v.start()

    @pl.when(c == 0)
    def _():
        for v in once:
            v.start()

    rows_b = rows_b.at[0]
    w_in = join_cols(refs[6 : 6 + nz])
    w_down = join_rows(refs[6 + nz : 6 + 2 * nz])
    rest = refs[6 + 2 * nz :]
    if carry:
        give_ref, act_b, gpre_b, sum_ref, take_ref, stay_s, a2a_s, a2a_r = rest
        experts = lax.axis_size("expert")
        e = lax.axis_index("expert")
        peers = [(lax.axis_index("dp"), (e + j) % experts) for j in range(1, experts)]
        spread, settle = front_lanes(
            give_ref, None, take_ref, None, stay_s, a2a_s, a2a_r, give_ref.shape[2]
        )

        @pl.when(pl.program_id(0) == 0)
        def _():
            pl.semaphore_wait(greet(peers), len(peers))
            spread(0)

    else:
        act_b, gpre_b, sum_ref = rest
    cot_b = cot_b.at[0]
    hidden_rows(rows_b, cot_b, w_in, w_down, act_b, gpre_b)
    for v in loads:
        v.wait()

    @pl.when(c == 0)
    def _():
        for v in once:
            v.wait()

    for z in range(nz):
        cols = slice(z * FFT, (z + 1) * FFT)
        gdown = dot(act_a[:, cols], cot_a[...], TN) + dot(act_b[0, :, cols], cot_b[...], TN)
        sum_ref[z, 0, :FFT] = gdown.astype(bf16)
        gin = dot(gpre_a[:, cols], rows_a[...], TN) + dot(gpre_b[0, :, cols], rows_b[...], TN)
        sum_ref[z, 0, FFT:] = gin.astype(bf16)
    if carry:

        @pl.when(pl.program_id(0) == pl.num_programs(0) - 1)
        def _():
            settle(0)


def expert_b_call(rows, act_a, gpre_a, cots, w_in, w_down, nz, first, count, give=None, deps=()):
    _, total, width = rows.shape
    tile = nz * FFT
    hidden = w_in.shape[1]

    def cot(s):
        return pl.BlockSpec((1, total, width), lambda c: (s, 0, 0))

    mid_out = pl.BlockSpec((1, total, tile), lambda c: (c, 0, 0))
    carry = give is not None
    args = [rows, cots, act_a, gpre_a, rows, cots, *([w_in] * nz), *([w_down] * nz)]
    in_specs = [ANY] * 4 + [cot(1), cot(1)] + weight_specs(width, hidden, nz, first)
    out_specs = [
        mid_out,
        mid_out,
        pl.BlockSpec((nz, 1, 2 * FFT, width), lambda c: (0, c, 0, 0)),
    ]
    out_shape = [
        sds((count, total, tile), bf16),
        sds((count, total, tile), bf16),
        sds((nz, count, 2 * FFT, width), bf16),
    ]
    dma = pltpu.SemaphoreType.DMA
    scratch = []
    options = dict(vmem_limit_bytes=60 << 20)
    if carry:
        experts = give.shape[1]
        args.append(give)
        in_specs.append(ANY)
        out_specs.append(ANY)
        out_shape.append(sds((1, total, width), bf16))
        scratch = [dma((1,)), dma((1, experts - 1)), dma((1, experts - 1))]
        options.update(collective_id=3, has_side_effects=True)
    scratch += [pltpu.VMEM((total, width), bf16)] * 2
    scratch += [pltpu.VMEM((total, tile), bf16)] * 2 + [dma((4,))]
    return kernel_call(
        functools.partial(expert_b_body, nz=nz, carry=carry, first=first),
        args=args,
        deps=deps,
        grid=(count,),
        in_specs=in_specs,
        out_specs=out_specs,
        out_shape=out_shape,
        scratch_shapes=scratch,
        compiler_params=pltpu.CompilerParams(**options),
        cost_estimate=cost(20 * count << 30, 30 << 20),
    )


def back_body(*refs, heads, capacity, split):
    pieces = len(split)
    acts_a = refs[0]
    acts_b, gpres_b = refs[1 : 1 + pieces], refs[1 + pieces : 1 + 2 * pieces]
    gtok_ref = refs[1 + 2 * pieces]
    (
        w_in,
        w_down,
        qkv_ref,
        mixed_ref,
        after_ref,
        cot_ref,
        fo_ref,
        lse_ref,
        slot_ref,
        g_ref,
        d_ref,
        ga_ref,
        gtoks_ref,
        outs_ref,
        gw_ref,
        sums_ref,
        slab_g,
        slab_o,
        qkv_v,
        mixed_v,
        after_v,
        cot_v,
        fo_v,
        load_s,
        mid_s,
        w_s,
        save_s,
        stay_s,
        a2a_s,
        a2a_r,
    ) = refs[2 + 2 * pieces :]
    nz = lax.axis_size("dp")
    experts = lax.axis_size("expert")
    z = lax.axis_index("dp")
    e = lax.axis_index("expert")
    seqs, total, width = gtoks_ref.shape
    length = after_ref.shape[1]
    hidden = w_in.shape[1]
    tile = nz * FFT
    chunks = hidden // tile
    peers = [(z, (e + j) % experts) for j in range(1, experts)]

    def load(n, src, dst):
        return pltpu.make_async_copy(src, dst, load_s.at[n])

    early = [load(0, fo_ref, fo_v), load(1, qkv_ref.at[0], qkv_v.at[0])]
    for s in range(seqs):
        early += [
            load(2 + 3 * s, after_ref.at[s], after_v.at[s]),
            load(3 + 3 * s, cot_ref.at[s], cot_v.at[s]),
            load(4 + 3 * s, mixed_ref.at[s], mixed_v.at[s]),
        ]
    pl.semaphore_wait(greet(peers), len(peers))
    spread, settle = front_lanes(
        slab_g, slab_o, gtoks_ref, outs_ref, stay_s, a2a_s, a2a_r, capacity
    )

    def second(arrays, c):
        for arr, k in zip(arrays, split):
            if c < k:
                return arr.at[c]
            c -= k

    def products(mid_v, in_v, down_v, acc):
        jobs = []
        for n in range(1, 2 * seqs):
            for c in range(chunks):
                first = n % seqs == 0
                if n < seqs:
                    src = second(gpres_b, c)
                else:
                    src = acts_a.at[c] if first else second(acts_b, c)
                jobs.append((n, c, src))

        def fetch(k):
            n, c, src = jobs[k]
            slot = k % 2
            got = [pltpu.make_async_copy(src, mid_v.at[slot], mid_s.at[slot])]
            for zz in range(nz):
                at = (zz * chunks + c) * FFT
                if n < seqs:
                    pair = (w_in.at[:, at : at + FFT], in_v.at[slot, :, zz * FFT : (zz + 1) * FFT])
                else:
                    pair = (w_down.at[at : at + FFT], down_v.at[slot, zz * FFT : (zz + 1) * FFT])
                got.append(pltpu.make_async_copy(*pair, w_s.at[slot, zz]))
            return got

        step = slot_chunk(total)
        for c in fetch(0):
            c.start()
        for k, (n, c, _) in enumerate(jobs):
            if k + 1 < len(jobs):
                for v in fetch(k + 1):
                    v.start()
            for v in fetch(k):
                v.wait()
            slot = k % 2
            w, dims = (in_v[slot], NT) if n < seqs else (down_v[slot], NN)
            for a in range(0, total, step):
                term = dot(mid_v[slot, a : a + step], w, dims)
                if c == 0:
                    acc[a : a + step] = term
                else:
                    acc[a : a + step] += term
            if c == chunks - 1:
                slab = slab_g if n < seqs else slab_o
                for ee in range(experts):
                    slab[n % seqs, ee] = acc[ee * capacity : (ee + 1) * capacity].astype(bf16)
                spread(n)
            if k == 1:
                for v in early:
                    v.start()

    pl.run_scoped(
        products,
        pltpu.VMEM((2, total, tile), bf16),
        pltpu.VMEM((2, width, tile), bf16),
        pltpu.VMEM((2, tile, width), bf16),
        pltpu.VMEM((total, width), f32),
    )
    hs = width // heads
    pairs = heads // 2
    blk = min(BLK, length)

    def backward(back_v, ga_v, gm_v, d_v, dqa, doa):
        sums_ref[...] = jnp.zeros_like(sums_ref)
        saves = {}
        for s in range(seqs):
            if s:
                settle(s)
            fill = load(2 + 3 * seqs, gtoks_ref.at[s] if s else gtok_ref.at[0], back_v)
            fill.start()
            if s:
                again = load(1, qkv_ref.at[s], qkv_v.at[0])
                again.start()
            else:
                for v in early:
                    v.wait()
            fill.wait()
            starts = list(range(0, length, blk))

            def take(a, s=s):
                return take_rows(back_v[...], slot_ref[s, a : a + blk])

            ahead = take(0)
            for at, a in enumerate(starts):
                gt = ahead
                if at + 1 < len(starts):
                    ahead = take(starts[at + 1])
                rows = slice(a, a + blk)
                hat, r = norm_parts(after_v[s, rows].astype(f32))
                sums_ref[2:3] += jnp.sum(gt * hat, axis=0, keepdims=True)
                sums_ref[3:4] += jnp.sum(gt, axis=0, keepdims=True)
                g = gt * row(g_ref)
                ga = cot_v[s, rows].astype(f32) + r * (
                    g
                    - jnp.mean(g, axis=-1, keepdims=True)
                    - hat * jnp.mean(g * hat, axis=-1, keepdims=True)
                )
                ga_v[s, rows] = ga.astype(bf16)
                gm_v[0, rows] = dot(ga_v[s, rows], fo_v[...], NT).astype(bf16)
            gw = dot(mixed_v[s], ga_v[s], TN)
            if s == 0:
                gw_ref[...] = gw
            else:
                gw_ref[...] += gw
                again.wait()
                saves[s - 1].wait()
            keep = pltpu.make_async_copy(ga_v.at[s], ga_ref.at[s], save_s.at[0, s])
            keep.start()

            def pair(p, carry, s=s):
                def cols(t):
                    return pl.ds(pl.multiple_of(t * width + p * 2 * hs, 128), 2 * hs)

                one = pl.ds(s, 1)
                attn_bwd_body(
                    qkv_v.at[:, :, cols(0)],
                    qkv_v.at[:, :, cols(1)],
                    qkv_v.at[:, :, cols(2)],
                    mixed_v.at[one, :, cols(0)],
                    gm_v.at[:, :, cols(0)],
                    lse_ref.at[one, pl.ds(p, 1)],
                    d_v.at[:, :, :, cols(0)],
                    dqa,
                    doa,
                    blk=blk,
                    hs=hs,
                    scale=hs**-0.5,
                    depth=2,
                )
                return carry

            lax.fori_loop(0, pairs, pair, 0)
            saves[s] = pltpu.make_async_copy(d_v.at[0], d_ref.at[s], save_s.at[1, s])
            saves[s].start()
            keep.wait()
        saves[seqs - 1].wait()

    pl.run_scoped(
        backward,
        pltpu.VMEM((total, width), bf16),
        pltpu.VMEM((seqs, length, width), bf16),
        pltpu.VMEM((1, length, width), bf16),
        pltpu.VMEM((1, 3, length, width), bf16),
        pltpu.VMEM((2 * hs, length), f32),
        pltpu.VMEM((2, length, 2 * hs), bf16),
    )
    for n in range(seqs, 2 * seqs):
        settle(n)


def back_call(
    acts_a, acts_b, gpres_b, gtok, w_in, w_down, qkv, mixed, after, cot, fo, lse, slot_col, gain, heads, nz, experts, capacity
):
    seqs, length, width = after.shape
    total = experts * capacity
    dma = pltpu.SemaphoreType.DMA
    slab = (seqs, experts, capacity, width)
    split = [v.shape[0] for v in acts_b]
    three = pltpu.VMEM((seqs, length, width), bf16)
    return pl.pallas_call(
        functools.partial(back_body, heads=heads, capacity=capacity, split=split),
        in_specs=[ANY] * (2 + 2 * len(split) + 7) + [VM] * 3,
        out_specs=[ANY] * 4 + [VM] * 2,
        out_shape=[
            sds((seqs, 3, length, width), bf16),
            sds((seqs, length, width), bf16),
            sds((seqs, total, width), bf16),
            sds((seqs, total, width), bf16),
            sds((width, width), f32),
            sds((8, width), f32),
        ],
        scratch_shapes=[
            pltpu.VMEM(slab, bf16),
            pltpu.VMEM(slab, bf16),
            pltpu.VMEM((1, length, 3 * width), bf16),
            three,
            three,
            three,
            pltpu.VMEM((width, width), bf16),
            dma((3 + 3 * seqs,)),
            dma((2,)),
            dma((2, nz)),
            dma((2, seqs)),
            dma((2 * seqs,)),
            dma((2 * seqs, experts - 1)),
            dma((2 * seqs, experts - 1)),
        ],
        compiler_params=pltpu.CompilerParams(
            vmem_limit_bytes=62 << 20, collective_id=2, has_side_effects=True
        ),
        cost_estimate=cost(110 << 30, 60 << 20),
    )(
        acts_a, *acts_b, *gpres_b, gtok, w_in, w_down, qkv, mixed, after, cot, fo, lse, slot_col, gain
    )


GROUPS = 4


def last_body(*refs, seqs, per_seq, plan):
    (dw_ref, d_ref, xw_ref, x_ref, w_any, g_ref, b_ref) = refs[:7]
    gwo_ref, sums_ref, backs_any, slot_ref = refs[7:11]
    gx_ref, res_ref, gq_ref, go_ref, tot_ref = refs[11:16]
    rest = refs[16:]
    acc, low, pay, r1, r2, s2, r3, fin, w0, v1, w1, v2, w2, v3, w_ref, backs = rest[:16]
    send_s, recv_s, vs_s, vr_s, load_s = rest[16:]
    nz = lax.axis_size("dp")
    experts = lax.axis_size("expert")
    z = lax.axis_index("dp")
    e = lax.axis_index("expert")
    chips = experts // 2
    core = e % 2
    chip = e // 2
    mate = (z, chip * 2 + 1 - core)
    others = [(z, lax.rem(chip + j, chips) * 2 + core) for j in range(1, chips)]
    layers = [(lax.rem(z + j, nz), e) for j in range(1, nz)]
    peers = [mate] + others + layers
    width = x_ref.shape[2]
    step = pl.program_id(0)
    last = pl.num_programs(0) - 1
    s1 = r1

    def copy(src, dst, at, peer, sems=None):
        a, b = sems or (send_s, recv_s)
        return pltpu.make_async_remote_copy(
            src_ref=src,
            dst_ref=dst,
            send_sem=a.at[at],
            recv_sem=b.at[at],
            device_id=peer,
            device_id_type=MESH,
        )

    def stage(n, t):
        if n == 1:
            return [copy(pay.at[t, 1 - core], r1.at[t], (t, 0), mate)]
        if n == 2:
            return [
                copy(
                    s1.at[t, lax.rem(chip + j, chips)], r2.at[t, j - 1], (t, j), others[j - 1]
                )
                for j in range(1, chips)
            ]
        if n == 3:
            return [
                copy(
                    s2.at[t, lax.rem(z + j, nz)], r3.at[t, j - 1], (t, chips + j), layers[j - 1]
                )
                for j in range(1, nz)
            ]
        if n == 4:
            here = fin.at[t, core, chip]
            return [
                copy(here, here, (t, chips + nz + j), others[j - 1]) for j in range(1, chips)
            ]
        side = fin.at[t, core]
        return [copy(side, side, (t, 2 * chips + nz), mate)]

    def vector(n):
        sems = (vs_s, vr_s)
        if n == 1:
            return [copy(w0, v1, 0, mate, sems)]
        if n == 2:
            return [copy(w1, v2.at[j - 1], j, others[j - 1], sems) for j in range(1, chips)]
        return [copy(w2, v3.at[j - 1], chips + j, layers[j - 1], sems) for j in range(1, nz)]

    def start(n, t):
        for c in vector(n) if t is None else stage(n, t):
            c.start()

    def finish(n, t):
        for c in vector(n) if t is None else stage(n, t):
            c.wait()
        if t is None:
            if n == 1:
                w1[...] = w0[...] + v1[...]
            elif n == 2:
                line = w1[...]
                for j in range(1, chips):
                    line = line + v2[j - 1]
                w2[...] = line
            else:
                line = w2[...]
                for j in range(1, nz):
                    line = line + v3[j - 1]
                tot_ref[...] = line
            if n < 3:
                start(n + 1, None)
            return
        if n == 1:
            for k in range(chips):
                s1[t, k] = (pay[t, core, k].astype(f32) + r1[t, k].astype(f32)).astype(bf16)
        elif n == 2:
            part = s1[t, chip].astype(f32)
            for j in range(1, chips):
                part = part + r2[t, j - 1].astype(f32)
            s2[t] = part.astype(bf16)
        elif n == 3:
            part = s2[t, z].astype(f32)
            for j in range(1, nz):
                part = part + r3[t, j - 1].astype(f32)
            fin[t, core, chip] = part.astype(bf16)
        elif n == 5:
            piece = fin.shape[3]
            for c in range(2):
                for k in range(chips):
                    at = (c * chips + k) * piece
                    value = fin[t, c, k].astype(f32)
                    if t < 3:
                        gq_ref[at : at + piece, t * width : (t + 1) * width] = value
                    else:
                        go_ref[at : at + piece, :] = value
        if n < 5:
            start(n + 1, t)

    def pack(value, t):
        per = value.shape[0] // nz
        piece = pay.shape[4]
        for zz in range(nz):
            for c in range(2):
                for k in range(chips):
                    at = zz * per + (c * chips + k) * piece
                    pay[t, c, k, zz] = value[at : at + piece].astype(bf16)
        start(1, t)

    loads = [pltpu.make_async_copy(w_any, w_ref, load_s.at[0])]
    loads += [
        pltpu.make_async_copy(backs_any.at[s], backs.at[s], load_s.at[1 + s]) for s in range(seqs)
    ]

    @pl.when(step == 0)
    def _():
        for c in loads:
            c.start()
        pl.semaphore_wait(greet(peers), len(peers))
        pack(gwo_ref[...], 3)

    for n in range(3 * seqs):
        t, s = n // seqs, n % seqs

        @pl.when(step == n)
        def _(t=t, s=s):
            if t == 0:
                hat, _ = norm_parts(xw_ref[0].astype(f32))
                low[s] = (hat * g_ref[...] + b_ref[...]).astype(bf16)
            term = dot(low[s], dw_ref[0, 0], TN)
            if s == 0:
                acc[...] = term
            elif s < seqs - 1:
                acc[...] += term
            else:
                pack(acc[...] + term, t)

    base = 3 * seqs

    @pl.when(step == base)
    def _():
        loads[0].wait()
        w0[0:2] = jnp.zeros((2, width), f32)
        w0[2:8] = sums_ref[2:8]

    @pl.when((step >= base) & (step < base + seqs * per_seq))
    def _():
        hat, r = norm_parts(x_ref[0].astype(f32))
        gn = 0.0
        for t in range(3):
            gn = gn + dot(d_ref[0, t], w_ref[:, t * width : (t + 1) * width], NT)
        w0[0:1] += jnp.sum(gn * hat, axis=0, keepdims=True)
        w0[1:2] += jnp.sum(gn, axis=0, keepdims=True)
        g = gn * g_ref[...]
        gx_ref[0] = (
            r
            * (
                g
                - jnp.mean(g, axis=-1, keepdims=True)
                - hat * jnp.mean(g * hat, axis=-1, keepdims=True)
            )
        ).astype(bf16)

    base = base + seqs * per_seq

    @pl.when(step == base)
    def _():
        for c in loads[1:]:
            c.wait()

    @pl.when(step == base - 1)
    def _():
        start(1, None)

    for s in range(seqs):

        @pl.when((step >= base + s * per_seq) & (step < base + (s + 1) * per_seq))
        def _(s=s):
            res_ref[0] = take_rows(backs[s], slot_ref[0]).astype(bf16)

    for when, events in plan:

        @pl.when(step == when)
        def _(events=events):
            for n, t in events:
                finish(n, t)


def last_plan(seqs, per_seq):
    dw = 3 * seqs
    end = dw + 2 * seqs * per_seq - 1
    mid = dw + seqs * per_seq
    first = [
        (2, [(1, 3)]),
        (4, [(1, 0)]),
        (dw, [(1, 1)]),
        (dw + 2, [(1, 2)]),
        (dw + 4, [(2, 3)]),
        (dw + 6, [(2, 0)]),
        (dw + 7, [(3, 3)]),
        (mid, [(2, 1)]),
        (mid + 1, [(3, 0)]),
        (mid + 2, [(1, None), (2, 2), (4, 3)]),
        (mid + 3, [(3, 1)]),
        (mid + 4, [(2, None), (4, 0), (5, 3)]),
        (mid + 5, [(3, 2)]),
        (mid + 6, [(3, None), (4, 1), (5, 0)]),
        (end, [(4, 2), (5, 1), (5, 2)]),
    ]
    return [(min(a, end), b) for a, b in first]


def last_call(d, x, w, gain, bias, gwo, sums, backs, slot_col, experts, nz):
    seqs, length, width = x.shape
    blk = min(BLK, length)
    per_seq = length // blk
    total = backs.shape[1]
    dw = 3 * seqs
    mid = dw + seqs * per_seq
    chips = experts // 2
    piece = width // nz // experts
    per = width // nz
    dma = pltpu.SemaphoreType.DMA
    once = pl.Buffered(1)

    def keep(*shape):
        return pl.BlockSpec(shape, lambda r: (0,) * len(shape), pipeline_mode=once)

    def at(first, r):
        n = jnp.clip(r - first, 0, seqs * per_seq - 1)
        return n // per_seq, n % per_seq

    def dw_at(r):
        n = jnp.minimum(r, dw - 1)
        return n % seqs, n // seqs, 0, 0

    def rows(first):
        return pl.BlockSpec((1, blk, width), lambda r: (*at(first, r), 0))

    def d_at(r):
        s, b = at(dw, r)
        return s, 0, b, 0

    steps = mid + seqs * per_seq
    in_specs = [
        pl.BlockSpec((1, 1, length, width), dw_at),
        pl.BlockSpec((1, 3, blk, width), d_at),
        pl.BlockSpec((1, length, width), lambda r: (jnp.minimum(r, seqs - 1), 0, 0)),
        rows(dw),
        ANY,
        keep(1, width),
        keep(1, width),
    ]
    in_specs += [keep(width, width), keep(8, width), ANY]
    in_specs += [pl.BlockSpec((1, blk, 1), lambda r: (*at(mid, r), 0))]
    return pl.pallas_call(
        functools.partial(last_body, seqs=seqs, per_seq=per_seq, plan=last_plan(seqs, per_seq)),
        grid=(steps,),
        in_specs=in_specs,
        out_specs=[rows(dw), rows(mid), keep(per, 3 * width), keep(per, width), keep(8, width)],
        out_shape=[
            sds((seqs, length, width), bf16),
            sds((seqs, length, width), bf16),
            sds((per, 3 * width), f32),
            sds((per, width), f32),
            sds((8, width), f32),
        ],
        scratch_shapes=[
            pltpu.VMEM((width, width), f32),
            pltpu.VMEM((seqs, length, width), bf16),
            pltpu.VMEM((GROUPS, 2, chips, nz, piece, width), bf16),
            pltpu.VMEM((GROUPS, chips, nz, piece, width), bf16),
            pltpu.VMEM((GROUPS, chips - 1, nz, piece, width), bf16),
            pltpu.VMEM((GROUPS, nz, piece, width), bf16),
            pltpu.VMEM((GROUPS, nz - 1, piece, width), bf16),
            pltpu.VMEM((GROUPS, 2, chips, piece, width), bf16),
            pltpu.VMEM((8, width), f32),
            pltpu.VMEM((8, width), f32),
            pltpu.VMEM((8, width), f32),
            pltpu.VMEM((chips - 1, 8, width), f32),
            pltpu.VMEM((8, width), f32),
            pltpu.VMEM((nz - 1, 8, width), f32),
            pltpu.VMEM((width, 3 * width), bf16),
            pltpu.VMEM((seqs, total, width), bf16),
        ]
        + [dma((GROUPS, 2 * chips + nz + 1))] * 2
        + [dma((chips + nz,))] * 2
        + [dma((1 + seqs,))],
        compiler_params=pltpu.CompilerParams(
            vmem_limit_bytes=62 << 20, collective_id=1, has_side_effects=True
        ),
        cost_estimate=cost(50 << 30, 150 << 20),
    )(
        d,
        d,
        x,
        x,
        w,
        gain.reshape(1, -1),
        bias.reshape(1, -1),
        gwo,
        sums,
        backs,
        slot_col,
    )


def close_body(*refs, counts):
    ga_ref, dx_ref, after_ref, back_ref, gq_ref, go_ref = refs[:6]
    n = len(counts)
    downs, ins = refs[6 : 6 + n], refs[6 + n : 6 + 2 * n]
    gx_out, res_out, gq_out, go_out, down_out, in_out = refs[6 + 2 * n :]
    step = pl.program_id(0)
    gx_out[...] = ga_ref[...].astype(f32) + dx_ref[...].astype(f32)
    res_out[...] = after_ref[...].astype(f32) + back_ref[...].astype(f32)
    gq_out[...] = gq_ref[...]
    go_out[...] = go_ref[...]
    at = 0
    for k, down, gin in zip(counts, downs, ins):
        down_out[at : at + k] = down[0].astype(f32)

        @pl.when((step >= at) & (step < at + k))
        def _(gin=gin):
            in_out[...] = gin[0, 0].astype(f32).T

        at += k


def close_call(ga, dx, after, back, gq, go, sums):
    seqs, length, width = ga.shape
    blk = min(BLK, length)
    per_seq = length // blk
    steps = seqs * per_seq
    counts = [v.shape[1] for v in sums]
    chunks = sum(counts)
    rows = pl.BlockSpec((1, blk, width), lambda r: (r // per_seq, r % per_seq, 0))

    def split(v):
        return pl.BlockSpec((v.shape[0] // steps, v.shape[1]), lambda r: (r, 0))

    def down(v):
        return pl.BlockSpec((1, v.shape[1], FFT // steps, width), lambda r: (0, 0, r, 0))

    def inward(n):
        lo = sum(counts[:n])
        return pl.BlockSpec(
            (1, 1, FFT, width), lambda r: (0, jnp.clip(r - lo, 0, counts[n] - 1), 1, 0)
        )

    return pl.pallas_call(
        functools.partial(close_body, counts=counts),
        grid=(steps,),
        in_specs=[rows] * 4
        + [split(gq), split(go)]
        + [down(v) for v in sums]
        + [inward(n) for n in range(len(sums))],
        out_specs=[
            rows,
            rows,
            split(gq),
            split(go),
            pl.BlockSpec((chunks, FFT // steps, width), lambda r: (0, r, 0)),
            pl.BlockSpec((width, FFT), lambda r: (0, jnp.minimum(r, chunks - 1))),
        ],
        out_shape=[
            sds((seqs, length, width), f32),
            sds((seqs, length, width), f32),
            sds(gq.shape, f32),
            sds(go.shape, f32),
            sds((chunks, FFT, width), f32),
            sds((width, chunks * FFT), f32),
        ],
        compiler_params=params(60),
        cost_estimate=cost(8 << 30, 40 << 20),
    )(ga, dx, after, back, gq, go, *sums, *sums)


def exchange(parts):
    got = lax.all_to_all(parts, "expert", split_axis=0, concat_axis=0, tiled=True)
    return got.reshape(-1, parts.shape[-1])


def on_device(
    tokens_in,
    buckets,
    ln1_gain,
    ln1_bias,
    w_qkv,
    w_out,
    ln2_gain,
    ln2_bias,
    w_in,
    w_down,
    cotangent,
):
    experts = lax.axis_size("expert")
    nz = lax.axis_size("dp")
    seqs, length, width = tokens_in.shape
    capacity = 5 * length // (4 * experts)
    total = experts * capacity
    w_in_local = w_in[0]
    w_down_local = w_down[0]
    hidden = w_in_local.shape[1]
    chunks = hidden // (nz * FFT)

    qkv, full_qkv, full_out, mixed, after, lse, slot_col, cots, rows, act_a, gpre_a, give = front_call(
        tokens_in,
        ln1_gain,
        ln1_bias,
        ln2_gain,
        ln2_bias,
        w_qkv,
        w_out,
        buckets,
        cotangent,
        w_in_local,
        w_down_local,
        HEADS,
        nz,
        experts,
        capacity,
    )
    last = ()
    acts, gpres, totals = [], [], []
    for first, many in ((0, 1), (1, chunks - 1)):
        made = expert_b_call(
            rows,
            act_a,
            gpre_a,
            cots,
            w_in_local,
            w_down_local,
            nz,
            first,
            many,
            give=give if first else None,
            deps=last,
        )
        last = (made[0],)
        acts.append(made[0])
        gpres.append(made[1])
        totals.append(lax.psum_scatter(made[2], "dp", scatter_dimension=0, tiled=True))
    gtok_a = made[3]
    d, ga, _, outs, gwo, sums = back_call(
        act_a,
        acts,
        gpres,
        gtok_a,
        w_in_local,
        w_down_local,
        qkv,
        mixed,
        after,
        cotangent,
        full_out,
        lse,
        slot_col,
        ln2_gain,
        HEADS,
        nz,
        experts,
        capacity,
    )
    dx, back, gq, go, sums = last_call(
        d,
        tokens_in,
        full_qkv,
        ln1_gain,
        ln1_bias,
        gwo,
        sums,
        outs,
        slot_col,
        experts,
        nz,
    )
    gxs, results, gq, go, gdown, gin = close_call(ga, dx, after, back, gq, go, totals)
    mine = lax.dynamic_slice_in_dim(
        sums, lax.axis_index("dp") * (width // nz), width // nz, axis=1
    )
    return (
        results,
        gxs,
        mine[0],
        mine[1],
        gq,
        go,
        mine[2],
        mine[3],
        gin[None],
        gdown.reshape(1, hidden // nz, width),
    )


def solution(mesh):
    placed = (
        P(("dp", "expert"), None, None),
        P(("dp", "expert"), None),
        P(),
        P(),
        P("dp", None),
        P("dp", None),
        P(),
        P(),
        P("expert", None, None),
        P("expert", None, None),
        P(("dp", "expert"), None, None),
    )
    return jax.shard_map(
        on_device,
        mesh=mesh,
        in_specs=placed,
        out_specs=(
            P(("dp", "expert"), None, None),
            P(("dp", "expert"), None, None),
            P("dp"),
            P("dp"),
            P("dp", None),
            P("dp", None),
            P("dp"),
            P("dp"),
            P("expert", None, "dp"),
            P("expert", "dp", None),
        ),
        check_vma=False,
    )
```
